128 devices in a mesh: section: 2 (over x_hi), dp: 16 (over x_lo, z, core), shard: 4 (over y).
Axes of the slice: x: 4 (x_hi: 2, x_lo: 2; x = x_hi * 2 + x_lo), y: 4, z: 4, core: 2. Of those that a mesh axis runs over, the one named last changes fastest.
Arguments:
- tokens: bfloat16 [128, 128, 1536], P(('dp', 'shard')), may hold values from -6 to 6
- cotangent: bfloat16 [128, 128, 1536], P(('dp', 'shard')), may hold values from -6 to 6
- lengths: int32 [128], P(('dp', 'shard')), may hold values from 1 to 128, 12288 in all
- norm_gain: bfloat16 [2, 1536], P('section', 'shard'), may hold values from 0.5 to 1.5
- in_weight: bfloat16 [2, 1536, 6448], P('section', 'shard'), may hold values from -0.15625 to 0.15625
- conv_weight: bfloat16 [2, 4, 3328], P('section', None, 'shard'), may hold values from -3 to 3
- conv_bias: bfloat16 [2, 3328], P('section', 'shard'), may hold values from -3 to 3
- dt_bias: bfloat16 [2, 48], P('section'), may hold values from -6 to -2
- a_log: bfloat16 [2, 48], P('section'), may hold values from 0 to 2
- d_skip: bfloat16 [2, 48], P('section'), may hold values from 0.5 to 1.5
- gate_gain: bfloat16 [2, 3072], P('section', 'shard'), may hold values from 0.5 to 1.5
- out_weight: bfloat16 [2, 3072, 1536], P('section', 'shard'), may hold values from -0.109375 to 0.109375
Outputs:
- ends: float32 [2, 128, 128, 1536], P('section', ('dp', 'shard'))
- grad_norm_gain: float32 [2, 1536], P('section', 'shard')
- grad_in_weight: float32 [2, 1536, 6448], P('section', 'shard')
- grad_conv_weight: float32 [2, 4, 3328], P('section', None, 'shard')
- grad_conv_bias: float32 [2, 3328], P('section', 'shard')
- grad_dt_bias: float32 [2, 48], P('section')
- grad_a_log: float32 [2, 48], P('section')
- grad_d_skip: float32 [2, 48], P('section')
- grad_gate_gain: float32 [2, 3072], P('section', 'shard')
- grad_out_weight: float32 [2, 3072, 1536], P('section', 'shard')
The draws below stay inside these ranges and needn't reach their ends.
Inputs may be any that keep to these rules, and one draw needn't show every extreme that they name: `lengths`: some sequence has all 128 positions live.
All inputs are finite; a program needn't handle non-finite values. No bound on the sum of `lengths` on one device may be relied on, other than what follows from the above.
Results may differ from the reference program's by a relative error of at most 0.015.
Values may be sent and summed in bfloat16 or wider, within the bound.
No kernel may reach another device: no remote copies, remote signals or barrier semaphores. Data moves between devices by JAX's collectives and lax.ppermute only.
A program may use at most 704 MiB of HBM per device.

```python
import math
import jax
import jax.numpy as jnp
import numpy as np
from jax import lax

D = 1536
HEADS = 48
KCONV = 4
SPAN = 256
LEN = 128
INNER = 3072
CONVCH = 3328
PROJ = 6448
SEQS = 128


def steps_of(stream_key, dims, split, smallest, top_value):
    factor_of, own = 1.0, jax.random.fold_in(stream_key, 6)
    for position, parts in split:
        draws = jnp.exp(jax.random.uniform(jax.random.fold_in(own, position), (parts,), jnp.float32, smallest / len(split), top_value / len(split)))
        factor_of = factor_of * jnp.repeat(draws, dims[position] // parts).reshape([-1 if axis == position else 1 for axis in range(len(dims))])
    return factor_of


def split_up(number_of, total, reach, lean):
    loads = [(1 << 20) // math.isqrt(standing ** lean) + 1 for standing in range(2, number_of + 1)]
    rest, given = total - reach - (number_of - 1), [1] * (number_of - 1)
    while rest > 0:
        free = [i for i in range(number_of - 1) if given[i] < reach]
        mass, budget = sum([loads[i] for i in free]), rest
        for i in free:
            more = min(reach - given[i], max(1, budget * loads[i] // mass), rest)
            given[i] = given[i] + more
            rest = rest - more
    return np.array([reach] + given)


def ragged(key, number_of, total, limit, slope):
    if number_of == 2:
        one = jax.random.randint(key, (), max(1, total - limit), min(limit, total - 1) + 1)
        return jnp.stack([one, total - one])
    sizes = jnp.asarray(split_up(number_of, total, limit, slope), jnp.int32)
    twos = (number_of - 1) // 2
    donor, receiver = sizes[1:1 + 2 * twos:2], sizes[2:2 + 2 * twos:2]
    room = jnp.minimum(donor - 1, limit - receiver)
    moved = jax.random.randint(jax.random.fold_in(key, 1), (twos,), 0, 1 << 20) % (room + 1)
    sizes = sizes.at[1:1 + 2 * twos:2].set(donor - moved).at[2:2 + 2 * twos:2].set(receiver + moved)
    return sizes[jax.random.permutation(jax.random.fold_in(key, 2), number_of)]


def normal_values(stream_key, shape, deviation, reach, shards=(), kind=jnp.bfloat16):
    values = jax.random.normal(stream_key, shape, jnp.float32) * deviation
    if len(shards) > 0:
        values = steps_of(stream_key, shape, shards, -0.22, 0.18) * values
    return jnp.clip(values, min=-reach, max=reach).astype(kind)


def setup_inputs(seed: int = 0) -> dict:
    key_list = jax.random.split(jax.random.key(seed), 13)
    return {
        "tokens": normal_values(key_list[0], (SEQS, LEN, D), 1.0, 6.0, ((0, 64),)),
        "cotangent": normal_values(key_list[1], (SEQS, LEN, D), 1.0, 6.0, ((0, 64),)),
        "lengths": ragged(key_list[2], SEQS, SEQS * LEN * 3 // 4, LEN, 2).astype(jnp.int32),
        "norm_gain": jnp.clip(1.0 + 0.1 * jax.random.normal(key_list[3], (2, D), jnp.float32), 0.5, 1.5).astype(jnp.bfloat16),
        "in_weight": normal_values(key_list[4], (2, D, PROJ), D ** -0.5, 0.15625, ((0, 2), (1, 4))),
        "conv_weight": normal_values(key_list[5], (2, KCONV, CONVCH), KCONV ** -0.5, 3.0, ((0, 2), (2, 4))),
        "conv_bias": normal_values(key_list[6], (2, CONVCH), 0.5, 3.0, ((0, 2), (1, 4))),
        "dt_bias": jnp.clip(-6.0 + 4.0 * jax.random.uniform(key_list[7], (2, HEADS), jnp.float32) ** steps_of(key_list[7], (2, HEADS), ((0, 2),), -0.2, 0.2), -6.0, -2.0).astype(jnp.bfloat16),
        "a_log": jnp.clip(2.0 * jax.random.uniform(key_list[8], (2, HEADS), jnp.float32) ** steps_of(key_list[8], (2, HEADS), ((0, 2),), -0.2, 0.2), 0.0, 2.0).astype(jnp.bfloat16),
        "d_skip": jnp.clip(0.5 + 1.0 * jax.random.uniform(key_list[9], (2, HEADS), jnp.float32) ** steps_of(key_list[9], (2, HEADS), ((0, 2),), -0.2, 0.2), 0.5, 1.5).astype(jnp.bfloat16),
        "gate_gain": jnp.clip(1.0 + 0.1 * jax.random.normal(key_list[10], (2, INNER), jnp.float32), 0.5, 1.5).astype(jnp.bfloat16),
        "out_weight": normal_values(key_list[11], (2, INNER, D), INNER ** -0.5, 0.109375, ((0, 2), (1, 4))),
    }


@jax.custom_vjp
def low(v):
    return lax.optimization_barrier(v.astype(jnp.bfloat16)).astype(jnp.float32)

@jax.custom_vjp
def low_back(v):
    return v

def low_keep(v):
    return (low(v), None)

def low_pass(kept, grad):
    return (grad,)

def back_keep(v):
    return (v, None)

def back_low(kept, grad):
    return (low(grad),)
low.defvjp(low_keep, low_pass)
low_back.defvjp(back_keep, back_low)

def scan_heads(values, inbound, outbound, step_size, rate):
    length = values.shape[0]
    heads = values.shape[1]
    head_dim = values.shape[2]
    state = inbound.shape[1]
    block_len = min(SPAN, length)
    blocks = length // block_len
    highest = lax.Precision.HIGHEST
    running = jnp.cumsum((step_size * rate[None, :]).reshape(blocks, block_len, heads), axis=1)
    scaled = (values * step_size[:, :, None]).reshape(blocks, block_len, heads, head_dim)
    keys_in = inbound.reshape(blocks, block_len, state)
    queries = outbound.reshape(blocks, block_len, state)
    scores = jnp.einsum('cqn,csn->cqs', queries, keys_in, precision=highest)
    causal = jnp.arange(block_len)[:, None] >= jnp.arange(block_len)[None, :]
    gaps = running[:, :, None, :] - running[:, None, :, :]
    decays = jnp.exp(jnp.where(causal[None, :, :, None], gaps, -1e+30))
    inner = jnp.einsum('cqs,cqsh,cshp->cqhp', scores, decays, scaled, precision=highest)
    tails = jnp.exp(running[:, -1:, :] - running)
    states = jnp.einsum('csn,csh,cshp->chpn', keys_in, tails, scaled, precision=highest)
    block_decay = jnp.exp(running[:, -1, :])

    def carry_state(carried, item):
        return (carried * item[0][:, None, None] + item[1], carried)
    _, before = lax.scan(carry_state, jnp.zeros((heads, head_dim, state), jnp.float32), (block_decay, states))
    outer = jnp.einsum('cqn,cqh,chpn->cqhp', queries, jnp.exp(running), before, precision=highest)
    return (inner + outer).reshape(length, heads, head_dim)

def mixer_block(params, inputs, row_mask):
    norm_gain, in_weight, conv_weight, conv_bias, dt_bias, a_log, d_skip, gate_gain, out_weight = params
    highest = lax.Precision.HIGHEST
    length = inputs.shape[0]
    inner_width = out_weight.shape[0]
    heads = dt_bias.shape[0]
    head_dim = inner_width // heads
    state = (in_weight.shape[1] - 2 * inner_width - heads) // 2
    normed = inputs * lax.rsqrt(lax.optimization_barrier(jnp.mean(inputs * inputs, axis=-1, keepdims=True)) + 1e-05) * norm_gain
    projected = low_back(jnp.dot(low(normed), in_weight, precision=highest))
    gate_in = projected[:, :inner_width]
    conv_in = projected[:, inner_width:2 * inner_width + 2 * state]
    step_raw = projected[:, 2 * inner_width + 2 * state:]
    padded = jnp.pad(conv_in, ((KCONV - 1, 0), (0, 0)))
    convolved = conv_bias[None, :] + jnp.zeros_like(conv_in)
    for offset in range(KCONV):
        convolved = convolved + padded[offset:offset + length] * conv_weight[offset][None, :]
    mixed = jax.nn.silu(convolved)
    values = mixed[:, :inner_width].reshape(length, heads, head_dim)
    inbound = mixed[:, inner_width:inner_width + state]
    outbound = mixed[:, inner_width + state:]
    step_size = jax.nn.softplus(step_raw + dt_bias[None, :])
    rate = -jnp.exp(a_log)
    scanned = scan_heads(values, inbound, outbound, step_size, rate) + d_skip[None, :, None] * values
    gated = scanned.reshape(length, inner_width) * jax.nn.silu(gate_in)
    normed_out = gated * lax.rsqrt(lax.optimization_barrier(jnp.mean(gated * gated, axis=-1, keepdims=True)) + 1e-05) * gate_gain
    branch = low_back(jnp.dot(low(normed_out), out_weight, precision=highest))
    return inputs + row_mask[:, None] * branch

def reference(tokens, cotangent, lengths, norm_gain, in_weight, conv_weight, conv_bias, dt_bias, a_log, d_skip, gate_gain, out_weight):
    params_all = tuple((array.astype(jnp.float32) for array in (norm_gain, in_weight, conv_weight, conv_bias, dt_bias, a_log, d_skip, gate_gain, out_weight)))
    row_masks = (jnp.arange(LEN, dtype=jnp.int32)[None, :] < lengths[:, None]).astype(jnp.float32)

    def two_layers(params, inputs, row_mask):
        first = tuple((array[0] for array in params))
        second = tuple((array[1] for array in params))
        middle = low_back(low(mixer_block(first, inputs, row_mask)))
        return mixer_block(second, middle, row_mask)
    saved = jax.checkpoint(two_layers)

    def forward(params, inputs):
        return lax.map(lambda item: saved(params, item[0], item[1]), (inputs, row_masks))
    result, pullback = jax.vjp(forward, params_all, tokens.astype(jnp.float32))
    param_grads, input_grad = pullback(cotangent.astype(jnp.float32))
    ends = jnp.stack([input_grad, result])
    return (ends, param_grads[0], param_grads[1], param_grads[2], param_grads[3], param_grads[4], param_grads[5], param_grads[6], param_grads[7], param_grads[8])
```

```python
import jax
import jax.numpy as jnp
from jax import lax
from jax.experimental import pallas as pl
from jax.experimental.pallas import tpu as pltpu
from jax.sharding import PartitionSpec as P

F32 = jnp.float32
BF16 = jnp.bfloat16
HI = lax.Precision.HIGHEST
EPS = 1e-05
T = 128
LANES = 128
HEAD = 64
SLOTS = 4
ROWS = SLOTS * T
PAIRS = 6
VMEM_LIMIT = 56 * 1024 * 1024


def sigmoid(v):
    return 0.5 * jnp.tanh(0.5 * v) + 0.5


def softplus(v):
    return jnp.maximum(v, 0.0) + jnp.log1p(jnp.exp(-jnp.abs(v)))


def dot(a, b):
    return jnp.dot(a, b, preferred_element_type=F32)


def dot_nt(a, b, precision=None):
    return lax.dot_general(
        a, b, (((1,), (1,)), ((), ())), preferred_element_type=F32, precision=precision
    )


def dot_tn(a, b, precision=None):
    return lax.dot_general(
        a, b, (((0,), (0,)), ((), ())), preferred_element_type=F32, precision=precision
    )


def iota(axis):
    return lax.broadcasted_iota(jnp.int32, (T, LANES), axis)


def shift_down(v, steps):
    return jnp.where(iota(0) >= steps, pltpu.roll(v, steps, 0), 0.0)


def shift_up(v, steps):
    return jnp.where(iota(0) < T - steps, pltpu.roll(v, T - steps, 0), 0.0)


def conv_taps(cin):
    return [shift_down(cin, 3), shift_down(cin, 2), shift_down(cin, 1), cin]


def conv_sum(taps, par):
    total = par[4:5, :] + taps[0] * par[0:1, :]
    for k in range(1, 4):
        total = total + taps[k] * par[k : k + 1, :]
    return total


def conv_back(dcv, par):
    total = dcv * par[3:4, :]
    for m in range(1, 4):
        total = total + shift_up(dcv, m) * par[3 - m : 4 - m, :]
    return total


def column_sum(v):
    return jnp.sum(v, axis=0, keepdims=True)


def slot(k):
    return slice(k * T, (k + 1) * T)


def tri(lower):
    if lower:
        return (iota(0) >= iota(1)).astype(F32)
    return (iota(0) <= iota(1)).astype(F32)


def step_prep(k, pbc, dtp, run_col, run_row, step_wide):
    step = softplus(pbc[slot(k), 256:384] + dtp[0:1, :])
    run = jnp.dot(tri(True), step * dtp[1:2, :], precision=HI, preferred_element_type=F32)
    run_row[k] = jnp.transpose(run)
    left = iota(1) < HEAD
    for p in range(PAIRS):
        a, b = 2 * p, 2 * p + 1
        run_col[a, slot(k), :] = jnp.broadcast_to(run[:, a : a + 1], (T, LANES))
        run_col[b, slot(k), :] = jnp.broadcast_to(run[:, b : b + 1], (T, LANES))
        step_wide[p, slot(k), :] = jnp.where(
            left,
            jnp.broadcast_to(step[:, a : a + 1], (T, LANES)),
            jnp.broadcast_to(step[:, b : b + 1], (T, LANES)),
        )
    return step


def halves(v):
    left = iota(1) < HEAD
    zero = jnp.zeros_like(v)
    return jnp.concatenate([jnp.where(left, v, zero), jnp.where(left, zero, v)], axis=0)


def forward_kernel(with_grad, *refs):
    xs = refs[:SLOTS]
    refs = refs[SLOTS:]
    if with_grad:
        gs = refs[:SLOTS]
        refs = refs[SLOTS:]
    (gain, wg, wv, wbc, wout, pv, pbcv, dtp) = refs[:8]
    refs = refs[8:]
    outs = refs[:SLOTS]
    (stats, normed, proj, y_out, pbc) = refs[SLOTS : SLOTS + 5]
    (scores, run_col, run_row, step_wide, u_all, square, cross, *more) = refs[SLOTS + 5 :]
    i = pl.program_id(0)

    @pl.when(i == 0)
    def _prep():
        for k in range(SLOTS):
            x = xs[k][...].astype(F32)
            scale = lax.rsqrt(jnp.mean(x * x, axis=1, keepdims=True) + EPS)
            normed[slot(k), :] = (x * scale * gain[...]).astype(BF16)
            if with_grad:
                more[0][slot(k), :] = gs[k][...]
        pbc[...] = dot(
            normed[...], jnp.concatenate([wbc[0], wbc[1], wbc[2]], axis=1)
        )
        for k in range(SLOTS):
            cv = conv_sum(conv_taps(pbc[slot(k), 0:128]), pbcv[:, 0:128])
            inbound = cv * sigmoid(cv)
            cv = conv_sum(conv_taps(pbc[slot(k), 128:256]), pbcv[:, 128:256])
            outbound = cv * sigmoid(cv)
            scores[k] = dot_nt(outbound, inbound, HI) * tri(True)
            step_prep(k, pbc, dtp, run_col, run_row, step_wide)
        square[...] = jnp.zeros_like(square)
        cross[...] = jnp.zeros_like(cross)

    @pl.when(i > 0)
    def _pair():
        p = i - 1
        proj[0] = dot(normed[...], jnp.concatenate([wg[0], wv[0]], axis=1))
        par = pv[...]
        if with_grad:
            q_all = dot_nt(more[0][...], wout[pl.ds(pl.multiple_of(p * T, T), T), :])
        for k in range(SLOTS):
            gate = proj[0, slot(k), 0:128]
            cv = conv_sum(conv_taps(proj[0, slot(k), 128:256]), par)
            values = cv * sigmoid(cv)
            scaled = (values * step_wide[p, slot(k), :]).astype(BF16)
            weights = []
            for h in range(2):
                gap = run_col[2 * p + h, slot(k), :] - run_row[k, pl.ds(2 * p + h, 1), :]
                decay = jnp.exp(jnp.minimum(gap, 0.0))
                weights.append((scores[k] * decay).astype(BF16))
            y = dot(jnp.concatenate(weights, axis=1), halves(scaled))
            y_out[0, slot(k), :] = y
            scanned = y + par[6:7, :] * values
            gated = scanned * (gate * sigmoid(gate))
            square[slot(k), :] += gated * gated
            scaled_out = gated * par[5:6, :]
            u_all[p, slot(k), :] = scaled_out.astype(BF16)
            if with_grad:
                cross[slot(k), :] += q_all[slot(k), :] * scaled_out

    @pl.when(i == PAIRS)
    def _finish():
        u = jnp.concatenate([u_all[p] for p in range(PAIRS)], axis=1)
        width = wout.shape[1]
        for n in range(0, width, 512):
            part = dot(u, wout[:, n : n + 512]).astype(BF16)
            for k in range(SLOTS):
                outs[k][:, n : n + 512] = part[slot(k), :]
        ones = jnp.ones((8, LANES), F32)
        stats[0] = dot_nt(ones, square[...], HI)
        stats[1] = dot_nt(ones, cross[...], HI)


def const_spec(shape):
    zeros = (0,) * len(shape)
    return pl.BlockSpec(shape, lambda i: zeros)


def pair_of(i):
    return jnp.clip(i - 1, 0, PAIRS - 1)


def forward(x_slots, g_slots, w, wout, gain, pv, pbcv, dtp):
    width = x_slots[0].shape[1]
    inner = wout.shape[0]
    with_grad = g_slots is not None
    xg = list(x_slots) + (list(g_slots) if with_grad else [])
    in_specs = [const_spec((T, width)) for _ in xg] + [
        const_spec((1, width)),
        pl.BlockSpec((1, width, LANES), lambda i: (pair_of(i), 0, 0)),
        pl.BlockSpec((1, width, LANES), lambda i: (PAIRS + pair_of(i), 0, 0)),
        pl.BlockSpec((4, width, LANES), lambda i: (3, 0, 0)),
        const_spec((inner, width)),
        pl.BlockSpec((8, LANES), lambda i: (0, pair_of(i))),
        const_spec((8, 256)),
        const_spec((8, LANES)),
    ]
    out_shape = [jax.ShapeDtypeStruct((T, width), BF16) for _ in range(SLOTS)] + [
        jax.ShapeDtypeStruct((2, 8, ROWS), F32),
        jax.ShapeDtypeStruct((ROWS, width), BF16),
        jax.ShapeDtypeStruct((PAIRS, ROWS, 256), F32),
        jax.ShapeDtypeStruct((PAIRS, ROWS, LANES), F32),
        jax.ShapeDtypeStruct((ROWS, 384), F32),
    ]
    out_specs = [const_spec((T, width)) for _ in range(SLOTS)] + [
        const_spec((2, 8, ROWS)),
        const_spec((ROWS, width)),
        pl.BlockSpec((1, ROWS, 256), lambda i: (pair_of(i), 0, 0)),
        pl.BlockSpec((1, ROWS, LANES), lambda i: (pair_of(i), 0, 0)),
        const_spec((ROWS, 384)),
    ]
    scratch = [
        pltpu.VMEM((SLOTS, T, T), F32),
        pltpu.VMEM((2 * PAIRS, ROWS, LANES), F32),
        pltpu.VMEM((SLOTS, T, LANES), F32),
        pltpu.VMEM((PAIRS, ROWS, LANES), F32),
        pltpu.VMEM((PAIRS, ROWS, LANES), BF16),
        pltpu.VMEM((ROWS, LANES), F32),
        pltpu.VMEM((ROWS, LANES), F32),
    ]
    if with_grad:
        scratch.append(pltpu.VMEM((ROWS, width), BF16))
    res = pl.pallas_call(
        lambda *refs: forward_kernel(with_grad, *refs),
        grid=(PAIRS + 1,),
        in_specs=in_specs,
        out_specs=out_specs,
        out_shape=out_shape,
        scratch_shapes=scratch,
        compiler_params=pltpu.CompilerParams(vmem_limit_bytes=VMEM_LIMIT),
        name="layer_forward",
    )(*xg, gain, w, w, w, wout, pv, pbcv, dtp)
    return res[:SLOTS], res[SLOTS], res[SLOTS + 1 :]


def head_columns(p):
    target = 2 * p + (iota(0) >= HEAD).astype(jnp.int32)
    one = (iota(1) == target).astype(BF16)
    return jnp.concatenate([one, one], axis=0)


def head_sum(v, columns):
    high = v.astype(BF16)
    low = (v - high.astype(F32)).astype(BF16)
    return dot(jnp.concatenate([high, low], axis=1), columns)


def backward_kernel(*refs):
    gs = refs[:SLOTS]
    (row_stats, normed_t, proj, y_in, pbc, wg, wv, wbc, wout, pv, pbcv, dtp) = refs[
        SLOTS : SLOTS + 12
    ]
    refs = refs[SLOTS + 12 :]
    outs = refs[:SLOTS]
    (grad_g, grad_v, grad_bc, grad_out, small, small_bc, small_dt) = refs[SLOTS : SLOTS + 7]
    (
        g_all,
        scores_t,
        mixed,
        run_col,
        run_row,
        step_wide,
        step_all,
        scale_row,
        cross_row,
        dscores_t,
        dstep,
        drun,
        total,
        u_all,
        d_all,
        d_bc,
    ) = refs[SLOTS + 7 :]
    i = pl.program_id(0)

    @pl.when(i == 0)
    def _prep():
        for k in range(SLOTS):
            g_all[slot(k), :] = gs[k][...]
            cv = conv_sum(conv_taps(pbc[slot(k), 0:128]), pbcv[:, 0:128])
            inbound = cv * sigmoid(cv)
            cv = conv_sum(conv_taps(pbc[slot(k), 128:256]), pbcv[:, 128:256])
            outbound = cv * sigmoid(cv)
            mixed[0, slot(k), :] = inbound
            mixed[1, slot(k), :] = outbound
            scores_t[k] = dot_nt(inbound, outbound, HI) * tri(False)
            step_all[slot(k), :] = step_prep(k, pbc, dtp, run_col, run_row, step_wide)
            scale_row[slot(k), :] = jnp.transpose(
                jnp.broadcast_to(row_stats[k, 0:1, :], (T, LANES))
            )
            cross_row[slot(k), :] = jnp.transpose(
                jnp.broadcast_to(row_stats[k, 1:2, :], (T, LANES))
            )
        dscores_t[...] = jnp.zeros_like(dscores_t)
        dstep[...] = jnp.zeros_like(dstep)
        drun[...] = jnp.zeros_like(drun)
        total[...] = jnp.zeros_like(total)

    @pl.when(i > 0)
    def _pair():
        p = i - 1
        par = pv[...]
        columns = head_columns(p)
        q_all = dot_nt(g_all[...], wout[...])
        sums = [jnp.zeros((1, LANES), F32) for _ in range(8)]
        for k in range(SLOTS):
            gate = proj[0, slot(k), 0:128]
            taps = conv_taps(proj[0, slot(k), 128:256])
            cv = conv_sum(taps, par)
            sig_c = sigmoid(cv)
            values = cv * sig_c
            sig_g = sigmoid(gate)
            silu_g = gate * sig_g
            y = y_in[0, slot(k), :]
            scanned = y + par[6:7, :] * values
            gated = scanned * silu_g
            grad_no = q_all[slot(k), :]
            scale = scale_row[slot(k), :]
            dgated = scale * (grad_no * par[5:6, :]) - cross_row[slot(k), :] * gated
            norm = gated * scale
            sums[5] += column_sum(grad_no * norm)
            u_all[slot(k), :] = (norm * par[5:6, :]).astype(BF16)
            dscan = dgated * silu_g
            dgate = dgated * scanned * (sig_g * (1.0 + gate * (1.0 - sig_g)))
            sums[6] += column_sum(dscan * values)
            wide = step_wide[p, slot(k), :]
            dy = dscan.astype(BF16)
            scaled = (values * wide).astype(BF16)
            dweights = dot_nt(halves(scaled), dy)
            weights = []
            dscore = dscores_t[k]
            for h in range(2):
                gap = run_row[k, pl.ds(2 * p + h, 1), :] - run_col[2 * p + h, slot(k), :]
                decay = jnp.exp(jnp.minimum(gap, 0.0))
                weights.append((scores_t[k] * decay).astype(BF16))
                dscore = dscore + dweights[slot(h), :] * decay
            dscores_t[k] = dscore
            dscaled = dot(jnp.concatenate(weights, axis=1), halves(dy))
            dstep[slot(k), :] += head_sum(dscaled * values, columns)
            drun[slot(k), :] += head_sum(
                dy.astype(F32) * y - scaled.astype(F32) * dscaled, columns
            )
            dvalues = dscaled * wide + par[6:7, :] * dscan
            dcv = dvalues * (sig_c * (1.0 + cv * (1.0 - sig_c)))
            for t in range(4):
                sums[t] += column_sum(dcv * taps[t])
            sums[4] += column_sum(dcv)
            d_all[slot(k), 0:128] = dgate.astype(BF16)
            d_all[slot(k), 128:256] = conv_back(dcv, par).astype(BF16)
        small[0] = jnp.concatenate(sums, axis=0)
        both = dot(normed_t[...], d_all[...])
        grad_g[0] = both[:, 0:128].astype(BF16)
        grad_v[0] = both[:, 128:256].astype(BF16)
        grad_out[...] = dot_tn(u_all[...], g_all[...]).astype(BF16)
        total[...] += dot_nt(d_all[...], jnp.concatenate([wg[0], wv[0]], axis=1))

    @pl.when(i == PAIRS)
    def _finish():
        sums = [[jnp.zeros((1, LANES), F32) for _ in range(8)] for _ in range(2)]
        dt_sums = [jnp.zeros((1, LANES), F32) for _ in range(8)]
        live = iota(1) < 2 * PAIRS
        for k in range(SLOTS):
            dscore = dscores_t[k] * tri(False)
            dmixed = (
                jnp.dot(dscore, mixed[1, slot(k), :], precision=HI, preferred_element_type=F32),
                dot_tn(dscore, mixed[0, slot(k), :], HI),
            )
            for c in range(2):
                lanes = slice(c * LANES, (c + 1) * LANES)
                par = pbcv[:, lanes]
                taps = conv_taps(pbc[slot(k), lanes])
                cv = conv_sum(taps, par)
                sig = sigmoid(cv)
                dcv = dmixed[c] * (sig * (1.0 + cv * (1.0 - sig)))
                for t in range(4):
                    sums[c][t] += column_sum(dcv * taps[t])
                sums[c][4] += column_sum(dcv)
                d_bc[slot(k), lanes] = conv_back(dcv, par).astype(BF16)
            dlog = jnp.dot(
                tri(False), drun[slot(k), :], precision=HI, preferred_element_type=F32
            )
            grad_step = dstep[slot(k), :] + dlog * dtp[1:2, :]
            dt_sums[1] += column_sum(dlog * step_all[slot(k), :])
            draw = grad_step * sigmoid(pbc[slot(k), 256:384] + dtp[0:1, :])
            draw = jnp.where(live, draw, 0.0)
            dt_sums[0] += column_sum(draw)
            d_bc[slot(k), 256:384] = draw.astype(BF16)
        small_bc[0] = jnp.concatenate(sums[0], axis=0)
        small_bc[1] = jnp.concatenate(sums[1], axis=0)
        dt_sums[1] = dt_sums[1] * dtp[1:2, :]
        small_dt[...] = jnp.concatenate(dt_sums, axis=0)
        for b in range(3):
            grad_bc[b] = dot(
                normed_t[...], d_bc[:, b * LANES : (b + 1) * LANES]
            ).astype(BF16)
        grad_bc[3] = jnp.zeros_like(grad_bc[3])
        final = total[...] + dot_nt(
            d_bc[...], jnp.concatenate([wbc[0], wbc[1], wbc[2]], axis=1)
        )
        for k in range(SLOTS):
            outs[k][...] = final[slot(k), :].astype(BF16)


def backward(g_slots, row_stats, normed_t, saved, w, wout, pv, pbcv, dtp):
    proj, y, pbc = saved
    width = g_slots[0].shape[1]
    inner = wout.shape[0]
    in_specs = [const_spec((T, width)) for _ in range(SLOTS)] + [
        const_spec((SLOTS, 8, LANES)),
        const_spec((width, ROWS)),
        pl.BlockSpec((1, ROWS, 256), lambda i: (pair_of(i), 0, 0)),
        pl.BlockSpec((1, ROWS, LANES), lambda i: (pair_of(i), 0, 0)),
        const_spec((ROWS, 384)),
        pl.BlockSpec((1, width, LANES), lambda i: (pair_of(i), 0, 0)),
        pl.BlockSpec((1, width, LANES), lambda i: (PAIRS + pair_of(i), 0, 0)),
        pl.BlockSpec((4, width, LANES), lambda i: (3, 0, 0)),
        pl.BlockSpec((T, width), lambda i: (pair_of(i), 0)),
        pl.BlockSpec((8, LANES), lambda i: (0, pair_of(i))),
        const_spec((8, 256)),
        const_spec((8, LANES)),
    ]
    out_shape = [jax.ShapeDtypeStruct((T, width), BF16) for _ in range(SLOTS)] + [
        jax.ShapeDtypeStruct((PAIRS, width, LANES), BF16),
        jax.ShapeDtypeStruct((PAIRS, width, LANES), BF16),
        jax.ShapeDtypeStruct((4, width, LANES), BF16),
        jax.ShapeDtypeStruct((inner, width), BF16),
        jax.ShapeDtypeStruct((PAIRS, 8, LANES), F32),
        jax.ShapeDtypeStruct((2, 8, LANES), F32),
        jax.ShapeDtypeStruct((8, LANES), F32),
    ]
    out_specs = [const_spec((T, width)) for _ in range(SLOTS)] + [
        pl.BlockSpec((1, width, LANES), lambda i: (pair_of(i), 0, 0)),
        pl.BlockSpec((1, width, LANES), lambda i: (pair_of(i), 0, 0)),
        const_spec((4, width, LANES)),
        pl.BlockSpec((T, width), lambda i: (pair_of(i), 0)),
        pl.BlockSpec((1, 8, LANES), lambda i: (pair_of(i), 0, 0)),
        const_spec((2, 8, LANES)),
        const_spec((8, LANES)),
    ]
    scratch = [
        pltpu.VMEM((ROWS, width), BF16),
        pltpu.VMEM((SLOTS, T, T), F32),
        pltpu.VMEM((2, ROWS, LANES), F32),
        pltpu.VMEM((2 * PAIRS, ROWS, LANES), F32),
        pltpu.VMEM((SLOTS, T, LANES), F32),
        pltpu.VMEM((PAIRS, ROWS, LANES), F32),
        pltpu.VMEM((ROWS, LANES), F32),
        pltpu.VMEM((ROWS, LANES), F32),
        pltpu.VMEM((ROWS, LANES), F32),
        pltpu.VMEM((SLOTS, T, T), F32),
        pltpu.VMEM((ROWS, LANES), F32),
        pltpu.VMEM((ROWS, LANES), F32),
        pltpu.VMEM((ROWS, width), F32),
        pltpu.VMEM((ROWS, LANES), BF16),
        pltpu.VMEM((ROWS, 256), BF16),
        pltpu.VMEM((ROWS, 384), BF16),
    ]
    res = pl.pallas_call(
        backward_kernel,
        grid=(PAIRS + 1,),
        in_specs=in_specs,
        out_specs=out_specs,
        out_shape=out_shape,
        scratch_shapes=scratch,
        compiler_params=pltpu.CompilerParams(vmem_limit_bytes=VMEM_LIMIT),
        name="layer_backward",
    )(*g_slots, row_stats, normed_t, proj, y, pbc, w, w, w, wout, pv, pbcv, dtp)
    return res[:SLOTS], res[SLOTS:]


def ring(n, k):
    return [(i, (i + k) % n) for i in range(n)]


def send_shard(v, k):
    return lax.ppermute(v, "shard", ring(SLOTS, k)) if k else v


def swap_section(v):
    return lax.ppermute(v, "section", [(0, 1), (1, 0)])


def dp_index(x, z, c):
    return x * 8 + z * 2 + c


def dp_pairs(move):
    pairs = []
    for x in range(2):
        for z in range(4):
            for c in range(2):
                pairs.append((dp_index(x, z, c), dp_index(*move(x, z, c))))
    return pairs


def section_pairs(k, layer):
    pairs = []
    for chip in range(4):
        to = (chip + k) % 4
        if to // 2 != layer:
            continue
        for z in range(4):
            for c in range(2):
                pairs.append(
                    (
                        (chip // 2) * 16 + dp_index(chip % 2, z, c),
                        (to // 2) * 16 + dp_index(to % 2, z, c),
                    )
                )
    return pairs


def pick(v, index, axis):
    return lax.dynamic_index_in_dim(v, index, axis, keepdims=False)


def gather_slots(v):
    return [send_shard(v, (-k) % SLOTS) for k in range(SLOTS)]


def scatter_sum(slots):
    parts = [send_shard(slots[k], k) for k in range(SLOTS)]
    return sum(p.astype(F32) for p in parts)


def to_owners(v, layer):
    d = lax.axis_index("dp")
    x, z, c = d // 8, (d // 2) % 4, d % 2
    v = v.reshape((2, 4, 2) + v.shape[1:])
    moved = lax.ppermute(pick(v, 1 - c, 2), "dp", dp_pairs(lambda x, z, c: (x, z, 1 - c)))
    v = (pick(v, c, 2).astype(F32) + moved.astype(F32)).astype(BF16)
    own = pick(v, z, 1).astype(F32)
    for k in range(1, 4):
        moved = lax.ppermute(
            pick(v, (z + k) % 4, 1), "dp", dp_pairs(lambda x, z, c: (x, (z + k) % 4, c))
        )
        own = own + moved.astype(F32)
    v = own.astype(BF16)
    own = pick(v, x, 0).astype(F32)
    for k in range(1, 4):
        moved = lax.ppermute(pick(v, (x + k) % 2, 0), ("section", "dp"), section_pairs(k, layer))
        own = own + moved.astype(F32)
    return own.astype(BF16)


def sum_small(v):
    v = v + lax.ppermute(v, "dp", dp_pairs(lambda x, z, c: (x, z, 1 - c)))
    v = v + sum(
        lax.ppermute(v, "dp", dp_pairs(lambda x, z, c: (x, (z + k) % 4, c))) for k in range(1, 4)
    )
    v = v + lax.ppermute(v, "dp", dp_pairs(lambda x, z, c: (1 - x, z, c)))
    return v + swap_section(v)


def in_order(parts, sign):
    j = lax.axis_index("shard")
    stacked = jnp.stack(parts)
    return jnp.take(stacked, (sign * (jnp.arange(SLOTS) - j)) % SLOTS, axis=0)


def shards(
    tokens,
    cotangent,
    lengths,
    norm_gain,
    in_weight,
    conv_weight,
    conv_bias,
    dt_bias,
    a_log,
    d_skip,
    gate_gain,
    out_weight,
):
    sec = lax.axis_index("section")
    d = lax.axis_index("dp")
    j = lax.axis_index("shard")
    width = tokens.shape[2]
    quarter = norm_gain.shape[1]
    channels = conv_bias.shape[1]
    own_cols = gate_gain.shape[1]
    inner = own_cols * SLOTS
    heads = dt_bias.shape[1]
    own_heads = heads // SLOTS
    out_rows = own_cols // 16

    x_own = pick(tokens, sec, 0)
    cot = pick(cotangent, sec, 0)
    length = pick(lengths, sec, 0)
    mask = (jnp.arange(T, dtype=jnp.int32) < length).astype(F32)[:, None]

    with jax.named_scope("weights"):
        padded = jnp.pad(in_weight[0], ((0, 0), (0, 256)))

        def start_of(to):
            return jnp.where(
                d < 6,
                own_cols * to + LANES * d,
                jnp.where(
                    d < 12,
                    inner + own_cols * to + LANES * (d - 6),
                    jnp.where(
                        d < 14, 2 * inner + LANES * (d - 12), 2 * inner + 256 + own_heads * to
                    ),
                ),
            )

        parts = [
            send_shard(
                lax.dynamic_slice(padded, (0, start_of((j + k) % SLOTS)), (quarter, LANES)), k
            )
            for k in range(SLOTS)
        ]
        w_own = in_order(parts, -1).reshape(width, LANES)
        o_own = lax.dynamic_slice(out_weight[0], (out_rows * d, 0), (out_rows, width))
        w_other, o_other = swap_section(w_own), swap_section(o_own)
        first = sec == 0
        w_low = [jnp.where(first, w_own, w_other), jnp.where(first, w_other, w_own)]
        o_low = [jnp.where(first, o_own, o_other), jnp.where(first, o_other, o_own)]
        w_full = [lax.all_gather(v, "dp", axis=0, tiled=False) for v in w_low]
        o_full = [
            lax.all_gather(v, "dp", axis=0, tiled=False).reshape(own_cols, width) for v in o_low
        ]

    with jax.named_scope("small_weights"):
        sizes = [quarter, 4 * channels, channels, own_cols, heads, heads, heads]
        flat = jnp.concatenate(
            [
                norm_gain[0],
                conv_weight[0].reshape(-1),
                conv_bias[0],
                gate_gain[0],
                dt_bias[0],
                a_log[0],
                d_skip[0],
            ]
        )
        flat = jnp.pad(flat, (0, -flat.shape[0] % LANES)).reshape(-1, LANES)
        own = in_order(gather_slots(flat), 1)
        other = swap_section(own)
        small = [jnp.where(first, own, other), jnp.where(first, other, own)]

        def unpack(v):
            v = v.reshape(SLOTS, -1).astype(F32)
            cut, at = [], 0
            for size in sizes:
                cut.append(v[:, at : at + size])
                at += size
            gain = cut[0].reshape(1, width)
            taps = cut[1].reshape(SLOTS, 4, channels).transpose(1, 0, 2).reshape(4, -1)
            bias = cut[2].reshape(1, -1)
            conv = jnp.concatenate([taps, bias, jnp.zeros((3, taps.shape[1]), F32)], axis=0)
            pbcv = conv[:, inner:]
            pv = lax.dynamic_slice(conv, (0, own_cols * j), (8, own_cols))
            pick_heads = lambda u: lax.dynamic_slice(u[0], (own_heads * j,), (own_heads,))
            wide = jnp.repeat(pick_heads(cut[6]), HEAD)[None]
            pv = jnp.concatenate([pv[:5], pick(cut[3], j, 0)[None], wide, pv[7:]], axis=0)
            dtp = jnp.stack([pick_heads(cut[4]), -jnp.exp(pick_heads(cut[5]))])
            dtp = jnp.pad(dtp, ((0, 6), (0, LANES - own_heads)))
            return gain, pv, pbcv, dtp

        params = [unpack(v) for v in small]

    x_f = x_own.astype(F32)
    x_slots = gather_slots(x_own)
    gain, pv, pbcv, dtp = params[0]
    parts, stats, (normed0, *saved0) = forward(
        x_slots, None, w_full[0], o_full[0], gain, pv, pbcv, dtp
    )
    branch = scatter_sum(parts)
    square = scatter_sum([stats[0, 0:1, slot(k)] for k in range(SLOTS)])[0]
    scale0 = lax.rsqrt(square / inner + EPS)
    branch0 = branch * scale0[:, None]
    middle = (x_f + mask * branch0).astype(BF16)
    normed0_t = jnp.transpose(normed0)

    g1 = (mask * cot.astype(F32)).astype(BF16)
    g1_slots = gather_slots(g1)
    m_slots = gather_slots(middle)
    gain1, pv1, pbcv1, dtp1 = params[1]
    parts, stats, (normed1, *saved1) = forward(
        m_slots, g1_slots, w_full[1], o_full[1], gain1, pv1, pbcv1, dtp1
    )
    normed1_t = jnp.transpose(normed1)
    own = stats[:, 0].reshape(2, SLOTS, T)
    back = [send_shard(own, k) for k in range(SLOTS)]
    summed = sum(jnp.roll(back[k], -k, axis=1) for k in range(SLOTS))
    scale1 = lax.rsqrt(summed[0] / inner + EPS)
    cross1 = scale1 * scale1 * scale1 * summed[1] / inner
    rows1 = jnp.pad(jnp.stack([scale1, cross1], axis=1), ((0, 0), (0, 6), (0, 0)))
    branch = scatter_sum(parts) * scale1[0][:, None]
    result = middle.astype(F32) + mask * branch

    def norm_back(x, gain, grad):
        scale = lax.rsqrt(jnp.mean(x * x, axis=1, keepdims=True) + EPS)
        unit = x * scale
        dn = grad * gain
        dx = scale * (dn - unit * jnp.mean(dn * unit, axis=1, keepdims=True))
        return dx, jnp.sum(grad * unit, axis=0)

    parts, grads1 = backward(
        g1_slots, rows1, normed1_t, saved1, w_full[1], o_full[1], pv1, pbcv1, dtp1
    )
    dx, gain_grad1 = norm_back(middle.astype(F32), gain1, scatter_sum(parts))
    dmiddle = (cot.astype(F32) + dx).astype(BF16)
    g0 = (mask * dmiddle.astype(F32)).astype(BF16)
    cross0 = scale0 * scale0 * jnp.sum(g0.astype(F32) * branch0, axis=1) / inner
    own = jnp.pad(jnp.stack([scale0, cross0]), ((0, 6), (0, 0)))
    rows0 = jnp.stack(gather_slots(own))
    g0_slots = gather_slots(g0)
    parts, grads0 = backward(
        g0_slots, rows0, normed0_t, saved0, w_full[0], o_full[0], pv, pbcv, dtp
    )
    dx, gain_grad0 = norm_back(x_f, gain, scatter_sum(parts))
    dtokens = dmiddle.astype(F32) + dx

    result_moved = lax.ppermute(result.astype(BF16), "section", [(0, 1)]).astype(F32)
    dtokens_moved = lax.ppermute(dtokens.astype(BF16), "section", [(1, 0)]).astype(F32)
    ends = jnp.where(
        first, jnp.stack([dtokens, dtokens_moved]), jnp.stack([result_moved, result])
    )[None]

    owned, small_sums = [], []
    for layer, grads, gain_grad in ((0, grads0, gain_grad0), (1, grads1, gain_grad1)):
        grad_g, grad_v, grad_bc, grad_out, sm, sm_bc, sm_dt = grads
        gw = jnp.concatenate([grad_g, grad_v, grad_bc], axis=0)
        go = grad_out.reshape(16, out_rows, width)
        owned.append((to_owners(gw, layer), to_owners(go, layer)))
        flat = jnp.concatenate(
            [sm.reshape(-1), sm_bc.reshape(-1), sm_dt.reshape(-1), gain_grad]
        ).reshape(-1, LANES)
        small_sums.append(sum_small(flat))
    w_grad = jnp.where(first, owned[0][0], owned[1][0]).reshape(SLOTS, quarter, LANES)
    o_grad = jnp.where(first, owned[0][1], owned[1][1])
    small_sum = jnp.where(first, small_sums[0], small_sums[1])

    parts = [send_shard(pick(w_grad, (j + k) % SLOTS, 0), k) for k in range(SLOTS)]
    w_grad = in_order(parts, -1)
    shared = jnp.sum(w_grad.astype(F32), axis=0, keepdims=True).astype(BF16)
    w_grad = jnp.where((d == 12) | (d == 13), jnp.broadcast_to(shared, w_grad.shape), w_grad)
    w_all = lax.all_gather(w_grad, "dp", axis=0, tiled=False)
    o_all = lax.all_gather(o_grad, "dp", axis=0, tiled=False)
    grad_out_weight = o_all.reshape(own_cols, width).astype(F32)
    by_row = lambda v: v.transpose(2, 1, 0, 3).reshape(quarter, inner).astype(F32)
    grad_in_weight = jnp.concatenate(
        [
            by_row(w_all[0:6]),
            by_row(w_all[6:12]),
            w_all[12:14, 0].transpose(1, 0, 2).reshape(quarter, 256).astype(F32),
            w_all[14, :, :, :own_heads].transpose(1, 0, 2).reshape(quarter, heads).astype(F32),
        ],
        axis=1,
    )

    everyone = in_order(gather_slots(small_sum), 1).reshape(SLOTS, -1)
    n_pair, n_bc = PAIRS * 8 * LANES, 2 * 8 * LANES
    by_pair = everyone[:, :n_pair].reshape(SLOTS, PAIRS, 8, LANES)
    by_pair = by_pair.transpose(2, 0, 1, 3).reshape(8, inner)
    by_bc = jnp.sum(everyone[:, n_pair : n_pair + n_bc], axis=0)
    by_bc = by_bc.reshape(2, 8, LANES).transpose(1, 0, 2).reshape(8, 256)
    at = n_pair + n_bc
    by_dt = everyone[:, at : at + 8 * LANES].reshape(SLOTS, 8, LANES)[:, :, :own_heads]
    by_dt = by_dt.transpose(1, 0, 2).reshape(8, heads)
    gain_total = jnp.sum(everyone[:, at + 8 * LANES :], axis=0)
    conv_total = jnp.concatenate([by_pair[:5], by_bc[:5]], axis=1)
    conv_own = lax.dynamic_slice(conv_total, (0, channels * j), (5, channels))
    grad_skip = jnp.sum(by_pair[6].reshape(heads, HEAD), axis=1)
    return (
        ends,
        lax.dynamic_slice(gain_total, (quarter * j,), (quarter,))[None],
        grad_in_weight[None],
        conv_own[None, :4],
        conv_own[4][None],
        by_dt[0][None],
        by_dt[1][None],
        grad_skip[None],
        lax.dynamic_slice(by_pair[5], (own_cols * j,), (own_cols,))[None],
        grad_out_weight[None],
    )


def solution(mesh):
    return jax.shard_map(
        shards,
        mesh=mesh,
        in_specs=(
            P(("dp", "shard"), None, None),
            P(("dp", "shard"), None, None),
            P(("dp", "shard")),
            P("section", "shard"),
            P("section", "shard", None),
            P("section", None, "shard"),
            P("section", "shard"),
            P("section", None),
            P("section", None),
            P("section", None),
            P("section", "shard"),
            P("section", "shard", None),
        ),
        out_specs=(
            P("section", ("dp", "shard"), None, None),
            P("section", "shard"),
            P("section", "shard", None),
            P("section", None, "shard"),
            P("section", "shard"),
            P("section", None),
            P("section", None),
            P("section", None),
            P("section", "shard"),
            P("section", "shard", None),
        ),
        check_vma=False,
    )
```

```python
import jax
import jax.numpy as jnp
from jax import lax
from jax.experimental import pallas as pl
from jax.experimental.pallas import tpu as pltpu
from jax.sharding import PartitionSpec as P

F32 = jnp.float32
BF16 = jnp.bfloat16
HI = lax.Precision.HIGHEST
EPS = 1e-05
T = 128
LANES = 128
HEAD = 64
SLOTS = 4
ROWS = SLOTS * T
PAIRS = 6
STEPS = 2
HALF = PAIRS // STEPS
WIDE = HALF * LANES
VMEM_LIMIT = 60 * 1024 * 1024


def sigmoid(v):
    return 0.5 * jnp.tanh(0.5 * v) + 0.5


def softplus(v):
    return jnp.maximum(v, 0.0) + jnp.log1p(jnp.exp(-jnp.abs(v)))


def dot(a, b):
    return jnp.dot(a, b, preferred_element_type=F32)


def dot_nt(a, b, precision=None):
    return lax.dot_general(
        a, b, (((1,), (1,)), ((), ())), preferred_element_type=F32, precision=precision
    )


def dot_tn(a, b, precision=None):
    return lax.dot_general(
        a, b, (((0,), (0,)), ((), ())), preferred_element_type=F32, precision=precision
    )


def iota(axis):
    return lax.broadcasted_iota(jnp.int32, (T, LANES), axis)


def shift_down(v, steps):
    return jnp.where(iota(0) >= steps, pltpu.roll(v, steps, 0), 0.0)


def shift_up(v, steps):
    return jnp.where(iota(0) < T - steps, pltpu.roll(v, T - steps, 0), 0.0)


def conv_taps(cin):
    return [shift_down(cin, 3), shift_down(cin, 2), shift_down(cin, 1), cin]


def conv_sum(taps, par):
    total = par[4:5, :] + taps[0] * par[0:1, :]
    for k in range(1, 4):
        total = total + taps[k] * par[k : k + 1, :]
    return total


def conv_back(dcv, par):
    total = dcv * par[3:4, :]
    for m in range(1, 4):
        total = total + shift_up(dcv, m) * par[3 - m : 4 - m, :]
    return total


def column_sum(v):
    return jnp.sum(v, axis=0, keepdims=True)


def slot(k):
    return slice(k * T, (k + 1) * T)


def tri(lower):
    if lower:
        return (iota(0) >= iota(1)).astype(F32)
    return (iota(0) <= iota(1)).astype(F32)


def step_prep(k, pbc, dtp, run_col, run_row, step_wide):
    step = softplus(pbc[slot(k), 256:384] + dtp[0:1, :])
    run = jnp.dot(tri(True), step * dtp[1:2, :], precision=HI, preferred_element_type=F32)
    run_row[k] = jnp.transpose(run)
    left = iota(1) < HEAD
    for p in range(PAIRS):
        a, b = 2 * p, 2 * p + 1
        run_col[a, slot(k), :] = jnp.broadcast_to(run[:, a : a + 1], (T, LANES))
        run_col[b, slot(k), :] = jnp.broadcast_to(run[:, b : b + 1], (T, LANES))
        step_wide[p, slot(k), :] = jnp.where(
            left,
            jnp.broadcast_to(step[:, a : a + 1], (T, LANES)),
            jnp.broadcast_to(step[:, b : b + 1], (T, LANES)),
        )
    return step


def halves(v):
    left = iota(1) < HEAD
    zero = jnp.zeros_like(v)
    return jnp.concatenate([jnp.where(left, v, zero), jnp.where(left, zero, v)], axis=0)


class Refs:
    pass


def kernel_call(body, name, ins, outs, scratch, cost_us):
    in_names, out_names, scratch_names = list(ins), list(outs), list(scratch)

    def run(*refs):
        rf = Refs()
        for key, ref in zip(in_names + out_names + scratch_names, refs):
            setattr(rf, key, ref)
        body(rf, pl.program_id(0))

    res = pl.pallas_call(
        run,
        grid=(STEPS,),
        in_specs=[pl.BlockSpec(ins[n][1], ins[n][2]) for n in in_names],
        out_specs=[pl.BlockSpec(outs[n][2], outs[n][3]) for n in out_names],
        out_shape=[jax.ShapeDtypeStruct(outs[n][0], outs[n][1]) for n in out_names],
        scratch_shapes=[pltpu.VMEM(*scratch[n]) for n in scratch_names],
        compiler_params=pltpu.CompilerParams(vmem_limit_bytes=VMEM_LIMIT),
        cost_estimate=pl.CostEstimate(
            flops=int(cost_us * 1.1e9), bytes_accessed=1 << 20, transcendentals=0
        ),
        name=name,
    )(*[ins[n][0] for n in in_names])
    return dict(zip(out_names, res))


def whole(v):
    return (v, v.shape, lambda h: (0,) * v.ndim)


def whole_out(shape, dtype):
    return (shape, dtype, shape, lambda h: (0,) * len(shape))


def by_step(v, block):
    return (v, block, lambda h: (h,) + (0,) * (len(block) - 1))


def by_step_out(shape, dtype, block):
    return (shape, dtype, block, lambda h: (h,) + (0,) * (len(block) - 1))


def lanes_by_step(v):
    return (v, (v.shape[0], WIDE), lambda h: (0, h))


def lanes_by_step_out(shape, dtype):
    return (shape, dtype, (shape[0], WIDE), lambda h: (0, h))


def weight_blocks(w):
    half = (8, 3, 16, w.shape[3])
    return {
        "wg": (w, half, lambda h: (h, 0, 0, 0)),
        "wv": (w, half, lambda h: (h, 1, 0, 0)),
        "wbc": (w, (16, 1, 16, w.shape[3]), lambda h: (0, 6, 0, 0)),
    }


def pair_lanes(p):
    return slice(p * LANES, (p + 1) * LANES)


def flat_rows(ref):
    v = ref[...]
    return v.reshape(-1, v.shape[-1])


def mixed_bc(rf, k, c):
    lanes = slice(c * LANES, (c + 1) * LANES)
    cv = conv_sum(conv_taps(rf.pbc[slot(k), lanes]), rf.pbcv[:, lanes])
    return cv * sigmoid(cv)


def forward(x_slots, g_slots, w, dtw, wout, gain, pv, pbcv, dtp):
    width = x_slots[0].shape[1]
    with_grad = g_slots is not None

    def body(rf, h):
        @pl.when(h == 0)
        def _prep():
            for k in range(SLOTS):
                x = getattr(rf, f"x{k}")[...].astype(F32)
                scale = lax.rsqrt(jnp.mean(x * x, axis=1, keepdims=True) + EPS)
                rf.normed[slot(k), :] = (x * scale * rf.gain[...]).astype(BF16)
                if with_grad:
                    rf.g_all[slot(k), :] = getattr(rf, f"g{k}")[...]
            rf.pbc[:, 0:256] = dot_nt(rf.normed[...], flat_rows(rf.wbc))
            rf.pbc[:, 256:384] = dot_nt(rf.normed[...], rf.dtw[...])
            for k in range(SLOTS):
                rf.scores[k] = dot_nt(mixed_bc(rf, k, 1), mixed_bc(rf, k, 0), HI) * tri(True)
                step_prep(k, rf.pbc, rf.dtp, rf.run_col, rf.run_row, rf.step_wide)
            rf.square[...] = jnp.zeros_like(rf.square)
            rf.cross[...] = jnp.zeros_like(rf.cross)

        rf.proj[0, :, 0:WIDE] = dot_nt(rf.normed[...], flat_rows(rf.wg))
        rf.proj[0, :, WIDE : 2 * WIDE] = dot_nt(rf.normed[...], flat_rows(rf.wv))
        if with_grad:
            q_all = dot_nt(rf.g_all[...], rf.wout[pl.ds(pl.multiple_of(h * WIDE, WIDE), WIDE), :])
        for p in range(HALF):
            lanes = pair_lanes(p)
            par = rf.pv[:, lanes]
            pair = HALF * h + p
            for k in range(SLOTS):
                gate = rf.proj[0, slot(k), lanes]
                cv = conv_sum(
                    conv_taps(rf.proj[0, slot(k), WIDE + p * LANES : WIDE + (p + 1) * LANES]), par
                )
                values = cv * sigmoid(cv)
                scaled = (values * rf.step_wide[pair, slot(k), :]).astype(BF16)
                weights = []
                for a in range(2):
                    gap = (
                        rf.run_col[2 * pair + a, slot(k), :]
                        - rf.run_row[k, pl.ds(2 * pair + a, 1), :]
                    )
                    decay = jnp.exp(jnp.minimum(gap, 0.0))
                    weights.append((rf.scores[k] * decay).astype(BF16))
                y = dot(jnp.concatenate(weights, axis=1), halves(scaled))
                rf.y[0, slot(k), lanes] = y
                scanned = y + par[6:7, :] * values
                gated = scanned * (gate * sigmoid(gate))
                rf.square[slot(k), :] += gated * gated
                scaled_out = gated * par[5:6, :]
                rf.u_all[h, slot(k), lanes] = scaled_out.astype(BF16)
                if with_grad:
                    rf.cross[slot(k), :] += q_all[slot(k), lanes] * scaled_out

        @pl.when(h == STEPS - 1)
        def _finish():
            u = jnp.concatenate([rf.u_all[a] for a in range(STEPS)], axis=1)
            for n in range(0, width, 512):
                part = dot(u, rf.wout[:, n : n + 512]).astype(BF16)
                for k in range(SLOTS):
                    getattr(rf, f"out{k}")[:, n : n + 512] = part[slot(k), :]
            ones = jnp.ones((8, LANES), F32)
            rf.stats[0] = dot_nt(ones, rf.square[...], HI)
            rf.stats[1] = dot_nt(ones, rf.cross[...], HI)

    ins = {f"x{k}": whole(v) for k, v in enumerate(x_slots)}
    if with_grad:
        ins.update({f"g{k}": whole(v) for k, v in enumerate(g_slots)})
    ins.update(
        gain=whole(gain),
        **weight_blocks(w),
        dtw=whole(dtw),
        wout=whole(wout),
        pv=lanes_by_step(pv),
        pbcv=whole(pbcv),
        dtp=whole(dtp),
    )
    outs = {f"out{k}": whole_out((T, width), BF16) for k in range(SLOTS)}
    outs.update(
        stats=whole_out((2, 8, ROWS), F32),
        normed=whole_out((ROWS, width), BF16),
        proj=by_step_out((STEPS, ROWS, 2 * WIDE), F32, (1, ROWS, 2 * WIDE)),
        y=by_step_out((STEPS, ROWS, WIDE), F32, (1, ROWS, WIDE)),
        pbc=whole_out((ROWS, 384), F32),
    )
    scratch = dict(
        scores=((SLOTS, T, T), F32),
        run_col=((2 * PAIRS, ROWS, LANES), F32),
        run_row=((SLOTS, T, LANES), F32),
        step_wide=((PAIRS, ROWS, LANES), F32),
        u_all=((STEPS, ROWS, WIDE), BF16),
        square=((ROWS, LANES), F32),
        cross=((ROWS, LANES), F32),
    )
    if with_grad:
        scratch["g_all"] = ((ROWS, width), BF16)
    res = kernel_call(body, "layer_forward", ins, outs, scratch, 18)
    return [res[f"out{k}"] for k in range(SLOTS)], res


def head_columns(pair):
    target = 2 * pair + (iota(0) >= HEAD).astype(jnp.int32)
    one = (iota(1) == target).astype(BF16)
    return jnp.concatenate([one, one], axis=0)


def head_sum(v, columns):
    high = v.astype(BF16)
    low = (v - high.astype(F32)).astype(BF16)
    return dot(jnp.concatenate([high, low], axis=1), columns)


def backward(stages, name, cost_us, saved, layer, have):
    gate, scan, inp, wgate, wscan = (
        s in stages for s in ("gate", "scan", "input", "wgate", "wscan")
    )
    width = saved["normed"].shape[1]
    w, dtw, wout, pv, pbcv, dtp = layer
    elementwise = gate or scan

    def body(rf, h):
        @pl.when(h == 0)
        def _prep():
            for k in range(SLOTS):
                if gate or wgate:
                    rf.g_all[slot(k), :] = getattr(rf, f"g{k}")[...]
                if gate:
                    for row, ref in ((0, rf.scale_row), (1, rf.cross_row)):
                        ref[slot(k), :] = jnp.transpose(
                            jnp.broadcast_to(rf.rows[k, row : row + 1, :], (T, LANES))
                        )
                if scan:
                    inbound, outbound = mixed_bc(rf, k, 0), mixed_bc(rf, k, 1)
                    rf.mixed[0, slot(k), :] = inbound
                    rf.mixed[1, slot(k), :] = outbound
                    rf.scores[k] = dot_nt(inbound, outbound, HI) * tri(False)
                    rf.step_all[slot(k), :] = step_prep(
                        k, rf.pbc, rf.dtp, rf.run_col, rf.run_row, rf.step_wide
                    )
            if scan:
                rf.dscores[...] = jnp.zeros_like(rf.dscores)
                rf.dstep[...] = jnp.zeros_like(rf.dstep)
                rf.drun[...] = jnp.zeros_like(rf.drun)
            if inp:
                rf.total[...] = jnp.zeros_like(rf.total)

        if gate:
            q_all = dot_nt(rf.g_all[...], rf.wout[...])
        for p in range(HALF if elementwise else 0):
            lanes = pair_lanes(p)
            par = rf.pv[:, lanes]
            pair = HALF * h + p
            sums = [jnp.zeros((1, LANES), F32) for _ in range(8)]
            if scan:
                columns = head_columns(pair)
            for k in range(SLOTS):
                taps = conv_taps(rf.proj[0, slot(k), WIDE + p * LANES : WIDE + (p + 1) * LANES])
                cv = conv_sum(taps, par)
                sig_c = sigmoid(cv)
                values = cv * sig_c
                y = rf.y[0, slot(k), lanes]
                if gate:
                    gate_in = rf.proj[0, slot(k), lanes]
                    sig_g = sigmoid(gate_in)
                    silu_g = gate_in * sig_g
                    scanned = y + par[6:7, :] * values
                    gated = scanned * silu_g
                    grad_no = q_all[slot(k), lanes]
                    scale = rf.scale_row[slot(k), :]
                    dgated = scale * (grad_no * par[5:6, :]) - rf.cross_row[slot(k), :] * gated
                    norm = gated * scale
                    sums[5] += column_sum(grad_no * norm)
                    rf.u[slot(k), lanes] = (norm * par[5:6, :]).astype(BF16)
                    dscan = dgated * silu_g
                    dgate = dgated * scanned * (sig_g * (1.0 + gate_in * (1.0 - sig_g)))
                    sums[6] += column_sum(dscan * values)
                    rf.dg[slot(k), lanes] = dgate.astype(BF16)
                    if not scan:
                        rf.dscan[slot(k), lanes] = dscan
                else:
                    dscan = rf.dscan[slot(k), lanes]
                if not scan:
                    continue
                wide = rf.step_wide[pair, slot(k), :]
                dy = dscan.astype(BF16)
                scaled = (values * wide).astype(BF16)
                dweights = dot_nt(halves(scaled), dy)
                weights = []
                dscore = rf.dscores[k]
                for a in range(2):
                    gap = (
                        rf.run_row[k, pl.ds(2 * pair + a, 1), :]
                        - rf.run_col[2 * pair + a, slot(k), :]
                    )
                    decay = jnp.exp(jnp.minimum(gap, 0.0))
                    weights.append((rf.scores[k] * decay).astype(BF16))
                    dscore = dscore + dweights[slot(a), :] * decay
                rf.dscores[k] = dscore
                dscaled = dot(jnp.concatenate(weights, axis=1), halves(dy))
                rf.dstep[slot(k), :] += head_sum(dscaled * values, columns)
                rf.drun[slot(k), :] += head_sum(
                    dy.astype(F32) * y - scaled.astype(F32) * dscaled, columns
                )
                dvalues = dscaled * wide + par[6:7, :] * dscan
                dcv = dvalues * (sig_c * (1.0 + cv * (1.0 - sig_c)))
                for t in range(4):
                    sums[t] += column_sum(dcv * taps[t])
                sums[4] += column_sum(dcv)
                rf.dv[slot(k), lanes] = conv_back(dcv, par).astype(BF16)
            rf.small[p] = jnp.concatenate(sums, axis=0)
        if wgate:
            part = dot_tn(rf.dg[...], rf.normed[...]).astype(BF16)
            rf.ga[:, 0:3] = part.reshape(8, 3, 16, width)
            part = dot_tn(rf.u[...], rf.g_all[...]).astype(BF16)
            rf.ga[:, 3:6] = part.reshape(8, 3, 16, width)
        if wscan:
            part = dot_tn(rf.dv[...], rf.normed[...]).astype(BF16)
            if wgate:
                rf.ga[:, 6:9] = part.reshape(8, 3, 16, width)
                part = dot_tn(rf.dbc_half[...], rf.normed[...]).astype(BF16)
                rf.ga[:, 9] = part.reshape(8, 16, width)
            else:
                rf.gb[pl.ds(8 * h, 8), 0:3] = part.reshape(8, 3, 16, width)
        if inp:
            rf.total[...] += dot(rf.dg[...], flat_rows(rf.wg)) + dot(rf.dv[...], flat_rows(rf.wv))

        @pl.when(h == STEPS - 1)
        def _finish():
            if scan:
                sums = [[jnp.zeros((1, LANES), F32) for _ in range(8)] for _ in range(2)]
                dt_sums = [jnp.zeros((1, LANES), F32) for _ in range(8)]
                live = iota(1) < 2 * PAIRS
                for k in range(SLOTS):
                    dscore = rf.dscores[k] * tri(False)
                    dmixed = (
                        jnp.dot(
                            dscore,
                            rf.mixed[1, slot(k), :],
                            precision=HI,
                            preferred_element_type=F32,
                        ),
                        dot_tn(dscore, rf.mixed[0, slot(k), :], HI),
                    )
                    for c in range(2):
                        lanes = slice(c * LANES, (c + 1) * LANES)
                        par = rf.pbcv[:, lanes]
                        taps = conv_taps(rf.pbc[slot(k), lanes])
                        cv = conv_sum(taps, par)
                        sig = sigmoid(cv)
                        dcv = dmixed[c] * (sig * (1.0 + cv * (1.0 - sig)))
                        for t in range(4):
                            sums[c][t] += column_sum(dcv * taps[t])
                        sums[c][4] += column_sum(dcv)
                        rf.dbc[slot(k), lanes] = conv_back(dcv, par).astype(BF16)
                    dlog = jnp.dot(
                        tri(False), rf.drun[slot(k), :], precision=HI, preferred_element_type=F32
                    )
                    grad_step = rf.dstep[slot(k), :] + dlog * rf.dtp[1:2, :]
                    dt_sums[1] += column_sum(dlog * rf.step_all[slot(k), :])
                    draw = grad_step * sigmoid(rf.pbc[slot(k), 256:384] + rf.dtp[0:1, :])
                    draw = jnp.where(live, draw, 0.0)
                    dt_sums[0] += column_sum(draw)
                    rf.dbc[slot(k), 256:384] = draw.astype(BF16)
                rf.small_bc[0] = jnp.concatenate(sums[0], axis=0)
                rf.small_bc[1] = jnp.concatenate(sums[1], axis=0)
                dt_sums[1] = dt_sums[1] * rf.dtp[1:2, :]
                rf.small_dt[...] = jnp.concatenate(dt_sums, axis=0)
            if wscan and not wgate:
                part = dot_tn(rf.dbc[:, 0:256], rf.normed[...]).astype(BF16)
                rf.gb[:, 3] = part.reshape(16, 16, width)
            if wscan:
                rf.gdt[...] = dot_tn(rf.dbc[:, 256:384], rf.normed[...])[0:16]
            if inp:
                final = (
                    rf.total[...]
                    + dot(rf.dbc[:, 0:256], flat_rows(rf.wbc))
                    + dot(rf.dbc[:, 256:384], rf.dtw[...])
                )
                for k in range(SLOTS):
                    getattr(rf, f"out{k}")[...] = final[slot(k), :].astype(BF16)

    ins, outs, scratch = {}, {}, {}
    heads_cols = STEPS * WIDE
    if gate or wgate:
        ins.update({f"g{k}": whole(v) for k, v in enumerate(have["g"])})
        scratch["g_all"] = ((ROWS, width), BF16)
    if gate:
        ins["rows"] = whole(have["rows"])
        ins["wout"] = (wout, (WIDE, width), lambda h: (h, 0))
        scratch["scale_row"] = ((ROWS, LANES), F32)
        scratch["cross_row"] = ((ROWS, LANES), F32)
        outs["u"] = lanes_by_step_out((ROWS, heads_cols), BF16)
        outs["dg"] = lanes_by_step_out((ROWS, heads_cols), BF16)
        if not scan:
            outs["dscan"] = lanes_by_step_out((ROWS, heads_cols), F32)
    if elementwise:
        ins["proj"] = by_step(saved["proj"], (1, ROWS, 2 * WIDE))
        ins["y"] = by_step(saved["y"], (1, ROWS, WIDE))
        ins["pv"] = lanes_by_step(pv)
        outs["small"] = by_step_out((PAIRS, 8, LANES), F32, (HALF, 8, LANES))
    if scan:
        ins["pbc"] = whole(saved["pbc"])
        ins["pbcv"] = whole(pbcv)
        ins["dtp"] = whole(dtp)
        if not gate:
            ins["dscan"] = lanes_by_step(have["dscan"])
        outs["dv"] = lanes_by_step_out((ROWS, heads_cols), BF16)
        outs["dbc"] = whole_out((ROWS, 384), BF16)
        outs["small_bc"] = whole_out((2, 8, LANES), F32)
        outs["small_dt"] = whole_out((8, LANES), F32)
        scratch.update(
            mixed=((2, ROWS, LANES), F32),
            scores=((SLOTS, T, T), F32),
            run_col=((2 * PAIRS, ROWS, LANES), F32),
            run_row=((SLOTS, T, LANES), F32),
            step_wide=((PAIRS, ROWS, LANES), F32),
            step_all=((ROWS, LANES), F32),
            dscores=((SLOTS, T, T), F32),
            dstep=((ROWS, LANES), F32),
            drun=((ROWS, LANES), F32),
        )
    if inp:
        ins.update(weight_blocks(w))
        ins["dtw"] = whole(dtw)
        scratch["total"] = ((ROWS, width), F32)
        outs.update({f"out{k}": whole_out((T, width), BF16) for k in range(SLOTS)})
    if wgate or wscan:
        ins["normed"] = whole(saved["normed"])
    if not gate and (wgate or inp):
        ins["dg"] = lanes_by_step(have["dg"])
    if wgate and not gate:
        ins["u"] = lanes_by_step(have["u"])
    if not scan and (wscan or inp):
        ins["dv"] = lanes_by_step(have["dv"])
        ins["dbc"] = whole(have["dbc"])
    if wgate and wscan:
        ins["dbc_half"] = (have["dbc"], (ROWS, LANES), lambda h: (0, h))
        outs["ga"] = by_step_out((16, 10, 16, width), BF16, (8, 10, 16, width))
    elif wgate:
        outs["ga"] = by_step_out((16, 6, 16, width), BF16, (8, 6, 16, width))
    elif wscan:
        outs["gb"] = whole_out((16, 4, 16, width), BF16)
    if wscan:
        outs["gdt"] = whole_out((16, width), F32)
    return kernel_call(body, name, ins, outs, scratch, cost_us)


def assemble(parts, dt_rows):
    quarter = parts.shape[2]
    block = 16 * 48
    total = 8 * block + 16 * 16 + dt_rows.shape[0]

    def body(inw, outw, shared, dt, grad_in, grad_out):
        i = pl.program_id(0)

        @pl.when(i < 8)
        def _columns():
            grad_in[...] = inw[...].reshape(block, quarter).astype(F32)

        @pl.when(i < SLOTS)
        def _out():
            grad_out[...] = outw[...].reshape(block, quarter).astype(F32)

        @pl.when(i == 8)
        def _shared():
            grad_in[...] = jnp.zeros_like(grad_in)
            grad_in[0:256, :] = shared[...].reshape(256, quarter).astype(F32)
            grad_in[256 : 256 + dt_rows.shape[0], :] = dt[...]

    last = SLOTS - 1
    return pl.pallas_call(
        body,
        grid=(9,),
        in_specs=[
            pl.BlockSpec(
                (16, 48, quarter),
                lambda i: (0, jnp.where(i < SLOTS, i, jnp.minimum(i + SLOTS, 11)), 0),
            ),
            pl.BlockSpec((16, 48, quarter), lambda i: (0, SLOTS + jnp.minimum(i, last), 0)),
            pl.BlockSpec((16, 16, quarter), lambda i: (0, 36, 0)),
            pl.BlockSpec(dt_rows.shape, lambda i: (0, 0)),
        ],
        out_specs=[
            pl.BlockSpec((block, quarter), lambda i: (i, 0)),
            pl.BlockSpec((block, quarter), lambda i: (0, jnp.minimum(i, last))),
        ],
        out_shape=[
            jax.ShapeDtypeStruct((total, quarter), F32),
            jax.ShapeDtypeStruct((block, SLOTS * quarter), F32),
        ],
        compiler_params=pltpu.CompilerParams(vmem_limit_bytes=VMEM_LIMIT),
        name="assemble",
    )(parts, parts, parts, dt_rows)


def ring(n, k):
    return [(i, (i + k) % n) for i in range(n)]


def send_shard(v, k):
    return lax.ppermute(v, "shard", ring(SLOTS, k)) if k else v


def swap_section(v):
    return lax.ppermute(v, "section", [(0, 1), (1, 0)])


def dp_index(x, z, c):
    return x * 8 + z * 2 + c


def dp_pairs(move):
    pairs = []
    for x in range(2):
        for z in range(4):
            for c in range(2):
                pairs.append((dp_index(x, z, c), dp_index(*move(x, z, c))))
    return pairs


def pick(v, index, axis):
    return lax.dynamic_index_in_dim(v, index, axis, keepdims=False)


def gather_slots(v):
    return [send_shard(v, (-k) % SLOTS) for k in range(SLOTS)]


def scatter_sum(slots):
    parts = [send_shard(slots[k], k) for k in range(SLOTS)]
    return sum(p.astype(F32) for p in parts)


def section_pairs(k, layer):
    pairs = []
    for chip in range(4):
        to = (chip + k) % 4
        if to // 2 != layer:
            continue
        for z in range(4):
            for c in range(2):
                pairs.append(
                    (
                        (chip // 2) * 16 + dp_index(chip % 2, z, c),
                        (to // 2) * 16 + dp_index(to % 2, z, c),
                    )
                )
    return pairs


def sum_cores(v):
    c = lax.axis_index("dp") % 2
    v = v.reshape((2, 4, 2) + v.shape[1:])
    moved = lax.ppermute(pick(v, 1 - c, 2), "dp", dp_pairs(lambda x, z, c: (x, z, 1 - c)))
    return (pick(v, c, 2).astype(F32) + moved.astype(F32)).astype(BF16)


def sum_z(v):
    z = lax.axis_index("dp") // 2 % 4
    own = pick(v, z, 1).astype(F32)
    for k in range(1, 4):
        moved = lax.ppermute(
            pick(v, (z + k) % 4, 1), "dp", dp_pairs(lambda x, z, c: (x, (z + k) % 4, c))
        )
        own = own + moved.astype(F32)
    return own.astype(BF16)


def sum_x(v, layer):
    x = lax.axis_index("dp") // 8
    own = pick(v, x, 0).astype(F32)
    for k in range(1, 4):
        moved = lax.ppermute(pick(v, (x + k) % 2, 0), ("section", "dp"), section_pairs(k, layer))
        own = own + moved.astype(F32)
    return own.astype(BF16)


def sum_small(v):
    v = v + lax.ppermute(v, "dp", dp_pairs(lambda x, z, c: (x, z, 1 - c)))
    v = v + sum(
        lax.ppermute(v, "dp", dp_pairs(lambda x, z, c: (x, (z + k) % 4, c))) for k in range(1, 4)
    )
    return v + lax.ppermute(v, "dp", dp_pairs(lambda x, z, c: (1 - x, z, c)))


def in_order(parts, sign):
    j = lax.axis_index("shard")
    stacked = jnp.stack(parts)
    return jnp.take(stacked, (sign * (jnp.arange(SLOTS) - j)) % SLOTS, axis=0)


def shards(
    tokens,
    cotangent,
    lengths,
    norm_gain,
    in_weight,
    conv_weight,
    conv_bias,
    dt_bias,
    a_log,
    d_skip,
    gate_gain,
    out_weight,
):
    sec = lax.axis_index("section")
    d = lax.axis_index("dp")
    j = lax.axis_index("shard")
    core = d % 2
    first = sec == 0
    width = tokens.shape[2]
    quarter = norm_gain.shape[1]
    channels = conv_bias.shape[1]
    own_cols = gate_gain.shape[1]
    inner = own_cols * SLOTS
    heads = dt_bias.shape[1]
    own_heads = heads // SLOTS
    n_state = 2 * LANES
    piece = own_cols // 16
    piece_bc = n_state // 16

    x_own = pick(tokens, sec, 0)
    cot = pick(cotangent, sec, 0)
    length = pick(lengths, sec, 0)
    mask = (jnp.arange(T, dtype=jnp.int32) < length).astype(F32)[:, None]

    columns = jnp.transpose(in_weight[0])
    with jax.named_scope("weights"):

        def cut(start, rows):
            return lax.dynamic_slice(columns, (start, 0), (rows, quarter))

        def columns_of(to):
            return jnp.concatenate(
                [
                    cut(own_cols * to + piece * d, piece),
                    cut(inner + own_cols * to + piece * d, piece),
                    cut(2 * inner + piece_bc * d, piece_bc),
                ],
                axis=0,
            )

        parts = [send_shard(columns_of((j + k) % SLOTS), k) for k in range(SLOTS)]
        w_own = jnp.transpose(in_order(parts, -1), (1, 0, 2)).reshape(-1, width)
        w_other = swap_section(w_own)
        w0 = jnp.where(first, w_own, w_other)
        w1 = jnp.where(first, w_other, w_own)
        w0, x_own, cot, out_weight, norm_gain = lax.optimization_barrier(
            (w0, x_own, cot, out_weight, norm_gain)
        )
        w0 = lax.all_gather(w0, "dp", axis=0, tiled=False)
        half = own_cols // 2
        o_half = swap_section(lax.dynamic_slice(out_weight[0], (half * core, 0), (half, width)))
        o_rest = lax.ppermute(o_half, "dp", dp_pairs(lambda x, z, c: (x, z, 1 - c)))
        even = core == 0
        o_other = jnp.concatenate(
            [jnp.where(even, o_half, o_rest), jnp.where(even, o_rest, o_half)], axis=0
        )
        o0 = jnp.where(first, out_weight[0], o_other)
        o1 = jnp.where(first, o_other, out_weight[0])

    with jax.named_scope("small_weights"):
        dt_columns = columns[2 * inner + n_state :]
        sizes = [quarter, 4 * channels, channels, own_cols, heads, heads, heads, heads * quarter]
        flat = jnp.concatenate(
            [
                norm_gain[0],
                conv_weight[0].reshape(-1),
                conv_bias[0],
                gate_gain[0],
                dt_bias[0],
                a_log[0],
                d_skip[0],
                dt_columns.reshape(-1),
            ]
        )
        flat = jnp.pad(flat, (0, -flat.shape[0] % LANES)).reshape(-1, LANES)
        own = in_order(gather_slots(flat), 1)
        other = swap_section(own)
        small = [jnp.where(first, own, other), jnp.where(first, other, own)]

        def unpack(v):
            low = v.reshape(SLOTS, -1)
            at = sum(sizes[:-1])
            dtw = low[:, at : at + sizes[-1]].reshape(SLOTS, heads, quarter)
            dtw = lax.dynamic_slice(dtw, (0, own_heads * j, 0), (SLOTS, own_heads, quarter))
            dtw = jnp.transpose(dtw, (1, 0, 2)).reshape(own_heads, width)
            dtw = jnp.pad(dtw, ((0, LANES - own_heads), (0, 0)))
            v = low[:, :at].astype(F32)
            cut, at = [], 0
            for size in sizes[:-1]:
                cut.append(v[:, at : at + size])
                at += size
            gain = cut[0].reshape(1, width)
            taps = cut[1].reshape(SLOTS, 4, channels).transpose(1, 0, 2).reshape(4, -1)
            bias = cut[2].reshape(1, -1)
            conv = jnp.concatenate([taps, bias, jnp.zeros((3, taps.shape[1]), F32)], axis=0)
            pbcv = conv[:, inner:]
            pv = lax.dynamic_slice(conv, (0, own_cols * j), (8, own_cols))
            pick_heads = lambda u: lax.dynamic_slice(u[0], (own_heads * j,), (own_heads,))
            wide = jnp.repeat(pick_heads(cut[6]), HEAD)[None]
            pv = jnp.concatenate([pv[:5], pick(cut[3], j, 0)[None], wide, pv[7:]], axis=0)
            dtp = jnp.stack([pick_heads(cut[4]), -jnp.exp(pick_heads(cut[5]))])
            dtp = jnp.pad(dtp, ((0, 6), (0, LANES - own_heads)))
            return gain, dtw, pv, pbcv, dtp

        gain0, *params0 = unpack(small[0])
        gain1, *params1 = unpack(small[1])

    x_f = x_own.astype(F32)
    g1 = (mask * cot.astype(F32)).astype(BF16)
    x_slots = gather_slots(x_own)
    g1_slots = gather_slots(g1)
    w0, o0, o1, x_slots, g1_slots, gain0, params0, gain1, params1, w1 = lax.optimization_barrier(
        (w0, o0, o1, x_slots, g1_slots, gain0, params0, gain1, params1, w1)
    )
    w1 = lax.all_gather(w1, "dp", axis=0, tiled=False)
    blocks = lambda v: v.reshape(16, 7, 16, width)

    def layer_of(w, o, params):
        dtw, pv, pbcv, dtp = params
        return blocks(w), dtw, o, pv, pbcv, dtp

    def forward_layer(x, g, w, o, gain, params):
        w, dtw, o, pv, pbcv, dtp = layer_of(w, o, params)
        return forward(x, g, w, dtw, o, gain, pv, pbcv, dtp)

    parts, saved0 = forward_layer(x_slots, None, w0, o0, gain0, params0)
    branch = scatter_sum(parts)
    square = scatter_sum([saved0["stats"][0, 0:1, slot(k)] for k in range(SLOTS)])[0]
    scale0 = lax.rsqrt(square / inner + EPS)
    branch0 = branch * scale0[:, None]
    middle = (x_f + mask * branch0).astype(BF16)

    m_slots = gather_slots(middle)
    parts, saved1 = forward_layer(m_slots, g1_slots, w1, o1, gain1, params1)
    own = saved1["stats"][:, 0].reshape(2, SLOTS, T)
    back = [send_shard(own, k) for k in range(SLOTS)]
    summed = sum(jnp.roll(back[k], -k, axis=1) for k in range(SLOTS))
    scale1 = lax.rsqrt(summed[0] / inner + EPS)
    cross1 = scale1 * scale1 * scale1 * summed[1] / inner
    rows1 = jnp.pad(jnp.stack([scale1, cross1], axis=1), ((0, 0), (0, 6), (0, 0)))

    def norm_back(x, gain, grad):
        scale = lax.rsqrt(jnp.mean(x * x, axis=1, keepdims=True) + EPS)
        unit = x * scale
        dn = grad * gain
        dx = scale * (dn - unit * jnp.mean(dn * unit, axis=1, keepdims=True))
        return dx, jnp.sum(grad * unit, axis=0)

    layer1 = layer_of(w1, o1, params1)
    back1 = backward(
        ("gate", "scan", "input"),
        "backward_1",
        28,
        saved1,
        layer1,
        {"g": g1_slots, "rows": rows1},
    )
    dx, gain_grad1 = norm_back(
        middle.astype(F32), gain1, scatter_sum([back1[f"out{k}"] for k in range(SLOTS)])
    )
    grads1 = backward(
        ("wgate", "wscan"), "weight_grads_1", 8, saved1, layer1, {"g": g1_slots, **back1}
    )
    back1.update(grads1)
    branch = scatter_sum(parts) * scale1[0][:, None]
    result = middle.astype(F32) + mask * branch

    by_owner = lambda v: v.reshape(16, -1, width)
    owned1 = lax.psum_scatter(by_owner(back1["ga"]), "dp", scatter_dimension=0, tiled=False)
    owned1 = owned1 + lax.ppermute(owned1, "section", [(0, 1)])

    dmiddle = (cot.astype(F32) + dx).astype(BF16)
    g0 = (mask * dmiddle.astype(F32)).astype(BF16)
    cross0 = scale0 * scale0 * jnp.sum(g0.astype(F32) * branch0, axis=1) / inner
    own = jnp.pad(jnp.stack([scale0, cross0]), ((0, 6), (0, 0)))
    rows0 = jnp.stack(gather_slots(own))
    g0_slots = gather_slots(g0)
    layer0 = layer_of(w0, o0, params0)
    back0 = backward(
        ("gate", "wgate"), "backward_0_gate", 14, saved0, layer0, {"g": g0_slots, "rows": rows0}
    )
    a0 = sum_cores(by_owner(back0["ga"]))
    small_gate = back0["small"]
    back0.update(backward(("scan", "wscan"), "backward_0_scan", 20, saved0, layer0, back0))
    a0 = sum_z(a0)
    b0 = sum_z(sum_cores(by_owner(back0["gb"])))
    small_scan = back0["small"]
    back0.update(backward(("input",), "backward_0_input", 6, saved0, layer0, back0))
    dx, gain_grad0 = norm_back(
        x_f, gain0, scatter_sum([back0[f"out{k}"] for k in range(SLOTS)])
    )
    dtokens = dmiddle.astype(F32) + dx

    result_moved = lax.ppermute(result.astype(BF16), "section", [(0, 1)]).astype(F32)
    dtokens_moved = lax.ppermute(dtokens.astype(BF16), "section", [(1, 0)]).astype(F32)
    ends = jnp.where(
        first, jnp.stack([dtokens, dtokens_moved]), jnp.stack([result_moved, result])
    )[None]

    def to_section(v0, v1):
        kept = jnp.where(first, v0, v1).astype(F32)
        return kept + swap_section(jnp.where(first, v1, v0)).astype(F32)

    def to_rows(v):
        v = v.reshape(-1, SLOTS, quarter)
        return in_order([send_shard(pick(v, (j + k) % SLOTS, 1), k) for k in range(SLOTS)], -1)

    owned0 = jnp.concatenate([sum_x(a0, 0), sum_x(b0, 0)], axis=0)
    owned = jnp.where(first, owned0, owned1)
    by_rows = to_rows(jnp.concatenate([owned[:piece], owned[2 * piece :]], axis=0))
    shared = jnp.sum(by_rows[:, 2 * piece :].astype(F32), axis=0).astype(BF16)
    out_rows = jnp.transpose(owned[piece : 2 * piece].reshape(piece, SLOTS, quarter), (1, 0, 2))
    flat_quarters = lambda v: v.reshape(-1, quarter)
    gathered = lax.all_gather(
        jnp.concatenate(
            [
                flat_quarters(by_rows[:, :piece]),
                flat_quarters(out_rows),
                flat_quarters(by_rows[:, piece : 2 * piece]),
                shared,
            ],
            axis=0,
        ),
        "dp",
        tiled=False,
    )

    def small_of(by_pair, back, gain_grad):
        return jnp.concatenate(
            [
                by_pair.reshape(-1, LANES),
                back["small_bc"].reshape(-1, LANES),
                back["small_dt"],
                gain_grad.reshape(-1, LANES),
                back["gdt"].reshape(-1, LANES),
            ],
            axis=0,
        )

    small0 = small_of(small_gate + small_scan, back0, gain_grad0)
    small1 = small_of(back1["small"], back1, gain_grad1)
    small_sum = sum_small(to_section(small0, small1))
    everyone = in_order(gather_slots(small_sum), 1)
    n_pair, n_bc = PAIRS * 8, 2 * 8
    by_pair = everyone[:, :n_pair].reshape(SLOTS, PAIRS, 8, LANES)
    by_pair = by_pair.transpose(2, 0, 1, 3).reshape(8, inner)
    by_bc = jnp.sum(everyone[:, n_pair : n_pair + n_bc], axis=0)
    by_bc = by_bc.reshape(2, 8, LANES).transpose(1, 0, 2).reshape(8, n_state)
    at = n_pair + n_bc
    by_dt = everyone[:, at : at + 8, :own_heads].transpose(1, 0, 2).reshape(8, heads)
    at += 8
    gain_total = jnp.sum(everyone[:, at : at + width // LANES], axis=0).reshape(-1)
    at += width // LANES
    dt_rows = everyone[:, at:].reshape(SLOTS, 16, SLOTS, quarter)[:, :own_heads]
    dt_rows = pick(dt_rows, j, 2).reshape(heads, quarter)
    conv_total = jnp.concatenate([by_pair[:5], by_bc[:5]], axis=1)
    conv_own = lax.dynamic_slice(conv_total, (0, channels * j), (5, channels))
    grad_skip = jnp.sum(by_pair[6].reshape(heads, HEAD), axis=1)

    grad_in_weight, grad_out_weight = assemble(gathered, dt_rows)
    return (
        ends,
        lax.dynamic_slice(gain_total, (quarter * j,), (quarter,))[None],
        jnp.transpose(grad_in_weight)[None],
        conv_own[None, :4],
        conv_own[4][None],
        by_dt[0][None],
        by_dt[1][None],
        grad_skip[None],
        lax.dynamic_slice(by_pair[5], (own_cols * j,), (own_cols,))[None],
        grad_out_weight[None],
    )


def solution(mesh):
    return jax.shard_map(
        shards,
        mesh=mesh,
        in_specs=(
            P(("dp", "shard"), None, None),
            P(("dp", "shard"), None, None),
            P(("dp", "shard")),
            P("section", "shard"),
            P("section", "shard", None),
            P("section", None, "shard"),
            P("section", "shard"),
            P("section", None),
            P("section", None),
            P("section", None),
            P("section", "shard"),
            P("section", "shard", None),
        ),
        out_specs=(
            P("section", ("dp", "shard"), None, None),
            P("section", "shard"),
            P("section", "shard", None),
            P("section", None, "shard"),
            P("section", "shard"),
            P("section", None),
            P("section", None),
            P("section", None),
            P("section", "shard"),
            P("section", "shard", None),
        ),
        check_vma=False,
    )
```

```python
import jax
import jax.numpy as jnp
from jax import lax
from jax.experimental import pallas as pl
from jax.experimental.pallas import tpu as pltpu
from jax.sharding import PartitionSpec as P

F32 = jnp.float32
BF16 = jnp.bfloat16
HI = lax.Precision.HIGHEST
EPS = 1e-05
T = 128
LANES = 128
HEAD = 64
SLOTS = 4
ROWS = SLOTS * T
PAIRS = 6
STEPS = 2
HALF = PAIRS // STEPS
WIDE = HALF * LANES
VMEM_LIMIT = 60 * 1024 * 1024


def sigmoid(v):
    return 0.5 * jnp.tanh(0.5 * v) + 0.5


def softplus(v):
    return jnp.maximum(v, 0.0) + jnp.log1p(jnp.exp(-jnp.abs(v)))


def dot(a, b):
    return jnp.dot(a, b, preferred_element_type=F32)


def dot_nt(a, b, precision=None):
    return lax.dot_general(
        a, b, (((1,), (1,)), ((), ())), preferred_element_type=F32, precision=precision
    )


def dot_tn(a, b, precision=None):
    return lax.dot_general(
        a, b, (((0,), (0,)), ((), ())), preferred_element_type=F32, precision=precision
    )


def iota(axis):
    return lax.broadcasted_iota(jnp.int32, (T, LANES), axis)


def shift_down(v, steps):
    return jnp.where(iota(0) >= steps, pltpu.roll(v, steps, 0), 0.0)


def shift_up(v, steps):
    return jnp.where(iota(0) < T - steps, pltpu.roll(v, T - steps, 0), 0.0)


def conv_taps(cin):
    return [shift_down(cin, 3), shift_down(cin, 2), shift_down(cin, 1), cin]


def conv_sum(taps, par):
    total = par[4:5, :] + taps[0] * par[0:1, :]
    for k in range(1, 4):
        total = total + taps[k] * par[k : k + 1, :]
    return total


def conv_back(dcv, par):
    total = dcv * par[3:4, :]
    for m in range(1, 4):
        total = total + shift_up(dcv, m) * par[3 - m : 4 - m, :]
    return total


def column_sum(v):
    return jnp.sum(v, axis=0, keepdims=True)


def slot(k):
    return slice(k * T, (k + 1) * T)


def tri(lower):
    if lower:
        return (iota(0) >= iota(1)).astype(F32)
    return (iota(0) <= iota(1)).astype(F32)


def step_prep(k, pbc, dtp, run_col, run_row, step_wide):
    step = softplus(pbc[slot(k), 256:384] + dtp[0:1, :])
    run = jnp.dot(tri(True), step * dtp[1:2, :], precision=HI, preferred_element_type=F32)
    run_row[k] = jnp.transpose(run)
    left = iota(1) < HEAD
    for p in range(PAIRS):
        a, b = 2 * p, 2 * p + 1
        run_col[a, slot(k), :] = jnp.broadcast_to(run[:, a : a + 1], (T, LANES))
        run_col[b, slot(k), :] = jnp.broadcast_to(run[:, b : b + 1], (T, LANES))
        step_wide[p, slot(k), :] = jnp.where(
            left,
            jnp.broadcast_to(step[:, a : a + 1], (T, LANES)),
            jnp.broadcast_to(step[:, b : b + 1], (T, LANES)),
        )
    return step


def halves(v):
    left = iota(1) < HEAD
    zero = jnp.zeros_like(v)
    return jnp.concatenate([jnp.where(left, v, zero), jnp.where(left, zero, v)], axis=0)


class Refs:
    pass


def kernel_call(body, name, ins, outs, scratch, cost_us):
    in_names, out_names, scratch_names = list(ins), list(outs), list(scratch)

    def run(*refs):
        rf = Refs()
        for key, ref in zip(in_names + out_names + scratch_names, refs):
            setattr(rf, key, ref)
        body(rf, pl.program_id(0))

    res = pl.pallas_call(
        run,
        grid=(STEPS,),
        in_specs=[
            pl.BlockSpec(*ins[n][1:]) if len(ins[n]) > 2 else pl.BlockSpec(memory_space=ins[n][1])
            for n in in_names
        ],
        out_specs=[pl.BlockSpec(outs[n][2], outs[n][3]) for n in out_names],
        out_shape=[jax.ShapeDtypeStruct(outs[n][0], outs[n][1]) for n in out_names],
        scratch_shapes=[pltpu.VMEM(*scratch[n]) for n in scratch_names],
        compiler_params=pltpu.CompilerParams(vmem_limit_bytes=VMEM_LIMIT),
        cost_estimate=pl.CostEstimate(
            flops=int(cost_us * 1.1e9), bytes_accessed=1 << 20, transcendentals=0
        ),
        name=name,
    )(*[ins[n][0] for n in in_names])
    return dict(zip(out_names, res))


def whole(v):
    return (v, v.shape, lambda h: (0,) * v.ndim)


def whole_out(shape, dtype):
    return (shape, dtype, shape, lambda h: (0,) * len(shape))


def by_step(v, block):
    return (v, block, lambda h: (h,) + (0,) * (len(block) - 1))


def by_step_out(shape, dtype, block):
    return (shape, dtype, block, lambda h: (h,) + (0,) * (len(block) - 1))


def lanes_by_step(v):
    return (v, (v.shape[0], WIDE), lambda h: (0, h))


def lanes_by_step_out(shape, dtype):
    return (shape, dtype, (shape[0], WIDE), lambda h: (0, h))


def weight_blocks(w):
    half = (8, 3, 16, w.shape[3])
    return {
        "wg": (w, half, lambda h: (h, 0, 0, 0)),
        "wv": (w, half, lambda h: (h, 1, 0, 0)),
        "wbc": (w, (16, 1, 16, w.shape[3]), lambda h: (0, 9, 0, 0)),
    }


def pair_lanes(p):
    return slice(p * LANES, (p + 1) * LANES)


def flat_rows(ref):
    v = ref[...]
    return v.reshape(-1, v.shape[-1])


def mixed_bc(rf, k, c):
    lanes = slice(c * LANES, (c + 1) * LANES)
    cv = conv_sum(conv_taps(rf.pbc[slot(k), lanes]), rf.pbcv[:, lanes])
    return cv * sigmoid(cv)


def forward(x_slots, g_slots, w, dtw, gain, pv, pbcv, dtp):
    width = x_slots[0].shape[1]
    with_grad = g_slots is not None

    def body(rf, h):
        @pl.when(h == 0)
        def _prep():
            for k in range(SLOTS):
                x = getattr(rf, f"x{k}")[...].astype(F32)
                scale = lax.rsqrt(jnp.mean(x * x, axis=1, keepdims=True) + EPS)
                rf.normed[slot(k), :] = (x * scale * rf.gain[...]).astype(BF16)
                if with_grad:
                    rf.g_all[slot(k), :] = getattr(rf, f"g{k}")[...]
            rf.pbc[:, 0:256] = dot_nt(rf.normed[...], flat_rows(rf.wbc))
            rf.pbc[:, 256:384] = dot_nt(rf.normed[...], rf.dtw[...])
            for k in range(SLOTS):
                rf.scores[k] = dot_nt(mixed_bc(rf, k, 1), mixed_bc(rf, k, 0), HI) * tri(True)
                step_prep(k, rf.pbc, rf.dtp, rf.run_col, rf.run_row, rf.step_wide)
            rf.square[...] = jnp.zeros_like(rf.square)
            rf.cross[...] = jnp.zeros_like(rf.cross)

        rf.proj[0, :, 0:WIDE] = dot_nt(rf.normed[...], flat_rows(rf.wg))
        rf.proj[0, :, WIDE : 2 * WIDE] = dot_nt(rf.normed[...], flat_rows(rf.wv))
        if with_grad:
            q_all = dot_nt(rf.g_all[...], rf.wout[pl.ds(8 * h, 8)].reshape(WIDE, width))
        for p in range(HALF):
            lanes = pair_lanes(p)
            par = rf.pv[:, lanes]
            pair = HALF * h + p
            for k in range(SLOTS):
                gate = rf.proj[0, slot(k), lanes]
                cv = conv_sum(
                    conv_taps(rf.proj[0, slot(k), WIDE + p * LANES : WIDE + (p + 1) * LANES]), par
                )
                values = cv * sigmoid(cv)
                scaled = (values * rf.step_wide[pair, slot(k), :]).astype(BF16)
                weights = []
                for a in range(2):
                    gap = (
                        rf.run_col[2 * pair + a, slot(k), :]
                        - rf.run_row[k, pl.ds(2 * pair + a, 1), :]
                    )
                    decay = jnp.exp(jnp.minimum(gap, 0.0))
                    weights.append((rf.scores[k] * decay).astype(BF16))
                y = dot(jnp.concatenate(weights, axis=1), halves(scaled))
                rf.y[0, slot(k), lanes] = y
                scanned = y + par[6:7, :] * values
                gated = scanned * (gate * sigmoid(gate))
                rf.square[slot(k), :] += gated * gated
                scaled_out = gated * par[5:6, :]
                rf.u_all[h, slot(k), lanes] = scaled_out.astype(BF16)
                if with_grad:
                    rf.cross[slot(k), :] += q_all[slot(k), lanes] * scaled_out

        @pl.when(h == STEPS - 1)
        def _finish():
            u = jnp.concatenate([rf.u_all[a] for a in range(STEPS)], axis=1)
            for n in range(0, width, 512):
                part = dot(u, rf.wout[:, :, :, n : n + 512].reshape(STEPS * WIDE, 512)).astype(BF16)
                for k in range(SLOTS):
                    getattr(rf, f"out{k}")[:, n : n + 512] = part[slot(k), :]
            ones = jnp.ones((8, LANES), F32)
            rf.stats[0] = dot_nt(ones, rf.square[...], HI)
            rf.stats[1] = dot_nt(ones, rf.cross[...], HI)

    ins = {f"x{k}": whole(v) for k, v in enumerate(x_slots)}
    if with_grad:
        ins.update({f"g{k}": whole(v) for k, v in enumerate(g_slots)})
    ins.update(
        gain=whole(gain),
        **weight_blocks(w),
        dtw=whole(dtw),
        wout=(w, (16, 3, 16, width), lambda h: (0, 2, 0, 0)),
        pv=lanes_by_step(pv),
        pbcv=whole(pbcv),
        dtp=whole(dtp),
    )
    outs = {f"out{k}": whole_out((T, width), BF16) for k in range(SLOTS)}
    outs.update(
        stats=whole_out((2, 8, ROWS), F32),
        normed=whole_out((ROWS, width), BF16),
        proj=by_step_out((STEPS, ROWS, 2 * WIDE), F32, (1, ROWS, 2 * WIDE)),
        y=by_step_out((STEPS, ROWS, WIDE), F32, (1, ROWS, WIDE)),
        pbc=whole_out((ROWS, 384), F32),
    )
    scratch = dict(
        scores=((SLOTS, T, T), F32),
        run_col=((2 * PAIRS, ROWS, LANES), F32),
        run_row=((SLOTS, T, LANES), F32),
        step_wide=((PAIRS, ROWS, LANES), F32),
        u_all=((STEPS, ROWS, WIDE), BF16),
        square=((ROWS, LANES), F32),
        cross=((ROWS, LANES), F32),
    )
    if with_grad:
        scratch["g_all"] = ((ROWS, width), BF16)
    res = kernel_call(body, "layer_forward", ins, outs, scratch, 18)
    return [res[f"out{k}"] for k in range(SLOTS)], res


def head_columns(pair):
    target = 2 * pair + (iota(0) >= HEAD).astype(jnp.int32)
    one = (iota(1) == target).astype(BF16)
    return jnp.concatenate([one, one], axis=0)


def head_sum(v, columns):
    high = v.astype(BF16)
    low = (v - high.astype(F32)).astype(BF16)
    return dot(jnp.concatenate([high, low], axis=1), columns)


def put_by_core(rf, key, x, at, part):
    keep, send = getattr(rf, key + "_keep"), getattr(rf, key + "_send")
    groups = slice(at, at + part.shape[2])
    for c in range(2):

        @pl.when(rf.core[0] == c)
        def _store(c=c):
            for z in range(4):
                keep[x, z, groups] = part[z, c]
                send[x, z, groups] = part[z, 1 - c]


def backward(stages, name, cost_us, saved, layer, have):
    gate, scan, inp, wgate, wscan = (
        s in stages for s in ("gate", "scan", "input", "wgate", "wscan")
    )
    width = saved["normed"].shape[1]
    w, dtw, pv, pbcv, dtp = layer
    elementwise = gate or scan

    def body(rf, h):
        @pl.when(h == 0)
        def _prep():
            for k in range(SLOTS):
                if gate or wgate:
                    rf.g_all[slot(k), :] = getattr(rf, f"g{k}")[...]
                if gate:
                    for row, ref in ((0, rf.scale_row), (1, rf.cross_row)):
                        ref[slot(k), :] = jnp.transpose(
                            jnp.broadcast_to(rf.rows[k, row : row + 1, :], (T, LANES))
                        )
                if scan:
                    inbound, outbound = mixed_bc(rf, k, 0), mixed_bc(rf, k, 1)
                    rf.mixed[0, slot(k), :] = inbound
                    rf.mixed[1, slot(k), :] = outbound
                    rf.scores[k] = dot_nt(inbound, outbound, HI) * tri(False)
                    rf.step_all[slot(k), :] = step_prep(
                        k, rf.pbc, rf.dtp, rf.run_col, rf.run_row, rf.step_wide
                    )
            if scan:
                rf.dscores[...] = jnp.zeros_like(rf.dscores)
                rf.dstep[...] = jnp.zeros_like(rf.dstep)
                rf.drun[...] = jnp.zeros_like(rf.drun)
            if inp:
                rf.total[...] = jnp.zeros_like(rf.total)

        if gate:
            q_all = dot_nt(rf.g_all[...], flat_rows(rf.wout))
        for p in range(HALF if elementwise else 0):
            lanes = pair_lanes(p)
            par = rf.pv[:, lanes]
            pair = HALF * h + p
            sums = [jnp.zeros((1, LANES), F32) for _ in range(8)]
            if scan:
                columns = head_columns(pair)
            for k in range(SLOTS):
                taps = conv_taps(rf.proj[0, slot(k), WIDE + p * LANES : WIDE + (p + 1) * LANES])
                cv = conv_sum(taps, par)
                sig_c = sigmoid(cv)
                values = cv * sig_c
                y = rf.y[0, slot(k), lanes]
                if gate:
                    gate_in = rf.proj[0, slot(k), lanes]
                    sig_g = sigmoid(gate_in)
                    silu_g = gate_in * sig_g
                    scanned = y + par[6:7, :] * values
                    gated = scanned * silu_g
                    grad_no = q_all[slot(k), lanes]
                    scale = rf.scale_row[slot(k), :]
                    dgated = scale * (grad_no * par[5:6, :]) - rf.cross_row[slot(k), :] * gated
                    norm = gated * scale
                    sums[5] += column_sum(grad_no * norm)
                    rf.u[slot(k), lanes] = (norm * par[5:6, :]).astype(BF16)
                    dscan = dgated * silu_g
                    dgate = dgated * scanned * (sig_g * (1.0 + gate_in * (1.0 - sig_g)))
                    sums[6] += column_sum(dscan * values)
                    rf.dg[slot(k), lanes] = dgate.astype(BF16)
                    if not scan:
                        rf.dscan[slot(k), lanes] = dscan
                else:
                    dscan = rf.dscan[slot(k), lanes]
                if not scan:
                    continue
                wide = rf.step_wide[pair, slot(k), :]
                dy = dscan.astype(BF16)
                scaled = (values * wide).astype(BF16)
                dweights = dot_nt(halves(scaled), dy)
                weights = []
                dscore = rf.dscores[k]
                for a in range(2):
                    gap = (
                        rf.run_row[k, pl.ds(2 * pair + a, 1), :]
                        - rf.run_col[2 * pair + a, slot(k), :]
                    )
                    decay = jnp.exp(jnp.minimum(gap, 0.0))
                    weights.append((rf.scores[k] * decay).astype(BF16))
                    dscore = dscore + dweights[slot(a), :] * decay
                rf.dscores[k] = dscore
                dscaled = dot(jnp.concatenate(weights, axis=1), halves(dy))
                rf.dstep[slot(k), :] += head_sum(dscaled * values, columns)
                rf.drun[slot(k), :] += head_sum(
                    dy.astype(F32) * y - scaled.astype(F32) * dscaled, columns
                )
                dvalues = dscaled * wide + par[6:7, :] * dscan
                dcv = dvalues * (sig_c * (1.0 + cv * (1.0 - sig_c)))
                for t in range(4):
                    sums[t] += column_sum(dcv * taps[t])
                sums[4] += column_sum(dcv)
                rf.dv[slot(k), lanes] = conv_back(dcv, par).astype(BF16)
            rf.small[p] = jnp.concatenate(sums, axis=0)
        if wgate and wscan:
            for at, left, right in (
                (0, rf.dg, rf.normed),
                (3, rf.u, rf.g_all),
                (6, rf.dv, rf.normed),
            ):
                part = dot_tn(left[...], right[...]).astype(BF16)
                rf.ga[:, at : at + 3] = part.reshape(8, 3, 16, width)
            part = dot_tn(rf.dbc_half[...], rf.normed[...]).astype(BF16)
            rf.ga[:, 9] = part.reshape(8, 16, width)
        elif wgate:
            for at, left, right in ((0, rf.dg, rf.normed), (3, rf.u, rf.g_all)):
                part = dot_tn(left[...], right[...]).astype(BF16)
                put_by_core(rf, "ga", h, at, part.reshape(4, 2, 3, 16, width))
        elif wscan:
            part = dot_tn(rf.dv[...], rf.normed[...]).astype(BF16)
            put_by_core(rf, "gb", h, 0, part.reshape(4, 2, 3, 16, width))
        if inp:
            rf.total[...] += dot(rf.dg[...], flat_rows(rf.wg)) + dot(rf.dv[...], flat_rows(rf.wv))

        @pl.when(h == STEPS - 1)
        def _finish():
            if scan:
                sums = [[jnp.zeros((1, LANES), F32) for _ in range(8)] for _ in range(2)]
                dt_sums = [jnp.zeros((1, LANES), F32) for _ in range(8)]
                live = iota(1) < 2 * PAIRS
                for k in range(SLOTS):
                    dscore = rf.dscores[k] * tri(False)
                    dmixed = (
                        jnp.dot(
                            dscore,
                            rf.mixed[1, slot(k), :],
                            precision=HI,
                            preferred_element_type=F32,
                        ),
                        dot_tn(dscore, rf.mixed[0, slot(k), :], HI),
                    )
                    for c in range(2):
                        lanes = slice(c * LANES, (c + 1) * LANES)
                        par = rf.pbcv[:, lanes]
                        taps = conv_taps(rf.pbc[slot(k), lanes])
                        cv = conv_sum(taps, par)
                        sig = sigmoid(cv)
                        dcv = dmixed[c] * (sig * (1.0 + cv * (1.0 - sig)))
                        for t in range(4):
                            sums[c][t] += column_sum(dcv * taps[t])
                        sums[c][4] += column_sum(dcv)
                        rf.dbc[slot(k), lanes] = conv_back(dcv, par).astype(BF16)
                    dlog = jnp.dot(
                        tri(False), rf.drun[slot(k), :], precision=HI, preferred_element_type=F32
                    )
                    grad_step = rf.dstep[slot(k), :] + dlog * rf.dtp[1:2, :]
                    dt_sums[1] += column_sum(dlog * rf.step_all[slot(k), :])
                    draw = grad_step * sigmoid(rf.pbc[slot(k), 256:384] + rf.dtp[0:1, :])
                    draw = jnp.where(live, draw, 0.0)
                    dt_sums[0] += column_sum(draw)
                    rf.dbc[slot(k), 256:384] = draw.astype(BF16)
                rf.small_bc[0] = jnp.concatenate(sums[0], axis=0)
                rf.small_bc[1] = jnp.concatenate(sums[1], axis=0)
                dt_sums[1] = dt_sums[1] * rf.dtp[1:2, :]
                rf.small_dt[...] = jnp.concatenate(dt_sums, axis=0)
            if wscan and not wgate:
                part = dot_tn(rf.dbc[:, 0:256], rf.normed[...]).astype(BF16)
                part = part.reshape(2, 4, 2, 1, 16, width)
                for a in range(2):
                    put_by_core(rf, "gb", a, 3, part[a])
            if wscan:
                rf.gdt[...] = dot_tn(rf.dbc[:, 256:384], rf.normed[...])[0:16]
            if inp:
                final = (
                    rf.total[...]
                    + dot(rf.dbc[:, 0:256], flat_rows(rf.wbc))
                    + dot(rf.dbc[:, 256:384], rf.dtw[...])
                )
                for k in range(SLOTS):
                    getattr(rf, f"out{k}")[...] = final[slot(k), :].astype(BF16)

    ins, outs, scratch = {}, {}, {}
    heads_cols = STEPS * WIDE
    if gate or wgate:
        ins.update({f"g{k}": whole(v) for k, v in enumerate(have["g"])})
        scratch["g_all"] = ((ROWS, width), BF16)
    if gate:
        ins["rows"] = whole(have["rows"])
        ins["wout"] = (w, (8, 3, 16, width), lambda h: (h, 2, 0, 0))
        scratch["scale_row"] = ((ROWS, LANES), F32)
        scratch["cross_row"] = ((ROWS, LANES), F32)
        outs["u"] = lanes_by_step_out((ROWS, heads_cols), BF16)
        outs["dg"] = lanes_by_step_out((ROWS, heads_cols), BF16)
        if not scan:
            outs["dscan"] = lanes_by_step_out((ROWS, heads_cols), F32)
    if elementwise:
        ins["proj"] = by_step(saved["proj"], (1, ROWS, 2 * WIDE))
        ins["y"] = by_step(saved["y"], (1, ROWS, WIDE))
        ins["pv"] = lanes_by_step(pv)
        outs["small"] = by_step_out((PAIRS, 8, LANES), F32, (HALF, 8, LANES))
    if scan:
        ins["pbc"] = whole(saved["pbc"])
        ins["pbcv"] = whole(pbcv)
        ins["dtp"] = whole(dtp)
        if not gate:
            ins["dscan"] = lanes_by_step(have["dscan"])
        outs["dv"] = lanes_by_step_out((ROWS, heads_cols), BF16)
        outs["dbc"] = whole_out((ROWS, 384), BF16)
        outs["small_bc"] = whole_out((2, 8, LANES), F32)
        outs["small_dt"] = whole_out((8, LANES), F32)
        scratch.update(
            mixed=((2, ROWS, LANES), F32),
            scores=((SLOTS, T, T), F32),
            run_col=((2 * PAIRS, ROWS, LANES), F32),
            run_row=((SLOTS, T, LANES), F32),
            step_wide=((PAIRS, ROWS, LANES), F32),
            step_all=((ROWS, LANES), F32),
            dscores=((SLOTS, T, T), F32),
            dstep=((ROWS, LANES), F32),
            drun=((ROWS, LANES), F32),
        )
    if inp:
        ins.update(weight_blocks(w))
        ins["dtw"] = whole(dtw)
        scratch["total"] = ((ROWS, width), F32)
        outs.update({f"out{k}": whole_out((T, width), BF16) for k in range(SLOTS)})
    if wgate or wscan:
        ins["normed"] = whole(saved["normed"])
    if not gate and (wgate or inp):
        ins["dg"] = lanes_by_step(have["dg"])
    if wgate and not gate:
        ins["u"] = lanes_by_step(have["u"])
    if not scan and (wscan or inp):
        ins["dv"] = lanes_by_step(have["dv"])
        ins["dbc"] = whole(have["dbc"])
    if wgate and wscan:
        ins["dbc_half"] = (have["dbc"], (ROWS, LANES), lambda h: (0, h))
        outs["ga"] = by_step_out((16, 10, 16, width), BF16, (8, 10, 16, width))
    elif wgate or wscan:
        ins["core"] = have["core"]
        key, groups = ("ga", 6) if wgate else ("gb", 4)
        for end in ("_keep", "_send"):
            outs[key + end] = whole_out((2, 4, groups, 16, width), BF16)
    if wscan:
        outs["gdt"] = whole_out((16, width), F32)
    return kernel_call(body, name, ins, outs, scratch, cost_us)


def assemble(parts, dt_rows):
    quarter = parts.shape[2]
    block = 16 * 48
    total = 8 * block + 16 * 16 + dt_rows.shape[0]

    def body(inw, outw, shared, dt, grad_in, grad_out):
        i = pl.program_id(0)

        @pl.when(i < 8)
        def _columns():
            grad_in[...] = inw[...].reshape(block, quarter).astype(F32)

        @pl.when(i < SLOTS)
        def _out():
            grad_out[...] = outw[...].reshape(block, quarter).astype(F32)

        @pl.when(i == 8)
        def _shared():
            grad_in[...] = jnp.zeros_like(grad_in)
            grad_in[0:256, :] = shared[...].reshape(256, quarter).astype(F32)
            grad_in[256 : 256 + dt_rows.shape[0], :] = dt[...]

    last = SLOTS - 1
    return pl.pallas_call(
        body,
        grid=(9,),
        in_specs=[
            pl.BlockSpec(
                (16, 48, quarter),
                lambda i: (0, jnp.where(i < SLOTS, i, jnp.minimum(i + SLOTS, 11)), 0),
            ),
            pl.BlockSpec((16, 48, quarter), lambda i: (0, SLOTS + jnp.minimum(i, last), 0)),
            pl.BlockSpec((16, 16, quarter), lambda i: (0, 36, 0)),
            pl.BlockSpec(dt_rows.shape, lambda i: (0, 0)),
        ],
        out_specs=[
            pl.BlockSpec((block, quarter), lambda i: (i, 0)),
            pl.BlockSpec((block, quarter), lambda i: (0, jnp.minimum(i, last))),
        ],
        out_shape=[
            jax.ShapeDtypeStruct((total, quarter), F32),
            jax.ShapeDtypeStruct((block, SLOTS * quarter), F32),
        ],
        compiler_params=pltpu.CompilerParams(vmem_limit_bytes=VMEM_LIMIT),
        name="assemble",
    )(parts, parts, parts, dt_rows)


def ring(n, k):
    return [(i, (i + k) % n) for i in range(n)]


def send_shard(v, k):
    return lax.ppermute(v, "shard", ring(SLOTS, k)) if k else v


def swap_section(v):
    return lax.ppermute(v, "section", [(0, 1), (1, 0)])


def dp_index(x, z, c):
    return x * 8 + z * 2 + c


def dp_pairs(move):
    pairs = []
    for x in range(2):
        for z in range(4):
            for c in range(2):
                pairs.append((dp_index(x, z, c), dp_index(*move(x, z, c))))
    return pairs


def pick(v, index, axis):
    return lax.dynamic_index_in_dim(v, index, axis, keepdims=False)


def gather_slots(v):
    return [send_shard(v, (-k) % SLOTS) for k in range(SLOTS)]


def scatter_sum(slots):
    parts = [send_shard(slots[k], k) for k in range(SLOTS)]
    return sum(p.astype(F32) for p in parts)


def section_pairs(k, layer):
    pairs = []
    for chip in range(4):
        to = (chip + k) % 4
        if to // 2 != layer:
            continue
        for z in range(4):
            for c in range(2):
                pairs.append(
                    (
                        (chip // 2) * 16 + dp_index(chip % 2, z, c),
                        (to // 2) * 16 + dp_index(to % 2, z, c),
                    )
                )
    return pairs


def sum_parts(parts):
    return sum(p.astype(F32) for p in parts).astype(BF16)


def cross_core(v):
    return lax.ppermute(v, "dp", dp_pairs(lambda x, z, c: (x, z, 1 - c)))


def by_distance(parts):
    z = lax.axis_index("dp") // 2 % 4
    return [sum_parts([pick(p, (z + k) % 4, 1) for p in parts]) for k in range(4)]


def cross_z(slots):
    return [slots[0]] + [
        lax.ppermute(slots[k], "dp", dp_pairs(lambda x, z, c: (x, (z + k) % 4, c)))
        for k in range(1, 4)
    ]


def sum_x(parts, layer):
    x = lax.axis_index("dp") // 8
    same = sum_parts([pick(p, x, 0) for p in parts])
    other = sum_parts([pick(p, 1 - x, 0) for p in parts])
    moved = [
        lax.ppermute(same if k == 2 else other, ("section", "dp"), section_pairs(k, layer))
        for k in range(1, 4)
    ]
    return sum_parts([same] + moved)


def sum_small(v):
    v = v + lax.ppermute(v, "dp", dp_pairs(lambda x, z, c: (x, z, 1 - c)))
    v = v + sum(
        lax.ppermute(v, "dp", dp_pairs(lambda x, z, c: (x, (z + k) % 4, c))) for k in range(1, 4)
    )
    return v + lax.ppermute(v, "dp", dp_pairs(lambda x, z, c: (1 - x, z, c)))


def in_order(parts, sign):
    j = lax.axis_index("shard")
    stacked = jnp.stack(parts)
    return jnp.take(stacked, (sign * (jnp.arange(SLOTS) - j)) % SLOTS, axis=0)


def shards(
    tokens,
    cotangent,
    lengths,
    norm_gain,
    in_weight,
    conv_weight,
    conv_bias,
    dt_bias,
    a_log,
    d_skip,
    gate_gain,
    out_weight,
):
    sec = lax.axis_index("section")
    d = lax.axis_index("dp")
    j = lax.axis_index("shard")
    core = d % 2
    first = sec == 0
    width = tokens.shape[2]
    quarter = norm_gain.shape[1]
    channels = conv_bias.shape[1]
    own_cols = gate_gain.shape[1]
    inner = own_cols * SLOTS
    heads = dt_bias.shape[1]
    own_heads = heads // SLOTS
    n_state = 2 * LANES
    piece = own_cols // 16
    piece_bc = n_state // 16
    own_core = (core.astype(jnp.int32)[None], pltpu.SMEM)

    x_own = pick(tokens, sec, 0)
    cot = pick(cotangent, sec, 0)
    length = pick(lengths, sec, 0)
    mask = (jnp.arange(T, dtype=jnp.int32) < length).astype(F32)[:, None]

    columns = jnp.transpose(in_weight[0])
    with jax.named_scope("weights"):

        def cut(start, rows):
            return lax.dynamic_slice(columns, (start, 0), (rows, quarter))

        def columns_of(to):
            return jnp.concatenate(
                [
                    cut(own_cols * to + piece * d, piece),
                    cut(inner + own_cols * to + piece * d, piece),
                    cut(2 * inner + piece_bc * d, piece_bc),
                ],
                axis=0,
            )

        parts = [send_shard(columns_of((j + k) % SLOTS), k) for k in range(SLOTS)]
        w_own = jnp.transpose(in_order(parts, -1), (1, 0, 2)).reshape(-1, width)
        o_own = lax.dynamic_slice(out_weight[0], (piece * d, 0), (piece, width))
        w_own = jnp.concatenate([w_own[: 2 * piece], o_own, w_own[2 * piece :]], axis=0)
        w_other = swap_section(w_own)
        w0 = jnp.where(first, w_own, w_other)
        w1 = jnp.where(first, w_other, w_own)
        w0, w1, x_own, cot, norm_gain = lax.optimization_barrier((w0, w1, x_own, cot, norm_gain))
        w0 = lax.all_gather(w0, "dp", axis=0, tiled=False)

    with jax.named_scope("small_weights"):
        dt_columns = columns[2 * inner + n_state :]
        sizes = [quarter, 4 * channels, channels, own_cols, heads, heads, heads, heads * quarter]
        flat = jnp.concatenate(
            [
                norm_gain[0],
                conv_weight[0].reshape(-1),
                conv_bias[0],
                gate_gain[0],
                dt_bias[0],
                a_log[0],
                d_skip[0],
                dt_columns.reshape(-1),
            ]
        )
        flat = jnp.pad(flat, (0, -flat.shape[0] % LANES)).reshape(-1, LANES)
        own = in_order(gather_slots(flat), 1)
        other = swap_section(own)
        small = [jnp.where(first, own, other), jnp.where(first, other, own)]

        def unpack(v):
            low = v.reshape(SLOTS, -1)
            at = sum(sizes[:-1])
            dtw = low[:, at : at + sizes[-1]].reshape(SLOTS, heads, quarter)
            dtw = lax.dynamic_slice(dtw, (0, own_heads * j, 0), (SLOTS, own_heads, quarter))
            dtw = jnp.transpose(dtw, (1, 0, 2)).reshape(own_heads, width)
            dtw = jnp.pad(dtw, ((0, LANES - own_heads), (0, 0)))
            v = low[:, :at].astype(F32)
            cut, at = [], 0
            for size in sizes[:-1]:
                cut.append(v[:, at : at + size])
                at += size
            gain = cut[0].reshape(1, width)
            taps = cut[1].reshape(SLOTS, 4, channels).transpose(1, 0, 2).reshape(4, -1)
            bias = cut[2].reshape(1, -1)
            conv = jnp.concatenate([taps, bias, jnp.zeros((3, taps.shape[1]), F32)], axis=0)
            pbcv = conv[:, inner:]
            pv = lax.dynamic_slice(conv, (0, own_cols * j), (8, own_cols))
            pick_heads = lambda u: lax.dynamic_slice(u[0], (own_heads * j,), (own_heads,))
            wide = jnp.repeat(pick_heads(cut[6]), HEAD)[None]
            pv = jnp.concatenate([pv[:5], pick(cut[3], j, 0)[None], wide, pv[7:]], axis=0)
            dtp = jnp.stack([pick_heads(cut[4]), -jnp.exp(pick_heads(cut[5]))])
            dtp = jnp.pad(dtp, ((0, 6), (0, LANES - own_heads)))
            return gain, dtw, pv, pbcv, dtp

        gain0, *params0 = unpack(small[0])
        gain1, *params1 = unpack(small[1])

    x_f = x_own.astype(F32)
    g1 = (mask * cot.astype(F32)).astype(BF16)
    x_slots = gather_slots(x_own)
    g1_slots = gather_slots(g1)
    w0, x_slots, g1_slots, gain0, params0, gain1, params1, w1 = lax.optimization_barrier(
        (w0, x_slots, g1_slots, gain0, params0, gain1, params1, w1)
    )
    w1 = lax.all_gather(w1, "dp", axis=0, tiled=False)
    blocks = lambda v: v.reshape(16, 10, 16, width)

    layer0 = (blocks(w0), *params0)
    layer1 = (blocks(w1), *params1)

    def forward_layer(x, g, gain, layer):
        w, dtw, pv, pbcv, dtp = layer
        return forward(x, g, w, dtw, gain, pv, pbcv, dtp)

    parts, saved0 = forward_layer(x_slots, None, gain0, layer0)
    branch = scatter_sum(parts)
    square = scatter_sum([saved0["stats"][0, 0:1, slot(k)] for k in range(SLOTS)])[0]
    scale0 = lax.rsqrt(square / inner + EPS)
    branch0 = branch * scale0[:, None]
    middle = (x_f + mask * branch0).astype(BF16)

    m_slots = gather_slots(middle)
    branch_parts, saved1 = forward_layer(m_slots, g1_slots, gain1, layer1)
    own = saved1["stats"][:, 0].reshape(2, SLOTS, T)
    back = [send_shard(own, k) for k in range(SLOTS)]
    summed = sum(jnp.roll(back[k], -k, axis=1) for k in range(SLOTS))
    scale1 = lax.rsqrt(summed[0] / inner + EPS)
    cross1 = scale1 * scale1 * scale1 * summed[1] / inner
    rows1 = jnp.pad(jnp.stack([scale1, cross1], axis=1), ((0, 0), (0, 6), (0, 0)))

    def norm_back(x, gain, grad):
        scale = lax.rsqrt(jnp.mean(x * x, axis=1, keepdims=True) + EPS)
        unit = x * scale
        dn = grad * gain
        dx = scale * (dn - unit * jnp.mean(dn * unit, axis=1, keepdims=True))
        return dx, jnp.sum(grad * unit, axis=0)

    back1 = backward(
        ("gate", "scan", "input"),
        "backward_1",
        28,
        saved1,
        layer1,
        {"g": g1_slots, "rows": rows1},
    )
    dx, gain_grad1 = norm_back(
        middle.astype(F32), gain1, scatter_sum([back1[f"out{k}"] for k in range(SLOTS)])
    )
    grads1 = backward(
        ("wgate", "wscan"), "weight_grads_1", 8, saved1, layer1, {"g": g1_slots, **back1}
    )
    back1.update(grads1)
    by_owner = lambda v: v.reshape(16, -1, width)
    owned1 = lax.psum_scatter(by_owner(back1["ga"]), "dp", scatter_dimension=0, tiled=False)
    owned1 = owned1 + lax.ppermute(owned1, "section", [(0, 1)])

    dmiddle = (cot.astype(F32) + dx).astype(BF16)
    g0 = (mask * dmiddle.astype(F32)).astype(BF16)
    cross0 = scale0 * scale0 * jnp.sum(g0.astype(F32) * branch0, axis=1) / inner
    own = jnp.pad(jnp.stack([scale0, cross0]), ((0, 6), (0, 0)))
    rows0 = jnp.stack(gather_slots(own))
    g0_slots = gather_slots(g0)
    g0_slots, branch_parts = lax.optimization_barrier((g0_slots, branch_parts))
    branch = scatter_sum(branch_parts) * scale1[0][:, None]
    result = middle.astype(F32) + mask * branch

    back0 = backward(
        ("gate", "wgate"),
        "backward_0_gate",
        14,
        saved0,
        layer0,
        {"g": g0_slots, "rows": rows0, "core": own_core},
    )
    a0 = by_distance([back0["ga_keep"], cross_core(back0["ga_send"])])
    a0, back0["dscan"] = lax.optimization_barrier((a0, back0["dscan"]))
    a0 = cross_z(a0)
    small_gate = back0["small"]
    back0["core"] = own_core
    back0.update(backward(("scan", "wscan"), "backward_0_scan", 20, saved0, layer0, back0))
    b0 = by_distance([back0["gb_keep"], cross_core(back0["gb_send"])])
    b0, back0["dv"] = lax.optimization_barrier((b0, back0["dv"]))
    b0 = cross_z(b0)
    small_scan = back0["small"]
    back0.update(backward(("input",), "backward_0_input", 9, saved0, layer0, back0))
    dx, gain_grad0 = norm_back(
        x_f, gain0, scatter_sum([back0[f"out{k}"] for k in range(SLOTS)])
    )
    dtokens = dmiddle.astype(F32) + dx

    result_moved = lax.ppermute(result.astype(BF16), "section", [(0, 1)]).astype(F32)
    dtokens_moved = lax.ppermute(dtokens.astype(BF16), "section", [(1, 0)]).astype(F32)
    ends = jnp.where(
        first, jnp.stack([dtokens, dtokens_moved]), jnp.stack([result_moved, result])
    )[None]

    def to_section(v0, v1):
        kept = jnp.where(first, v0, v1).astype(F32)
        return kept + swap_section(jnp.where(first, v1, v0)).astype(F32)

    def to_rows(v):
        v = v.reshape(-1, SLOTS, quarter)
        return in_order([send_shard(pick(v, (j + k) % SLOTS, 1), k) for k in range(SLOTS)], -1)

    owned0 = jnp.concatenate([sum_x(a0, 0), sum_x(b0, 0)], axis=0).reshape(-1, width)
    owned = jnp.where(first, owned0, owned1)
    by_rows = to_rows(jnp.concatenate([owned[:piece], owned[2 * piece :]], axis=0))
    shared = jnp.sum(by_rows[:, 2 * piece :].astype(F32), axis=0).astype(BF16)
    out_rows = jnp.transpose(owned[piece : 2 * piece].reshape(piece, SLOTS, quarter), (1, 0, 2))
    flat_quarters = lambda v: v.reshape(-1, quarter)
    gathered = lax.all_gather(
        jnp.concatenate(
            [
                flat_quarters(by_rows[:, :piece]),
                flat_quarters(out_rows),
                flat_quarters(by_rows[:, piece : 2 * piece]),
                shared,
            ],
            axis=0,
        ),
        "dp",
        tiled=False,
    )

    def small_of(by_pair, back, gain_grad):
        return jnp.concatenate(
            [
                by_pair.reshape(-1, LANES),
                back["small_bc"].reshape(-1, LANES),
                back["small_dt"],
                gain_grad.reshape(-1, LANES),
                back["gdt"].reshape(-1, LANES),
            ],
            axis=0,
        )

    small0 = small_of(small_gate + small_scan, back0, gain_grad0)
    small1 = small_of(back1["small"], back1, gain_grad1)
    small_sum = sum_small(to_section(small0, small1))
    everyone = in_order(gather_slots(small_sum), 1)
    n_pair, n_bc = PAIRS * 8, 2 * 8
    by_pair = everyone[:, :n_pair].reshape(SLOTS, PAIRS, 8, LANES)
    by_pair = by_pair.transpose(2, 0, 1, 3).reshape(8, inner)
    by_bc = jnp.sum(everyone[:, n_pair : n_pair + n_bc], axis=0)
    by_bc = by_bc.reshape(2, 8, LANES).transpose(1, 0, 2).reshape(8, n_state)
    at = n_pair + n_bc
    by_dt = everyone[:, at : at + 8, :own_heads].transpose(1, 0, 2).reshape(8, heads)
    at += 8
    gain_total = jnp.sum(everyone[:, at : at + width // LANES], axis=0).reshape(-1)
    at += width // LANES
    dt_rows = everyone[:, at:].reshape(SLOTS, 16, SLOTS, quarter)[:, :own_heads]
    dt_rows = pick(dt_rows, j, 2).reshape(heads, quarter)
    conv_total = jnp.concatenate([by_pair[:5], by_bc[:5]], axis=1)
    conv_own = lax.dynamic_slice(conv_total, (0, channels * j), (5, channels))
    grad_skip = jnp.sum(by_pair[6].reshape(heads, HEAD), axis=1)

    grad_in_weight, grad_out_weight = assemble(gathered, dt_rows)
    return (
        ends,
        lax.dynamic_slice(gain_total, (quarter * j,), (quarter,))[None],
        jnp.transpose(grad_in_weight)[None],
        conv_own[None, :4],
        conv_own[4][None],
        by_dt[0][None],
        by_dt[1][None],
        grad_skip[None],
        lax.dynamic_slice(by_pair[5], (own_cols * j,), (own_cols,))[None],
        grad_out_weight[None],
    )


def solution(mesh):
    return jax.shard_map(
        shards,
        mesh=mesh,
        in_specs=(
            P(("dp", "shard"), None, None),
            P(("dp", "shard"), None, None),
            P(("dp", "shard")),
            P("section", "shard"),
            P("section", "shard", None),
            P("section", None, "shard"),
            P("section", "shard"),
            P("section", None),
            P("section", None),
            P("section", None),
            P("section", "shard"),
            P("section", "shard", None),
        ),
        out_specs=(
            P("section", ("dp", "shard"), None, None),
            P("section", "shard"),
            P("section", "shard", None),
            P("section", None, "shard"),
            P("section", "shard"),
            P("section", None),
            P("section", None),
            P("section", None),
            P("section", "shard"),
            P("section", "shard", None),
        ),
        check_vma=False,
    )
```

```python
import jax
import jax.numpy as jnp
from jax import lax
from jax.experimental import pallas as pl
from jax.experimental.pallas import tpu as pltpu
from jax.sharding import PartitionSpec as P

F32 = jnp.float32
BF16 = jnp.bfloat16
HI = lax.Precision.HIGHEST
EPS = 1e-05
T = 128
LANES = 128
HEAD = 64
SLOTS = 4
ROWS = SLOTS * T
PAIRS = 6
STEPS = 2
HALF = PAIRS // STEPS
WIDE = HALF * LANES
VMEM_LIMIT = 60 * 1024 * 1024


def sigmoid(v):
    return 0.5 * jnp.tanh(0.5 * v) + 0.5


def softplus(v):
    return jnp.maximum(v, 0.0) + jnp.log1p(jnp.exp(-jnp.abs(v)))


def dot(a, b):
    return jnp.dot(a, b, preferred_element_type=F32)


def dot_nt(a, b, precision=None):
    return lax.dot_general(
        a, b, (((1,), (1,)), ((), ())), preferred_element_type=F32, precision=precision
    )


def dot_tn(a, b, precision=None):
    return lax.dot_general(
        a, b, (((0,), (0,)), ((), ())), preferred_element_type=F32, precision=precision
    )


def iota(axis):
    return lax.broadcasted_iota(jnp.int32, (T, LANES), axis)


def shift_down(v, steps):
    return jnp.where(iota(0) >= steps, pltpu.roll(v, steps, 0), 0.0)


def shift_up(v, steps):
    return jnp.where(iota(0) < T - steps, pltpu.roll(v, T - steps, 0), 0.0)


def conv_taps(cin):
    return [shift_down(cin, 3), shift_down(cin, 2), shift_down(cin, 1), cin]


def conv_sum(taps, par):
    total = par[4:5, :] + taps[0] * par[0:1, :]
    for k in range(1, 4):
        total = total + taps[k] * par[k : k + 1, :]
    return total


def conv_back(dcv, par):
    total = dcv * par[3:4, :]
    for m in range(1, 4):
        total = total + shift_up(dcv, m) * par[3 - m : 4 - m, :]
    return total


def column_sum(v):
    return jnp.sum(v, axis=0, keepdims=True)


def slot(k):
    return slice(k * T, (k + 1) * T)


def tri(lower):
    if lower:
        return (iota(0) >= iota(1)).astype(F32)
    return (iota(0) <= iota(1)).astype(F32)


def step_prep(k, pbc, dtp, run_col, run_row, step_wide):
    step = softplus(pbc[slot(k), 256:384] + dtp[0:1, :])
    run = jnp.dot(tri(True), step * dtp[1:2, :], precision=HI, preferred_element_type=F32)
    run_row[k] = jnp.transpose(run)
    left = iota(1) < HEAD
    for p in range(PAIRS):
        a, b = 2 * p, 2 * p + 1
        run_col[a, slot(k), :] = jnp.broadcast_to(run[:, a : a + 1], (T, LANES))
        run_col[b, slot(k), :] = jnp.broadcast_to(run[:, b : b + 1], (T, LANES))
        step_wide[p, slot(k), :] = jnp.where(
            left,
            jnp.broadcast_to(step[:, a : a + 1], (T, LANES)),
            jnp.broadcast_to(step[:, b : b + 1], (T, LANES)),
        )
    return step


def halves(v):
    left = iota(1) < HEAD
    zero = jnp.zeros_like(v)
    return jnp.concatenate([jnp.where(left, v, zero), jnp.where(left, zero, v)], axis=0)


class Refs:
    pass


def kernel_call(body, name, ins, outs, scratch, cost_us):
    in_names, out_names, scratch_names = list(ins), list(outs), list(scratch)

    def run(*refs):
        rf = Refs()
        for key, ref in zip(in_names + out_names + scratch_names, refs):
            setattr(rf, key, ref)
        body(rf, pl.program_id(0))

    res = pl.pallas_call(
        run,
        grid=(STEPS,),
        in_specs=[
            pl.BlockSpec(*ins[n][1:]) if len(ins[n]) > 2 else pl.BlockSpec(memory_space=ins[n][1])
            for n in in_names
        ],
        out_specs=[pl.BlockSpec(outs[n][2], outs[n][3]) for n in out_names],
        out_shape=[jax.ShapeDtypeStruct(outs[n][0], outs[n][1]) for n in out_names],
        scratch_shapes=[pltpu.VMEM(*scratch[n]) for n in scratch_names],
        compiler_params=pltpu.CompilerParams(vmem_limit_bytes=VMEM_LIMIT),
        cost_estimate=pl.CostEstimate(
            flops=int(cost_us * 1.1e9), bytes_accessed=1 << 20, transcendentals=0
        ),
        name=name,
    )(*[ins[n][0] for n in in_names])
    return dict(zip(out_names, res))


def whole(v):
    return (v, v.shape, lambda h: (0,) * v.ndim)


def whole_out(shape, dtype):
    return (shape, dtype, shape, lambda h: (0,) * len(shape))


def by_step(v, block):
    return (v, block, lambda h: (h,) + (0,) * (len(block) - 1))


def by_step_out(shape, dtype, block):
    return (shape, dtype, block, lambda h: (h,) + (0,) * (len(block) - 1))


def lanes_by_step(v):
    return (v, (v.shape[0], WIDE), lambda h: (0, h))


def lanes_by_step_out(shape, dtype):
    return (shape, dtype, (shape[0], WIDE), lambda h: (0, h))


def weight_blocks(w):
    half = (8, 3, 16, w.shape[3])
    return {
        "wg": (w, half, lambda h: (h, 1, 0, 0)),
        "wv": (w, half, lambda h: (h, 2, 0, 0)),
        "wbc": (w, (16, 1, 16, w.shape[3]), lambda h: (0, 9, 0, 0)),
    }


def pair_lanes(p):
    return slice(p * LANES, (p + 1) * LANES)


def flat_rows(ref):
    v = ref[...]
    return v.reshape(-1, v.shape[-1])


def mixed_bc(rf, k, c):
    lanes = slice(c * LANES, (c + 1) * LANES)
    cv = conv_sum(conv_taps(rf.pbc[slot(k), lanes]), rf.pbcv[:, lanes])
    return cv * sigmoid(cv)


def forward(x_slots, g_slots, w, dtw, gain, pv, pbcv, dtp):
    width = x_slots[0].shape[1]
    with_grad = g_slots is not None

    def body(rf, h):
        @pl.when(h == 0)
        def _prep():
            for k in range(SLOTS):
                x = getattr(rf, f"x{k}")[...].astype(F32)
                scale = lax.rsqrt(jnp.mean(x * x, axis=1, keepdims=True) + EPS)
                rf.normed[slot(k), :] = (x * scale * rf.gain[...]).astype(BF16)
                if with_grad:
                    rf.g_all[slot(k), :] = getattr(rf, f"g{k}")[...]
            rf.pbc[:, 0:256] = dot_nt(rf.normed[...], flat_rows(rf.wbc))
            rf.pbc[:, 256:384] = dot_nt(rf.normed[...], rf.dtw[...])
            for k in range(SLOTS):
                rf.scores[k] = dot_nt(mixed_bc(rf, k, 1), mixed_bc(rf, k, 0), HI) * tri(True)
                step_prep(k, rf.pbc, rf.dtp, rf.run_col, rf.run_row, rf.step_wide)
            rf.square[...] = jnp.zeros_like(rf.square)
            rf.cross[...] = jnp.zeros_like(rf.cross)

        rf.proj[0, :, 0:WIDE] = dot_nt(rf.normed[...], flat_rows(rf.wg))
        rf.proj[0, :, WIDE : 2 * WIDE] = dot_nt(rf.normed[...], flat_rows(rf.wv))
        if with_grad:
            q_all = dot_nt(rf.g_all[...], rf.wout[pl.ds(8 * h, 8)].reshape(WIDE, width))
        for p in range(HALF):
            lanes = pair_lanes(p)
            par = rf.pv[:, lanes]
            pair = HALF * h + p
            for k in range(SLOTS):
                gate = rf.proj[0, slot(k), lanes]
                cv = conv_sum(
                    conv_taps(rf.proj[0, slot(k), WIDE + p * LANES : WIDE + (p + 1) * LANES]), par
                )
                values = cv * sigmoid(cv)
                scaled = (values * rf.step_wide[pair, slot(k), :]).astype(BF16)
                weights = []
                for a in range(2):
                    gap = (
                        rf.run_col[2 * pair + a, slot(k), :]
                        - rf.run_row[k, pl.ds(2 * pair + a, 1), :]
                    )
                    decay = jnp.exp(jnp.minimum(gap, 0.0))
                    weights.append((rf.scores[k] * decay).astype(BF16))
                y = dot(jnp.concatenate(weights, axis=1), halves(scaled))
                rf.y[0, slot(k), lanes] = y
                scanned = y + par[6:7, :] * values
                gated = scanned * (gate * sigmoid(gate))
                rf.square[slot(k), :] += gated * gated
                scaled_out = gated * par[5:6, :]
                rf.u_all[h, slot(k), lanes] = scaled_out.astype(BF16)
                if with_grad:
                    rf.cross[slot(k), :] += q_all[slot(k), lanes] * scaled_out

        @pl.when(h == STEPS - 1)
        def _finish():
            u = jnp.concatenate([rf.u_all[a] for a in range(STEPS)], axis=1)
            for n in range(0, width, 512):
                part = dot(u, rf.wout[:, :, :, n : n + 512].reshape(STEPS * WIDE, 512)).astype(BF16)
                for k in range(SLOTS):
                    getattr(rf, f"out{k}")[:, n : n + 512] = part[slot(k), :]
            ones = jnp.ones((8, LANES), F32)
            rf.stats[0] = dot_nt(ones, rf.square[...], HI)
            rf.stats[1] = dot_nt(ones, rf.cross[...], HI)

    ins = {f"x{k}": whole(v) for k, v in enumerate(x_slots)}
    if with_grad:
        ins.update({f"g{k}": whole(v) for k, v in enumerate(g_slots)})
    ins.update(
        gain=whole(gain),
        **weight_blocks(w),
        dtw=whole(dtw),
        wout=(w, (16, 3, 16, width), lambda h: (0, 0, 0, 0)),
        pv=lanes_by_step(pv),
        pbcv=whole(pbcv),
        dtp=whole(dtp),
    )
    outs = {f"out{k}": whole_out((T, width), BF16) for k in range(SLOTS)}
    outs.update(
        stats=whole_out((2, 8, ROWS), F32),
        normed=whole_out((ROWS, width), BF16),
        proj=by_step_out((STEPS, ROWS, 2 * WIDE), F32, (1, ROWS, 2 * WIDE)),
        y=by_step_out((STEPS, ROWS, WIDE), F32, (1, ROWS, WIDE)),
        pbc=whole_out((ROWS, 384), F32),
    )
    scratch = dict(
        scores=((SLOTS, T, T), F32),
        run_col=((2 * PAIRS, ROWS, LANES), F32),
        run_row=((SLOTS, T, LANES), F32),
        step_wide=((PAIRS, ROWS, LANES), F32),
        u_all=((STEPS, ROWS, WIDE), BF16),
        square=((ROWS, LANES), F32),
        cross=((ROWS, LANES), F32),
    )
    if with_grad:
        scratch["g_all"] = ((ROWS, width), BF16)
    res = kernel_call(body, "layer_forward", ins, outs, scratch, 18)
    return [res[f"out{k}"] for k in range(SLOTS)], res


def head_columns(pair):
    target = 2 * pair + (iota(0) >= HEAD).astype(jnp.int32)
    one = (iota(1) == target).astype(BF16)
    return jnp.concatenate([one, one], axis=0)


def head_sum(v, columns):
    high = v.astype(BF16)
    low = (v - high.astype(F32)).astype(BF16)
    return dot(jnp.concatenate([high, low], axis=1), columns)


def put_by_core(rf, key, x, at, part):
    keep, send = getattr(rf, key + "_keep"), getattr(rf, key + "_send")
    groups = slice(at, at + part.shape[2])
    for c in range(2):

        @pl.when(rf.core[0] == c)
        def _store(c=c):
            for z in range(4):
                keep[x, z, groups] = part[z, c]
                send[x, z, groups] = part[z, 1 - c]


def backward(stages, name, cost_us, saved, layer, have):
    gate, scan, inp, wgate, wscan = (
        s in stages for s in ("gate", "scan", "input", "wgate", "wscan")
    )
    width = saved["normed"].shape[1]
    w, dtw, pv, pbcv, dtp = layer
    elementwise = gate or scan

    def body(rf, h):
        @pl.when(h == 0)
        def _prep():
            for k in range(SLOTS):
                if gate or wgate:
                    rf.g_all[slot(k), :] = getattr(rf, f"g{k}")[...]
                if gate:
                    for row, ref in ((0, rf.scale_row), (1, rf.cross_row)):
                        ref[slot(k), :] = jnp.transpose(
                            jnp.broadcast_to(rf.rows[k, row : row + 1, :], (T, LANES))
                        )
                if scan:
                    inbound, outbound = mixed_bc(rf, k, 0), mixed_bc(rf, k, 1)
                    rf.mixed[0, slot(k), :] = inbound
                    rf.mixed[1, slot(k), :] = outbound
                    rf.scores[k] = dot_nt(inbound, outbound, HI) * tri(False)
                    rf.step_all[slot(k), :] = step_prep(
                        k, rf.pbc, rf.dtp, rf.run_col, rf.run_row, rf.step_wide
                    )
            if scan:
                rf.dscores[...] = jnp.zeros_like(rf.dscores)
                rf.dstep[...] = jnp.zeros_like(rf.dstep)
                rf.drun[...] = jnp.zeros_like(rf.drun)
            if inp:
                rf.total[...] = jnp.zeros_like(rf.total)

        if gate:
            q_all = dot_nt(rf.g_all[...], flat_rows(rf.wout))
        for p in range(HALF if elementwise else 0):
            lanes = pair_lanes(p)
            par = rf.pv[:, lanes]
            pair = HALF * h + p
            sums = [jnp.zeros((1, LANES), F32) for _ in range(8)]
            if scan:
                columns = head_columns(pair)
            for k in range(SLOTS):
                taps = conv_taps(rf.proj[0, slot(k), WIDE + p * LANES : WIDE + (p + 1) * LANES])
                cv = conv_sum(taps, par)
                sig_c = sigmoid(cv)
                values = cv * sig_c
                y = rf.y[0, slot(k), lanes]
                if gate:
                    gate_in = rf.proj[0, slot(k), lanes]
                    sig_g = sigmoid(gate_in)
                    silu_g = gate_in * sig_g
                    scanned = y + par[6:7, :] * values
                    gated = scanned * silu_g
                    grad_no = q_all[slot(k), lanes]
                    scale = rf.scale_row[slot(k), :]
                    dgated = scale * (grad_no * par[5:6, :]) - rf.cross_row[slot(k), :] * gated
                    norm = gated * scale
                    sums[5] += column_sum(grad_no * norm)
                    rf.u[slot(k), lanes] = (norm * par[5:6, :]).astype(BF16)
                    dscan = dgated * silu_g
                    dgate = dgated * scanned * (sig_g * (1.0 + gate_in * (1.0 - sig_g)))
                    sums[6] += column_sum(dscan * values)
                    rf.dg[slot(k), lanes] = dgate.astype(BF16)
                    if not scan:
                        rf.dscan[slot(k), lanes] = dscan
                else:
                    dscan = rf.dscan[slot(k), lanes]
                if not scan:
                    continue
                wide = rf.step_wide[pair, slot(k), :]
                dy = dscan.astype(BF16)
                scaled = (values * wide).astype(BF16)
                dweights = dot_nt(halves(scaled), dy)
                weights = []
                dscore = rf.dscores[k]
                for a in range(2):
                    gap = (
                        rf.run_row[k, pl.ds(2 * pair + a, 1), :]
                        - rf.run_col[2 * pair + a, slot(k), :]
                    )
                    decay = jnp.exp(jnp.minimum(gap, 0.0))
                    weights.append((rf.scores[k] * decay).astype(BF16))
                    dscore = dscore + dweights[slot(a), :] * decay
                rf.dscores[k] = dscore
                dscaled = dot(jnp.concatenate(weights, axis=1), halves(dy))
                rf.dstep[slot(k), :] += head_sum(dscaled * values, columns)
                rf.drun[slot(k), :] += head_sum(
                    dy.astype(F32) * y - scaled.astype(F32) * dscaled, columns
                )
                dvalues = dscaled * wide + par[6:7, :] * dscan
                dcv = dvalues * (sig_c * (1.0 + cv * (1.0 - sig_c)))
                for t in range(4):
                    sums[t] += column_sum(dcv * taps[t])
                sums[4] += column_sum(dcv)
                rf.dv[slot(k), lanes] = conv_back(dcv, par).astype(BF16)
            rf.small[p] = jnp.concatenate(sums, axis=0)
        if wgate and wscan:
            for at, left, right in (
                (0, rf.dg, rf.normed),
                (3, rf.u, rf.g_all),
                (6, rf.dv, rf.normed),
            ):
                part = dot_tn(left[...], right[...]).astype(BF16)
                rf.ga[:, at : at + 3] = part.reshape(8, 3, 16, width)
            part = dot_tn(rf.dbc_half[...], rf.normed[...]).astype(BF16)
            rf.ga[:, 9] = part.reshape(8, 16, width)
        elif wgate:
            for at, left, right in ((0, rf.dg, rf.normed), (3, rf.u, rf.g_all)):
                part = dot_tn(left[...], right[...]).astype(BF16)
                put_by_core(rf, "ga", h, at, part.reshape(4, 2, 3, 16, width))
        elif wscan:
            part = dot_tn(rf.dv[...], rf.normed[...]).astype(BF16)
            put_by_core(rf, "gb", h, 0, part.reshape(4, 2, 3, 16, width))
        if inp:
            rf.total[...] += dot(rf.dg[...], flat_rows(rf.wg)) + dot(rf.dv[...], flat_rows(rf.wv))

        @pl.when(h == STEPS - 1)
        def _finish():
            if scan:
                sums = [[jnp.zeros((1, LANES), F32) for _ in range(8)] for _ in range(2)]
                dt_sums = [jnp.zeros((1, LANES), F32) for _ in range(8)]
                live = iota(1) < 2 * PAIRS
                for k in range(SLOTS):
                    dscore = rf.dscores[k] * tri(False)
                    dmixed = (
                        jnp.dot(
                            dscore,
                            rf.mixed[1, slot(k), :],
                            precision=HI,
                            preferred_element_type=F32,
                        ),
                        dot_tn(dscore, rf.mixed[0, slot(k), :], HI),
                    )
                    for c in range(2):
                        lanes = slice(c * LANES, (c + 1) * LANES)
                        par = rf.pbcv[:, lanes]
                        taps = conv_taps(rf.pbc[slot(k), lanes])
                        cv = conv_sum(taps, par)
                        sig = sigmoid(cv)
                        dcv = dmixed[c] * (sig * (1.0 + cv * (1.0 - sig)))
                        for t in range(4):
                            sums[c][t] += column_sum(dcv * taps[t])
                        sums[c][4] += column_sum(dcv)
                        rf.dbc[slot(k), lanes] = conv_back(dcv, par).astype(BF16)
                    dlog = jnp.dot(
                        tri(False), rf.drun[slot(k), :], precision=HI, preferred_element_type=F32
                    )
                    grad_step = rf.dstep[slot(k), :] + dlog * rf.dtp[1:2, :]
                    dt_sums[1] += column_sum(dlog * rf.step_all[slot(k), :])
                    draw = grad_step * sigmoid(rf.pbc[slot(k), 256:384] + rf.dtp[0:1, :])
                    draw = jnp.where(live, draw, 0.0)
                    dt_sums[0] += column_sum(draw)
                    rf.dbc[slot(k), 256:384] = draw.astype(BF16)
                rf.small_bc[0] = jnp.concatenate(sums[0], axis=0)
                rf.small_bc[1] = jnp.concatenate(sums[1], axis=0)
                dt_sums[1] = dt_sums[1] * rf.dtp[1:2, :]
                rf.small_dt[...] = jnp.concatenate(dt_sums, axis=0)
            if wscan and not wgate:
                part = dot_tn(rf.dbc[:, 0:256], rf.normed[...]).astype(BF16)
                part = part.reshape(2, 4, 2, 1, 16, width)
                for a in range(2):
                    put_by_core(rf, "gb", a, 3, part[a])
            if wscan:
                rf.gdt[...] = dot_tn(rf.dbc[:, 256:384], rf.normed[...])[0:16]
            if inp:
                final = (
                    rf.total[...]
                    + dot(rf.dbc[:, 0:256], flat_rows(rf.wbc))
                    + dot(rf.dbc[:, 256:384], rf.dtw[...])
                )
                for k in range(SLOTS):
                    getattr(rf, f"out{k}")[...] = final[slot(k), :].astype(BF16)

    ins, outs, scratch = {}, {}, {}
    heads_cols = STEPS * WIDE
    if gate or wgate:
        ins.update({f"g{k}": whole(v) for k, v in enumerate(have["g"])})
        scratch["g_all"] = ((ROWS, width), BF16)
    if gate:
        ins["rows"] = whole(have["rows"])
        ins["wout"] = (w, (8, 3, 16, width), lambda h: (h, 0, 0, 0))
        scratch["scale_row"] = ((ROWS, LANES), F32)
        scratch["cross_row"] = ((ROWS, LANES), F32)
        outs["u"] = lanes_by_step_out((ROWS, heads_cols), BF16)
        outs["dg"] = lanes_by_step_out((ROWS, heads_cols), BF16)
        if not scan:
            outs["dscan"] = lanes_by_step_out((ROWS, heads_cols), F32)
    if elementwise:
        ins["proj"] = by_step(saved["proj"], (1, ROWS, 2 * WIDE))
        ins["y"] = by_step(saved["y"], (1, ROWS, WIDE))
        ins["pv"] = lanes_by_step(pv)
        outs["small"] = by_step_out((PAIRS, 8, LANES), F32, (HALF, 8, LANES))
    if scan:
        ins["pbc"] = whole(saved["pbc"])
        ins["pbcv"] = whole(pbcv)
        ins["dtp"] = whole(dtp)
        if not gate:
            ins["dscan"] = lanes_by_step(have["dscan"])
        outs["dv"] = lanes_by_step_out((ROWS, heads_cols), BF16)
        outs["dbc"] = whole_out((ROWS, 384), BF16)
        outs["small_bc"] = whole_out((2, 8, LANES), F32)
        outs["small_dt"] = whole_out((8, LANES), F32)
        scratch.update(
            mixed=((2, ROWS, LANES), F32),
            scores=((SLOTS, T, T), F32),
            run_col=((2 * PAIRS, ROWS, LANES), F32),
            run_row=((SLOTS, T, LANES), F32),
            step_wide=((PAIRS, ROWS, LANES), F32),
            step_all=((ROWS, LANES), F32),
            dscores=((SLOTS, T, T), F32),
            dstep=((ROWS, LANES), F32),
            drun=((ROWS, LANES), F32),
        )
    if inp:
        ins.update(weight_blocks(w))
        ins["dtw"] = whole(dtw)
        scratch["total"] = ((ROWS, width), F32)
        outs.update({f"out{k}": whole_out((T, width), BF16) for k in range(SLOTS)})
    if wgate or wscan:
        ins["normed"] = whole(saved["normed"])
    if not gate and (wgate or inp):
        ins["dg"] = lanes_by_step(have["dg"])
    if wgate and not gate:
        ins["u"] = lanes_by_step(have["u"])
    if not scan and (wscan or inp):
        ins["dv"] = lanes_by_step(have["dv"])
        ins["dbc"] = whole(have["dbc"])
    if wgate and wscan:
        ins["dbc_half"] = (have["dbc"], (ROWS, LANES), lambda h: (0, h))
        outs["ga"] = by_step_out((16, 10, 16, width), BF16, (8, 10, 16, width))
    elif wgate or wscan:
        ins["core"] = have["core"]
        key, groups = ("ga", 6) if wgate else ("gb", 4)
        for end in ("_keep", "_send"):
            outs[key + end] = whole_out((2, 4, groups, 16, width), BF16)
    if wscan:
        outs["gdt"] = whole_out((16, width), F32)
    return kernel_call(body, name, ins, outs, scratch, cost_us)


def assemble(parts, dt_rows, shard):
    quarter = parts.shape[2]
    block = 16 * 48
    total = 8 * block + 16 * 16 + dt_rows.shape[0]

    def body(_, inw, outw, shared, dt, grad_in, grad_out):
        i = pl.program_id(0)

        @pl.when(i < 8)
        def _columns():
            grad_in[...] = inw[...].reshape(block, quarter).astype(F32)

        @pl.when(i < SLOTS)
        def _out():
            grad_out[...] = outw[...].reshape(block, quarter).astype(F32)

        @pl.when(i == 8)
        def _shared():
            grad_in[...] = jnp.zeros_like(grad_in)
            grad_in[0:256, :] = shared[...].reshape(256, quarter).astype(F32)
            grad_in[256 : 256 + dt_rows.shape[0], :] = dt[...]

    last = SLOTS - 1
    spec = pltpu.PrefetchScalarGridSpec(
        num_scalar_prefetch=1,
        grid=(9,),
        in_specs=[
            pl.BlockSpec(
                (16, 48, quarter),
                lambda i, j: (0, jnp.where(i < SLOTS, 0, 8) + (j[0] + 3 * SLOTS - i) % SLOTS, 0),
            ),
            pl.BlockSpec((16, 48, quarter), lambda i, j: (0, SLOTS + jnp.minimum(i, last), 0)),
            pl.BlockSpec((16, 16, quarter), lambda i, j: (0, 36, 0)),
            pl.BlockSpec(dt_rows.shape, lambda i, j: (0, 0)),
        ],
        out_specs=[
            pl.BlockSpec((block, quarter), lambda i, j: (i, 0)),
            pl.BlockSpec((block, quarter), lambda i, j: (0, jnp.minimum(i, last))),
        ],
    )
    return pl.pallas_call(
        body,
        grid_spec=spec,
        out_shape=[
            jax.ShapeDtypeStruct((total, quarter), F32),
            jax.ShapeDtypeStruct((block, SLOTS * quarter), F32),
        ],
        compiler_params=pltpu.CompilerParams(vmem_limit_bytes=VMEM_LIMIT),
        name="assemble",
    )(shard.astype(jnp.int32)[None], parts, parts, parts, dt_rows)


def ring(n, k):
    return [(i, (i + k) % n) for i in range(n)]


def send_shard(v, k):
    return lax.ppermute(v, "shard", ring(SLOTS, k)) if k else v


def send_across(v, k):
    pairs = [
        (sec * SLOTS + y, (1 - sec) * SLOTS + (y + k) % SLOTS)
        for sec in range(2)
        for y in range(SLOTS)
    ]
    return lax.ppermute(v, ("section", "shard"), pairs)


def swap_section(v):
    return lax.ppermute(v, "section", [(0, 1), (1, 0)])


def dp_index(x, z, c):
    return x * 8 + z * 2 + c


def dp_pairs(move):
    pairs = []
    for x in range(2):
        for z in range(4):
            for c in range(2):
                pairs.append((dp_index(x, z, c), dp_index(*move(x, z, c))))
    return pairs


def pick(v, index, axis):
    return lax.dynamic_index_in_dim(v, index, axis, keepdims=False)


def gather_slots(v):
    return [send_shard(v, (-k) % SLOTS) for k in range(SLOTS)]


def scatter_sum(slots):
    parts = [send_shard(slots[k], k) for k in range(SLOTS)]
    return sum(p.astype(F32) for p in parts)


def section_pairs(k, layer):
    pairs = []
    for chip in range(4):
        to = (chip + k) % 4
        if to // 2 != layer:
            continue
        for z in range(4):
            for c in range(2):
                pairs.append(
                    (
                        (chip // 2) * 16 + dp_index(chip % 2, z, c),
                        (to // 2) * 16 + dp_index(to % 2, z, c),
                    )
                )
    return pairs


def sum_parts(parts):
    return sum(p.astype(F32) for p in parts).astype(BF16)


def cross_core(v):
    return lax.ppermute(v, "dp", dp_pairs(lambda x, z, c: (x, z, 1 - c)))


def by_distance(parts):
    z = lax.axis_index("dp") // 2 % 4
    return [sum_parts([pick(p, (z + k) % 4, 1) for p in parts]) for k in range(4)]


def cross_z(slots):
    return [slots[0]] + [
        lax.ppermute(slots[k], "dp", dp_pairs(lambda x, z, c: (x, (z + k) % 4, c)))
        for k in range(1, 4)
    ]


def cross_x(parts, layer):
    x = lax.axis_index("dp") // 8
    same = sum_parts([pick(p, x, 0) for p in parts])
    other = sum_parts([pick(p, 1 - x, 0) for p in parts])
    return [same] + [
        lax.ppermute(same if k == 2 else other, ("section", "dp"), section_pairs(k, layer))
        for k in range(1, 4)
    ]


def sum_small(v):
    v = v + lax.ppermute(v, "dp", dp_pairs(lambda x, z, c: (x, z, 1 - c)))
    v = v + sum(
        lax.ppermute(v, "dp", dp_pairs(lambda x, z, c: (x, (z + k) % 4, c))) for k in range(1, 4)
    )
    return v + lax.ppermute(v, "dp", dp_pairs(lambda x, z, c: (1 - x, z, c)))


def in_order(parts, sign):
    j = lax.axis_index("shard")
    stacked = jnp.stack(parts)
    return jnp.take(stacked, (sign * (jnp.arange(SLOTS) - j)) % SLOTS, axis=0)


def shards(
    tokens,
    cotangent,
    lengths,
    norm_gain,
    in_weight,
    conv_weight,
    conv_bias,
    dt_bias,
    a_log,
    d_skip,
    gate_gain,
    out_weight,
):
    sec = lax.axis_index("section")
    d = lax.axis_index("dp")
    j = lax.axis_index("shard")
    core = d % 2
    first = sec == 0
    width = tokens.shape[2]
    quarter = norm_gain.shape[1]
    channels = conv_bias.shape[1]
    own_cols = gate_gain.shape[1]
    inner = own_cols * SLOTS
    heads = dt_bias.shape[1]
    own_heads = heads // SLOTS
    n_state = 2 * LANES
    piece = own_cols // 16
    piece_bc = n_state // 16
    own_core = (core.astype(jnp.int32)[None], pltpu.SMEM)

    x_own = pick(tokens, sec, 0)
    cot = pick(cotangent, sec, 0)
    length = pick(lengths, sec, 0)
    mask = (jnp.arange(T, dtype=jnp.int32) < length).astype(F32)[:, None]

    columns = jnp.transpose(in_weight[0])
    with jax.named_scope("weights"):

        def cut(start, rows):
            return lax.dynamic_slice(columns, (start, 0), (rows, quarter))

        def columns_of(to):
            return jnp.concatenate(
                [
                    cut(own_cols * to + piece * d, piece),
                    cut(inner + own_cols * to + piece * d, piece),
                    cut(2 * inner + piece_bc * d, piece_bc),
                ],
                axis=0,
            )

        cuts = [columns_of((j + k) % SLOTS) for k in range(SLOTS)]
        o_own = lax.dynamic_slice(out_weight[0], (piece * d, 0), (piece, width))
        o_other = swap_section(o_own)

        w_own = [send_shard(cuts[k], k) for k in range(SLOTS)]
        w_other = [send_across(cuts[k], k) for k in range(SLOTS)]

        def from_parts(parts, others, o, o_others, own):
            pieces = [jnp.where(own, p, q) for p, q in zip(parts, others)]
            lanes = []
            for y in range(SLOTS):
                v = pieces[0]
                for k in range(1, SLOTS):
                    v = jnp.where((j - y) % SLOTS == k, pieces[k], v)
                lanes.append(v)
            return jnp.concatenate(
                [jnp.where(own, o, o_others), jnp.concatenate(lanes, axis=1)], axis=0
            )

        w0 = from_parts(w_own, w_other, o_own, o_other, first)
        w1 = from_parts(w_own, w_other, o_own, o_other, ~first)
        w0, w1, x_own, cot = lax.optimization_barrier((w0, w1, x_own, cot))
        w0 = lax.all_gather(w0, "dp", axis=0, tiled=False)
        x_slots = gather_slots(x_own)
        x_slots, norm_gain = lax.optimization_barrier((x_slots, norm_gain))

    with jax.named_scope("small_weights"):
        dt_columns = columns[2 * inner + n_state :]
        sizes = [quarter, 4 * channels, channels, own_cols, heads, heads, heads, heads * quarter]
        flat = jnp.concatenate(
            [
                norm_gain[0],
                conv_weight[0].reshape(-1),
                conv_bias[0],
                gate_gain[0],
                dt_bias[0],
                a_log[0],
                d_skip[0],
                dt_columns.reshape(-1),
            ]
        )
        flat = jnp.pad(flat, (0, -flat.shape[0] % LANES)).reshape(-1, LANES)
        own = in_order(gather_slots(flat), 1)
        other = swap_section(own)
        small = [jnp.where(first, own, other), jnp.where(first, other, own)]

        def unpack(v):
            low = v.reshape(SLOTS, -1)
            at = sum(sizes[:-1])
            dtw = low[:, at : at + sizes[-1]].reshape(SLOTS, heads, quarter)
            dtw = lax.dynamic_slice(dtw, (0, own_heads * j, 0), (SLOTS, own_heads, quarter))
            dtw = jnp.transpose(dtw, (1, 0, 2)).reshape(own_heads, width)
            dtw = jnp.pad(dtw, ((0, LANES - own_heads), (0, 0)))
            v = low[:, :at].astype(F32)
            cut, at = [], 0
            for size in sizes[:-1]:
                cut.append(v[:, at : at + size])
                at += size
            gain = cut[0].reshape(1, width)
            taps = cut[1].reshape(SLOTS, 4, channels).transpose(1, 0, 2).reshape(4, -1)
            bias = cut[2].reshape(1, -1)
            conv = jnp.concatenate([taps, bias, jnp.zeros((3, taps.shape[1]), F32)], axis=0)
            pbcv = conv[:, inner:]
            pv = lax.dynamic_slice(conv, (0, own_cols * j), (8, own_cols))
            pick_heads = lambda u: lax.dynamic_slice(u[0], (own_heads * j,), (own_heads,))
            wide = jnp.repeat(pick_heads(cut[6]), HEAD)[None]
            pv = jnp.concatenate([pv[:5], pick(cut[3], j, 0)[None], wide, pv[7:]], axis=0)
            dtp = jnp.stack([pick_heads(cut[4]), -jnp.exp(pick_heads(cut[5]))])
            dtp = jnp.pad(dtp, ((0, 6), (0, LANES - own_heads)))
            return gain, dtw, pv, pbcv, dtp

        gain0, *params0 = unpack(small[0])
        gain1, *params1 = unpack(small[1])

    x_f = x_own.astype(F32)
    g1 = (mask * cot.astype(F32)).astype(BF16)
    g1_slots = gather_slots(g1)
    w0, x_slots, g1_slots, gain0, params0, gain1, params1, w1 = lax.optimization_barrier(
        (w0, x_slots, g1_slots, gain0, params0, gain1, params1, w1)
    )
    w1 = lax.all_gather(w1, "dp", axis=0, tiled=False)
    blocks = lambda v: v.reshape(16, 10, 16, width)

    layer0 = (blocks(w0), *params0)
    layer1 = (blocks(w1), *params1)

    def forward_layer(x, g, gain, layer):
        w, dtw, pv, pbcv, dtp = layer
        return forward(x, g, w, dtw, gain, pv, pbcv, dtp)

    parts, saved0 = forward_layer(x_slots, None, gain0, layer0)
    branch = scatter_sum(parts)
    square = scatter_sum([saved0["stats"][0, 0:1, slot(k)] for k in range(SLOTS)])[0]
    scale0 = lax.rsqrt(square / inner + EPS)
    branch0 = branch * scale0[:, None]
    middle = (x_f + mask * branch0).astype(BF16)

    m_slots = gather_slots(middle)
    branch_parts, saved1 = forward_layer(m_slots, g1_slots, gain1, layer1)
    own = saved1["stats"][:, 0].reshape(2, SLOTS, T)
    back = [send_shard(own, k) for k in range(SLOTS)]
    summed = sum(jnp.roll(back[k], -k, axis=1) for k in range(SLOTS))
    scale1 = lax.rsqrt(summed[0] / inner + EPS)
    cross1 = scale1 * scale1 * scale1 * summed[1] / inner
    rows1 = jnp.pad(jnp.stack([scale1, cross1], axis=1), ((0, 0), (0, 6), (0, 0)))

    def norm_back(x, gain, grad):
        scale = lax.rsqrt(jnp.mean(x * x, axis=1, keepdims=True) + EPS)
        unit = x * scale
        dn = grad * gain
        dx = scale * (dn - unit * jnp.mean(dn * unit, axis=1, keepdims=True))
        return dx, jnp.sum(grad * unit, axis=0)

    back1 = backward(
        ("gate", "scan", "input"),
        "backward_1",
        28,
        saved1,
        layer1,
        {"g": g1_slots, "rows": rows1},
    )
    moved = [send_shard(back1[f"out{k}"], k) for k in range(SLOTS)]
    grads1 = backward(
        ("wgate", "wscan"), "weight_grads_1", 8, saved1, layer1, {"g": g1_slots, **back1}
    )
    back1.update(grads1)
    moved, back1["ga"] = lax.optimization_barrier((moved, back1["ga"]))
    dx, gain_grad1 = norm_back(middle.astype(F32), gain1, sum(p.astype(F32) for p in moved))
    by_owner = lambda v: v.reshape(16, -1, width)
    owned1 = lax.psum_scatter(by_owner(back1["ga"]), "dp", scatter_dimension=0, tiled=False)

    dmiddle = (cot.astype(F32) + dx).astype(BF16)
    g0 = (mask * dmiddle.astype(F32)).astype(BF16)
    cross0 = scale0 * scale0 * jnp.sum(g0.astype(F32) * branch0, axis=1) / inner
    own = jnp.pad(jnp.stack([scale0, cross0]), ((0, 6), (0, 0)))
    rows0 = jnp.stack(gather_slots(own))
    g0_slots = gather_slots(g0)
    g0_slots, branch_parts = lax.optimization_barrier((g0_slots, branch_parts))
    branch = scatter_sum(branch_parts) * scale1[0][:, None]
    result = middle.astype(F32) + mask * branch

    back0 = backward(
        ("gate", "wgate"),
        "backward_0_gate",
        14,
        saved0,
        layer0,
        {"g": g0_slots, "rows": rows0, "core": own_core},
    )
    a0 = by_distance([back0["ga_keep"], cross_core(back0["ga_send"])])
    a0, back0["dscan"] = lax.optimization_barrier((a0, back0["dscan"]))
    a0 = cross_z(a0)
    small_gate = back0["small"]
    back0["core"] = own_core
    back0.update(backward(("scan", "wscan"), "backward_0_scan", 20, saved0, layer0, back0))
    a0[1], a0[3], gb_send = lax.optimization_barrier((a0[1], a0[3], back0["gb_send"]))
    a0, b_moved, owned1 = lax.optimization_barrier((a0, cross_core(gb_send), owned1))
    b0 = by_distance([back0["gb_keep"], b_moved])
    b0, back0["dv"], a0 = lax.optimization_barrier((b0, back0["dv"], a0))
    b0 = cross_z(b0)
    a0 = cross_x(a0, 0)
    small_scan = back0["small"]
    back0.update(backward(("input",), "backward_0_input", 9, saved0, layer0, back0))
    outs0 = [back0[f"out{k}"] for k in range(SLOTS)]
    a0, outs0 = lax.optimization_barrier((a0, outs0))
    moved0 = [send_shard(outs0[k], k) for k in range(SLOTS)]

    owned1 = (owned1 + lax.ppermute(owned1, "section", [(0, 1)])).reshape(10, 16, width)

    def to_rows(parts, kept):
        slots = []
        for k in range(SLOTS):
            cut = lambda v: lax.dynamic_slice_in_dim(v, quarter * ((j + k) % SLOTS), quarter, 2)
            mine = jnp.where(first, sum_parts([cut(p) for p in parts]), cut(kept))
            slots.append(send_shard(mine.reshape(-1, quarter), k))
        return slots

    gate_rows = to_rows([p[:3] for p in a0], owned1[:3])
    out_rows = jnp.where(first, sum_parts([p[3:] for p in a0]), owned1[3:6])
    out_rows = jnp.transpose(out_rows.reshape(piece, SLOTS, quarter), (1, 0, 2))
    gate_rows, out_rows, b0, moved0 = lax.optimization_barrier((gate_rows, out_rows, b0, moved0))
    value_rows = to_rows(cross_x(b0, 0), owned1[6:])
    dx, gain_grad0 = norm_back(x_f, gain0, sum(p.astype(F32) for p in moved0))
    dtokens = dmiddle.astype(F32) + dx

    result_moved = lax.ppermute(result.astype(BF16), "section", [(0, 1)]).astype(F32)
    dtokens_moved = lax.ppermute(dtokens.astype(BF16), "section", [(1, 0)]).astype(F32)
    ends = jnp.where(
        first, jnp.stack([dtokens, dtokens_moved]), jnp.stack([result_moved, result])
    )[None]

    def to_section(v0, v1):
        kept = jnp.where(first, v0, v1).astype(F32)
        return kept + swap_section(jnp.where(first, v1, v0)).astype(F32)

    shared = sum(v[piece:].astype(F32) for v in value_rows).astype(BF16)
    gathered = lax.all_gather(
        jnp.concatenate(
            gate_rows
            + [out_rows.reshape(-1, quarter)]
            + [v[:piece] for v in value_rows]
            + [shared],
            axis=0,
        ),
        "dp",
        tiled=False,
    )

    def small_of(by_pair, back, gain_grad):
        return jnp.concatenate(
            [
                by_pair.reshape(-1, LANES),
                back["small_bc"].reshape(-1, LANES),
                back["small_dt"],
                gain_grad.reshape(-1, LANES),
                back["gdt"].reshape(-1, LANES),
            ],
            axis=0,
        )

    small0 = small_of(small_gate + small_scan, back0, gain_grad0)
    small1 = small_of(back1["small"], back1, gain_grad1)
    small_sum = sum_small(to_section(small0, small1))
    everyone = in_order(gather_slots(small_sum), 1)
    n_pair, n_bc = PAIRS * 8, 2 * 8
    by_pair = everyone[:, :n_pair].reshape(SLOTS, PAIRS, 8, LANES)
    by_pair = by_pair.transpose(2, 0, 1, 3).reshape(8, inner)
    by_bc = jnp.sum(everyone[:, n_pair : n_pair + n_bc], axis=0)
    by_bc = by_bc.reshape(2, 8, LANES).transpose(1, 0, 2).reshape(8, n_state)
    at = n_pair + n_bc
    by_dt = everyone[:, at : at + 8, :own_heads].transpose(1, 0, 2).reshape(8, heads)
    at += 8
    gain_total = jnp.sum(everyone[:, at : at + width // LANES], axis=0).reshape(-1)
    at += width // LANES
    dt_rows = everyone[:, at:].reshape(SLOTS, 16, SLOTS, quarter)[:, :own_heads]
    dt_rows = pick(dt_rows, j, 2).reshape(heads, quarter)
    conv_total = jnp.concatenate([by_pair[:5], by_bc[:5]], axis=1)
    conv_own = lax.dynamic_slice(conv_total, (0, channels * j), (5, channels))
    grad_skip = jnp.sum(by_pair[6].reshape(heads, HEAD), axis=1)

    grad_in_weight, grad_out_weight = assemble(gathered, dt_rows, j)
    return (
        ends,
        lax.dynamic_slice(gain_total, (quarter * j,), (quarter,))[None],
        jnp.transpose(grad_in_weight)[None],
        conv_own[None, :4],
        conv_own[4][None],
        by_dt[0][None],
        by_dt[1][None],
        grad_skip[None],
        lax.dynamic_slice(by_pair[5], (own_cols * j,), (own_cols,))[None],
        grad_out_weight[None],
    )


def solution(mesh):
    return jax.shard_map(
        shards,
        mesh=mesh,
        in_specs=(
            P(("dp", "shard"), None, None),
            P(("dp", "shard"), None, None),
            P(("dp", "shard")),
            P("section", "shard"),
            P("section", "shard", None),
            P("section", None, "shard"),
            P("section", "shard"),
            P("section", None),
            P("section", None),
            P("section", None),
            P("section", "shard"),
            P("section", "shard", None),
        ),
        out_specs=(
            P("section", ("dp", "shard"), None, None),
            P("section", "shard"),
            P("section", "shard", None),
            P("section", None, "shard"),
            P("section", "shard"),
            P("section", None),
            P("section", None),
            P("section", None),
            P("section", "shard"),
            P("section", "shard", None),
        ),
        check_vma=False,
    )
```

```python
import jax
import jax.numpy as jnp
from jax import lax
from jax.experimental import pallas as pl
from jax.experimental.pallas import tpu as pltpu
from jax.sharding import PartitionSpec as P

F32 = jnp.float32
BF16 = jnp.bfloat16
HI = lax.Precision.HIGHEST
EPS = 1e-05
T = 128
LANES = 128
HEAD = 64
SLOTS = 4
ROWS = SLOTS * T
PAIRS = 6
STEPS = 2
HALF = PAIRS // STEPS
WIDE = HALF * LANES
VMEM_LIMIT = 60 * 1024 * 1024
DP = ("x", "z", "core")


def sigmoid(v):
    return 0.5 * jnp.tanh(0.5 * v) + 0.5


def softplus(v):
    return jnp.maximum(v, 0.0) + jnp.log1p(jnp.exp(-jnp.abs(v)))


def dot(a, b):
    return jnp.dot(a, b, preferred_element_type=F32)


def dot_nt(a, b, precision=None):
    return lax.dot_general(
        a, b, (((1,), (1,)), ((), ())), preferred_element_type=F32, precision=precision
    )


def dot_tn(a, b, precision=None):
    return lax.dot_general(
        a, b, (((0,), (0,)), ((), ())), preferred_element_type=F32, precision=precision
    )


def iota(axis):
    return lax.broadcasted_iota(jnp.int32, (T, LANES), axis)


def shift_down(v, steps):
    return jnp.where(iota(0) >= steps, pltpu.roll(v, steps, 0), 0.0)


def shift_up(v, steps):
    return jnp.where(iota(0) < T - steps, pltpu.roll(v, T - steps, 0), 0.0)


def conv_taps(cin):
    return [shift_down(cin, 3), shift_down(cin, 2), shift_down(cin, 1), cin]


def conv_sum(taps, par):
    total = par[4:5, :] + taps[0] * par[0:1, :]
    for k in range(1, 4):
        total = total + taps[k] * par[k : k + 1, :]
    return total


def conv_back(dcv, par):
    total = dcv * par[3:4, :]
    for m in range(1, 4):
        total = total + shift_up(dcv, m) * par[3 - m : 4 - m, :]
    return total


def column_sum(v):
    return jnp.sum(v, axis=0, keepdims=True)


def slot(k):
    return slice(k * T, (k + 1) * T)


def tri(lower):
    if lower:
        return (iota(0) >= iota(1)).astype(F32)
    return (iota(0) <= iota(1)).astype(F32)


def step_prep(k, pbc, dtp, run_col, run_row, step_wide):
    step = softplus(pbc[slot(k), 256:384] + dtp[0:1, :])
    run = jnp.dot(tri(True), step * dtp[1:2, :], precision=HI, preferred_element_type=F32)
    run_row[k] = jnp.transpose(run)
    left = iota(1) < HEAD
    for p in range(PAIRS):
        a, b = 2 * p, 2 * p + 1
        run_col[a, slot(k), :] = jnp.broadcast_to(run[:, a : a + 1], (T, LANES))
        run_col[b, slot(k), :] = jnp.broadcast_to(run[:, b : b + 1], (T, LANES))
        step_wide[p, slot(k), :] = jnp.where(
            left,
            jnp.broadcast_to(step[:, a : a + 1], (T, LANES)),
            jnp.broadcast_to(step[:, b : b + 1], (T, LANES)),
        )
    return step


def halves(v):
    left = iota(1) < HEAD
    zero = jnp.zeros_like(v)
    return jnp.concatenate([jnp.where(left, v, zero), jnp.where(left, zero, v)], axis=0)


def in_lanes(columns):
    lane = lax.broadcasted_iota(jnp.int32, (columns[0].shape[0], LANES), 1)
    out = jnp.zeros(lane.shape, F32)
    for n, v in enumerate(columns):
        for k in range(3):
            part = v.astype(BF16).astype(F32)
            out = jnp.where(lane == 3 * n + k, part, out)
            v = v - part
    return out.astype(BF16)


def from_lanes(v, n):
    return sum(v[:, 3 * n + k : 3 * n + k + 1].astype(F32) for k in range(3))


class Refs:
    pass


def kernel_call(body, name, ins, outs, scratch, cost_us):
    in_names, out_names, scratch_names = list(ins), list(outs), list(scratch)

    def run(*refs):
        rf = Refs()
        for key, ref in zip(in_names + out_names + scratch_names, refs):
            setattr(rf, key, ref)
        body(rf, pl.program_id(0))

    res = pl.pallas_call(
        run,
        grid=(STEPS,),
        in_specs=[
            pl.BlockSpec(*ins[n][1:]) if len(ins[n]) > 2 else pl.BlockSpec(memory_space=ins[n][1])
            for n in in_names
        ],
        out_specs=[pl.BlockSpec(outs[n][2], outs[n][3]) for n in out_names],
        out_shape=[jax.ShapeDtypeStruct(outs[n][0], outs[n][1]) for n in out_names],
        scratch_shapes=[pltpu.VMEM(*scratch[n]) for n in scratch_names],
        compiler_params=pltpu.CompilerParams(vmem_limit_bytes=VMEM_LIMIT),
        cost_estimate=pl.CostEstimate(
            flops=int(cost_us * 1.1e9), bytes_accessed=1 << 20, transcendentals=0
        ),
        name=name,
    )(*[ins[n][0] for n in in_names])
    return dict(zip(out_names, res))


def whole(v):
    return (v, v.shape, lambda h: (0,) * v.ndim)


def whole_out(shape, dtype):
    return (shape, dtype, shape, lambda h: (0,) * len(shape))


def by_step(v, block):
    return (v, block, lambda h: (h,) + (0,) * (len(block) - 1))


def by_step_out(shape, dtype, block):
    return (shape, dtype, block, lambda h: (h,) + (0,) * (len(block) - 1))


def lanes_by_step(v):
    return (v, (v.shape[0], WIDE), lambda h: (0, h))


def lanes_by_step_out(shape, dtype):
    return (shape, dtype, (shape[0], WIDE), lambda h: (0, h))


def weight_blocks(w):
    half = (8, 3, 16, w.shape[3])
    return {
        "wg": (w, half, lambda h: (h, 1, 0, 0)),
        "wv": (w, half, lambda h: (h, 2, 0, 0)),
        "wbc": (w, (16, 1, 16, w.shape[3]), lambda h: (0, 9, 0, 0)),
    }


def pair_lanes(p):
    return slice(p * LANES, (p + 1) * LANES)


def flat_rows(ref):
    v = ref[...]
    return v.reshape(-1, v.shape[-1])


def mixed_bc(rf, k, c):
    lanes = slice(c * LANES, (c + 1) * LANES)
    cv = conv_sum(conv_taps(rf.pbc[slot(k), lanes]), rf.pbcv[:, lanes])
    return cv * sigmoid(cv)


def forward(x_slots, g_slots, w, dtw, gain, pv, pbcv, dtp):
    width = x_slots[0].shape[1]
    with_grad = g_slots is not None

    def body(rf, h):
        @pl.when(h == 0)
        def _prep():
            for k in range(SLOTS):
                x = getattr(rf, f"x{k}")[...].astype(F32)
                scale = lax.rsqrt(jnp.mean(x * x, axis=1, keepdims=True) + EPS)
                rf.normed[slot(k), :] = (x * scale * rf.gain[...]).astype(BF16)
                if with_grad:
                    rf.g_all[slot(k), :] = getattr(rf, f"g{k}")[...]
            rf.pbc[:, 0:256] = dot_nt(rf.normed[...], flat_rows(rf.wbc))
            rf.pbc[:, 256:384] = dot_nt(rf.normed[...], rf.dtw[...])
            for k in range(SLOTS):
                rf.scores[k] = dot_nt(mixed_bc(rf, k, 1), mixed_bc(rf, k, 0), HI) * tri(True)
                step_prep(k, rf.pbc, rf.dtp, rf.run_col, rf.run_row, rf.step_wide)
            rf.square[...] = jnp.zeros_like(rf.square)
            rf.cross[...] = jnp.zeros_like(rf.cross)

        rf.proj[0, :, 0:WIDE] = dot_nt(rf.normed[...], flat_rows(rf.wg))
        rf.proj[0, :, WIDE : 2 * WIDE] = dot_nt(rf.normed[...], flat_rows(rf.wv))
        if with_grad:
            q_all = dot_nt(rf.g_all[...], rf.wout[pl.ds(8 * h, 8)].reshape(WIDE, width))
        for p in range(HALF):
            lanes = pair_lanes(p)
            par = rf.pv[:, lanes]
            pair = HALF * h + p
            for k in range(SLOTS):
                gate = rf.proj[0, slot(k), lanes]
                cv = conv_sum(
                    conv_taps(rf.proj[0, slot(k), WIDE + p * LANES : WIDE + (p + 1) * LANES]), par
                )
                values = cv * sigmoid(cv)
                scaled = (values * rf.step_wide[pair, slot(k), :]).astype(BF16)
                weights = []
                for a in range(2):
                    gap = (
                        rf.run_col[2 * pair + a, slot(k), :]
                        - rf.run_row[k, pl.ds(2 * pair + a, 1), :]
                    )
                    decay = jnp.exp(jnp.minimum(gap, 0.0))
                    weights.append((rf.scores[k] * decay).astype(BF16))
                y = dot(jnp.concatenate(weights, axis=1), halves(scaled))
                rf.y[0, slot(k), lanes] = y
                scanned = y + par[6:7, :] * values
                gated = scanned * (gate * sigmoid(gate))
                rf.square[slot(k), :] += gated * gated
                scaled_out = gated * par[5:6, :]
                rf.u_all[h, slot(k), lanes] = scaled_out.astype(BF16)
                if with_grad:
                    rf.cross[slot(k), :] += q_all[slot(k), lanes] * scaled_out

        @pl.when(h == STEPS - 1)
        def _finish():
            u = jnp.concatenate([rf.u_all[a] for a in range(STEPS)], axis=1)
            for n in range(0, width, 512):
                part = dot(u, rf.wout[:, :, :, n : n + 512].reshape(STEPS * WIDE, 512)).astype(BF16)
                for k in range(SLOTS):
                    getattr(rf, f"out{k}")[:, n : n + 512] = part[slot(k), :]
            for k in range(SLOTS):
                total = jnp.sum(rf.square[slot(k), :], axis=1, keepdims=True)
                getattr(rf, f"out{k}")[:, width:] = in_lanes([total])
            ones = jnp.ones((8, LANES), F32)
            rf.stats[0] = dot_nt(ones, rf.square[...], HI)
            rf.stats[1] = dot_nt(ones, rf.cross[...], HI)

    ins = {f"x{k}": whole(v) for k, v in enumerate(x_slots)}
    if with_grad:
        ins.update({f"g{k}": whole(v) for k, v in enumerate(g_slots)})
    ins.update(
        gain=whole(gain),
        **weight_blocks(w),
        dtw=whole(dtw),
        wout=(w, (16, 3, 16, width), lambda h: (0, 0, 0, 0)),
        pv=lanes_by_step(pv),
        pbcv=whole(pbcv),
        dtp=whole(dtp),
    )
    outs = {f"out{k}": whole_out((T, width + LANES), BF16) for k in range(SLOTS)}
    outs.update(
        stats=whole_out((2, 8, ROWS), F32),
        normed=whole_out((ROWS, width), BF16),
        proj=by_step_out((STEPS, ROWS, 2 * WIDE), F32, (1, ROWS, 2 * WIDE)),
        y=by_step_out((STEPS, ROWS, WIDE), F32, (1, ROWS, WIDE)),
        pbc=whole_out((ROWS, 384), F32),
    )
    scratch = dict(
        scores=((SLOTS, T, T), F32),
        run_col=((2 * PAIRS, ROWS, LANES), F32),
        run_row=((SLOTS, T, LANES), F32),
        step_wide=((PAIRS, ROWS, LANES), F32),
        u_all=((STEPS, ROWS, WIDE), BF16),
        square=((ROWS, LANES), F32),
        cross=((ROWS, LANES), F32),
    )
    if with_grad:
        scratch["g_all"] = ((ROWS, width), BF16)
    res = kernel_call(body, "layer_forward", ins, outs, scratch, 18)
    return [res[f"out{k}"] for k in range(SLOTS)], res


def head_columns(pair):
    target = 2 * pair + (iota(0) >= HEAD).astype(jnp.int32)
    one = (iota(1) == target).astype(BF16)
    return jnp.concatenate([one, one], axis=0)


def head_sum(v, columns):
    high = v.astype(BF16)
    low = (v - high.astype(F32)).astype(BF16)
    return dot(jnp.concatenate([high, low], axis=1), columns)


def put_by_core(rf, key, x, at, part):
    keep, send = getattr(rf, key + "_keep"), getattr(rf, key + "_send")
    groups = slice(at, at + part.shape[2])
    for c in range(2):

        @pl.when(rf.core[0] == c)
        def _store(c=c):
            for z in range(4):
                keep[x, z, groups] = part[z, c]
                send[x, z, groups] = part[z, 1 - c]


def backward(stages, name, cost_us, saved, layer, have):
    gate, scan, inp, wgate, wscan = (
        s in stages for s in ("gate", "scan", "input", "wgate", "wscan")
    )
    width = saved["normed"].shape[1]
    w, dtw, pv, pbcv, dtp = layer
    elementwise = gate or scan

    def body(rf, h):
        @pl.when(h == 0)
        def _prep():
            for k in range(SLOTS):
                if gate or wgate:
                    rf.g_all[slot(k), :] = getattr(rf, f"g{k}")[...]
                if gate:
                    for row, ref in ((0, rf.scale_row), (1, rf.cross_row)):
                        if "rows" in have:
                            ref[slot(k), :] = jnp.transpose(
                                jnp.broadcast_to(rf.rows[k, row : row + 1, :], (T, LANES))
                            )
                        else:
                            column = from_lanes(getattr(rf, f"e{k}")[...], row)
                            ref[slot(k), :] = jnp.broadcast_to(column, (T, LANES))
                if scan:
                    inbound, outbound = mixed_bc(rf, k, 0), mixed_bc(rf, k, 1)
                    rf.mixed[0, slot(k), :] = inbound
                    rf.mixed[1, slot(k), :] = outbound
                    rf.scores[k] = dot_nt(inbound, outbound, HI) * tri(False)
                    rf.step_all[slot(k), :] = step_prep(
                        k, rf.pbc, rf.dtp, rf.run_col, rf.run_row, rf.step_wide
                    )
            if scan:
                rf.dscores[...] = jnp.zeros_like(rf.dscores)
                rf.dstep[...] = jnp.zeros_like(rf.dstep)
                rf.drun[...] = jnp.zeros_like(rf.drun)
            if inp:
                rf.total[...] = jnp.zeros_like(rf.total)

        if gate:
            q_all = dot_nt(rf.g_all[...], flat_rows(rf.wout))
        for p in range(HALF if elementwise else 0):
            lanes = pair_lanes(p)
            par = rf.pv[:, lanes]
            pair = HALF * h + p
            sums = [jnp.zeros((1, LANES), F32) for _ in range(8)]
            if scan:
                columns = head_columns(pair)
            for k in range(SLOTS):
                taps = conv_taps(rf.proj[0, slot(k), WIDE + p * LANES : WIDE + (p + 1) * LANES])
                cv = conv_sum(taps, par)
                sig_c = sigmoid(cv)
                values = cv * sig_c
                y = rf.y[0, slot(k), lanes]
                if gate:
                    gate_in = rf.proj[0, slot(k), lanes]
                    sig_g = sigmoid(gate_in)
                    silu_g = gate_in * sig_g
                    scanned = y + par[6:7, :] * values
                    gated = scanned * silu_g
                    grad_no = q_all[slot(k), lanes]
                    scale = rf.scale_row[slot(k), :]
                    dgated = scale * (grad_no * par[5:6, :]) - rf.cross_row[slot(k), :] * gated
                    norm = gated * scale
                    sums[5] += column_sum(grad_no * norm)
                    rf.u[slot(k), lanes] = (norm * par[5:6, :]).astype(BF16)
                    dscan = dgated * silu_g
                    dgate = dgated * scanned * (sig_g * (1.0 + gate_in * (1.0 - sig_g)))
                    sums[6] += column_sum(dscan * values)
                    rf.dg[slot(k), lanes] = dgate.astype(BF16)
                    if not scan:
                        rf.dscan[slot(k), lanes] = dscan
                else:
                    dscan = rf.dscan[slot(k), lanes]
                if not scan:
                    continue
                wide = rf.step_wide[pair, slot(k), :]
                dy = dscan.astype(BF16)
                scaled = (values * wide).astype(BF16)
                dweights = dot_nt(halves(scaled), dy)
                weights = []
                dscore = rf.dscores[k]
                for a in range(2):
                    gap = (
                        rf.run_row[k, pl.ds(2 * pair + a, 1), :]
                        - rf.run_col[2 * pair + a, slot(k), :]
                    )
                    decay = jnp.exp(jnp.minimum(gap, 0.0))
                    weights.append((rf.scores[k] * decay).astype(BF16))
                    dscore = dscore + dweights[slot(a), :] * decay
                rf.dscores[k] = dscore
                dscaled = dot(jnp.concatenate(weights, axis=1), halves(dy))
                rf.dstep[slot(k), :] += head_sum(dscaled * values, columns)
                rf.drun[slot(k), :] += head_sum(
                    dy.astype(F32) * y - scaled.astype(F32) * dscaled, columns
                )
                dvalues = dscaled * wide + par[6:7, :] * dscan
                dcv = dvalues * (sig_c * (1.0 + cv * (1.0 - sig_c)))
                for t in range(4):
                    sums[t] += column_sum(dcv * taps[t])
                sums[4] += column_sum(dcv)
                rf.dv[slot(k), lanes] = conv_back(dcv, par).astype(BF16)
            rf.small[p] = jnp.concatenate(sums, axis=0)
        if wgate and wscan:
            for at, left, right in (
                (0, rf.dg, rf.normed),
                (3, rf.u, rf.g_all),
                (6, rf.dv, rf.normed),
            ):
                part = dot_tn(left[...], right[...]).astype(BF16)
                rf.ga[:, at : at + 3] = part.reshape(8, 3, 16, width)
            part = dot_tn(rf.dbc_half[...], rf.normed[...]).astype(BF16)
            rf.ga[:, 9] = part.reshape(8, 16, width)
        elif wgate:
            for at, left, right in ((0, rf.dg, rf.normed), (3, rf.u, rf.g_all)):
                part = dot_tn(left[...], right[...]).astype(BF16)
                put_by_core(rf, "ga", h, at, part.reshape(4, 2, 3, 16, width))
        elif wscan:
            part = dot_tn(rf.dv[...], rf.normed[...]).astype(BF16)
            put_by_core(rf, "gb", h, 0, part.reshape(4, 2, 3, 16, width))
        if inp:
            rf.total[...] += dot(rf.dg[...], flat_rows(rf.wg)) + dot(rf.dv[...], flat_rows(rf.wv))

        @pl.when(h == STEPS - 1)
        def _finish():
            if scan:
                sums = [[jnp.zeros((1, LANES), F32) for _ in range(8)] for _ in range(2)]
                dt_sums = [jnp.zeros((1, LANES), F32) for _ in range(8)]
                live = iota(1) < 2 * PAIRS
                for k in range(SLOTS):
                    dscore = rf.dscores[k] * tri(False)
                    dmixed = (
                        jnp.dot(
                            dscore,
                            rf.mixed[1, slot(k), :],
                            precision=HI,
                            preferred_element_type=F32,
                        ),
                        dot_tn(dscore, rf.mixed[0, slot(k), :], HI),
                    )
                    for c in range(2):
                        lanes = slice(c * LANES, (c + 1) * LANES)
                        par = rf.pbcv[:, lanes]
                        taps = conv_taps(rf.pbc[slot(k), lanes])
                        cv = conv_sum(taps, par)
                        sig = sigmoid(cv)
                        dcv = dmixed[c] * (sig * (1.0 + cv * (1.0 - sig)))
                        for t in range(4):
                            sums[c][t] += column_sum(dcv * taps[t])
                        sums[c][4] += column_sum(dcv)
                        rf.dbc[slot(k), lanes] = conv_back(dcv, par).astype(BF16)
                    dlog = jnp.dot(
                        tri(False), rf.drun[slot(k), :], precision=HI, preferred_element_type=F32
                    )
                    grad_step = rf.dstep[slot(k), :] + dlog * rf.dtp[1:2, :]
                    dt_sums[1] += column_sum(dlog * rf.step_all[slot(k), :])
                    draw = grad_step * sigmoid(rf.pbc[slot(k), 256:384] + rf.dtp[0:1, :])
                    draw = jnp.where(live, draw, 0.0)
                    dt_sums[0] += column_sum(draw)
                    rf.dbc[slot(k), 256:384] = draw.astype(BF16)
                rf.small_bc[0] = jnp.concatenate(sums[0], axis=0)
                rf.small_bc[1] = jnp.concatenate(sums[1], axis=0)
                dt_sums[1] = dt_sums[1] * rf.dtp[1:2, :]
                rf.small_dt[...] = jnp.concatenate(dt_sums, axis=0)
            if wscan and not wgate:
                part = dot_tn(rf.dbc[:, 0:256], rf.normed[...]).astype(BF16)
                part = part.reshape(2, 4, 2, 1, 16, width)
                for a in range(2):
                    put_by_core(rf, "gb", a, 3, part[a])
            if wscan:
                rf.gdt[...] = dot_tn(rf.dbc[:, 256:384], rf.normed[...])[0:16]
            if inp:
                final = (
                    rf.total[...]
                    + dot(rf.dbc[:, 0:256], flat_rows(rf.wbc))
                    + dot(rf.dbc[:, 256:384], rf.dtw[...])
                )
                for k in range(SLOTS):
                    getattr(rf, f"out{k}")[...] = final[slot(k), :].astype(BF16)

    ins, outs, scratch = {}, {}, {}
    heads_cols = STEPS * WIDE
    if gate or wgate:
        for k, v in enumerate(have["g"]):
            ins[f"g{k}"] = (v, (T, width), lambda h: (0, 0))
        scratch["g_all"] = ((ROWS, width), BF16)
    if gate:
        if "rows" in have:
            ins["rows"] = whole(have["rows"])
        else:
            for k, v in enumerate(have["g"]):
                ins[f"e{k}"] = (v, (T, LANES), lambda h: (0, width // LANES))
        ins["wout"] = (w, (8, 3, 16, width), lambda h: (h, 0, 0, 0))
        scratch["scale_row"] = ((ROWS, LANES), F32)
        scratch["cross_row"] = ((ROWS, LANES), F32)
        outs["u"] = lanes_by_step_out((ROWS, heads_cols), BF16)
        outs["dg"] = lanes_by_step_out((ROWS, heads_cols), BF16)
        if not scan:
            outs["dscan"] = lanes_by_step_out((ROWS, heads_cols), F32)
    if elementwise:
        ins["proj"] = by_step(saved["proj"], (1, ROWS, 2 * WIDE))
        ins["y"] = by_step(saved["y"], (1, ROWS, WIDE))
        ins["pv"] = lanes_by_step(pv)
        outs["small"] = by_step_out((PAIRS, 8, LANES), F32, (HALF, 8, LANES))
    if scan:
        ins["pbc"] = whole(saved["pbc"])
        ins["pbcv"] = whole(pbcv)
        ins["dtp"] = whole(dtp)
        if not gate:
            ins["dscan"] = lanes_by_step(have["dscan"])
        outs["dv"] = lanes_by_step_out((ROWS, heads_cols), BF16)
        outs["dbc"] = whole_out((ROWS, 384), BF16)
        outs["small_bc"] = whole_out((2, 8, LANES), F32)
        outs["small_dt"] = whole_out((8, LANES), F32)
        scratch.update(
            mixed=((2, ROWS, LANES), F32),
            scores=((SLOTS, T, T), F32),
            run_col=((2 * PAIRS, ROWS, LANES), F32),
            run_row=((SLOTS, T, LANES), F32),
            step_wide=((PAIRS, ROWS, LANES), F32),
            step_all=((ROWS, LANES), F32),
            dscores=((SLOTS, T, T), F32),
            dstep=((ROWS, LANES), F32),
            drun=((ROWS, LANES), F32),
        )
    if inp:
        ins.update(weight_blocks(w))
        ins["dtw"] = whole(dtw)
        scratch["total"] = ((ROWS, width), F32)
        outs.update({f"out{k}": whole_out((T, width), BF16) for k in range(SLOTS)})
    if wgate or wscan:
        ins["normed"] = whole(saved["normed"])
    if not gate and (wgate or inp):
        ins["dg"] = lanes_by_step(have["dg"])
    if wgate and not gate:
        ins["u"] = lanes_by_step(have["u"])
    if not scan and (wscan or inp):
        ins["dv"] = lanes_by_step(have["dv"])
        ins["dbc"] = whole(have["dbc"])
    if wgate and wscan:
        ins["dbc_half"] = (have["dbc"], (ROWS, LANES), lambda h: (0, h))
        outs["ga"] = by_step_out((16, 10, 16, width), BF16, (8, 10, 16, width))
    elif wgate or wscan:
        ins["core"] = have["core"]
        key, groups = ("ga", 6) if wgate else ("gb", 4)
        for end in ("_keep", "_send"):
            outs[key + end] = whole_out((2, 4, groups, 16, width), BF16)
    if wscan:
        outs["gdt"] = whole_out((16, width), F32)
    return kernel_call(body, name, ins, outs, scratch, cost_us)


def assemble(parts, dt_rows, shard):
    quarter = parts.shape[2]
    block = 16 * 48
    total = 8 * block + 16 * 16 + dt_rows.shape[0]

    def body(_, inw, outw, shared, dt, grad_in, grad_out):
        i = pl.program_id(0)

        @pl.when(i < 8)
        def _columns():
            grad_in[...] = inw[...].reshape(block, quarter).astype(F32)

        @pl.when(i < SLOTS)
        def _out():
            grad_out[...] = outw[...].reshape(block, quarter).astype(F32)

        @pl.when(i == 8)
        def _shared():
            grad_in[...] = jnp.zeros_like(grad_in)
            grad_in[0:256, :] = shared[...].reshape(256, quarter).astype(F32)
            grad_in[256 : 256 + dt_rows.shape[0], :] = dt[...]

    last = SLOTS - 1
    spec = pltpu.PrefetchScalarGridSpec(
        num_scalar_prefetch=1,
        grid=(9,),
        in_specs=[
            pl.BlockSpec(
                (16, 48, quarter),
                lambda i, j: (0, jnp.where(i < SLOTS, 0, 8) + (j[0] + 3 * SLOTS - i) % SLOTS, 0),
            ),
            pl.BlockSpec((16, 48, quarter), lambda i, j: (0, SLOTS + jnp.minimum(i, last), 0)),
            pl.BlockSpec((16, 16, quarter), lambda i, j: (0, 36, 0)),
            pl.BlockSpec(dt_rows.shape, lambda i, j: (0, 0)),
        ],
        out_specs=[
            pl.BlockSpec((block, quarter), lambda i, j: (i, 0)),
            pl.BlockSpec((block, quarter), lambda i, j: (0, jnp.minimum(i, last))),
        ],
    )
    return pl.pallas_call(
        body,
        grid_spec=spec,
        out_shape=[
            jax.ShapeDtypeStruct((total, quarter), F32),
            jax.ShapeDtypeStruct((block, SLOTS * quarter), F32),
        ],
        compiler_params=pltpu.CompilerParams(vmem_limit_bytes=VMEM_LIMIT),
        name="assemble",
    )(shard.astype(jnp.int32)[None], parts, parts, parts, dt_rows)


def ring(n, k):
    return [(i, (i + k) % n) for i in range(n)]


def send_shard(v, k):
    return lax.ppermute(v, "shard", ring(SLOTS, k)) if k else v


def send_across(v, k):
    pairs = [
        (sec * SLOTS + y, (1 - sec) * SLOTS + (y + k) % SLOTS)
        for sec in range(2)
        for y in range(SLOTS)
    ]
    return lax.ppermute(v, ("section", "shard"), pairs)


def swap_section(v):
    return lax.ppermute(v, "section", [(0, 1), (1, 0)])


def dp_index(x, z, c):
    return x * 8 + z * 2 + c


def dp_pairs(move):
    pairs = []
    for x in range(2):
        for z in range(4):
            for c in range(2):
                pairs.append((dp_index(x, z, c), dp_index(*move(x, z, c))))
    return pairs


def pick(v, index, axis):
    return lax.dynamic_index_in_dim(v, index, axis, keepdims=False)


def gather_slots(v):
    return [send_shard(v, (-k) % SLOTS) for k in range(SLOTS)]


def scatter_sum(slots):
    parts = [send_shard(slots[k], k) for k in range(SLOTS)]
    return sum(p.astype(F32) for p in parts)


def cross_core(v):
    return lax.ppermute(v, DP, dp_pairs(lambda x, z, c: (x, z, 1 - c)))


def sum_small(v):
    v = v + lax.ppermute(v, DP, dp_pairs(lambda x, z, c: (x, z, 1 - c)))
    v = v + sum(
        lax.ppermute(v, DP, dp_pairs(lambda x, z, c: (x, (z + k) % 4, c))) for k in range(1, 4)
    )
    return v + lax.ppermute(v, DP, dp_pairs(lambda x, z, c: (1 - x, z, c)))


def in_order(parts, sign):
    j = lax.axis_index("shard")
    stacked = jnp.stack(parts)
    return jnp.take(stacked, (sign * (jnp.arange(SLOTS) - j)) % SLOTS, axis=0)


def shards(
    tokens,
    cotangent,
    lengths,
    norm_gain,
    in_weight,
    conv_weight,
    conv_bias,
    dt_bias,
    a_log,
    d_skip,
    gate_gain,
    out_weight,
):
    sec = lax.axis_index("section")
    d = lax.axis_index(DP)
    j = lax.axis_index("shard")
    core = d % 2
    first = sec == 0
    width = tokens.shape[2]
    quarter = norm_gain.shape[1]
    channels = conv_bias.shape[1]
    own_cols = gate_gain.shape[1]
    inner = own_cols * SLOTS
    heads = dt_bias.shape[1]
    own_heads = heads // SLOTS
    n_state = 2 * LANES
    piece = own_cols // 16
    piece_bc = n_state // 16
    own_core = (core.astype(jnp.int32)[None], pltpu.SMEM)

    x_own = pick(tokens, sec, 0)
    cot = pick(cotangent, sec, 0)
    length = pick(lengths, sec, 0)
    mask = (jnp.arange(T, dtype=jnp.int32) < length).astype(F32)[:, None]

    columns = jnp.transpose(in_weight[0])
    with jax.named_scope("weights"):

        def cut(start, rows):
            return lax.dynamic_slice(columns, (start, 0), (rows, quarter))

        def columns_of(to):
            return jnp.concatenate(
                [
                    cut(own_cols * to + piece * d, piece),
                    cut(inner + own_cols * to + piece * d, piece),
                    cut(2 * inner + piece_bc * d, piece_bc),
                ],
                axis=0,
            )

        cuts = [columns_of((j + k) % SLOTS) for k in range(SLOTS)]
        o_own = lax.dynamic_slice(out_weight[0], (piece * d, 0), (piece, width))
        o_other = swap_section(o_own)

        w_own = [send_shard(cuts[k], k) for k in range(SLOTS)]
        w_other = [send_across(cuts[k], k) for k in range(SLOTS)]

        def from_parts(parts, others, o, o_others, own):
            pieces = [jnp.where(own, p, q) for p, q in zip(parts, others)]
            lanes = []
            for y in range(SLOTS):
                v = pieces[0]
                for k in range(1, SLOTS):
                    v = jnp.where((j - y) % SLOTS == k, pieces[k], v)
                lanes.append(v)
            return jnp.concatenate(
                [jnp.where(own, o, o_others), jnp.concatenate(lanes, axis=1)], axis=0
            )

        w0 = from_parts(w_own, w_other, o_own, o_other, first)
        w1 = from_parts(w_own, w_other, o_own, o_other, ~first)
        w0, w1, x_own, cot = lax.optimization_barrier((w0, w1, x_own, cot))
        w0 = lax.all_gather(w0, DP, axis=0, tiled=False)
        x_slots = gather_slots(x_own)
        x_slots, norm_gain = lax.optimization_barrier((x_slots, norm_gain))

    with jax.named_scope("small_weights"):
        dt_columns = columns[2 * inner + n_state :]
        sizes = [quarter, 4 * channels, channels, own_cols, heads, heads, heads, heads * quarter]
        flat = jnp.concatenate(
            [
                norm_gain[0],
                conv_weight[0].reshape(-1),
                conv_bias[0],
                gate_gain[0],
                dt_bias[0],
                a_log[0],
                d_skip[0],
                dt_columns.reshape(-1),
            ]
        )
        flat = jnp.pad(flat, (0, -flat.shape[0] % LANES)).reshape(-1, LANES)
        own = in_order(gather_slots(flat), 1)
        other = swap_section(own)
        small = [jnp.where(first, own, other), jnp.where(first, other, own)]

        def unpack(v):
            low = v.reshape(SLOTS, -1)
            at = sum(sizes[:-1])
            dtw = low[:, at : at + sizes[-1]].reshape(SLOTS, heads, quarter)
            dtw = lax.dynamic_slice(dtw, (0, own_heads * j, 0), (SLOTS, own_heads, quarter))
            dtw = jnp.transpose(dtw, (1, 0, 2)).reshape(own_heads, width)
            dtw = jnp.pad(dtw, ((0, LANES - own_heads), (0, 0)))
            v = low[:, :at].astype(F32)
            cut, at = [], 0
            for size in sizes[:-1]:
                cut.append(v[:, at : at + size])
                at += size
            gain = cut[0].reshape(1, width)
            taps = cut[1].reshape(SLOTS, 4, channels).transpose(1, 0, 2).reshape(4, -1)
            bias = cut[2].reshape(1, -1)
            conv = jnp.concatenate([taps, bias, jnp.zeros((3, taps.shape[1]), F32)], axis=0)
            pbcv = conv[:, inner:]
            pv = lax.dynamic_slice(conv, (0, own_cols * j), (8, own_cols))
            pick_heads = lambda u: lax.dynamic_slice(u[0], (own_heads * j,), (own_heads,))
            wide = jnp.repeat(pick_heads(cut[6]), HEAD)[None]
            pv = jnp.concatenate([pv[:5], pick(cut[3], j, 0)[None], wide, pv[7:]], axis=0)
            dtp = jnp.stack([pick_heads(cut[4]), -jnp.exp(pick_heads(cut[5]))])
            dtp = jnp.pad(dtp, ((0, 6), (0, LANES - own_heads)))
            return gain, dtw, pv, pbcv, dtp

        gain0, *params0 = unpack(small[0])
        gain1, *params1 = unpack(small[1])

    x_f = x_own.astype(F32)
    g1 = (mask * cot.astype(F32)).astype(BF16)
    g1_slots = gather_slots(g1)
    w0, x_slots, g1_slots, gain0, params0, gain1, params1, w1 = lax.optimization_barrier(
        (w0, x_slots, g1_slots, gain0, params0, gain1, params1, w1)
    )
    w1 = lax.all_gather(w1, DP, axis=0, tiled=False)
    blocks = lambda v: v.reshape(16, 10, 16, width)

    layer0 = (blocks(w0), *params0)
    layer1 = (blocks(w1), *params1)

    def forward_layer(x, g, gain, layer):
        w, dtw, pv, pbcv, dtp = layer
        return forward(x, g, w, dtw, gain, pv, pbcv, dtp)

    parts, saved0 = forward_layer(x_slots, None, gain0, layer0)
    branch = scatter_sum(parts)
    square = jnp.sum(branch[:, width : width + 3], axis=1, keepdims=True)
    scale0 = lax.rsqrt(square / inner + EPS)
    branch0 = branch[:, :width] * scale0
    middle = (x_f + mask * branch0).astype(BF16)

    m_slots = gather_slots(middle)
    branch_parts, saved1 = forward_layer(m_slots, g1_slots, gain1, layer1)
    own = saved1["stats"][:, 0].reshape(2, SLOTS, T)
    back = [send_shard(own, k) for k in range(SLOTS)]
    summed = sum(jnp.roll(back[k], -k, axis=1) for k in range(SLOTS))
    scale1 = lax.rsqrt(summed[0] / inner + EPS)
    cross1 = scale1 * scale1 * scale1 * summed[1] / inner
    rows1 = jnp.pad(jnp.stack([scale1, cross1], axis=1), ((0, 0), (0, 6), (0, 0)))

    def norm_back(x, gain, grad):
        scale = lax.rsqrt(jnp.mean(x * x, axis=1, keepdims=True) + EPS)
        unit = x * scale
        dn = grad * gain
        dx = scale * (dn - unit * jnp.mean(dn * unit, axis=1, keepdims=True))
        return dx, jnp.sum(grad * unit, axis=0)

    back1 = backward(
        ("gate", "scan", "input"),
        "backward_1",
        28,
        saved1,
        layer1,
        {"g": g1_slots, "rows": rows1},
    )
    moved = [send_shard(back1[f"out{k}"], k) for k in range(SLOTS)]
    grads1 = backward(
        ("wgate", "wscan"), "weight_grads_1", 8, saved1, layer1, {"g": g1_slots, **back1}
    )
    back1.update(grads1)
    moved, back1["ga"] = lax.optimization_barrier((moved, back1["ga"]))
    dx, gain_grad1 = norm_back(middle.astype(F32), gain1, sum(p.astype(F32) for p in moved))
    by_owner = lambda v: v.reshape(16, -1, width)
    owned1 = lax.psum_scatter(by_owner(back1["ga"]), DP, scatter_dimension=0, tiled=False)

    dmiddle = (cot.astype(F32) + dx).astype(BF16)
    g0 = (mask * dmiddle.astype(F32)).astype(BF16)
    cross0 = scale0 * scale0 * jnp.sum(g0.astype(F32) * branch0, axis=1, keepdims=True) / inner
    g0_slots = gather_slots(jnp.concatenate([g0, in_lanes([scale0, cross0])], axis=1))
    g0_slots, branch_parts = lax.optimization_barrier((g0_slots, branch_parts))
    branch = scatter_sum(branch_parts)[:, :width] * scale1[0][:, None]
    result = middle.astype(F32) + mask * branch

    back0 = backward(
        ("gate", "wgate"),
        "backward_0_gate",
        14,
        saved0,
        layer0,
        {"g": g0_slots, "core": own_core},
    )
    both = lambda kept, moved: (kept.astype(F32) + moved.astype(F32)).astype(BF16)
    a_moved = cross_core(back0["ga_send"])
    small_gate = back0["small"]
    back0["core"] = own_core
    back0.update(backward(("scan", "wscan"), "backward_0_scan", 20, saved0, layer0, back0))
    gb_send, a_moved = lax.optimization_barrier((back0["gb_send"], a_moved))
    a0 = both(back0["ga_keep"], a_moved)
    b0 = both(back0["gb_keep"], cross_core(gb_send))
    owned0 = jnp.pad(a0, ((0, 0), (0, 0), (0, 4), (0, 0), (0, 0)))
    owned0 = lax.dynamic_update_slice(owned0, b0, (0, 0, 6, 0, 0)).reshape(8, -1, width)
    owned0 = lax.psum_scatter(owned0, ("x", "z"), scatter_dimension=0, tiled=False)
    small_scan = back0["small"]
    back0.update(backward(("input",), "backward_0_input", 9, saved0, layer0, back0))
    moved0 = [send_shard(back0[f"out{k}"], k) for k in range(SLOTS)]
    dx, gain_grad0 = norm_back(x_f, gain0, sum(p.astype(F32) for p in moved0))
    dtokens = dmiddle.astype(F32) + dx
    owned1 = owned1 + lax.ppermute(owned1, "section", [(0, 1)])
    owned0, owned1, gain_grad0, dtokens, result = lax.optimization_barrier(
        (owned0, owned1, gain_grad0, dtokens, result)
    )

    kept = jnp.where(first, owned0, owned1).reshape(10, 16, width)
    arrived = lax.ppermute(owned0, "section", [(1, 0)]).reshape(10, 16, width)

    def total_of(cut):
        return (cut(kept).astype(F32) + cut(arrived).astype(F32)).astype(BF16)

    row_slots = []
    for k in range(SLOTS):

        def cut(v):
            v = lax.dynamic_slice_in_dim(v, quarter * ((j + k) % SLOTS), quarter, 2)
            return jnp.concatenate([v[:3], v[6:]], axis=0)

        row_slots.append(send_shard(total_of(cut).reshape(-1, quarter), k))
    out_rows = total_of(lambda v: v[3:6])
    out_rows = jnp.transpose(out_rows.reshape(piece, SLOTS, quarter), (1, 0, 2))
    result_moved = lax.ppermute(result.astype(BF16), "section", [(0, 1)]).astype(F32)
    dtokens_moved = lax.ppermute(dtokens.astype(BF16), "section", [(1, 0)]).astype(F32)
    ends = jnp.where(
        first, jnp.stack([dtokens, dtokens_moved]), jnp.stack([result_moved, result])
    )[None]

    def to_section(v0, v1):
        kept = jnp.where(first, v0, v1).astype(F32)
        return kept + swap_section(jnp.where(first, v1, v0)).astype(F32)

    shared = sum(v[2 * piece :].astype(F32) for v in row_slots).astype(BF16)
    gathered = lax.all_gather(
        jnp.concatenate(
            [v[:piece] for v in row_slots]
            + [out_rows.reshape(-1, quarter)]
            + [v[piece : 2 * piece] for v in row_slots]
            + [shared],
            axis=0,
        ),
        DP,
        tiled=False,
    )

    def small_of(by_pair, back, gain_grad):
        return jnp.concatenate(
            [
                by_pair.reshape(-1, LANES),
                back["small_bc"].reshape(-1, LANES),
                back["small_dt"],
                gain_grad.reshape(-1, LANES),
                back["gdt"].reshape(-1, LANES),
            ],
            axis=0,
        )

    small0 = small_of(small_gate + small_scan, back0, gain_grad0)
    small1 = small_of(back1["small"], back1, gain_grad1)
    small_sum = sum_small(to_section(small0, small1))
    everyone = in_order(gather_slots(small_sum), 1)
    n_pair, n_bc = PAIRS * 8, 2 * 8
    by_pair = everyone[:, :n_pair].reshape(SLOTS, PAIRS, 8, LANES)
    by_pair = by_pair.transpose(2, 0, 1, 3).reshape(8, inner)
    by_bc = jnp.sum(everyone[:, n_pair : n_pair + n_bc], axis=0)
    by_bc = by_bc.reshape(2, 8, LANES).transpose(1, 0, 2).reshape(8, n_state)
    at = n_pair + n_bc
    by_dt = everyone[:, at : at + 8, :own_heads].transpose(1, 0, 2).reshape(8, heads)
    at += 8
    gain_total = jnp.sum(everyone[:, at : at + width // LANES], axis=0).reshape(-1)
    at += width // LANES
    dt_rows = everyone[:, at:].reshape(SLOTS, 16, SLOTS, quarter)[:, :own_heads]
    dt_rows = pick(dt_rows, j, 2).reshape(heads, quarter)
    conv_total = jnp.concatenate([by_pair[:5], by_bc[:5]], axis=1)
    conv_own = lax.dynamic_slice(conv_total, (0, channels * j), (5, channels))
    grad_skip = jnp.sum(by_pair[6].reshape(heads, HEAD), axis=1)

    grad_in_weight, grad_out_weight = assemble(gathered, dt_rows, j)
    return (
        ends,
        lax.dynamic_slice(gain_total, (quarter * j,), (quarter,))[None],
        jnp.transpose(grad_in_weight)[None],
        conv_own[None, :4],
        conv_own[4][None],
        by_dt[0][None],
        by_dt[1][None],
        grad_skip[None],
        lax.dynamic_slice(by_pair[5], (own_cols * j,), (own_cols,))[None],
        grad_out_weight[None],
    )


def solution(mesh):
    sections, copies, owners = mesh.devices.shape
    fine = jax.sharding.Mesh(
        mesh.devices.reshape(sections, 2, copies // 4, 2, owners), ("section", *DP, "shard")
    )
    return jax.shard_map(
        shards,
        mesh=fine,
        in_specs=(
            P((*DP, "shard"), None, None),
            P((*DP, "shard"), None, None),
            P((*DP, "shard")),
            P("section", "shard"),
            P("section", "shard", None),
            P("section", None, "shard"),
            P("section", "shard"),
            P("section", None),
            P("section", None),
            P("section", None),
            P("section", "shard"),
            P("section", "shard", None),
        ),
        out_specs=(
            P("section", (*DP, "shard"), None, None),
            P("section", "shard"),
            P("section", "shard", None),
            P("section", None, "shard"),
            P("section", "shard"),
            P("section", None),
            P("section", None),
            P("section", None),
            P("section", "shard"),
            P("section", "shard", None),
        ),
        check_vma=False,
    )
```

```python
import jax
import jax.numpy as jnp
from jax import lax
from jax.experimental import pallas as pl
from jax.experimental.pallas import tpu as pltpu
from jax.sharding import PartitionSpec as P

F32 = jnp.float32
BF16 = jnp.bfloat16
HI = lax.Precision.HIGHEST
EPS = 1e-05
T = 128
LANES = 128
HEAD = 64
SLOTS = 4
ROWS = SLOTS * T
PAIRS = 6
STEPS = 2
HALF = PAIRS // STEPS
WIDE = HALF * LANES
VMEM_LIMIT = 34 * 1024 * 1024
DP = ("x", "z", "core")


def sigmoid(v):
    return 0.5 * jnp.tanh(0.5 * v) + 0.5


def softplus(v):
    return jnp.maximum(v, 0.0) + jnp.log1p(jnp.exp(-jnp.abs(v)))


def dot(a, b):
    return jnp.dot(a, b, preferred_element_type=F32)


def dot_nt(a, b, precision=None):
    return lax.dot_general(
        a, b, (((1,), (1,)), ((), ())), preferred_element_type=F32, precision=precision
    )


def dot_tn(a, b, precision=None):
    return lax.dot_general(
        a, b, (((0,), (0,)), ((), ())), preferred_element_type=F32, precision=precision
    )


def iota(axis):
    return lax.broadcasted_iota(jnp.int32, (T, LANES), axis)


def shift_down(v, steps):
    return jnp.where(iota(0) >= steps, pltpu.roll(v, steps, 0), 0.0)


def shift_up(v, steps):
    return jnp.where(iota(0) < T - steps, pltpu.roll(v, T - steps, 0), 0.0)


def conv_taps(cin):
    return [shift_down(cin, 3), shift_down(cin, 2), shift_down(cin, 1), cin]


def conv_sum(taps, par):
    total = par[4:5, :] + taps[0] * par[0:1, :]
    for k in range(1, 4):
        total = total + taps[k] * par[k : k + 1, :]
    return total


def conv_back(dcv, par):
    total = dcv * par[3:4, :]
    for m in range(1, 4):
        total = total + shift_up(dcv, m) * par[3 - m : 4 - m, :]
    return total


def column_sum(v):
    return jnp.sum(v, axis=0, keepdims=True)


def slot(k):
    return slice(k * T, (k + 1) * T)


def tri(lower):
    if lower:
        return (iota(0) >= iota(1)).astype(F32)
    return (iota(0) <= iota(1)).astype(F32)


def step_prep(k, pbc, dtp, run_col, run_row, step_wide):
    step = softplus(pbc[slot(k), 256:384] + dtp[0:1, :])
    run = jnp.dot(tri(True), step * dtp[1:2, :], precision=HI, preferred_element_type=F32)
    run_row[k] = jnp.transpose(run)
    left = iota(1) < HEAD
    for p in range(PAIRS):
        a, b = 2 * p, 2 * p + 1
        run_col[a, slot(k), :] = jnp.broadcast_to(run[:, a : a + 1], (T, LANES))
        run_col[b, slot(k), :] = jnp.broadcast_to(run[:, b : b + 1], (T, LANES))
        step_wide[p, slot(k), :] = jnp.where(
            left,
            jnp.broadcast_to(step[:, a : a + 1], (T, LANES)),
            jnp.broadcast_to(step[:, b : b + 1], (T, LANES)),
        )
    return step


def halves(v):
    left = iota(1) < HEAD
    zero = jnp.zeros_like(v)
    return jnp.concatenate([jnp.where(left, v, zero), jnp.where(left, zero, v)], axis=0)


def in_lanes(columns):
    lane = lax.broadcasted_iota(jnp.int32, (columns[0].shape[0], LANES), 1)
    out = jnp.zeros(lane.shape, F32)
    for n, v in enumerate(columns):
        for k in range(3):
            part = v.astype(BF16).astype(F32)
            out = jnp.where(lane == 3 * n + k, part, out)
            v = v - part
    return out.astype(BF16)


def from_lanes(v, n):
    return sum(v[:, 3 * n + k : 3 * n + k + 1].astype(F32) for k in range(3))


class Refs:
    pass


def kernel_call(body, name, ins, outs, scratch, cost_us):
    in_names, out_names, scratch_names = list(ins), list(outs), list(scratch)

    def run(*refs):
        rf = Refs()
        for key, ref in zip(in_names + out_names + scratch_names, refs):
            setattr(rf, key, ref)
        body(rf, pl.program_id(0))

    res = pl.pallas_call(
        run,
        grid=(STEPS,),
        in_specs=[
            pl.BlockSpec(*ins[n][1:]) if len(ins[n]) > 2 else pl.BlockSpec(memory_space=ins[n][1])
            for n in in_names
        ],
        out_specs=[pl.BlockSpec(outs[n][2], outs[n][3]) for n in out_names],
        out_shape=[jax.ShapeDtypeStruct(outs[n][0], outs[n][1]) for n in out_names],
        scratch_shapes=[pltpu.VMEM(*scratch[n]) for n in scratch_names],
        compiler_params=pltpu.CompilerParams(vmem_limit_bytes=VMEM_LIMIT),
        cost_estimate=pl.CostEstimate(
            flops=int(cost_us * 1.1e9), bytes_accessed=1 << 20, transcendentals=0
        ),
        name=name,
    )(*[ins[n][0] for n in in_names])
    return dict(zip(out_names, res))


def whole(v):
    return (v, v.shape, lambda h: (0,) * v.ndim)


def whole_out(shape, dtype):
    return (shape, dtype, shape, lambda h: (0,) * len(shape))


def by_step(v, block):
    return (v, block, lambda h: (h,) + (0,) * (len(block) - 1))


def by_step_out(shape, dtype, block):
    return (shape, dtype, block, lambda h: (h,) + (0,) * (len(block) - 1))


def lanes_by_step(v):
    return (v, (v.shape[0], WIDE), lambda h: (0, h))


def lanes_by_step_out(shape, dtype):
    return (shape, dtype, (shape[0], WIDE), lambda h: (0, h))


def weight_blocks(w):
    half = (8, 3, 16, w.shape[3])
    return {
        "wg": (w, half, lambda h: (h, 1, 0, 0)),
        "wv": (w, half, lambda h: (h, 2, 0, 0)),
        "wbc": (w, (16, 1, 16, w.shape[3]), lambda h: (0, 9, 0, 0)),
    }


def pair_lanes(p):
    return slice(p * LANES, (p + 1) * LANES)


def flat_rows(ref):
    v = ref[...]
    return v.reshape(-1, v.shape[-1])


def mixed_bc(rf, k, c):
    lanes = slice(c * LANES, (c + 1) * LANES)
    cv = conv_sum(conv_taps(rf.pbc[slot(k), lanes]), rf.pbcv[:, lanes])
    return cv * sigmoid(cv)


def forward(x_slots, g_slots, w, dtw, gain, pv, pbcv, dtp):
    width = x_slots[0].shape[1]
    with_grad = g_slots is not None

    def body(rf, h):
        @pl.when(h == 0)
        def _prep():
            for k in range(SLOTS):
                x = getattr(rf, f"x{k}")[...].astype(F32)
                scale = lax.rsqrt(jnp.mean(x * x, axis=1, keepdims=True) + EPS)
                rf.normed[slot(k), :] = (x * scale * rf.gain[...]).astype(BF16)
                if with_grad:
                    rf.g_all[slot(k), :] = getattr(rf, f"g{k}")[...]
            rf.pbc[:, 0:256] = dot_nt(rf.normed[...], flat_rows(rf.wbc))
            rf.pbc[:, 256:384] = dot_nt(rf.normed[...], rf.dtw[...])
            for k in range(SLOTS):
                rf.scores[k] = dot_nt(mixed_bc(rf, k, 1), mixed_bc(rf, k, 0), HI) * tri(True)
                step_prep(k, rf.pbc, rf.dtp, rf.run_col, rf.run_row, rf.step_wide)
            rf.square[...] = jnp.zeros_like(rf.square)
            rf.cross[...] = jnp.zeros_like(rf.cross)

        rf.proj[0, :, 0:WIDE] = dot_nt(rf.normed[...], flat_rows(rf.wg))
        rf.proj[0, :, WIDE : 2 * WIDE] = dot_nt(rf.normed[...], flat_rows(rf.wv))
        if with_grad:
            q_all = dot_nt(rf.g_all[...], rf.wout[pl.ds(8 * h, 8)].reshape(WIDE, width))
        for p in range(HALF):
            lanes = pair_lanes(p)
            par = rf.pv[:, lanes]
            pair = HALF * h + p
            for k in range(SLOTS):
                gate = rf.proj[0, slot(k), lanes]
                cv = conv_sum(
                    conv_taps(rf.proj[0, slot(k), WIDE + p * LANES : WIDE + (p + 1) * LANES]), par
                )
                values = cv * sigmoid(cv)
                scaled = (values * rf.step_wide[pair, slot(k), :]).astype(BF16)
                weights = []
                for a in range(2):
                    gap = (
                        rf.run_col[2 * pair + a, slot(k), :]
                        - rf.run_row[k, pl.ds(2 * pair + a, 1), :]
                    )
                    decay = jnp.exp(jnp.minimum(gap, 0.0))
                    weights.append((rf.scores[k] * decay).astype(BF16))
                y = dot(jnp.concatenate(weights, axis=1), halves(scaled))
                rf.y[0, slot(k), lanes] = y
                scanned = y + par[6:7, :] * values
                gated = scanned * (gate * sigmoid(gate))
                rf.square[slot(k), :] += gated * gated
                scaled_out = gated * par[5:6, :]
                rf.u_all[h, slot(k), lanes] = scaled_out.astype(BF16)
                if with_grad:
                    rf.cross[slot(k), :] += q_all[slot(k), lanes] * scaled_out

        @pl.when(h == STEPS - 1)
        def _finish():
            u = jnp.concatenate([rf.u_all[a] for a in range(STEPS)], axis=1)
            for n in range(0, width, 512):
                part = dot(u, rf.wout[:, :, :, n : n + 512].reshape(STEPS * WIDE, 512)).astype(BF16)
                for k in range(SLOTS):
                    getattr(rf, f"out{k}")[:, n : n + 512] = part[slot(k), :]
            for k in range(SLOTS):
                total = jnp.sum(rf.square[slot(k), :], axis=1, keepdims=True)
                getattr(rf, f"out{k}")[:, width:] = in_lanes([total])
            ones = jnp.ones((8, LANES), F32)
            rf.stats[0] = dot_nt(ones, rf.square[...], HI)
            rf.stats[1] = dot_nt(ones, rf.cross[...], HI)

    ins = {f"x{k}": whole(v) for k, v in enumerate(x_slots)}
    if with_grad:
        ins.update({f"g{k}": whole(v) for k, v in enumerate(g_slots)})
    ins.update(
        gain=whole(gain),
        **weight_blocks(w),
        dtw=whole(dtw),
        wout=(w, (16, 3, 16, width), lambda h: (0, 0, 0, 0)),
        pv=lanes_by_step(pv),
        pbcv=whole(pbcv),
        dtp=whole(dtp),
    )
    outs = {f"out{k}": whole_out((T, width + LANES), BF16) for k in range(SLOTS)}
    outs.update(
        stats=whole_out((2, 8, ROWS), F32),
        normed=whole_out((ROWS, width), BF16),
        proj=by_step_out((STEPS, ROWS, 2 * WIDE), F32, (1, ROWS, 2 * WIDE)),
        y=by_step_out((STEPS, ROWS, WIDE), F32, (1, ROWS, WIDE)),
        pbc=whole_out((ROWS, 384), F32),
    )
    scratch = dict(
        scores=((SLOTS, T, T), F32),
        run_col=((2 * PAIRS, ROWS, LANES), F32),
        run_row=((SLOTS, T, LANES), F32),
        step_wide=((PAIRS, ROWS, LANES), F32),
        u_all=((STEPS, ROWS, WIDE), BF16),
        square=((ROWS, LANES), F32),
        cross=((ROWS, LANES), F32),
    )
    if with_grad:
        scratch["g_all"] = ((ROWS, width), BF16)
    res = kernel_call(body, "layer_forward", ins, outs, scratch, 18)
    return [res[f"out{k}"] for k in range(SLOTS)], res


def head_columns(pair):
    target = 2 * pair + (iota(0) >= HEAD).astype(jnp.int32)
    one = (iota(1) == target).astype(BF16)
    return jnp.concatenate([one, one], axis=0)


def head_sum(v, columns):
    high = v.astype(BF16)
    low = (v - high.astype(F32)).astype(BF16)
    return dot(jnp.concatenate([high, low], axis=1), columns)


def put_by_core(rf, key, x, at, part):
    keep, send = getattr(rf, key + "_keep"), getattr(rf, key + "_send")
    groups = slice(at, at + part.shape[2])
    for c in range(2):

        @pl.when(rf.core[0] == c)
        def _store(c=c):
            for z in range(4):
                keep[x, z, groups] = part[z, c]
                send[x, z, groups] = part[z, 1 - c]


def backward(stages, name, cost_us, saved, layer, have):
    gate, scan, inp, wgate, wscan = (
        s in stages for s in ("gate", "scan", "input", "wgate", "wscan")
    )
    width = saved["normed"].shape[1]
    w, dtw, pv, pbcv, dtp = layer
    elementwise = gate or scan

    def body(rf, h):
        @pl.when(h == 0)
        def _prep():
            for k in range(SLOTS):
                if gate or wgate:
                    rf.g_all[slot(k), :] = getattr(rf, f"g{k}")[...]
                if gate:
                    for row, ref in ((0, rf.scale_row), (1, rf.cross_row)):
                        if "rows" in have:
                            ref[slot(k), :] = jnp.transpose(
                                jnp.broadcast_to(rf.rows[k, row : row + 1, :], (T, LANES))
                            )
                        else:
                            column = from_lanes(getattr(rf, f"e{k}")[...], row)
                            ref[slot(k), :] = jnp.broadcast_to(column, (T, LANES))
                if scan:
                    inbound, outbound = mixed_bc(rf, k, 0), mixed_bc(rf, k, 1)
                    rf.mixed[0, slot(k), :] = inbound
                    rf.mixed[1, slot(k), :] = outbound
                    rf.scores[k] = dot_nt(inbound, outbound, HI) * tri(False)
                    rf.step_all[slot(k), :] = step_prep(
                        k, rf.pbc, rf.dtp, rf.run_col, rf.run_row, rf.step_wide
                    )
            if scan:
                rf.dscores[...] = jnp.zeros_like(rf.dscores)
                rf.dstep[...] = jnp.zeros_like(rf.dstep)
                rf.drun[...] = jnp.zeros_like(rf.drun)
            if inp:
                rf.total[...] = jnp.zeros_like(rf.total)

        if gate:
            q_all = dot_nt(rf.g_all[...], flat_rows(rf.wout))
        for p in range(HALF if elementwise else 0):
            lanes = pair_lanes(p)
            par = rf.pv[:, lanes]
            pair = HALF * h + p
            sums = [jnp.zeros((1, LANES), F32) for _ in range(8)]
            if scan:
                columns = head_columns(pair)
            for k in range(SLOTS):
                taps = conv_taps(rf.proj[0, slot(k), WIDE + p * LANES : WIDE + (p + 1) * LANES])
                cv = conv_sum(taps, par)
                sig_c = sigmoid(cv)
                values = cv * sig_c
                y = rf.y[0, slot(k), lanes]
                if gate:
                    gate_in = rf.proj[0, slot(k), lanes]
                    sig_g = sigmoid(gate_in)
                    silu_g = gate_in * sig_g
                    scanned = y + par[6:7, :] * values
                    gated = scanned * silu_g
                    grad_no = q_all[slot(k), lanes]
                    scale = rf.scale_row[slot(k), :]
                    dgated = scale * (grad_no * par[5:6, :]) - rf.cross_row[slot(k), :] * gated
                    norm = gated * scale
                    sums[5] += column_sum(grad_no * norm)
                    rf.u[slot(k), lanes] = (norm * par[5:6, :]).astype(BF16)
                    dscan = dgated * silu_g
                    dgate = dgated * scanned * (sig_g * (1.0 + gate_in * (1.0 - sig_g)))
                    sums[6] += column_sum(dscan * values)
                    rf.dg[slot(k), lanes] = dgate.astype(BF16)
                    if not scan:
                        rf.dscan[slot(k), lanes] = dscan
                else:
                    dscan = rf.dscan[slot(k), lanes]
                if not scan:
                    continue
                wide = rf.step_wide[pair, slot(k), :]
                dy = dscan.astype(BF16)
                scaled = (values * wide).astype(BF16)
                dweights = dot_nt(halves(scaled), dy)
                weights = []
                dscore = rf.dscores[k]
                for a in range(2):
                    gap = (
                        rf.run_row[k, pl.ds(2 * pair + a, 1), :]
                        - rf.run_col[2 * pair + a, slot(k), :]
                    )
                    decay = jnp.exp(jnp.minimum(gap, 0.0))
                    weights.append((rf.scores[k] * decay).astype(BF16))
                    dscore = dscore + dweights[slot(a), :] * decay
                rf.dscores[k] = dscore
                dscaled = dot(jnp.concatenate(weights, axis=1), halves(dy))
                rf.dstep[slot(k), :] += head_sum(dscaled * values, columns)
                rf.drun[slot(k), :] += head_sum(
                    dy.astype(F32) * y - scaled.astype(F32) * dscaled, columns
                )
                dvalues = dscaled * wide + par[6:7, :] * dscan
                dcv = dvalues * (sig_c * (1.0 + cv * (1.0 - sig_c)))
                for t in range(4):
                    sums[t] += column_sum(dcv * taps[t])
                sums[4] += column_sum(dcv)
                rf.dv[slot(k), lanes] = conv_back(dcv, par).astype(BF16)
            rf.small[p] = jnp.concatenate(sums, axis=0)
        if wgate and wscan:
            for at, left, right in (
                (0, rf.dg, rf.normed),
                (3, rf.u, rf.g_all),
                (6, rf.dv, rf.normed),
            ):
                part = dot_tn(left[...], right[...]).astype(BF16)
                rf.ga[:, at : at + 3] = part.reshape(8, 3, 16, width)
            part = dot_tn(rf.dbc_half[...], rf.normed[...]).astype(BF16)
            rf.ga[:, 9] = part.reshape(8, 16, width)
        elif wgate:
            for at, left, right in ((0, rf.dg, rf.normed), (3, rf.u, rf.g_all)):
                part = dot_tn(left[...], right[...]).astype(BF16)
                put_by_core(rf, "ga", h, at, part.reshape(4, 2, 3, 16, width))
        elif wscan:
            part = dot_tn(rf.dv[...], rf.normed[...]).astype(BF16)
            put_by_core(rf, "gb", h, 0, part.reshape(4, 2, 3, 16, width))
        if inp:
            rf.total[...] += dot(rf.dg[...], flat_rows(rf.wg)) + dot(rf.dv[...], flat_rows(rf.wv))

        @pl.when(h == STEPS - 1)
        def _finish():
            if scan:
                sums = [[jnp.zeros((1, LANES), F32) for _ in range(8)] for _ in range(2)]
                dt_sums = [jnp.zeros((1, LANES), F32) for _ in range(8)]
                live = iota(1) < 2 * PAIRS
                for k in range(SLOTS):
                    dscore = rf.dscores[k] * tri(False)
                    dmixed = (
                        jnp.dot(
                            dscore,
                            rf.mixed[1, slot(k), :],
                            precision=HI,
                            preferred_element_type=F32,
                        ),
                        dot_tn(dscore, rf.mixed[0, slot(k), :], HI),
                    )
                    for c in range(2):
                        lanes = slice(c * LANES, (c + 1) * LANES)
                        par = rf.pbcv[:, lanes]
                        taps = conv_taps(rf.pbc[slot(k), lanes])
                        cv = conv_sum(taps, par)
                        sig = sigmoid(cv)
                        dcv = dmixed[c] * (sig * (1.0 + cv * (1.0 - sig)))
                        for t in range(4):
                            sums[c][t] += column_sum(dcv * taps[t])
                        sums[c][4] += column_sum(dcv)
                        rf.dbc[slot(k), lanes] = conv_back(dcv, par).astype(BF16)
                    dlog = jnp.dot(
                        tri(False), rf.drun[slot(k), :], precision=HI, preferred_element_type=F32
                    )
                    grad_step = rf.dstep[slot(k), :] + dlog * rf.dtp[1:2, :]
                    dt_sums[1] += column_sum(dlog * rf.step_all[slot(k), :])
                    draw = grad_step * sigmoid(rf.pbc[slot(k), 256:384] + rf.dtp[0:1, :])
                    draw = jnp.where(live, draw, 0.0)
                    dt_sums[0] += column_sum(draw)
                    rf.dbc[slot(k), 256:384] = draw.astype(BF16)
                rf.small_bc[0] = jnp.concatenate(sums[0], axis=0)
                rf.small_bc[1] = jnp.concatenate(sums[1], axis=0)
                dt_sums[1] = dt_sums[1] * rf.dtp[1:2, :]
                rf.small_dt[...] = jnp.concatenate(dt_sums, axis=0)
            if wscan and not wgate:
                part = dot_tn(rf.dbc[:, 0:256], rf.normed[...]).astype(BF16)
                part = part.reshape(2, 4, 2, 1, 16, width)
                for a in range(2):
                    put_by_core(rf, "gb", a, 3, part[a])
            if wscan:
                rf.gdt[...] = dot_tn(rf.dbc[:, 256:384], rf.normed[...])[0:16]
            if inp:
                final = (
                    rf.total[...]
                    + dot(rf.dbc[:, 0:256], flat_rows(rf.wbc))
                    + dot(rf.dbc[:, 256:384], rf.dtw[...])
                )
                for k in range(SLOTS):
                    getattr(rf, f"out{k}")[...] = final[slot(k), :].astype(BF16)

    ins, outs, scratch = {}, {}, {}
    heads_cols = STEPS * WIDE
    if gate or wgate:
        for k, v in enumerate(have["g"]):
            ins[f"g{k}"] = (v, (T, width), lambda h: (0, 0))
        scratch["g_all"] = ((ROWS, width), BF16)
    if gate:
        if "rows" in have:
            ins["rows"] = whole(have["rows"])
        else:
            for k, v in enumerate(have["g"]):
                ins[f"e{k}"] = (v, (T, LANES), lambda h: (0, width // LANES))
        ins["wout"] = (w, (8, 3, 16, width), lambda h: (h, 0, 0, 0))
        scratch["scale_row"] = ((ROWS, LANES), F32)
        scratch["cross_row"] = ((ROWS, LANES), F32)
        outs["u"] = lanes_by_step_out((ROWS, heads_cols), BF16)
        outs["dg"] = lanes_by_step_out((ROWS, heads_cols), BF16)
        if not scan:
            outs["dscan"] = lanes_by_step_out((ROWS, heads_cols), F32)
    if elementwise:
        ins["proj"] = by_step(saved["proj"], (1, ROWS, 2 * WIDE))
        ins["y"] = by_step(saved["y"], (1, ROWS, WIDE))
        ins["pv"] = lanes_by_step(pv)
        outs["small"] = by_step_out((PAIRS, 8, LANES), F32, (HALF, 8, LANES))
    if scan:
        ins["pbc"] = whole(saved["pbc"])
        ins["pbcv"] = whole(pbcv)
        ins["dtp"] = whole(dtp)
        if not gate:
            ins["dscan"] = lanes_by_step(have["dscan"])
        outs["dv"] = lanes_by_step_out((ROWS, heads_cols), BF16)
        outs["dbc"] = whole_out((ROWS, 384), BF16)
        outs["small_bc"] = whole_out((2, 8, LANES), F32)
        outs["small_dt"] = whole_out((8, LANES), F32)
        scratch.update(
            mixed=((2, ROWS, LANES), F32),
            scores=((SLOTS, T, T), F32),
            run_col=((2 * PAIRS, ROWS, LANES), F32),
            run_row=((SLOTS, T, LANES), F32),
            step_wide=((PAIRS, ROWS, LANES), F32),
            step_all=((ROWS, LANES), F32),
            dscores=((SLOTS, T, T), F32),
            dstep=((ROWS, LANES), F32),
            drun=((ROWS, LANES), F32),
        )
    if inp:
        ins.update(weight_blocks(w))
        ins["dtw"] = whole(dtw)
        scratch["total"] = ((ROWS, width), F32)
        outs.update({f"out{k}": whole_out((T, width), BF16) for k in range(SLOTS)})
    if wgate or wscan:
        ins["normed"] = whole(saved["normed"])
    if not gate and (wgate or inp):
        ins["dg"] = lanes_by_step(have["dg"])
    if wgate and not gate:
        ins["u"] = lanes_by_step(have["u"])
    if not scan and (wscan or inp):
        ins["dv"] = lanes_by_step(have["dv"])
        ins["dbc"] = whole(have["dbc"])
    if wgate and wscan:
        ins["dbc_half"] = (have["dbc"], (ROWS, LANES), lambda h: (0, h))
        outs["ga"] = by_step_out((16, 10, 16, width), BF16, (8, 10, 16, width))
    elif wgate or wscan:
        ins["core"] = have["core"]
        key, groups = ("ga", 6) if wgate else ("gb", 4)
        for end in ("_keep", "_send"):
            outs[key + end] = whole_out((2, 4, groups, 16, width), BF16)
    if wscan:
        outs["gdt"] = whole_out((16, width), F32)
    return kernel_call(body, name, ins, outs, scratch, cost_us)


def assemble(parts, dt_rows, shard):
    quarter = parts.shape[2]
    block = 16 * 48
    total = 8 * block + 16 * 16 + dt_rows.shape[0]

    def body(_, inw, outw, shared, dt, grad_in, grad_out):
        i = pl.program_id(0)

        @pl.when(i < 8)
        def _columns():
            grad_in[...] = inw[...].reshape(block, quarter).astype(F32)

        @pl.when(i < SLOTS)
        def _out():
            grad_out[...] = outw[...].reshape(block, quarter).astype(F32)

        @pl.when(i == 8)
        def _shared():
            grad_in[...] = jnp.zeros_like(grad_in)
            grad_in[0:256, :] = shared[...].reshape(256, quarter).astype(F32)
            grad_in[256 : 256 + dt_rows.shape[0], :] = dt[...]

    last = SLOTS - 1
    spec = pltpu.PrefetchScalarGridSpec(
        num_scalar_prefetch=1,
        grid=(9,),
        in_specs=[
            pl.BlockSpec(
                (16, 48, quarter),
                lambda i, j: (0, jnp.where(i < SLOTS, 0, 8) + (j[0] + 3 * SLOTS - i) % SLOTS, 0),
            ),
            pl.BlockSpec((16, 48, quarter), lambda i, j: (0, SLOTS + jnp.minimum(i, last), 0)),
            pl.BlockSpec((16, 16, quarter), lambda i, j: (0, 36, 0)),
            pl.BlockSpec(dt_rows.shape, lambda i, j: (0, 0)),
        ],
        out_specs=[
            pl.BlockSpec((block, quarter), lambda i, j: (i, 0)),
            pl.BlockSpec((block, quarter), lambda i, j: (0, jnp.minimum(i, last))),
        ],
    )
    return pl.pallas_call(
        body,
        grid_spec=spec,
        out_shape=[
            jax.ShapeDtypeStruct((total, quarter), F32),
            jax.ShapeDtypeStruct((block, SLOTS * quarter), F32),
        ],
        compiler_params=pltpu.CompilerParams(vmem_limit_bytes=VMEM_LIMIT),
        name="assemble",
    )(shard.astype(jnp.int32)[None], parts, parts, parts, dt_rows)


def ring(n, k):
    return [(i, (i + k) % n) for i in range(n)]


def send_shard(v, k):
    return lax.ppermute(v, "shard", ring(SLOTS, k)) if k else v


def send_across(v, k):
    pairs = [
        (sec * SLOTS + y, (1 - sec) * SLOTS + (y + k) % SLOTS)
        for sec in range(2)
        for y in range(SLOTS)
    ]
    return lax.ppermute(v, ("section", "shard"), pairs)


def swap_section(v):
    return lax.ppermute(v, "section", [(0, 1), (1, 0)])


def dp_index(x, z, c):
    return x * 8 + z * 2 + c


def dp_pairs(move):
    pairs = []
    for x in range(2):
        for z in range(4):
            for c in range(2):
                pairs.append((dp_index(x, z, c), dp_index(*move(x, z, c))))
    return pairs


def pick(v, index, axis):
    return lax.dynamic_index_in_dim(v, index, axis, keepdims=False)


def gather_slots(v):
    return [send_shard(v, (-k) % SLOTS) for k in range(SLOTS)]


def scatter_sum(slots):
    parts = [send_shard(slots[k], k) for k in range(SLOTS)]
    return sum(p.astype(F32) for p in parts)


def cross_core(v):
    return lax.ppermute(v, DP, dp_pairs(lambda x, z, c: (x, z, 1 - c)))


def sum_small(v):
    v = v + lax.ppermute(v, DP, dp_pairs(lambda x, z, c: (x, z, 1 - c)))
    v = v + sum(
        lax.ppermute(v, DP, dp_pairs(lambda x, z, c: (x, (z + k) % 4, c))) for k in range(1, 4)
    )
    return v + lax.ppermute(v, DP, dp_pairs(lambda x, z, c: (1 - x, z, c)))


def in_order(parts, sign):
    j = lax.axis_index("shard")
    stacked = jnp.stack(parts)
    return jnp.take(stacked, (sign * (jnp.arange(SLOTS) - j)) % SLOTS, axis=0)


def shards(
    tokens,
    cotangent,
    lengths,
    norm_gain,
    in_weight,
    conv_weight,
    conv_bias,
    dt_bias,
    a_log,
    d_skip,
    gate_gain,
    out_weight,
):
    sec = lax.axis_index("section")
    d = lax.axis_index(DP)
    j = lax.axis_index("shard")
    core = d % 2
    first = sec == 0
    width = tokens.shape[2]
    quarter = norm_gain.shape[1]
    channels = conv_bias.shape[1]
    own_cols = gate_gain.shape[1]
    inner = own_cols * SLOTS
    heads = dt_bias.shape[1]
    own_heads = heads // SLOTS
    n_state = 2 * LANES
    piece = own_cols // 16
    piece_bc = n_state // 16
    own_core = (core.astype(jnp.int32)[None], pltpu.SMEM)

    x_own = pick(tokens, sec, 0)
    cot = pick(cotangent, sec, 0)
    length = pick(lengths, sec, 0)
    mask = (jnp.arange(T, dtype=jnp.int32) < length).astype(F32)[:, None]

    columns = jnp.transpose(in_weight[0])
    with jax.named_scope("weights"):

        def cut(start, rows):
            return lax.dynamic_slice(columns, (start, 0), (rows, quarter))

        def columns_of(to):
            return jnp.concatenate(
                [
                    cut(own_cols * to + piece * d, piece),
                    cut(inner + own_cols * to + piece * d, piece),
                    cut(2 * inner + piece_bc * d, piece_bc),
                ],
                axis=0,
            )

        cuts = [columns_of((j + k) % SLOTS) for k in range(SLOTS)]
        o_own = lax.dynamic_slice(out_weight[0], (piece * d, 0), (piece, width))
        o_other = swap_section(o_own)

        w_own = [send_shard(cuts[k], k) for k in range(SLOTS)]
        w_other = [send_across(cuts[k], k) for k in range(SLOTS)]

        def from_parts(parts, others, o, o_others, own):
            pieces = [jnp.where(own, p, q) for p, q in zip(parts, others)]
            lanes = []
            for y in range(SLOTS):
                v = pieces[0]
                for k in range(1, SLOTS):
                    v = jnp.where((j - y) % SLOTS == k, pieces[k], v)
                lanes.append(v)
            return jnp.concatenate(
                [jnp.where(own, o, o_others), jnp.concatenate(lanes, axis=1)], axis=0
            )

        w0 = from_parts(w_own, w_other, o_own, o_other, first)
        w1 = from_parts(w_own, w_other, o_own, o_other, ~first)
        w0, w1, x_own, cot = lax.optimization_barrier((w0, w1, x_own, cot))
        w0 = lax.all_gather(w0, DP, axis=0, tiled=False)
        x_slots = gather_slots(x_own)
        x_slots, norm_gain = lax.optimization_barrier((x_slots, norm_gain))

    with jax.named_scope("small_weights"):
        dt_columns = columns[2 * inner + n_state :]
        sizes = [quarter, 4 * channels, channels, own_cols, heads, heads, heads, heads * quarter]
        flat = jnp.concatenate(
            [
                norm_gain[0],
                conv_weight[0].reshape(-1),
                conv_bias[0],
                gate_gain[0],
                dt_bias[0],
                a_log[0],
                d_skip[0],
                dt_columns.reshape(-1),
            ]
        )
        flat = jnp.pad(flat, (0, -flat.shape[0] % LANES)).reshape(-1, LANES)
        own = in_order(gather_slots(flat), 1)
        other = swap_section(own)
        small = [jnp.where(first, own, other), jnp.where(first, other, own)]

        def unpack(v):
            low = v.reshape(SLOTS, -1)
            at = sum(sizes[:-1])
            dtw = low[:, at : at + sizes[-1]].reshape(SLOTS, heads, quarter)
            dtw = lax.dynamic_slice(dtw, (0, own_heads * j, 0), (SLOTS, own_heads, quarter))
            dtw = jnp.transpose(dtw, (1, 0, 2)).reshape(own_heads, width)
            dtw = jnp.pad(dtw, ((0, LANES - own_heads), (0, 0)))
            v = low[:, :at].astype(F32)
            cut, at = [], 0
            for size in sizes[:-1]:
                cut.append(v[:, at : at + size])
                at += size
            gain = cut[0].reshape(1, width)
            taps = cut[1].reshape(SLOTS, 4, channels).transpose(1, 0, 2).reshape(4, -1)
            bias = cut[2].reshape(1, -1)
            conv = jnp.concatenate([taps, bias, jnp.zeros((3, taps.shape[1]), F32)], axis=0)
            pbcv = conv[:, inner:]
            pv = lax.dynamic_slice(conv, (0, own_cols * j), (8, own_cols))
            pick_heads = lambda u: lax.dynamic_slice(u[0], (own_heads * j,), (own_heads,))
            wide = jnp.repeat(pick_heads(cut[6]), HEAD)[None]
            pv = jnp.concatenate([pv[:5], pick(cut[3], j, 0)[None], wide, pv[7:]], axis=0)
            dtp = jnp.stack([pick_heads(cut[4]), -jnp.exp(pick_heads(cut[5]))])
            dtp = jnp.pad(dtp, ((0, 6), (0, LANES - own_heads)))
            return gain, dtw, pv, pbcv, dtp

        gain0, *params0 = unpack(small[0])
        gain1, *params1 = unpack(small[1])

    x_f = x_own.astype(F32)
    g1 = (mask * cot.astype(F32)).astype(BF16)
    g1_slots = gather_slots(g1)
    w0, x_slots, g1_slots, gain0, params0, gain1, params1, w1 = lax.optimization_barrier(
        (w0, x_slots, g1_slots, gain0, params0, gain1, params1, w1)
    )
    w1 = lax.all_gather(w1, DP, axis=0, tiled=False)
    blocks = lambda v: v.reshape(16, 10, 16, width)

    layer0 = (blocks(w0), *params0)
    layer1 = (blocks(w1), *params1)

    def forward_layer(x, g, gain, layer):
        w, dtw, pv, pbcv, dtp = layer
        return forward(x, g, w, dtw, gain, pv, pbcv, dtp)

    parts, saved0 = forward_layer(x_slots, None, gain0, layer0)
    branch = scatter_sum(parts)
    square = jnp.sum(branch[:, width : width + 3], axis=1, keepdims=True)
    scale0 = lax.rsqrt(square / inner + EPS)
    branch0 = branch[:, :width] * scale0
    middle = (x_f + mask * branch0).astype(BF16)

    m_slots = gather_slots(middle)
    branch_parts, saved1 = forward_layer(m_slots, g1_slots, gain1, layer1)
    own = saved1["stats"][:, 0].reshape(2, SLOTS, T)
    back = [send_shard(own, k) for k in range(SLOTS)]
    summed = sum(jnp.roll(back[k], -k, axis=1) for k in range(SLOTS))
    scale1 = lax.rsqrt(summed[0] / inner + EPS)
    cross1 = scale1 * scale1 * scale1 * summed[1] / inner
    rows1 = jnp.pad(jnp.stack([scale1, cross1], axis=1), ((0, 0), (0, 6), (0, 0)))

    def norm_back(x, gain, grad):
        scale = lax.rsqrt(jnp.mean(x * x, axis=1, keepdims=True) + EPS)
        unit = x * scale
        dn = grad * gain
        dx = scale * (dn - unit * jnp.mean(dn * unit, axis=1, keepdims=True))
        return dx, jnp.sum(grad * unit, axis=0)

    back1 = backward(
        ("gate", "scan", "input"),
        "backward_1",
        28,
        saved1,
        layer1,
        {"g": g1_slots, "rows": rows1},
    )
    moved = [send_shard(back1[f"out{k}"], k) for k in range(SLOTS)]
    grads1 = backward(
        ("wgate", "wscan"), "weight_grads_1", 8, saved1, layer1, {"g": g1_slots, **back1}
    )
    back1.update(grads1)
    moved[1], back1["ga"] = lax.optimization_barrier((moved[1], back1["ga"]))
    dx, gain_grad1 = norm_back(middle.astype(F32), gain1, sum(p.astype(F32) for p in moved))
    by_owner = lambda v: v.reshape(16, -1, width)
    owned1 = lax.psum_scatter(by_owner(back1["ga"]), DP, scatter_dimension=0, tiled=False)

    dmiddle = (cot.astype(F32) + dx).astype(BF16)
    g0 = (mask * dmiddle.astype(F32)).astype(BF16)
    cross0 = scale0 * scale0 * jnp.sum(g0.astype(F32) * branch0, axis=1, keepdims=True) / inner
    g0_slots = gather_slots(jnp.concatenate([g0, in_lanes([scale0, cross0])], axis=1))
    g0_slots, branch_parts = lax.optimization_barrier((g0_slots, branch_parts))
    branch = scatter_sum(branch_parts)[:, :width] * scale1[0][:, None]
    result = middle.astype(F32) + mask * branch

    back0 = backward(
        ("gate", "wgate"),
        "backward_0_gate",
        14,
        saved0,
        layer0,
        {"g": g0_slots, "core": own_core},
    )
    both = lambda kept, moved: (kept.astype(F32) + moved.astype(F32)).astype(BF16)
    a_moved = cross_core(back0["ga_send"])
    small_gate = back0["small"]
    back0["core"] = own_core
    back0.update(backward(("scan", "wscan"), "backward_0_scan", 20, saved0, layer0, back0))
    gb_send, a_moved = lax.optimization_barrier((back0["gb_send"], a_moved))
    a0 = both(back0["ga_keep"], a_moved)
    b0 = both(back0["gb_keep"], cross_core(gb_send))
    owned0 = jnp.pad(a0, ((0, 0), (0, 0), (0, 4), (0, 0), (0, 0)))
    owned0 = lax.dynamic_update_slice(owned0, b0, (0, 0, 6, 0, 0)).reshape(8, -1, width)
    owned0 = lax.psum_scatter(owned0, ("x", "z"), scatter_dimension=0, tiled=False)
    small_scan = back0["small"]
    back0.update(backward(("input",), "backward_0_input", 9, saved0, layer0, back0))
    moved0 = [send_shard(back0[f"out{k}"], k) for k in range(SLOTS)]
    dx, gain_grad0 = norm_back(x_f, gain0, sum(p.astype(F32) for p in moved0))
    dtokens = dmiddle.astype(F32) + dx
    owned1 = owned1 + lax.ppermute(owned1, "section", [(0, 1)])
    owned0, owned1, gain_grad0, dtokens, result = lax.optimization_barrier(
        (owned0, owned1, gain_grad0, dtokens, result)
    )

    kept = jnp.where(first, owned0, owned1).reshape(10, 16, width)
    arrived = lax.ppermute(owned0, "section", [(1, 0)]).reshape(10, 16, width)

    def total_of(cut):
        return (cut(kept).astype(F32) + cut(arrived).astype(F32)).astype(BF16)

    row_slots = []
    for k in range(SLOTS):

        def cut(v):
            v = lax.dynamic_slice_in_dim(v, quarter * ((j + k) % SLOTS), quarter, 2)
            return jnp.concatenate([v[:3], v[6:]], axis=0)

        row_slots.append(send_shard(total_of(cut).reshape(-1, quarter), k))
    out_rows = total_of(lambda v: v[3:6])
    out_rows = jnp.transpose(out_rows.reshape(piece, SLOTS, quarter), (1, 0, 2))
    result_moved = lax.ppermute(result.astype(BF16), "section", [(0, 1)]).astype(F32)
    dtokens_moved = lax.ppermute(dtokens.astype(BF16), "section", [(1, 0)]).astype(F32)
    ends = jnp.where(
        first, jnp.stack([dtokens, dtokens_moved]), jnp.stack([result_moved, result])
    )[None]

    def to_section(v0, v1):
        kept = jnp.where(first, v0, v1).astype(F32)
        return kept + swap_section(jnp.where(first, v1, v0)).astype(F32)

    shared = sum(v[2 * piece :].astype(F32) for v in row_slots).astype(BF16)
    gathered = lax.all_gather(
        jnp.concatenate(
            [v[:piece] for v in row_slots]
            + [out_rows.reshape(-1, quarter)]
            + [v[piece : 2 * piece] for v in row_slots]
            + [shared],
            axis=0,
        ),
        DP,
        tiled=False,
    )

    def small_of(by_pair, back, gain_grad):
        return jnp.concatenate(
            [
                by_pair.reshape(-1, LANES),
                back["small_bc"].reshape(-1, LANES),
                back["small_dt"],
                gain_grad.reshape(-1, LANES),
                back["gdt"].reshape(-1, LANES),
            ],
            axis=0,
        )

    small0 = small_of(small_gate + small_scan, back0, gain_grad0)
    small1 = small_of(back1["small"], back1, gain_grad1)
    small_sum = sum_small(to_section(small0, small1))
    everyone = in_order(gather_slots(small_sum), 1)
    n_pair, n_bc = PAIRS * 8, 2 * 8
    by_pair = everyone[:, :n_pair].reshape(SLOTS, PAIRS, 8, LANES)
    by_pair = by_pair.transpose(2, 0, 1, 3).reshape(8, inner)
    by_bc = jnp.sum(everyone[:, n_pair : n_pair + n_bc], axis=0)
    by_bc = by_bc.reshape(2, 8, LANES).transpose(1, 0, 2).reshape(8, n_state)
    at = n_pair + n_bc
    by_dt = everyone[:, at : at + 8, :own_heads].transpose(1, 0, 2).reshape(8, heads)
    at += 8
    gain_total = jnp.sum(everyone[:, at : at + width // LANES], axis=0).reshape(-1)
    at += width // LANES
    dt_rows = everyone[:, at:].reshape(SLOTS, 16, SLOTS, quarter)[:, :own_heads]
    dt_rows = pick(dt_rows, j, 2).reshape(heads, quarter)
    conv_total = jnp.concatenate([by_pair[:5], by_bc[:5]], axis=1)
    conv_own = lax.dynamic_slice(conv_total, (0, channels * j), (5, channels))
    grad_skip = jnp.sum(by_pair[6].reshape(heads, HEAD), axis=1)

    grad_in_weight, grad_out_weight = assemble(gathered, dt_rows, j)
    return (
        ends,
        lax.dynamic_slice(gain_total, (quarter * j,), (quarter,))[None],
        jnp.transpose(grad_in_weight)[None],
        conv_own[None, :4],
        conv_own[4][None],
        by_dt[0][None],
        by_dt[1][None],
        grad_skip[None],
        lax.dynamic_slice(by_pair[5], (own_cols * j,), (own_cols,))[None],
        grad_out_weight[None],
    )


def solution(mesh):
    sections, copies, owners = mesh.devices.shape
    fine = jax.sharding.Mesh(
        mesh.devices.reshape(sections, 2, copies // 4, 2, owners), ("section", *DP, "shard")
    )
    return jax.shard_map(
        shards,
        mesh=fine,
        in_specs=(
            P((*DP, "shard"), None, None),
            P((*DP, "shard"), None, None),
            P((*DP, "shard")),
            P("section", "shard"),
            P("section", "shard", None),
            P("section", None, "shard"),
            P("section", "shard"),
            P("section", None),
            P("section", None),
            P("section", None),
            P("section", "shard"),
            P("section", "shard", None),
        ),
        out_specs=(
            P("section", (*DP, "shard"), None, None),
            P("section", "shard"),
            P("section", "shard", None),
            P("section", None, "shard"),
            P("section", "shard"),
            P("section", None),
            P("section", None),
            P("section", None),
            P("section", "shard"),
            P("section", "shard", None),
        ),
        check_vma=False,
    )
```

```python
import jax
import jax.numpy as jnp
from jax import lax
from jax.experimental import pallas as pl
from jax.experimental.pallas import tpu as pltpu
from jax.sharding import PartitionSpec as P

F32 = jnp.float32
BF16 = jnp.bfloat16
HI = lax.Precision.HIGHEST
EPS = 1e-05
T = 128
LANES = 128
HEAD = 64
SLOTS = 4
ROWS = SLOTS * T
PAIRS = 6
STEPS = 2
HALF = PAIRS // STEPS
WIDE = HALF * LANES
VMEM_LIMIT = 34 * 1024 * 1024
VMEM_MOST = 60 * 1024 * 1024
DP = ("x", "z", "core")


def sigmoid(v):
    return 0.5 * jnp.tanh(0.5 * v) + 0.5


def softplus(v):
    return jnp.maximum(v, 0.0) + jnp.log1p(jnp.exp(-jnp.abs(v)))


def dot(a, b):
    return jnp.dot(a, b, preferred_element_type=F32)


def dot_nt(a, b, precision=None):
    return lax.dot_general(
        a, b, (((1,), (1,)), ((), ())), preferred_element_type=F32, precision=precision
    )


def dot_tn(a, b, precision=None):
    return lax.dot_general(
        a, b, (((0,), (0,)), ((), ())), preferred_element_type=F32, precision=precision
    )


def iota(axis):
    return lax.broadcasted_iota(jnp.int32, (T, LANES), axis)


def shift_down(v, steps):
    return jnp.where(iota(0) >= steps, pltpu.roll(v, steps, 0), 0.0)


def shift_up(v, steps):
    return jnp.where(iota(0) < T - steps, pltpu.roll(v, T - steps, 0), 0.0)


def conv_taps(cin):
    return [shift_down(cin, 3), shift_down(cin, 2), shift_down(cin, 1), cin]


def conv_sum(taps, par):
    total = par[4:5, :] + taps[0] * par[0:1, :]
    for k in range(1, 4):
        total = total + taps[k] * par[k : k + 1, :]
    return total


def conv_back(dcv, par):
    total = dcv * par[3:4, :]
    for m in range(1, 4):
        total = total + shift_up(dcv, m) * par[3 - m : 4 - m, :]
    return total


def column_sum(v):
    return jnp.sum(v, axis=0, keepdims=True)


def slot(k):
    return slice(k * T, (k + 1) * T)


def tri(lower):
    if lower:
        return (iota(0) >= iota(1)).astype(F32)
    return (iota(0) <= iota(1)).astype(F32)


def step_prep(k, pbc, dtp, run_col, run_row, step_wide):
    step = softplus(pbc[slot(k), 256:384] + dtp[0:1, :])
    run = jnp.dot(tri(True), step * dtp[1:2, :], precision=HI, preferred_element_type=F32)
    run_row[k] = jnp.transpose(run)
    left = iota(1) < HEAD
    for p in range(PAIRS):
        a, b = 2 * p, 2 * p + 1
        run_col[a, slot(k), :] = jnp.broadcast_to(run[:, a : a + 1], (T, LANES))
        run_col[b, slot(k), :] = jnp.broadcast_to(run[:, b : b + 1], (T, LANES))
        step_wide[p, slot(k), :] = jnp.where(
            left,
            jnp.broadcast_to(step[:, a : a + 1], (T, LANES)),
            jnp.broadcast_to(step[:, b : b + 1], (T, LANES)),
        )
    return step


def halves(v):
    left = iota(1) < HEAD
    zero = jnp.zeros_like(v)
    return jnp.concatenate([jnp.where(left, v, zero), jnp.where(left, zero, v)], axis=0)


def in_lanes(columns):
    lane = lax.broadcasted_iota(jnp.int32, (columns[0].shape[0], LANES), 1)
    out = jnp.zeros(lane.shape, F32)
    for n, v in enumerate(columns):
        for k in range(3):
            part = v.astype(BF16).astype(F32)
            out = jnp.where(lane == 3 * n + k, part, out)
            v = v - part
    return out.astype(BF16)


def from_lanes(v, n):
    return sum(v[:, 3 * n + k : 3 * n + k + 1].astype(F32) for k in range(3))


class Refs:
    pass


def kernel_call(body, name, ins, outs, scratch, cost_us, limit=VMEM_LIMIT):
    in_names, out_names, scratch_names = list(ins), list(outs), list(scratch)

    def run(*refs):
        for h in range(STEPS):
            rf = Refs()
            for key, ref in zip(in_names + out_names + scratch_names, refs):
                spec = ins.get(key) or outs.get(key)
                blocks = spec[-2:] if spec and len(spec) > 2 else None
                if blocks and blocks[1](1) != blocks[1](0):
                    at = [
                        slice(n * size, (n + 1) * size) if n else slice(0, size)
                        for n, size in zip(blocks[1](h), blocks[0])
                    ]
                    ref = ref.at[tuple(at)]
                setattr(rf, key, ref)
            body(rf, h)

    res = pl.pallas_call(
        run,
        in_specs=[
            pl.BlockSpec(memory_space=pltpu.VMEM if len(ins[n]) > 2 else ins[n][1])
            for n in in_names
        ],
        out_specs=[pl.BlockSpec(memory_space=pltpu.VMEM) for n in out_names],
        out_shape=[jax.ShapeDtypeStruct(outs[n][0], outs[n][1]) for n in out_names],
        scratch_shapes=[
            pltpu.VMEM(*scratch[n]) if isinstance(scratch[n], tuple) else scratch[n]
            for n in scratch_names
        ],
        compiler_params=pltpu.CompilerParams(vmem_limit_bytes=limit),
        cost_estimate=pl.CostEstimate(
            flops=int(cost_us * 1.1e9), bytes_accessed=1 << 20, transcendentals=0
        ),
        name=name,
    )(*[ins[n][0] for n in in_names])
    return dict(zip(out_names, res))


def when(condition):
    return (lambda f: f()) if condition else (lambda f: None)


def whole(v):
    return (v, v.shape, lambda h: (0,) * v.ndim)


def whole_out(shape, dtype):
    return (shape, dtype, shape, lambda h: (0,) * len(shape))


def by_step(v, block):
    return (v, block, lambda h: (h,) + (0,) * (len(block) - 1))


def by_step_out(shape, dtype, block):
    return (shape, dtype, block, lambda h: (h,) + (0,) * (len(block) - 1))


def lanes_by_step(v):
    return (v, (v.shape[0], WIDE), lambda h: (0, h))


def lanes_by_step_out(shape, dtype):
    return (shape, dtype, (shape[0], WIDE), lambda h: (0, h))


def in_hbm(v):
    return (v, pltpu.HBM)


WEIGHT_GROUPS = {"wo": (0, 3), "wg": (3, 3), "wv": (6, 3), "ws": (9, 1)}


class Copies:
    def __init__(self, sems):
        self.sems, self.copies = sems, {}

    def add(self, key, source, target):
        self.copies[key] = (source, target, self.sems.at[len(self.copies)])

    def add_weights(self, rf, keys):
        for key in keys:
            at, count = WEIGHT_GROUPS[key]
            self.add(key, rf.w.at[:, pl.ds(at, count)], getattr(rf, key))

    def start(self):
        for copy in self.copies.values():
            pltpu.make_async_copy(*copy).start()

    def wait(self, *keys):
        for key in keys:
            pltpu.make_async_copy(*self.copies[key]).wait()


def weight_scratch(scratch, keys, width):
    for key in keys:
        scratch[key] = ((16, WEIGHT_GROUPS[key][1], 16, width), BF16)


def half_rows(ref, h):
    v = ref[pl.ds(8 * h, 8)]
    return v.reshape(WIDE, v.shape[-1])


def pair_lanes(p):
    return slice(p * LANES, (p + 1) * LANES)


def flat_rows(ref):
    v = ref[...]
    return v.reshape(-1, v.shape[-1])


def mixed_bc(rf, k, c):
    lanes = slice(c * LANES, (c + 1) * LANES)
    cv = conv_sum(conv_taps(rf.pbc[slot(k), lanes]), rf.pbcv[:, lanes])
    return cv * sigmoid(cv)


def forward(x_slots, g_slots, w, dtw, gain, pv, pbcv, dtp):
    width = x_slots[0].shape[1]
    with_grad = g_slots is not None

    def body(rf, h):
        copies = Copies(rf.sems)
        for k in range(SLOTS):
            copies.add(f"x{k}", getattr(rf, f"x{k}"), rf.x_all.at[k])
        copies.add_weights(rf, ("ws", "wg", "wv", "wo"))
        if with_grad:
            for k in range(SLOTS):
                copies.add(f"g{k}", getattr(rf, f"g{k}"), rf.g_all.at[slot(k)])

        @when(h == 0)
        def _prep():
            copies.start()
            for k in range(SLOTS):
                copies.wait(f"x{k}")
                x = rf.x_all[k].astype(F32)
                scale = lax.rsqrt(jnp.mean(x * x, axis=1, keepdims=True) + EPS)
                rf.normed[slot(k), :] = (x * scale * rf.gain[...]).astype(BF16)
            copies.wait("ws")
            rf.pbc[:, 0:256] = dot_nt(rf.normed[...], flat_rows(rf.ws))
            rf.pbc[:, 256:384] = dot_nt(rf.normed[...], rf.dtw[...])
            for k in range(SLOTS):
                rf.scores[k] = dot_nt(mixed_bc(rf, k, 1), mixed_bc(rf, k, 0), HI) * tri(True)
                step_prep(k, rf.pbc, rf.dtp, rf.run_col, rf.run_row, rf.step_wide)
            rf.square[...] = jnp.zeros_like(rf.square)
            rf.cross[...] = jnp.zeros_like(rf.cross)
            copies.wait("wg", "wv", "wo")
            if with_grad:
                copies.wait(*[f"g{k}" for k in range(SLOTS)])

        rf.proj[0, :, 0:WIDE] = dot_nt(rf.normed[...], half_rows(rf.wg, h))
        rf.proj[0, :, WIDE : 2 * WIDE] = dot_nt(rf.normed[...], half_rows(rf.wv, h))
        if with_grad:
            q_all = dot_nt(rf.g_all[...], half_rows(rf.wo, h))
        for p in range(HALF):
            lanes = pair_lanes(p)
            par = rf.pv[:, lanes]
            pair = HALF * h + p
            for k in range(SLOTS):
                gate = rf.proj[0, slot(k), lanes]
                cv = conv_sum(
                    conv_taps(rf.proj[0, slot(k), WIDE + p * LANES : WIDE + (p + 1) * LANES]), par
                )
                values = cv * sigmoid(cv)
                scaled = (values * rf.step_wide[pair, slot(k), :]).astype(BF16)
                weights = []
                for a in range(2):
                    gap = (
                        rf.run_col[2 * pair + a, slot(k), :]
                        - rf.run_row[k, pl.ds(2 * pair + a, 1), :]
                    )
                    decay = jnp.exp(jnp.minimum(gap, 0.0))
                    weights.append((rf.scores[k] * decay).astype(BF16))
                y = dot(jnp.concatenate(weights, axis=1), halves(scaled))
                rf.y[0, slot(k), lanes] = y
                scanned = y + par[6:7, :] * values
                gated = scanned * (gate * sigmoid(gate))
                rf.square[slot(k), :] += gated * gated
                scaled_out = gated * par[5:6, :]
                rf.u_all[h, slot(k), lanes] = scaled_out.astype(BF16)
                if with_grad:
                    rf.cross[slot(k), :] += q_all[slot(k), lanes] * scaled_out

        @when(h == STEPS - 1)
        def _finish():
            u = jnp.concatenate([rf.u_all[a] for a in range(STEPS)], axis=1)
            for n in range(0, width, 512):
                part = dot(u, rf.wo[:, :, :, n : n + 512].reshape(STEPS * WIDE, 512)).astype(BF16)
                for k in range(SLOTS):
                    getattr(rf, f"out{k}")[:, n : n + 512] = part[slot(k), :]
            for k in range(SLOTS):
                total = jnp.sum(rf.square[slot(k), :], axis=1, keepdims=True)
                getattr(rf, f"out{k}")[:, width:] = in_lanes([total])
            ones = jnp.ones((8, LANES), F32)
            rf.stats[0] = dot_nt(ones, rf.square[...], HI)
            rf.stats[1] = dot_nt(ones, rf.cross[...], HI)

    ins = {f"x{k}": in_hbm(v) for k, v in enumerate(x_slots)}
    if with_grad:
        ins.update({f"g{k}": in_hbm(v) for k, v in enumerate(g_slots)})
    ins.update(
        gain=whole(gain),
        w=in_hbm(w),
        dtw=whole(dtw),
        pv=lanes_by_step(pv),
        pbcv=whole(pbcv),
        dtp=whole(dtp),
    )
    outs = {f"out{k}": whole_out((T, width + LANES), BF16) for k in range(SLOTS)}
    outs.update(
        stats=whole_out((2, 8, ROWS), F32),
        normed=whole_out((ROWS, width), BF16),
        proj=by_step_out((STEPS, ROWS, 2 * WIDE), F32, (1, ROWS, 2 * WIDE)),
        y=by_step_out((STEPS, ROWS, WIDE), F32, (1, ROWS, WIDE)),
        pbc=whole_out((ROWS, 384), F32),
    )
    scratch = dict(
        scores=((SLOTS, T, T), F32),
        run_col=((2 * PAIRS, ROWS, LANES), F32),
        run_row=((SLOTS, T, LANES), F32),
        step_wide=((PAIRS, ROWS, LANES), F32),
        u_all=((STEPS, ROWS, WIDE), BF16),
        square=((ROWS, LANES), F32),
        cross=((ROWS, LANES), F32),
        x_all=((SLOTS, T, width), BF16),
        sems=pltpu.SemaphoreType.DMA((2 * SLOTS + 4,)),
    )
    weight_scratch(scratch, ("ws", "wg", "wv", "wo"), width)
    if with_grad:
        scratch["g_all"] = ((ROWS, width), BF16)
    limit = VMEM_LIMIT if with_grad else VMEM_MOST
    res = kernel_call(body, "layer_forward", ins, outs, scratch, 18, limit)
    return [res[f"out{k}"] for k in range(SLOTS)], res


def head_columns(pair):
    target = 2 * pair + (iota(0) >= HEAD).astype(jnp.int32)
    one = (iota(1) == target).astype(BF16)
    return jnp.concatenate([one, one], axis=0)


def head_sum(v, columns):
    high = v.astype(BF16)
    low = (v - high.astype(F32)).astype(BF16)
    return dot(jnp.concatenate([high, low], axis=1), columns)


def put_by_core(rf, key, x, at, part):
    keep, send = getattr(rf, key + "_keep"), getattr(rf, key + "_send")
    groups = slice(at, at + part.shape[2])
    for c in range(2):

        @pl.when(rf.core[0] == c)
        def _store(c=c):
            for z in range(4):
                keep[x, z, groups] = part[z, c]
                send[x, z, groups] = part[z, 1 - c]


def backward(stages, name, cost_us, saved, layer, have):
    gate, scan, inp, wgate, wscan = (
        s in stages for s in ("gate", "scan", "input", "wgate", "wscan")
    )
    width = saved["normed"].shape[1]
    w, dtw, pv, pbcv, dtp = layer
    elementwise = gate or scan
    fetched = (("wo",) if gate else ()) + (("wg", "wv", "ws") if inp else ())
    in_slots = gate and "rows" not in have

    def body(rf, h):
        copies = Copies(rf.sems) if gate or wgate or inp else None
        if gate or wgate:
            for k in range(SLOTS):
                source = getattr(rf, f"g{k}")
                copies.add(f"g{k}", source.at[:, pl.ds(0, width)], rf.g_all.at[slot(k)])
                if in_slots:
                    copies.add(f"e{k}", source.at[:, pl.ds(width, LANES)], rf.e_all.at[k])
        if copies:
            copies.add_weights(rf, fetched)

        @when(h == 0)
        def _prep():
            if copies:
                copies.start()
            for k in range(SLOTS):
                if gate or wgate:
                    copies.wait(f"g{k}")
                if in_slots:
                    copies.wait(f"e{k}")
                if gate:
                    for row, ref in ((0, rf.scale_row), (1, rf.cross_row)):
                        if "rows" in have:
                            ref[slot(k), :] = jnp.transpose(
                                jnp.broadcast_to(rf.rows[k, row : row + 1, :], (T, LANES))
                            )
                        else:
                            column = from_lanes(rf.e_all[k], row)
                            ref[slot(k), :] = jnp.broadcast_to(column, (T, LANES))
                if scan:
                    inbound, outbound = mixed_bc(rf, k, 0), mixed_bc(rf, k, 1)
                    rf.mixed[0, slot(k), :] = inbound
                    rf.mixed[1, slot(k), :] = outbound
                    rf.scores[k] = dot_nt(inbound, outbound, HI) * tri(False)
                    rf.step_all[slot(k), :] = step_prep(
                        k, rf.pbc, rf.dtp, rf.run_col, rf.run_row, rf.step_wide
                    )
            if scan:
                rf.dscores[...] = jnp.zeros_like(rf.dscores)
                rf.dstep[...] = jnp.zeros_like(rf.dstep)
                rf.drun[...] = jnp.zeros_like(rf.drun)
            if inp:
                rf.total[...] = jnp.zeros_like(rf.total)
            if copies:
                copies.wait(*fetched)

        if gate:
            q_all = dot_nt(rf.g_all[...], half_rows(rf.wo, h))
        for p in range(HALF if elementwise else 0):
            lanes = pair_lanes(p)
            par = rf.pv[:, lanes]
            pair = HALF * h + p
            sums = [jnp.zeros((1, LANES), F32) for _ in range(8)]
            if scan:
                columns = head_columns(pair)
            for k in range(SLOTS):
                taps = conv_taps(rf.proj[0, slot(k), WIDE + p * LANES : WIDE + (p + 1) * LANES])
                cv = conv_sum(taps, par)
                sig_c = sigmoid(cv)
                values = cv * sig_c
                y = rf.y[0, slot(k), lanes]
                if gate:
                    gate_in = rf.proj[0, slot(k), lanes]
                    sig_g = sigmoid(gate_in)
                    silu_g = gate_in * sig_g
                    scanned = y + par[6:7, :] * values
                    gated = scanned * silu_g
                    grad_no = q_all[slot(k), lanes]
                    scale = rf.scale_row[slot(k), :]
                    dgated = scale * (grad_no * par[5:6, :]) - rf.cross_row[slot(k), :] * gated
                    norm = gated * scale
                    sums[5] += column_sum(grad_no * norm)
                    rf.u[slot(k), lanes] = (norm * par[5:6, :]).astype(BF16)
                    dscan = dgated * silu_g
                    dgate = dgated * scanned * (sig_g * (1.0 + gate_in * (1.0 - sig_g)))
                    sums[6] += column_sum(dscan * values)
                    rf.dg[slot(k), lanes] = dgate.astype(BF16)
                    if not scan:
                        rf.dscan[slot(k), lanes] = dscan
                else:
                    dscan = rf.dscan[slot(k), lanes]
                if not scan:
                    continue
                wide = rf.step_wide[pair, slot(k), :]
                dy = dscan.astype(BF16)
                scaled = (values * wide).astype(BF16)
                dweights = dot_nt(halves(scaled), dy)
                weights = []
                dscore = rf.dscores[k]
                for a in range(2):
                    gap = (
                        rf.run_row[k, pl.ds(2 * pair + a, 1), :]
                        - rf.run_col[2 * pair + a, slot(k), :]
                    )
                    decay = jnp.exp(jnp.minimum(gap, 0.0))
                    weights.append((rf.scores[k] * decay).astype(BF16))
                    dscore = dscore + dweights[slot(a), :] * decay
                rf.dscores[k] = dscore
                dscaled = dot(jnp.concatenate(weights, axis=1), halves(dy))
                rf.dstep[slot(k), :] += head_sum(dscaled * values, columns)
                rf.drun[slot(k), :] += head_sum(
                    dy.astype(F32) * y - scaled.astype(F32) * dscaled, columns
                )
                dvalues = dscaled * wide + par[6:7, :] * dscan
                dcv = dvalues * (sig_c * (1.0 + cv * (1.0 - sig_c)))
                for t in range(4):
                    sums[t] += column_sum(dcv * taps[t])
                sums[4] += column_sum(dcv)
                rf.dv[slot(k), lanes] = conv_back(dcv, par).astype(BF16)
            rf.small[p] = jnp.concatenate(sums, axis=0)
        if wgate and wscan:
            for at, left, right in (
                (0, rf.dg, rf.normed),
                (3, rf.u, rf.g_all),
                (6, rf.dv, rf.normed),
            ):
                part = dot_tn(left[...], right[...]).astype(BF16)
                rf.ga[:, at : at + 3] = part.reshape(8, 3, 16, width)
            part = dot_tn(rf.dbc_half[...], rf.normed[...]).astype(BF16)
            rf.ga[:, 9] = part.reshape(8, 16, width)
        elif wgate:
            for at, left, right in ((0, rf.dg, rf.normed), (3, rf.u, rf.g_all)):
                part = dot_tn(left[...], right[...]).astype(BF16)
                put_by_core(rf, "ga", h, at, part.reshape(4, 2, 3, 16, width))
        elif wscan:
            part = dot_tn(rf.dv[...], rf.normed[...]).astype(BF16)
            put_by_core(rf, "gb", h, 0, part.reshape(4, 2, 3, 16, width))
        if inp:
            rf.total[...] += dot(rf.dg[...], half_rows(rf.wg, h)) + dot(
                rf.dv[...], half_rows(rf.wv, h)
            )

        @when(h == STEPS - 1)
        def _finish():
            if scan:
                sums = [[jnp.zeros((1, LANES), F32) for _ in range(8)] for _ in range(2)]
                dt_sums = [jnp.zeros((1, LANES), F32) for _ in range(8)]
                live = iota(1) < 2 * PAIRS
                for k in range(SLOTS):
                    dscore = rf.dscores[k] * tri(False)
                    dmixed = (
                        jnp.dot(
                            dscore,
                            rf.mixed[1, slot(k), :],
                            precision=HI,
                            preferred_element_type=F32,
                        ),
                        dot_tn(dscore, rf.mixed[0, slot(k), :], HI),
                    )
                    for c in range(2):
                        lanes = slice(c * LANES, (c + 1) * LANES)
                        par = rf.pbcv[:, lanes]
                        taps = conv_taps(rf.pbc[slot(k), lanes])
                        cv = conv_sum(taps, par)
                        sig = sigmoid(cv)
                        dcv = dmixed[c] * (sig * (1.0 + cv * (1.0 - sig)))
                        for t in range(4):
                            sums[c][t] += column_sum(dcv * taps[t])
                        sums[c][4] += column_sum(dcv)
                        rf.dbc[slot(k), lanes] = conv_back(dcv, par).astype(BF16)
                    dlog = jnp.dot(
                        tri(False), rf.drun[slot(k), :], precision=HI, preferred_element_type=F32
                    )
                    grad_step = rf.dstep[slot(k), :] + dlog * rf.dtp[1:2, :]
                    dt_sums[1] += column_sum(dlog * rf.step_all[slot(k), :])
                    draw = grad_step * sigmoid(rf.pbc[slot(k), 256:384] + rf.dtp[0:1, :])
                    draw = jnp.where(live, draw, 0.0)
                    dt_sums[0] += column_sum(draw)
                    rf.dbc[slot(k), 256:384] = draw.astype(BF16)
                rf.small_bc[0] = jnp.concatenate(sums[0], axis=0)
                rf.small_bc[1] = jnp.concatenate(sums[1], axis=0)
                dt_sums[1] = dt_sums[1] * rf.dtp[1:2, :]
                rf.small_dt[...] = jnp.concatenate(dt_sums, axis=0)
            if wscan and not wgate:
                part = dot_tn(rf.dbc[:, 0:256], rf.normed[...]).astype(BF16)
                part = part.reshape(2, 4, 2, 1, 16, width)
                for a in range(2):
                    put_by_core(rf, "gb", a, 3, part[a])
            if wscan:
                rf.gdt[...] = dot_tn(rf.dbc[:, 256:384], rf.normed[...])[0:16]
            if inp:
                final = (
                    rf.total[...]
                    + dot(rf.dbc[:, 0:256], flat_rows(rf.ws))
                    + dot(rf.dbc[:, 256:384], rf.dtw[...])
                )
                for k in range(SLOTS):
                    getattr(rf, f"out{k}")[...] = final[slot(k), :].astype(BF16)

    ins, outs, scratch = {}, {}, {}
    heads_cols = STEPS * WIDE
    if gate or wgate:
        for k, v in enumerate(have["g"]):
            ins[f"g{k}"] = in_hbm(v)
        scratch["g_all"] = ((ROWS, width), BF16)
    if gate:
        if in_slots:
            scratch["e_all"] = ((SLOTS, T, LANES), BF16)
        else:
            ins["rows"] = whole(have["rows"])
        scratch["scale_row"] = ((ROWS, LANES), F32)
        scratch["cross_row"] = ((ROWS, LANES), F32)
        outs["u"] = lanes_by_step_out((ROWS, heads_cols), BF16)
        outs["dg"] = lanes_by_step_out((ROWS, heads_cols), BF16)
        if not scan:
            outs["dscan"] = lanes_by_step_out((ROWS, heads_cols), F32)
    if elementwise:
        ins["proj"] = by_step(saved["proj"], (1, ROWS, 2 * WIDE))
        ins["y"] = by_step(saved["y"], (1, ROWS, WIDE))
        ins["pv"] = lanes_by_step(pv)
        outs["small"] = by_step_out((PAIRS, 8, LANES), F32, (HALF, 8, LANES))
    if scan:
        ins["pbc"] = whole(saved["pbc"])
        ins["pbcv"] = whole(pbcv)
        ins["dtp"] = whole(dtp)
        if not gate:
            ins["dscan"] = lanes_by_step(have["dscan"])
        outs["dv"] = lanes_by_step_out((ROWS, heads_cols), BF16)
        outs["dbc"] = whole_out((ROWS, 384), BF16)
        outs["small_bc"] = whole_out((2, 8, LANES), F32)
        outs["small_dt"] = whole_out((8, LANES), F32)
        scratch.update(
            mixed=((2, ROWS, LANES), F32),
            scores=((SLOTS, T, T), F32),
            run_col=((2 * PAIRS, ROWS, LANES), F32),
            run_row=((SLOTS, T, LANES), F32),
            step_wide=((PAIRS, ROWS, LANES), F32),
            step_all=((ROWS, LANES), F32),
            dscores=((SLOTS, T, T), F32),
            dstep=((ROWS, LANES), F32),
            drun=((ROWS, LANES), F32),
        )
    if inp:
        ins["dtw"] = whole(dtw)
        scratch["total"] = ((ROWS, width), F32)
        outs.update({f"out{k}": whole_out((T, width), BF16) for k in range(SLOTS)})
    if fetched:
        ins["w"] = in_hbm(w)
        weight_scratch(scratch, fetched, width)
    if gate or wgate or inp:
        scratch["sems"] = pltpu.SemaphoreType.DMA((2 * SLOTS + 4,))
    if wgate or wscan:
        ins["normed"] = whole(saved["normed"])
    if not gate and (wgate or inp):
        ins["dg"] = lanes_by_step(have["dg"])
    if wgate and not gate:
        ins["u"] = lanes_by_step(have["u"])
    if not scan and (wscan or inp):
        ins["dv"] = lanes_by_step(have["dv"])
        ins["dbc"] = whole(have["dbc"])
    if wgate and wscan:
        ins["dbc_half"] = (have["dbc"], (ROWS, LANES), lambda h: (0, h))
        outs["ga"] = by_step_out((16, 10, 16, width), BF16, (8, 10, 16, width))
    elif wgate or wscan:
        ins["core"] = have["core"]
        key, groups = ("ga", 6) if wgate else ("gb", 4)
        for end in ("_keep", "_send"):
            outs[key + end] = whole_out((2, 4, groups, 16, width), BF16)
    if wscan:
        outs["gdt"] = whole_out((16, width), F32)
    return kernel_call(body, name, ins, outs, scratch, cost_us)


def assemble(parts, dt_rows, shard):
    quarter = parts.shape[2]
    block = 16 * 48
    total = 8 * block + 16 * 16 + dt_rows.shape[0]

    def body(_, inw, outw, shared, dt, grad_in, grad_out):
        i = pl.program_id(0)

        @pl.when(i < 8)
        def _columns():
            grad_in[...] = inw[...].reshape(block, quarter).astype(F32)

        @pl.when(i < SLOTS)
        def _out():
            grad_out[...] = outw[...].reshape(block, quarter).astype(F32)

        @pl.when(i == 8)
        def _shared():
            grad_in[...] = jnp.zeros_like(grad_in)
            grad_in[0:256, :] = shared[...].reshape(256, quarter).astype(F32)
            grad_in[256 : 256 + dt_rows.shape[0], :] = dt[...]

    last = SLOTS - 1
    spec = pltpu.PrefetchScalarGridSpec(
        num_scalar_prefetch=1,
        grid=(9,),
        in_specs=[
            pl.BlockSpec(
                (16, 48, quarter),
                lambda i, j: (0, jnp.where(i < SLOTS, 0, 8) + (j[0] + 3 * SLOTS - i) % SLOTS, 0),
            ),
            pl.BlockSpec((16, 48, quarter), lambda i, j: (0, SLOTS + jnp.minimum(i, last), 0)),
            pl.BlockSpec((16, 16, quarter), lambda i, j: (0, 36, 0)),
            pl.BlockSpec(dt_rows.shape, lambda i, j: (0, 0)),
        ],
        out_specs=[
            pl.BlockSpec((block, quarter), lambda i, j: (i, 0)),
            pl.BlockSpec((block, quarter), lambda i, j: (0, jnp.minimum(i, last))),
        ],
    )
    return pl.pallas_call(
        body,
        grid_spec=spec,
        out_shape=[
            jax.ShapeDtypeStruct((total, quarter), F32),
            jax.ShapeDtypeStruct((block, SLOTS * quarter), F32),
        ],
        compiler_params=pltpu.CompilerParams(vmem_limit_bytes=VMEM_MOST),
        name="assemble",
    )(shard.astype(jnp.int32)[None], parts, parts, parts, dt_rows)


def ring(n, k):
    return [(i, (i + k) % n) for i in range(n)]


def send_shard(v, k):
    return lax.ppermute(v, "shard", ring(SLOTS, k)) if k else v


def send_across(v, k):
    pairs = [
        (sec * SLOTS + y, (1 - sec) * SLOTS + (y + k) % SLOTS)
        for sec in range(2)
        for y in range(SLOTS)
    ]
    return lax.ppermute(v, ("section", "shard"), pairs)


def swap_section(v):
    return lax.ppermute(v, "section", [(0, 1), (1, 0)])


def dp_index(x, z, c):
    return x * 8 + z * 2 + c


def dp_pairs(move):
    pairs = []
    for x in range(2):
        for z in range(4):
            for c in range(2):
                pairs.append((dp_index(x, z, c), dp_index(*move(x, z, c))))
    return pairs


def pick(v, index, axis):
    return lax.dynamic_index_in_dim(v, index, axis, keepdims=False)


def gather_slots(v):
    return [send_shard(v, (-k) % SLOTS) for k in range(SLOTS)]


def scatter_sum(slots):
    parts = [send_shard(slots[k], k) for k in range(SLOTS)]
    return sum(p.astype(F32) for p in parts)


def cross_core(v):
    return lax.ppermute(v, DP, dp_pairs(lambda x, z, c: (x, z, 1 - c)))


def sum_small(v):
    v = v + lax.ppermute(v, DP, dp_pairs(lambda x, z, c: (x, z, 1 - c)))
    v = v + sum(
        lax.ppermute(v, DP, dp_pairs(lambda x, z, c: (x, (z + k) % 4, c))) for k in range(1, 4)
    )
    return v + lax.ppermute(v, DP, dp_pairs(lambda x, z, c: (1 - x, z, c)))


def in_order(parts, sign):
    j = lax.axis_index("shard")
    stacked = jnp.stack(parts)
    return jnp.take(stacked, (sign * (jnp.arange(SLOTS) - j)) % SLOTS, axis=0)


def shards(
    tokens,
    cotangent,
    lengths,
    norm_gain,
    in_weight,
    conv_weight,
    conv_bias,
    dt_bias,
    a_log,
    d_skip,
    gate_gain,
    out_weight,
):
    sec = lax.axis_index("section")
    d = lax.axis_index(DP)
    j = lax.axis_index("shard")
    core = d % 2
    first = sec == 0
    width = tokens.shape[2]
    quarter = norm_gain.shape[1]
    channels = conv_bias.shape[1]
    own_cols = gate_gain.shape[1]
    inner = own_cols * SLOTS
    heads = dt_bias.shape[1]
    own_heads = heads // SLOTS
    n_state = 2 * LANES
    piece = own_cols // 16
    piece_bc = n_state // 16
    own_core = (core.astype(jnp.int32)[None], pltpu.SMEM)

    x_own = pick(tokens, sec, 0)
    cot = pick(cotangent, sec, 0)
    length = pick(lengths, sec, 0)
    mask = (jnp.arange(T, dtype=jnp.int32) < length).astype(F32)[:, None]

    columns = jnp.transpose(in_weight[0])
    with jax.named_scope("weights"):

        def cut(start, rows):
            return lax.dynamic_slice(columns, (start, 0), (rows, quarter))

        def columns_of(to):
            return jnp.concatenate(
                [
                    cut(own_cols * to + piece * d, piece),
                    cut(inner + own_cols * to + piece * d, piece),
                    cut(2 * inner + piece_bc * d, piece_bc),
                ],
                axis=0,
            )

        cuts = [columns_of((j + k) % SLOTS) for k in range(SLOTS)]
        o_own = lax.dynamic_slice(out_weight[0], (piece * d, 0), (piece, width))
        o_other = swap_section(o_own)

        w_own = [send_shard(cuts[k], k) for k in range(SLOTS)]
        w_other = [send_across(cuts[k], k) for k in range(SLOTS)]

        def from_parts(parts, others, o, o_others, own):
            pieces = [jnp.where(own, p, q) for p, q in zip(parts, others)]
            lanes = []
            for y in range(SLOTS):
                v = pieces[0]
                for k in range(1, SLOTS):
                    v = jnp.where((j - y) % SLOTS == k, pieces[k], v)
                lanes.append(v)
            return jnp.concatenate(
                [jnp.where(own, o, o_others), jnp.concatenate(lanes, axis=1)], axis=0
            )

        w0 = from_parts(w_own, w_other, o_own, o_other, first)
        w1 = from_parts(w_own, w_other, o_own, o_other, ~first)
        w0, w1, x_own, cot = lax.optimization_barrier((w0, w1, x_own, cot))
        w0 = lax.all_gather(w0, DP, axis=0, tiled=False)
        x_slots = gather_slots(x_own)
        x_slots, norm_gain = lax.optimization_barrier((x_slots, norm_gain))

    with jax.named_scope("small_weights"):
        dt_columns = columns[2 * inner + n_state :]
        sizes = [quarter, 4 * channels, channels, own_cols, heads, heads, heads, heads * quarter]
        flat = jnp.concatenate(
            [
                norm_gain[0],
                conv_weight[0].reshape(-1),
                conv_bias[0],
                gate_gain[0],
                dt_bias[0],
                a_log[0],
                d_skip[0],
                dt_columns.reshape(-1),
            ]
        )
        flat = jnp.pad(flat, (0, -flat.shape[0] % LANES)).reshape(-1, LANES)
        own = in_order(gather_slots(flat), 1)
        other = swap_section(own)
        small = [jnp.where(first, own, other), jnp.where(first, other, own)]

        def unpack(v):
            low = v.reshape(SLOTS, -1)
            at = sum(sizes[:-1])
            dtw = low[:, at : at + sizes[-1]].reshape(SLOTS, heads, quarter)
            dtw = lax.dynamic_slice(dtw, (0, own_heads * j, 0), (SLOTS, own_heads, quarter))
            dtw = jnp.transpose(dtw, (1, 0, 2)).reshape(own_heads, width)
            dtw = jnp.pad(dtw, ((0, LANES - own_heads), (0, 0)))
            v = low[:, :at].astype(F32)
            cut, at = [], 0
            for size in sizes[:-1]:
                cut.append(v[:, at : at + size])
                at += size
            gain = cut[0].reshape(1, width)
            taps = cut[1].reshape(SLOTS, 4, channels).transpose(1, 0, 2).reshape(4, -1)
            bias = cut[2].reshape(1, -1)
            conv = jnp.concatenate([taps, bias, jnp.zeros((3, taps.shape[1]), F32)], axis=0)
            pbcv = conv[:, inner:]
            pv = lax.dynamic_slice(conv, (0, own_cols * j), (8, own_cols))
            pick_heads = lambda u: lax.dynamic_slice(u[0], (own_heads * j,), (own_heads,))
            wide = jnp.repeat(pick_heads(cut[6]), HEAD)[None]
            pv = jnp.concatenate([pv[:5], pick(cut[3], j, 0)[None], wide, pv[7:]], axis=0)
            dtp = jnp.stack([pick_heads(cut[4]), -jnp.exp(pick_heads(cut[5]))])
            dtp = jnp.pad(dtp, ((0, 6), (0, LANES - own_heads)))
            return gain, dtw, pv, pbcv, dtp

        gain0, *params0 = unpack(small[0])
        gain1, *params1 = unpack(small[1])

    x_f = x_own.astype(F32)
    g1 = (mask * cot.astype(F32)).astype(BF16)
    g1_slots = gather_slots(g1)
    w0, x_slots, g1_slots, gain0, params0, gain1, params1, w1 = lax.optimization_barrier(
        (w0, x_slots, g1_slots, gain0, params0, gain1, params1, w1)
    )
    w1 = lax.all_gather(w1, DP, axis=0, tiled=False)
    blocks = lambda v: v.reshape(16, 10, 16, width)

    layer0 = (blocks(w0), *params0)
    layer1 = (blocks(w1), *params1)

    def forward_layer(x, g, gain, layer):
        w, dtw, pv, pbcv, dtp = layer
        return forward(x, g, w, dtw, gain, pv, pbcv, dtp)

    parts, saved0 = forward_layer(x_slots, None, gain0, layer0)
    branch = scatter_sum(parts)
    square = jnp.sum(branch[:, width : width + 3], axis=1, keepdims=True)
    scale0 = lax.rsqrt(square / inner + EPS)
    branch0 = branch[:, :width] * scale0
    middle = (x_f + mask * branch0).astype(BF16)

    m_slots = gather_slots(middle)
    branch_parts, saved1 = forward_layer(m_slots, g1_slots, gain1, layer1)
    own = saved1["stats"][:, 0].reshape(2, SLOTS, T)
    back = [send_shard(own, k) for k in range(SLOTS)]
    summed = sum(jnp.roll(back[k], -k, axis=1) for k in range(SLOTS))
    scale1 = lax.rsqrt(summed[0] / inner + EPS)
    cross1 = scale1 * scale1 * scale1 * summed[1] / inner
    rows1 = jnp.pad(jnp.stack([scale1, cross1], axis=1), ((0, 0), (0, 6), (0, 0)))

    def norm_back(x, gain, grad):
        scale = lax.rsqrt(jnp.mean(x * x, axis=1, keepdims=True) + EPS)
        unit = x * scale
        dn = grad * gain
        dx = scale * (dn - unit * jnp.mean(dn * unit, axis=1, keepdims=True))
        return dx, jnp.sum(grad * unit, axis=0)

    back1 = backward(
        ("gate", "scan", "input"),
        "backward_1",
        28,
        saved1,
        layer1,
        {"g": g1_slots, "rows": rows1},
    )
    moved = [send_shard(back1[f"out{k}"], k) for k in range(SLOTS)]
    grads1 = backward(
        ("wgate", "wscan"), "weight_grads_1", 8, saved1, layer1, {"g": g1_slots, **back1}
    )
    back1.update(grads1)
    moved, back1["ga"] = lax.optimization_barrier((moved, back1["ga"]))
    dx, gain_grad1 = norm_back(middle.astype(F32), gain1, sum(p.astype(F32) for p in moved))
    by_owner = lambda v: v.reshape(16, -1, width)
    owned1 = lax.psum_scatter(by_owner(back1["ga"]), DP, scatter_dimension=0, tiled=False)

    dmiddle = (cot.astype(F32) + dx).astype(BF16)
    g0 = (mask * dmiddle.astype(F32)).astype(BF16)
    cross0 = scale0 * scale0 * jnp.sum(g0.astype(F32) * branch0, axis=1, keepdims=True) / inner
    g0_slots = gather_slots(jnp.concatenate([g0, in_lanes([scale0, cross0])], axis=1))
    g0_slots, branch_parts = lax.optimization_barrier((g0_slots, branch_parts))
    branch = scatter_sum(branch_parts)[:, :width] * scale1[0][:, None]
    result = middle.astype(F32) + mask * branch

    back0 = backward(
        ("gate", "wgate"),
        "backward_0_gate",
        14,
        saved0,
        layer0,
        {"g": g0_slots, "core": own_core},
    )
    both = lambda kept, moved: (kept.astype(F32) + moved.astype(F32)).astype(BF16)
    a_moved = cross_core(back0["ga_send"])
    small_gate = back0["small"]
    back0["core"] = own_core
    back0.update(backward(("scan", "wscan"), "backward_0_scan", 20, saved0, layer0, back0))
    gb_send, a_moved = lax.optimization_barrier((back0["gb_send"], a_moved))
    a0 = both(back0["ga_keep"], a_moved)
    b0 = both(back0["gb_keep"], cross_core(gb_send))
    owned0 = jnp.pad(a0, ((0, 0), (0, 0), (0, 4), (0, 0), (0, 0)))
    owned0 = lax.dynamic_update_slice(owned0, b0, (0, 0, 6, 0, 0)).reshape(8, -1, width)
    owned0 = lax.psum_scatter(owned0, ("x", "z"), scatter_dimension=0, tiled=False)
    small_scan = back0["small"]
    back0.update(backward(("input",), "backward_0_input", 9, saved0, layer0, back0))
    moved0 = [send_shard(back0[f"out{k}"], k) for k in range(SLOTS)]
    dx, gain_grad0 = norm_back(x_f, gain0, sum(p.astype(F32) for p in moved0))
    dtokens = dmiddle.astype(F32) + dx
    owned1 = owned1 + lax.ppermute(owned1, "section", [(0, 1)])
    owned0, owned1, gain_grad0, dtokens, result = lax.optimization_barrier(
        (owned0, owned1, gain_grad0, dtokens, result)
    )

    kept = jnp.where(first, owned0, owned1).reshape(10, 16, width)
    arrived = lax.ppermute(owned0, "section", [(1, 0)]).reshape(10, 16, width)

    def total_of(cut):
        return (cut(kept).astype(F32) + cut(arrived).astype(F32)).astype(BF16)

    row_slots = []
    for k in range(SLOTS):

        def cut(v):
            v = lax.dynamic_slice_in_dim(v, quarter * ((j + k) % SLOTS), quarter, 2)
            return jnp.concatenate([v[:3], v[6:]], axis=0)

        row_slots.append(send_shard(total_of(cut).reshape(-1, quarter), k))
    out_rows = total_of(lambda v: v[3:6])
    out_rows = jnp.transpose(out_rows.reshape(piece, SLOTS, quarter), (1, 0, 2))
    result_moved = lax.ppermute(result.astype(BF16), "section", [(0, 1)]).astype(F32)
    dtokens_moved = lax.ppermute(dtokens.astype(BF16), "section", [(1, 0)]).astype(F32)
    ends = jnp.where(
        first, jnp.stack([dtokens, dtokens_moved]), jnp.stack([result_moved, result])
    )[None]

    def to_section(v0, v1):
        kept = jnp.where(first, v0, v1).astype(F32)
        return kept + swap_section(jnp.where(first, v1, v0)).astype(F32)

    shared = sum(v[2 * piece :].astype(F32) for v in row_slots).astype(BF16)
    gathered = lax.all_gather(
        jnp.concatenate(
            [v[:piece] for v in row_slots]
            + [out_rows.reshape(-1, quarter)]
            + [v[piece : 2 * piece] for v in row_slots]
            + [shared],
            axis=0,
        ),
        DP,
        tiled=False,
    )

    def small_of(by_pair, back, gain_grad):
        return jnp.concatenate(
            [
                by_pair.reshape(-1, LANES),
                back["small_bc"].reshape(-1, LANES),
                back["small_dt"],
                gain_grad.reshape(-1, LANES),
                back["gdt"].reshape(-1, LANES),
            ],
            axis=0,
        )

    small0 = small_of(small_gate + small_scan, back0, gain_grad0)
    small1 = small_of(back1["small"], back1, gain_grad1)
    small_sum = sum_small(to_section(small0, small1))
    everyone = in_order(gather_slots(small_sum), 1)
    n_pair, n_bc = PAIRS * 8, 2 * 8
    by_pair = everyone[:, :n_pair].reshape(SLOTS, PAIRS, 8, LANES)
    by_pair = by_pair.transpose(2, 0, 1, 3).reshape(8, inner)
    by_bc = jnp.sum(everyone[:, n_pair : n_pair + n_bc], axis=0)
    by_bc = by_bc.reshape(2, 8, LANES).transpose(1, 0, 2).reshape(8, n_state)
    at = n_pair + n_bc
    by_dt = everyone[:, at : at + 8, :own_heads].transpose(1, 0, 2).reshape(8, heads)
    at += 8
    gain_total = jnp.sum(everyone[:, at : at + width // LANES], axis=0).reshape(-1)
    at += width // LANES
    dt_rows = everyone[:, at:].reshape(SLOTS, 16, SLOTS, quarter)[:, :own_heads]
    dt_rows = pick(dt_rows, j, 2).reshape(heads, quarter)
    conv_total = jnp.concatenate([by_pair[:5], by_bc[:5]], axis=1)
    conv_own = lax.dynamic_slice(conv_total, (0, channels * j), (5, channels))
    grad_skip = jnp.sum(by_pair[6].reshape(heads, HEAD), axis=1)

    grad_in_weight, grad_out_weight = assemble(gathered, dt_rows, j)
    return (
        ends,
        lax.dynamic_slice(gain_total, (quarter * j,), (quarter,))[None],
        jnp.transpose(grad_in_weight)[None],
        conv_own[None, :4],
        conv_own[4][None],
        by_dt[0][None],
        by_dt[1][None],
        grad_skip[None],
        lax.dynamic_slice(by_pair[5], (own_cols * j,), (own_cols,))[None],
        grad_out_weight[None],
    )


def solution(mesh):
    sections, copies, owners = mesh.devices.shape
    fine = jax.sharding.Mesh(
        mesh.devices.reshape(sections, 2, copies // 4, 2, owners), ("section", *DP, "shard")
    )
    return jax.shard_map(
        shards,
        mesh=fine,
        in_specs=(
            P((*DP, "shard"), None, None),
            P((*DP, "shard"), None, None),
            P((*DP, "shard")),
            P("section", "shard"),
            P("section", "shard", None),
            P("section", None, "shard"),
            P("section", "shard"),
            P("section", None),
            P("section", None),
            P("section", None),
            P("section", "shard"),
            P("section", "shard", None),
        ),
        out_specs=(
            P("section", (*DP, "shard"), None, None),
            P("section", "shard"),
            P("section", "shard", None),
            P("section", None, "shard"),
            P("section", "shard"),
            P("section", None),
            P("section", None),
            P("section", None),
            P("section", "shard"),
            P("section", "shard", None),
        ),
        check_vma=False,
    )
```

```python
import jax
import jax.numpy as jnp
from jax import lax
from jax.experimental import pallas as pl
from jax.experimental.pallas import tpu as pltpu
from jax.sharding import PartitionSpec as P

F32 = jnp.float32
BF16 = jnp.bfloat16
HI = lax.Precision.HIGHEST
EPS = 1e-05
T = 128
LANES = 128
HEAD = 64
SLOTS = 4
ROWS = SLOTS * T
PAIRS = 6
STEPS = 2
HALF = PAIRS // STEPS
WIDE = HALF * LANES
VMEM_LIMIT = 34 * 1024 * 1024
VMEM_MOST = 60 * 1024 * 1024
VMEM_BACK = 56 * 1024 * 1024
DP = ("x", "z", "core")


def sigmoid(v):
    return 0.5 * jnp.tanh(0.5 * v) + 0.5


def softplus(v):
    return jnp.maximum(v, 0.0) + jnp.log1p(jnp.exp(-jnp.abs(v)))


def dot(a, b):
    return jnp.dot(a, b, preferred_element_type=F32)


def dot_nt(a, b, precision=None):
    return lax.dot_general(
        a, b, (((1,), (1,)), ((), ())), preferred_element_type=F32, precision=precision
    )


def dot_tn(a, b, precision=None):
    return lax.dot_general(
        a, b, (((0,), (0,)), ((), ())), preferred_element_type=F32, precision=precision
    )


def iota(axis):
    return lax.broadcasted_iota(jnp.int32, (T, LANES), axis)


def shift_down(v, steps):
    return jnp.where(iota(0) >= steps, pltpu.roll(v, steps, 0), 0.0)


def shift_up(v, steps):
    return jnp.where(iota(0) < T - steps, pltpu.roll(v, T - steps, 0), 0.0)


def conv_taps(cin):
    return [shift_down(cin, 3), shift_down(cin, 2), shift_down(cin, 1), cin]


def conv_sum(taps, par):
    total = par[4:5, :] + taps[0] * par[0:1, :]
    for k in range(1, 4):
        total = total + taps[k] * par[k : k + 1, :]
    return total


def conv_back(dcv, par):
    total = dcv * par[3:4, :]
    for m in range(1, 4):
        total = total + shift_up(dcv, m) * par[3 - m : 4 - m, :]
    return total


def column_sum(v):
    return jnp.sum(v, axis=0, keepdims=True)


def slot(k):
    return slice(k * T, (k + 1) * T)


def tri(lower):
    if lower:
        return (iota(0) >= iota(1)).astype(F32)
    return (iota(0) <= iota(1)).astype(F32)


def step_prep(k, pbc, dtp, run_col, run_row, step_wide):
    step = softplus(pbc[slot(k), 256:384] + dtp[0:1, :])
    run = jnp.dot(tri(True), step * dtp[1:2, :], precision=HI, preferred_element_type=F32)
    run_row[k] = jnp.transpose(run)
    left = iota(1) < HEAD
    for p in range(PAIRS):
        a, b = 2 * p, 2 * p + 1
        run_col[a, slot(k), :] = jnp.broadcast_to(run[:, a : a + 1], (T, LANES))
        run_col[b, slot(k), :] = jnp.broadcast_to(run[:, b : b + 1], (T, LANES))
        step_wide[p, slot(k), :] = jnp.where(
            left,
            jnp.broadcast_to(step[:, a : a + 1], (T, LANES)),
            jnp.broadcast_to(step[:, b : b + 1], (T, LANES)),
        )
    return step


def halves(v):
    left = iota(1) < HEAD
    zero = jnp.zeros_like(v)
    return jnp.concatenate([jnp.where(left, v, zero), jnp.where(left, zero, v)], axis=0)


def in_lanes(columns):
    lane = lax.broadcasted_iota(jnp.int32, (columns[0].shape[0], LANES), 1)
    out = jnp.zeros(lane.shape, F32)
    for n, v in enumerate(columns):
        for k in range(3):
            part = v.astype(BF16).astype(F32)
            out = jnp.where(lane == 3 * n + k, part, out)
            v = v - part
    return out.astype(BF16)


def from_lanes(v, n):
    return sum(v[:, 3 * n + k : 3 * n + k + 1].astype(F32) for k in range(3))


class Refs:
    pass


def kernel_call(body, name, ins, outs, scratch, cost_us, limit=VMEM_LIMIT):
    in_names, out_names, scratch_names = list(ins), list(outs), list(scratch)

    def run(*refs):
        for h in range(STEPS):
            rf = Refs()
            for key, ref in zip(in_names + out_names + scratch_names, refs):
                spec = ins.get(key) or outs.get(key)
                blocks = spec[-2:] if spec and len(spec) > 2 else None
                if blocks and blocks[1](1) != blocks[1](0):
                    at = [
                        slice(n * size, (n + 1) * size) if n else slice(0, size)
                        for n, size in zip(blocks[1](h), blocks[0])
                    ]
                    setattr(rf, key + "_whole", ref)
                    ref = ref.at[tuple(at)]
                setattr(rf, key, ref)
            body(rf, h)

    res = pl.pallas_call(
        run,
        in_specs=[
            pl.BlockSpec(memory_space=pltpu.VMEM if len(ins[n]) > 2 else ins[n][1])
            for n in in_names
        ],
        out_specs=[pl.BlockSpec(memory_space=pltpu.VMEM) for n in out_names],
        out_shape=[jax.ShapeDtypeStruct(outs[n][0], outs[n][1]) for n in out_names],
        scratch_shapes=[
            pltpu.VMEM(*scratch[n]) if isinstance(scratch[n], tuple) else scratch[n]
            for n in scratch_names
        ],
        compiler_params=pltpu.CompilerParams(vmem_limit_bytes=limit),
        cost_estimate=pl.CostEstimate(
            flops=int(cost_us * 1.1e9), bytes_accessed=1 << 20, transcendentals=0
        ),
        name=name,
    )(*[ins[n][0] for n in in_names])
    return dict(zip(out_names, res))


def when(condition):
    return (lambda f: f()) if condition else (lambda f: None)


def whole(v):
    return (v, v.shape, lambda h: (0,) * v.ndim)


def whole_out(shape, dtype):
    return (shape, dtype, shape, lambda h: (0,) * len(shape))


def by_step(v, block):
    return (v, block, lambda h: (h,) + (0,) * (len(block) - 1))


def by_step_out(shape, dtype, block):
    return (shape, dtype, block, lambda h: (h,) + (0,) * (len(block) - 1))


def lanes_by_step(v):
    return (v, (v.shape[0], WIDE), lambda h: (0, h))


def lanes_by_step_out(shape, dtype):
    return (shape, dtype, (shape[0], WIDE), lambda h: (0, h))


def in_hbm(v):
    return (v, pltpu.HBM)


WEIGHT_GROUPS = {"wo": (0, 3), "wg": (3, 3), "wv": (6, 3), "ws": (9, 1)}


class Copies:
    def __init__(self, sems):
        self.sems, self.copies = sems, {}

    def add(self, key, source, target):
        self.copies[key] = (source, target, self.sems.at[len(self.copies)])

    def add_weights(self, rf, keys):
        for key in keys:
            at, count = WEIGHT_GROUPS[key]
            self.add(key, rf.w.at[:, pl.ds(at, count)], getattr(rf, key))

    def start(self):
        for copy in self.copies.values():
            pltpu.make_async_copy(*copy).start()

    def wait(self, *keys):
        for key in keys:
            pltpu.make_async_copy(*self.copies[key]).wait()


def weight_scratch(scratch, keys, width):
    for key in keys:
        scratch[key] = ((16, WEIGHT_GROUPS[key][1], 16, width), BF16)


def half_rows(ref, h):
    v = ref[pl.ds(8 * h, 8)]
    return v.reshape(WIDE, v.shape[-1])


def pair_lanes(p):
    return slice(p * LANES, (p + 1) * LANES)


def flat_rows(ref):
    v = ref[...]
    return v.reshape(-1, v.shape[-1])


def mixed_bc(rf, k, c):
    lanes = slice(c * LANES, (c + 1) * LANES)
    cv = conv_sum(conv_taps(rf.pbc[slot(k), lanes]), rf.pbcv[:, lanes])
    return cv * sigmoid(cv)


def forward(x_slots, g_slots, w, dtw, gain, pv, pbcv, dtp):
    width = x_slots[0].shape[1]
    with_grad = g_slots is not None

    def body(rf, h):
        copies = Copies(rf.sems)
        for k in range(SLOTS):
            copies.add(f"x{k}", getattr(rf, f"x{k}"), rf.x_all.at[k])
        copies.add_weights(rf, ("ws", "wg", "wv", "wo"))
        if with_grad:
            for k in range(SLOTS):
                copies.add(f"g{k}", getattr(rf, f"g{k}"), rf.g_all.at[slot(k)])

        @when(h == 0)
        def _prep():
            copies.start()
            for k in range(SLOTS):
                copies.wait(f"x{k}")
                x = rf.x_all[k].astype(F32)
                scale = lax.rsqrt(jnp.mean(x * x, axis=1, keepdims=True) + EPS)
                rf.normed[slot(k), :] = (x * scale * rf.gain[...]).astype(BF16)
            copies.wait("ws")
            rf.pbc[:, 0:256] = dot_nt(rf.normed[...], flat_rows(rf.ws))
            rf.pbc[:, 256:384] = dot_nt(rf.normed[...], rf.dtw[...])
            for k in range(SLOTS):
                rf.scores[k] = dot_nt(mixed_bc(rf, k, 1), mixed_bc(rf, k, 0), HI) * tri(True)
                step_prep(k, rf.pbc, rf.dtp, rf.run_col, rf.run_row, rf.step_wide)
            rf.square[...] = jnp.zeros_like(rf.square)
            rf.cross[...] = jnp.zeros_like(rf.cross)
            copies.wait("wg", "wv", "wo")
            if with_grad:
                copies.wait(*[f"g{k}" for k in range(SLOTS)])

        rf.proj[0, :, 0:WIDE] = dot_nt(rf.normed[...], half_rows(rf.wg, h))
        rf.proj[0, :, WIDE : 2 * WIDE] = dot_nt(rf.normed[...], half_rows(rf.wv, h))
        if with_grad:
            q_all = dot_nt(rf.g_all[...], half_rows(rf.wo, h))
        for p in range(HALF):
            lanes = pair_lanes(p)
            par = rf.pv[:, lanes]
            pair = HALF * h + p
            for k in range(SLOTS):
                gate = rf.proj[0, slot(k), lanes]
                cv = conv_sum(
                    conv_taps(rf.proj[0, slot(k), WIDE + p * LANES : WIDE + (p + 1) * LANES]), par
                )
                values = cv * sigmoid(cv)
                scaled = (values * rf.step_wide[pair, slot(k), :]).astype(BF16)
                weights = []
                for a in range(2):
                    gap = (
                        rf.run_col[2 * pair + a, slot(k), :]
                        - rf.run_row[k, pl.ds(2 * pair + a, 1), :]
                    )
                    decay = jnp.exp(jnp.minimum(gap, 0.0))
                    weights.append((rf.scores[k] * decay).astype(BF16))
                y = dot(jnp.concatenate(weights, axis=1), halves(scaled))
                rf.y[0, slot(k), lanes] = y
                scanned = y + par[6:7, :] * values
                gated = scanned * (gate * sigmoid(gate))
                rf.square[slot(k), :] += gated * gated
                scaled_out = gated * par[5:6, :]
                rf.u_all[h, slot(k), lanes] = scaled_out.astype(BF16)
                if with_grad:
                    rf.cross[slot(k), :] += q_all[slot(k), lanes] * scaled_out

        @when(h == STEPS - 1)
        def _finish():
            u = jnp.concatenate([rf.u_all[a] for a in range(STEPS)], axis=1)
            for n in range(0, width, 512):
                part = dot(u, rf.wo[:, :, :, n : n + 512].reshape(STEPS * WIDE, 512)).astype(BF16)
                for k in range(SLOTS):
                    getattr(rf, f"out{k}")[:, n : n + 512] = part[slot(k), :]
            for k in range(SLOTS):
                total = jnp.sum(rf.square[slot(k), :], axis=1, keepdims=True)
                getattr(rf, f"out{k}")[:, width:] = in_lanes([total])
            ones = jnp.ones((8, LANES), F32)
            rf.stats[0] = dot_nt(ones, rf.square[...], HI)
            rf.stats[1] = dot_nt(ones, rf.cross[...], HI)

    ins = {f"x{k}": in_hbm(v) for k, v in enumerate(x_slots)}
    if with_grad:
        ins.update({f"g{k}": in_hbm(v) for k, v in enumerate(g_slots)})
    ins.update(
        gain=whole(gain),
        w=in_hbm(w),
        dtw=whole(dtw),
        pv=lanes_by_step(pv),
        pbcv=whole(pbcv),
        dtp=whole(dtp),
    )
    outs = {f"out{k}": whole_out((T, width + LANES), BF16) for k in range(SLOTS)}
    outs.update(
        stats=whole_out((2, 8, ROWS), F32),
        normed=whole_out((ROWS, width), BF16),
        proj=by_step_out((STEPS, ROWS, 2 * WIDE), F32, (1, ROWS, 2 * WIDE)),
        y=by_step_out((STEPS, ROWS, WIDE), F32, (1, ROWS, WIDE)),
        pbc=whole_out((ROWS, 384), F32),
    )
    scratch = dict(
        scores=((SLOTS, T, T), F32),
        run_col=((2 * PAIRS, ROWS, LANES), F32),
        run_row=((SLOTS, T, LANES), F32),
        step_wide=((PAIRS, ROWS, LANES), F32),
        u_all=((STEPS, ROWS, WIDE), BF16),
        square=((ROWS, LANES), F32),
        cross=((ROWS, LANES), F32),
        x_all=((SLOTS, T, width), BF16),
        sems=pltpu.SemaphoreType.DMA((2 * SLOTS + 4,)),
    )
    weight_scratch(scratch, ("ws", "wg", "wv", "wo"), width)
    if with_grad:
        scratch["g_all"] = ((ROWS, width), BF16)
    res = kernel_call(body, "layer_forward", ins, outs, scratch, 18, VMEM_MOST)
    return [res[f"out{k}"] for k in range(SLOTS)], res


def head_columns(pair):
    target = 2 * pair + (iota(0) >= HEAD).astype(jnp.int32)
    one = (iota(1) == target).astype(BF16)
    return jnp.concatenate([one, one], axis=0)


def head_sum(v, columns):
    high = v.astype(BF16)
    low = (v - high.astype(F32)).astype(BF16)
    return dot(jnp.concatenate([high, low], axis=1), columns)


def put_by_core(rf, key, x, at, part):
    keep, send = getattr(rf, key + "_keep"), getattr(rf, key + "_send")
    groups = slice(at, at + part.shape[2])
    for c in range(2):

        @pl.when(rf.core[0] == c)
        def _store(c=c):
            for z in range(4):
                keep[x, z, groups] = part[z, c]
                send[x, z, groups] = part[z, 1 - c]


def backward(stages, name, cost_us, saved, layer, have, limit=VMEM_LIMIT):
    gate, scan, inp, wgate, wscan = (
        s in stages for s in ("gate", "scan", "input", "wgate", "wscan")
    )
    width = saved["normed"].shape[1]
    w, dtw, pv, pbcv, dtp = layer
    elementwise = gate or scan
    fetched = (("wo",) if gate else ()) + (("wg", "wv", "ws") if inp else ())
    in_slots = gate and "rows" not in have

    def body(rf, h):
        copies = Copies(rf.sems) if gate or wgate or inp else None
        if gate or wgate:
            for k in range(SLOTS):
                source = getattr(rf, f"g{k}")
                copies.add(f"g{k}", source.at[:, pl.ds(0, width)], rf.g_all.at[slot(k)])
                if in_slots:
                    copies.add(f"e{k}", source.at[:, pl.ds(width, LANES)], rf.e_all.at[k])
        if copies:
            copies.add_weights(rf, fetched)

        @when(h == 0)
        def _prep():
            if copies:
                copies.start()
            for k in range(SLOTS):
                if gate or wgate:
                    copies.wait(f"g{k}")
                if in_slots:
                    copies.wait(f"e{k}")
                if gate:
                    for row, ref in ((0, rf.scale_row), (1, rf.cross_row)):
                        if "rows" in have:
                            ref[slot(k), :] = jnp.transpose(
                                jnp.broadcast_to(rf.rows[k, row : row + 1, :], (T, LANES))
                            )
                        else:
                            column = from_lanes(rf.e_all[k], row)
                            ref[slot(k), :] = jnp.broadcast_to(column, (T, LANES))
                if scan:
                    inbound, outbound = mixed_bc(rf, k, 0), mixed_bc(rf, k, 1)
                    rf.mixed[0, slot(k), :] = inbound
                    rf.mixed[1, slot(k), :] = outbound
                    rf.scores[k] = dot_nt(inbound, outbound, HI) * tri(False)
                    rf.step_all[slot(k), :] = step_prep(
                        k, rf.pbc, rf.dtp, rf.run_col, rf.run_row, rf.step_wide
                    )
            if scan:
                rf.dscores[...] = jnp.zeros_like(rf.dscores)
                rf.dstep[...] = jnp.zeros_like(rf.dstep)
                rf.drun[...] = jnp.zeros_like(rf.drun)
            if inp:
                rf.total[...] = jnp.zeros_like(rf.total)
            if copies:
                copies.wait(*fetched)

        if gate:
            q_all = dot_nt(rf.g_all[...], half_rows(rf.wo, h))
        for p in range(HALF if elementwise else 0):
            lanes = pair_lanes(p)
            par = rf.pv[:, lanes]
            pair = HALF * h + p
            sums = [jnp.zeros((1, LANES), F32) for _ in range(8)]
            if scan:
                columns = head_columns(pair)
            for k in range(SLOTS):
                taps = conv_taps(rf.proj[0, slot(k), WIDE + p * LANES : WIDE + (p + 1) * LANES])
                cv = conv_sum(taps, par)
                sig_c = sigmoid(cv)
                values = cv * sig_c
                y = rf.y[0, slot(k), lanes]
                if gate:
                    gate_in = rf.proj[0, slot(k), lanes]
                    sig_g = sigmoid(gate_in)
                    silu_g = gate_in * sig_g
                    scanned = y + par[6:7, :] * values
                    gated = scanned * silu_g
                    grad_no = q_all[slot(k), lanes]
                    scale = rf.scale_row[slot(k), :]
                    dgated = scale * (grad_no * par[5:6, :]) - rf.cross_row[slot(k), :] * gated
                    norm = gated * scale
                    sums[5] += column_sum(grad_no * norm)
                    rf.u[slot(k), lanes] = (norm * par[5:6, :]).astype(BF16)
                    dscan = dgated * silu_g
                    dgate = dgated * scanned * (sig_g * (1.0 + gate_in * (1.0 - sig_g)))
                    sums[6] += column_sum(dscan * values)
                    rf.dg[slot(k), lanes] = dgate.astype(BF16)
                    if not scan:
                        rf.dscan[slot(k), lanes] = dscan
                else:
                    dscan = rf.dscan[slot(k), lanes]
                if not scan:
                    continue
                wide = rf.step_wide[pair, slot(k), :]
                dy = dscan.astype(BF16)
                scaled = (values * wide).astype(BF16)
                dweights = dot_nt(halves(scaled), dy)
                weights = []
                dscore = rf.dscores[k]
                for a in range(2):
                    gap = (
                        rf.run_row[k, pl.ds(2 * pair + a, 1), :]
                        - rf.run_col[2 * pair + a, slot(k), :]
                    )
                    decay = jnp.exp(jnp.minimum(gap, 0.0))
                    weights.append((rf.scores[k] * decay).astype(BF16))
                    dscore = dscore + dweights[slot(a), :] * decay
                rf.dscores[k] = dscore
                dscaled = dot(jnp.concatenate(weights, axis=1), halves(dy))
                rf.dstep[slot(k), :] += head_sum(dscaled * values, columns)
                rf.drun[slot(k), :] += head_sum(
                    dy.astype(F32) * y - scaled.astype(F32) * dscaled, columns
                )
                dvalues = dscaled * wide + par[6:7, :] * dscan
                dcv = dvalues * (sig_c * (1.0 + cv * (1.0 - sig_c)))
                for t in range(4):
                    sums[t] += column_sum(dcv * taps[t])
                sums[4] += column_sum(dcv)
                rf.dv[slot(k), lanes] = conv_back(dcv, par).astype(BF16)
            rf.small[p] = jnp.concatenate(sums, axis=0)
        if wgate and wscan:
            for at, left, right in (
                (0, rf.dg, rf.normed),
                (3, rf.u, rf.g_all),
                (6, rf.dv, rf.normed),
            ):
                part = dot_tn(left[...], right[...]).astype(BF16)
                rf.ga[:, at : at + 3] = part.reshape(8, 3, 16, width)
            if not scan:
                part = dot_tn(rf.dbc_half[...], rf.normed[...]).astype(BF16)
                rf.ga[:, 9] = part.reshape(8, 16, width)
        elif wgate:
            for at, left, right in ((0, rf.dg, rf.normed), (3, rf.u, rf.g_all)):
                part = dot_tn(left[...], right[...]).astype(BF16)
                put_by_core(rf, "ga", h, at, part.reshape(4, 2, 3, 16, width))
        elif wscan:
            part = dot_tn(rf.dv[...], rf.normed[...]).astype(BF16)
            put_by_core(rf, "gb", h, 0, part.reshape(4, 2, 3, 16, width))
        if inp:
            rf.total[...] += dot(rf.dg[...], half_rows(rf.wg, h)) + dot(
                rf.dv[...], half_rows(rf.wv, h)
            )

        @when(h == STEPS - 1)
        def _finish():
            if scan:
                sums = [[jnp.zeros((1, LANES), F32) for _ in range(8)] for _ in range(2)]
                dt_sums = [jnp.zeros((1, LANES), F32) for _ in range(8)]
                live = iota(1) < 2 * PAIRS
                for k in range(SLOTS):
                    dscore = rf.dscores[k] * tri(False)
                    dmixed = (
                        jnp.dot(
                            dscore,
                            rf.mixed[1, slot(k), :],
                            precision=HI,
                            preferred_element_type=F32,
                        ),
                        dot_tn(dscore, rf.mixed[0, slot(k), :], HI),
                    )
                    for c in range(2):
                        lanes = slice(c * LANES, (c + 1) * LANES)
                        par = rf.pbcv[:, lanes]
                        taps = conv_taps(rf.pbc[slot(k), lanes])
                        cv = conv_sum(taps, par)
                        sig = sigmoid(cv)
                        dcv = dmixed[c] * (sig * (1.0 + cv * (1.0 - sig)))
                        for t in range(4):
                            sums[c][t] += column_sum(dcv * taps[t])
                        sums[c][4] += column_sum(dcv)
                        rf.dbc[slot(k), lanes] = conv_back(dcv, par).astype(BF16)
                    dlog = jnp.dot(
                        tri(False), rf.drun[slot(k), :], precision=HI, preferred_element_type=F32
                    )
                    grad_step = rf.dstep[slot(k), :] + dlog * rf.dtp[1:2, :]
                    dt_sums[1] += column_sum(dlog * rf.step_all[slot(k), :])
                    draw = grad_step * sigmoid(rf.pbc[slot(k), 256:384] + rf.dtp[0:1, :])
                    draw = jnp.where(live, draw, 0.0)
                    dt_sums[0] += column_sum(draw)
                    rf.dbc[slot(k), 256:384] = draw.astype(BF16)
                rf.small_bc[0] = jnp.concatenate(sums[0], axis=0)
                rf.small_bc[1] = jnp.concatenate(sums[1], axis=0)
                dt_sums[1] = dt_sums[1] * rf.dtp[1:2, :]
                rf.small_dt[...] = jnp.concatenate(dt_sums, axis=0)
            if wscan and wgate and scan:
                part = dot_tn(rf.dbc[:, 0:256], rf.normed[...]).astype(BF16)
                rf.ga_whole[:, 9] = part.reshape(16, 16, width)
            if wscan and not wgate:
                part = dot_tn(rf.dbc[:, 0:256], rf.normed[...]).astype(BF16)
                part = part.reshape(2, 4, 2, 1, 16, width)
                for a in range(2):
                    put_by_core(rf, "gb", a, 3, part[a])
            if wscan:
                rf.gdt[...] = dot_tn(rf.dbc[:, 256:384], rf.normed[...])[0:16]
            if inp:
                final = (
                    rf.total[...]
                    + dot(rf.dbc[:, 0:256], flat_rows(rf.ws))
                    + dot(rf.dbc[:, 256:384], rf.dtw[...])
                )
                for k in range(SLOTS):
                    getattr(rf, f"out{k}")[...] = final[slot(k), :].astype(BF16)

    ins, outs, scratch = {}, {}, {}
    heads_cols = STEPS * WIDE
    if gate or wgate:
        for k, v in enumerate(have["g"]):
            ins[f"g{k}"] = in_hbm(v)
        scratch["g_all"] = ((ROWS, width), BF16)
    if gate:
        if in_slots:
            scratch["e_all"] = ((SLOTS, T, LANES), BF16)
        else:
            ins["rows"] = whole(have["rows"])
        scratch["scale_row"] = ((ROWS, LANES), F32)
        scratch["cross_row"] = ((ROWS, LANES), F32)
        outs["u"] = lanes_by_step_out((ROWS, heads_cols), BF16)
        outs["dg"] = lanes_by_step_out((ROWS, heads_cols), BF16)
        if not scan:
            outs["dscan"] = lanes_by_step_out((ROWS, heads_cols), F32)
    if elementwise:
        ins["proj"] = by_step(saved["proj"], (1, ROWS, 2 * WIDE))
        ins["y"] = by_step(saved["y"], (1, ROWS, WIDE))
        ins["pv"] = lanes_by_step(pv)
        outs["small"] = by_step_out((PAIRS, 8, LANES), F32, (HALF, 8, LANES))
    if scan:
        ins["pbc"] = whole(saved["pbc"])
        ins["pbcv"] = whole(pbcv)
        ins["dtp"] = whole(dtp)
        if not gate:
            ins["dscan"] = lanes_by_step(have["dscan"])
        outs["dv"] = lanes_by_step_out((ROWS, heads_cols), BF16)
        outs["dbc"] = whole_out((ROWS, 384), BF16)
        outs["small_bc"] = whole_out((2, 8, LANES), F32)
        outs["small_dt"] = whole_out((8, LANES), F32)
        scratch.update(
            mixed=((2, ROWS, LANES), F32),
            scores=((SLOTS, T, T), F32),
            run_col=((2 * PAIRS, ROWS, LANES), F32),
            run_row=((SLOTS, T, LANES), F32),
            step_wide=((PAIRS, ROWS, LANES), F32),
            step_all=((ROWS, LANES), F32),
            dscores=((SLOTS, T, T), F32),
            dstep=((ROWS, LANES), F32),
            drun=((ROWS, LANES), F32),
        )
    if inp:
        ins["dtw"] = whole(dtw)
        scratch["total"] = ((ROWS, width), F32)
        outs.update({f"out{k}": whole_out((T, width), BF16) for k in range(SLOTS)})
    if fetched:
        ins["w"] = in_hbm(w)
        weight_scratch(scratch, fetched, width)
    if gate or wgate or inp:
        scratch["sems"] = pltpu.SemaphoreType.DMA((2 * SLOTS + 4,))
    if wgate or wscan:
        ins["normed"] = whole(saved["normed"])
    if not gate and (wgate or inp):
        ins["dg"] = lanes_by_step(have["dg"])
    if wgate and not gate:
        ins["u"] = lanes_by_step(have["u"])
    if not scan and (wscan or inp):
        ins["dv"] = lanes_by_step(have["dv"])
        ins["dbc"] = whole(have["dbc"])
    if wgate and wscan:
        if not scan:
            ins["dbc_half"] = (have["dbc"], (ROWS, LANES), lambda h: (0, h))
        outs["ga"] = by_step_out((16, 10, 16, width), BF16, (8, 10, 16, width))
    elif wgate or wscan:
        ins["core"] = have["core"]
        key, groups = ("ga", 6) if wgate else ("gb", 4)
        for end in ("_keep", "_send"):
            outs[key + end] = whole_out((2, 4, groups, 16, width), BF16)
    if wscan:
        outs["gdt"] = whole_out((16, width), F32)
    return kernel_call(body, name, ins, outs, scratch, cost_us, limit)


def assemble(parts, dt_rows, shard):
    quarter = parts.shape[2]
    block = 16 * 48
    total = 8 * block + 16 * 16 + dt_rows.shape[0]

    def body(_, inw, outw, shared, dt, grad_in, grad_out):
        i = pl.program_id(0)

        @pl.when(i < 8)
        def _columns():
            grad_in[...] = inw[...].reshape(block, quarter).astype(F32)

        @pl.when(i < SLOTS)
        def _out():
            grad_out[...] = outw[...].reshape(block, quarter).astype(F32)

        @pl.when(i == 8)
        def _shared():
            grad_in[...] = jnp.zeros_like(grad_in)
            grad_in[0:256, :] = shared[...].reshape(256, quarter).astype(F32)
            grad_in[256 : 256 + dt_rows.shape[0], :] = dt[...]

    last = SLOTS - 1
    spec = pltpu.PrefetchScalarGridSpec(
        num_scalar_prefetch=1,
        grid=(9,),
        in_specs=[
            pl.BlockSpec(
                (16, 48, quarter),
                lambda i, j: (0, jnp.where(i < SLOTS, 0, 8) + (j[0] + 3 * SLOTS - i) % SLOTS, 0),
            ),
            pl.BlockSpec((16, 48, quarter), lambda i, j: (0, SLOTS + jnp.minimum(i, last), 0)),
            pl.BlockSpec((16, 16, quarter), lambda i, j: (0, 36, 0)),
            pl.BlockSpec(dt_rows.shape, lambda i, j: (0, 0)),
        ],
        out_specs=[
            pl.BlockSpec((block, quarter), lambda i, j: (i, 0)),
            pl.BlockSpec((block, quarter), lambda i, j: (0, jnp.minimum(i, last))),
        ],
    )
    return pl.pallas_call(
        body,
        grid_spec=spec,
        out_shape=[
            jax.ShapeDtypeStruct((total, quarter), F32),
            jax.ShapeDtypeStruct((block, SLOTS * quarter), F32),
        ],
        compiler_params=pltpu.CompilerParams(vmem_limit_bytes=VMEM_MOST),
        name="assemble",
    )(shard.astype(jnp.int32)[None], parts, parts, parts, dt_rows)


def ring(n, k):
    return [(i, (i + k) % n) for i in range(n)]


def send_shard(v, k):
    return lax.ppermute(v, "shard", ring(SLOTS, k)) if k else v


def send_across(v, k):
    pairs = [
        (sec * SLOTS + y, (1 - sec) * SLOTS + (y + k) % SLOTS)
        for sec in range(2)
        for y in range(SLOTS)
    ]
    return lax.ppermute(v, ("section", "shard"), pairs)


def swap_section(v):
    return lax.ppermute(v, "section", [(0, 1), (1, 0)])


def dp_index(x, z, c):
    return x * 8 + z * 2 + c


def dp_pairs(move):
    pairs = []
    for x in range(2):
        for z in range(4):
            for c in range(2):
                pairs.append((dp_index(x, z, c), dp_index(*move(x, z, c))))
    return pairs


def pick(v, index, axis):
    return lax.dynamic_index_in_dim(v, index, axis, keepdims=False)


def gather_slots(v):
    return [send_shard(v, (-k) % SLOTS) for k in range(SLOTS)]


def scatter_sum(slots):
    parts = [send_shard(slots[k], k) for k in range(SLOTS)]
    return sum(p.astype(F32) for p in parts)


def cross_core(v):
    return lax.ppermute(v, DP, dp_pairs(lambda x, z, c: (x, z, 1 - c)))


def sum_small(v):
    v = v + lax.ppermute(v, DP, dp_pairs(lambda x, z, c: (x, z, 1 - c)))
    v = v + sum(
        lax.ppermute(v, DP, dp_pairs(lambda x, z, c: (x, (z + k) % 4, c))) for k in range(1, 4)
    )
    return v + lax.ppermute(v, DP, dp_pairs(lambda x, z, c: (1 - x, z, c)))


def in_order(parts, sign):
    j = lax.axis_index("shard")
    stacked = jnp.stack(parts)
    return jnp.take(stacked, (sign * (jnp.arange(SLOTS) - j)) % SLOTS, axis=0)


def shards(
    tokens,
    cotangent,
    lengths,
    norm_gain,
    in_weight,
    conv_weight,
    conv_bias,
    dt_bias,
    a_log,
    d_skip,
    gate_gain,
    out_weight,
):
    sec = lax.axis_index("section")
    d = lax.axis_index(DP)
    j = lax.axis_index("shard")
    core = d % 2
    first = sec == 0
    width = tokens.shape[2]
    quarter = norm_gain.shape[1]
    channels = conv_bias.shape[1]
    own_cols = gate_gain.shape[1]
    inner = own_cols * SLOTS
    heads = dt_bias.shape[1]
    own_heads = heads // SLOTS
    n_state = 2 * LANES
    piece = own_cols // 16
    piece_bc = n_state // 16
    own_core = (core.astype(jnp.int32)[None], pltpu.SMEM)

    x_own = pick(tokens, sec, 0)
    cot = pick(cotangent, sec, 0)
    length = pick(lengths, sec, 0)
    mask = (jnp.arange(T, dtype=jnp.int32) < length).astype(F32)[:, None]

    columns = jnp.transpose(in_weight[0])
    with jax.named_scope("weights"):

        def cut(start, rows):
            return lax.dynamic_slice(columns, (start, 0), (rows, quarter))

        def columns_of(to):
            return jnp.concatenate(
                [
                    cut(own_cols * to + piece * d, piece),
                    cut(inner + own_cols * to + piece * d, piece),
                    cut(2 * inner + piece_bc * d, piece_bc),
                ],
                axis=0,
            )

        cuts = [columns_of((j + k) % SLOTS) for k in range(SLOTS)]
        o_own = lax.dynamic_slice(out_weight[0], (piece * d, 0), (piece, width))
        o_other = swap_section(o_own)

        w_own = [send_shard(cuts[k], k) for k in range(SLOTS)]
        w_other = [send_across(cuts[k], k) for k in range(SLOTS)]

        def from_parts(parts, others, o, o_others, own):
            pieces = [jnp.where(own, p, q) for p, q in zip(parts, others)]
            lanes = []
            for y in range(SLOTS):
                v = pieces[0]
                for k in range(1, SLOTS):
                    v = jnp.where((j - y) % SLOTS == k, pieces[k], v)
                lanes.append(v)
            return jnp.concatenate(
                [jnp.where(own, o, o_others), jnp.concatenate(lanes, axis=1)], axis=0
            )

        w0 = from_parts(w_own, w_other, o_own, o_other, first)
        w1 = from_parts(w_own, w_other, o_own, o_other, ~first)
        w0, w1, x_own, cot = lax.optimization_barrier((w0, w1, x_own, cot))
        w0 = lax.all_gather(w0, DP, axis=0, tiled=False)
        x_slots = gather_slots(x_own)
        x_slots, norm_gain = lax.optimization_barrier((x_slots, norm_gain))

    with jax.named_scope("small_weights"):
        dt_columns = columns[2 * inner + n_state :]
        sizes = [quarter, 4 * channels, channels, own_cols, heads, heads, heads, heads * quarter]
        flat = jnp.concatenate(
            [
                norm_gain[0],
                conv_weight[0].reshape(-1),
                conv_bias[0],
                gate_gain[0],
                dt_bias[0],
                a_log[0],
                d_skip[0],
                dt_columns.reshape(-1),
            ]
        )
        flat = jnp.pad(flat, (0, -flat.shape[0] % LANES)).reshape(-1, LANES)
        own = in_order(gather_slots(flat), 1)
        other = swap_section(own)
        small = [jnp.where(first, own, other), jnp.where(first, other, own)]

        def unpack(v):
            low = v.reshape(SLOTS, -1)
            at = sum(sizes[:-1])
            dtw = low[:, at : at + sizes[-1]].reshape(SLOTS, heads, quarter)
            dtw = lax.dynamic_slice(dtw, (0, own_heads * j, 0), (SLOTS, own_heads, quarter))
            dtw = jnp.transpose(dtw, (1, 0, 2)).reshape(own_heads, width)
            dtw = jnp.pad(dtw, ((0, LANES - own_heads), (0, 0)))
            v = low[:, :at].astype(F32)
            cut, at = [], 0
            for size in sizes[:-1]:
                cut.append(v[:, at : at + size])
                at += size
            gain = cut[0].reshape(1, width)
            taps = cut[1].reshape(SLOTS, 4, channels).transpose(1, 0, 2).reshape(4, -1)
            bias = cut[2].reshape(1, -1)
            conv = jnp.concatenate([taps, bias, jnp.zeros((3, taps.shape[1]), F32)], axis=0)
            pbcv = conv[:, inner:]
            pv = lax.dynamic_slice(conv, (0, own_cols * j), (8, own_cols))
            pick_heads = lambda u: lax.dynamic_slice(u[0], (own_heads * j,), (own_heads,))
            wide = jnp.repeat(pick_heads(cut[6]), HEAD)[None]
            pv = jnp.concatenate([pv[:5], pick(cut[3], j, 0)[None], wide, pv[7:]], axis=0)
            dtp = jnp.stack([pick_heads(cut[4]), -jnp.exp(pick_heads(cut[5]))])
            dtp = jnp.pad(dtp, ((0, 6), (0, LANES - own_heads)))
            return gain, dtw, pv, pbcv, dtp

        gain0, *params0 = unpack(small[0])
        gain1, *params1 = unpack(small[1])

    x_f = x_own.astype(F32)
    g1 = (mask * cot.astype(F32)).astype(BF16)
    g1_slots = gather_slots(g1)
    w0, x_slots, g1_slots, gain0, params0, gain1, params1, w1 = lax.optimization_barrier(
        (w0, x_slots, g1_slots, gain0, params0, gain1, params1, w1)
    )
    w1 = lax.all_gather(w1, DP, axis=0, tiled=False)
    blocks = lambda v: v.reshape(16, 10, 16, width)

    layer0 = (blocks(w0), *params0)
    layer1 = (blocks(w1), *params1)

    def forward_layer(x, g, gain, layer):
        w, dtw, pv, pbcv, dtp = layer
        return forward(x, g, w, dtw, gain, pv, pbcv, dtp)

    parts, saved0 = forward_layer(x_slots, None, gain0, layer0)
    branch = scatter_sum(parts)
    square = jnp.sum(branch[:, width : width + 3], axis=1, keepdims=True)
    scale0 = lax.rsqrt(square / inner + EPS)
    branch0 = branch[:, :width] * scale0
    middle = (x_f + mask * branch0).astype(BF16)

    m_slots = gather_slots(middle)
    branch_parts, saved1 = forward_layer(m_slots, g1_slots, gain1, layer1)
    own = saved1["stats"][:, 0].reshape(2, SLOTS, T)
    back = [send_shard(own, k) for k in range(SLOTS)]
    summed = sum(jnp.roll(back[k], -k, axis=1) for k in range(SLOTS))
    scale1 = lax.rsqrt(summed[0] / inner + EPS)
    cross1 = scale1 * scale1 * scale1 * summed[1] / inner
    rows1 = jnp.pad(jnp.stack([scale1, cross1], axis=1), ((0, 0), (0, 6), (0, 0)))

    def norm_back(x, gain, grad):
        scale = lax.rsqrt(jnp.mean(x * x, axis=1, keepdims=True) + EPS)
        unit = x * scale
        dn = grad * gain
        dx = scale * (dn - unit * jnp.mean(dn * unit, axis=1, keepdims=True))
        return dx, jnp.sum(grad * unit, axis=0)

    back1 = backward(
        ("gate", "scan", "input", "wgate", "wscan"),
        "backward_1",
        28,
        saved1,
        layer1,
        {"g": g1_slots, "rows": rows1},
        VMEM_BACK,
    )
    moved = [send_shard(back1[f"out{k}"], k) for k in range(SLOTS)]
    dx, gain_grad1 = norm_back(middle.astype(F32), gain1, sum(p.astype(F32) for p in moved))
    by_owner = lambda v: v.reshape(16, -1, width)
    owned1 = lax.psum_scatter(by_owner(back1["ga"]), DP, scatter_dimension=0, tiled=False)

    dmiddle = (cot.astype(F32) + dx).astype(BF16)
    g0 = (mask * dmiddle.astype(F32)).astype(BF16)
    cross0 = scale0 * scale0 * jnp.sum(g0.astype(F32) * branch0, axis=1, keepdims=True) / inner
    g0_slots = gather_slots(jnp.concatenate([g0, in_lanes([scale0, cross0])], axis=1))
    g0_slots, branch_parts = lax.optimization_barrier((g0_slots, branch_parts))
    branch = scatter_sum(branch_parts)[:, :width] * scale1[0][:, None]
    result = middle.astype(F32) + mask * branch

    back0 = backward(
        ("gate", "wgate"),
        "backward_0_gate",
        14,
        saved0,
        layer0,
        {"g": g0_slots, "core": own_core},
    )
    both = lambda kept, moved: (kept.astype(F32) + moved.astype(F32)).astype(BF16)
    a_moved = cross_core(back0["ga_send"])
    small_gate = back0["small"]
    back0["core"] = own_core
    back0.update(backward(("scan", "wscan"), "backward_0_scan", 20, saved0, layer0, back0))
    gb_send, a_moved = lax.optimization_barrier((back0["gb_send"], a_moved))
    a0 = both(back0["ga_keep"], a_moved)
    b0 = both(back0["gb_keep"], cross_core(gb_send))
    owned0 = jnp.pad(a0, ((0, 0), (0, 0), (0, 4), (0, 0), (0, 0)))
    owned0 = lax.dynamic_update_slice(owned0, b0, (0, 0, 6, 0, 0)).reshape(8, -1, width)
    owned0 = lax.psum_scatter(owned0, ("x", "z"), scatter_dimension=0, tiled=False)
    small_scan = back0["small"]
    back0.update(backward(("input",), "backward_0_input", 9, saved0, layer0, back0))
    moved0 = [send_shard(back0[f"out{k}"], k) for k in range(SLOTS)]
    dx, gain_grad0 = norm_back(x_f, gain0, sum(p.astype(F32) for p in moved0))
    dtokens = dmiddle.astype(F32) + dx
    owned1 = owned1 + lax.ppermute(owned1, "section", [(0, 1)])
    owned0, owned1, gain_grad0, dtokens, result = lax.optimization_barrier(
        (owned0, owned1, gain_grad0, dtokens, result)
    )

    kept = jnp.where(first, owned0, owned1).reshape(10, 16, width)
    arrived = lax.ppermute(owned0, "section", [(1, 0)]).reshape(10, 16, width)

    def total_of(cut):
        return (cut(kept).astype(F32) + cut(arrived).astype(F32)).astype(BF16)

    row_slots = []
    for k in range(SLOTS):

        def cut(v):
            v = lax.dynamic_slice_in_dim(v, quarter * ((j + k) % SLOTS), quarter, 2)
            return jnp.concatenate([v[:3], v[6:]], axis=0)

        row_slots.append(send_shard(total_of(cut).reshape(-1, quarter), k))
    out_rows = total_of(lambda v: v[3:6])
    out_rows = jnp.transpose(out_rows.reshape(piece, SLOTS, quarter), (1, 0, 2))
    result_moved = lax.ppermute(result.astype(BF16), "section", [(0, 1)]).astype(F32)
    dtokens_moved = lax.ppermute(dtokens.astype(BF16), "section", [(1, 0)]).astype(F32)
    ends = jnp.where(
        first, jnp.stack([dtokens, dtokens_moved]), jnp.stack([result_moved, result])
    )[None]

    def to_section(v0, v1):
        kept = jnp.where(first, v0, v1).astype(F32)
        return kept + swap_section(jnp.where(first, v1, v0)).astype(F32)

    shared = sum(v[2 * piece :].astype(F32) for v in row_slots).astype(BF16)
    gathered = lax.all_gather(
        jnp.concatenate(
            [v[:piece] for v in row_slots]
            + [out_rows.reshape(-1, quarter)]
            + [v[piece : 2 * piece] for v in row_slots]
            + [shared],
            axis=0,
        ),
        DP,
        tiled=False,
    )

    def small_of(by_pair, back, gain_grad):
        return jnp.concatenate(
            [
                by_pair.reshape(-1, LANES),
                back["small_bc"].reshape(-1, LANES),
                back["small_dt"],
                gain_grad.reshape(-1, LANES),
                back["gdt"].reshape(-1, LANES),
            ],
            axis=0,
        )

    small0 = small_of(small_gate + small_scan, back0, gain_grad0)
    small1 = small_of(back1["small"], back1, gain_grad1)
    small_sum = sum_small(to_section(small0, small1))
    everyone = in_order(gather_slots(small_sum), 1)
    n_pair, n_bc = PAIRS * 8, 2 * 8
    by_pair = everyone[:, :n_pair].reshape(SLOTS, PAIRS, 8, LANES)
    by_pair = by_pair.transpose(2, 0, 1, 3).reshape(8, inner)
    by_bc = jnp.sum(everyone[:, n_pair : n_pair + n_bc], axis=0)
    by_bc = by_bc.reshape(2, 8, LANES).transpose(1, 0, 2).reshape(8, n_state)
    at = n_pair + n_bc
    by_dt = everyone[:, at : at + 8, :own_heads].transpose(1, 0, 2).reshape(8, heads)
    at += 8
    gain_total = jnp.sum(everyone[:, at : at + width // LANES], axis=0).reshape(-1)
    at += width // LANES
    dt_rows = everyone[:, at:].reshape(SLOTS, 16, SLOTS, quarter)[:, :own_heads]
    dt_rows = pick(dt_rows, j, 2).reshape(heads, quarter)
    conv_total = jnp.concatenate([by_pair[:5], by_bc[:5]], axis=1)
    conv_own = lax.dynamic_slice(conv_total, (0, channels * j), (5, channels))
    grad_skip = jnp.sum(by_pair[6].reshape(heads, HEAD), axis=1)

    grad_in_weight, grad_out_weight = assemble(gathered, dt_rows, j)
    return (
        ends,
        lax.dynamic_slice(gain_total, (quarter * j,), (quarter,))[None],
        jnp.transpose(grad_in_weight)[None],
        conv_own[None, :4],
        conv_own[4][None],
        by_dt[0][None],
        by_dt[1][None],
        grad_skip[None],
        lax.dynamic_slice(by_pair[5], (own_cols * j,), (own_cols,))[None],
        grad_out_weight[None],
    )


def solution(mesh):
    sections, copies, owners = mesh.devices.shape
    fine = jax.sharding.Mesh(
        mesh.devices.reshape(sections, 2, copies // 4, 2, owners), ("section", *DP, "shard")
    )
    return jax.shard_map(
        shards,
        mesh=fine,
        in_specs=(
            P((*DP, "shard"), None, None),
            P((*DP, "shard"), None, None),
            P((*DP, "shard")),
            P("section", "shard"),
            P("section", "shard", None),
            P("section", None, "shard"),
            P("section", "shard"),
            P("section", None),
            P("section", None),
            P("section", None),
            P("section", "shard"),
            P("section", "shard", None),
        ),
        out_specs=(
            P("section", (*DP, "shard"), None, None),
            P("section", "shard"),
            P("section", "shard", None),
            P("section", None, "shard"),
            P("section", "shard"),
            P("section", None),
            P("section", None),
            P("section", None),
            P("section", "shard"),
            P("section", "shard", None),
        ),
        check_vma=False,
    )
```

```python
import jax
import jax.numpy as jnp
from jax import lax
from jax.experimental import pallas as pl
from jax.experimental.pallas import tpu as pltpu
from jax.sharding import PartitionSpec as P

F32 = jnp.float32
BF16 = jnp.bfloat16
HI = lax.Precision.HIGHEST
EPS = 1e-05
T = 128
LANES = 128
HEAD = 64
SLOTS = 4
ROWS = SLOTS * T
PAIRS = 6
STEPS = 2
HALF = PAIRS // STEPS
WIDE = HALF * LANES
VMEM_LIMIT = 34 * 1024 * 1024
VMEM_MOST = 60 * 1024 * 1024
VMEM_BACK = 56 * 1024 * 1024
DP = ("x", "z", "core")


def sigmoid(v):
    return 0.5 * jnp.tanh(0.5 * v) + 0.5


def softplus(v):
    return jnp.maximum(v, 0.0) + jnp.log1p(jnp.exp(-jnp.abs(v)))


def dot(a, b):
    return jnp.dot(a, b, preferred_element_type=F32)


def dot_nt(a, b, precision=None):
    return lax.dot_general(
        a, b, (((1,), (1,)), ((), ())), preferred_element_type=F32, precision=precision
    )


def dot_tn(a, b, precision=None):
    return lax.dot_general(
        a, b, (((0,), (0,)), ((), ())), preferred_element_type=F32, precision=precision
    )


def iota(axis):
    return lax.broadcasted_iota(jnp.int32, (T, LANES), axis)


def shift_down(v, steps):
    return jnp.where(iota(0) >= steps, pltpu.roll(v, steps, 0), 0.0)


def shift_up(v, steps):
    return jnp.where(iota(0) < T - steps, pltpu.roll(v, T - steps, 0), 0.0)


def conv_taps(cin):
    return [shift_down(cin, 3), shift_down(cin, 2), shift_down(cin, 1), cin]


def conv_sum(taps, par):
    total = par[4:5, :] + taps[0] * par[0:1, :]
    for k in range(1, 4):
        total = total + taps[k] * par[k : k + 1, :]
    return total


def conv_back(dcv, par):
    total = dcv * par[3:4, :]
    for m in range(1, 4):
        total = total + shift_up(dcv, m) * par[3 - m : 4 - m, :]
    return total


def column_sum(v):
    return jnp.sum(v, axis=0, keepdims=True)


def slot(k):
    return slice(k * T, (k + 1) * T)


def tri(lower):
    if lower:
        return (iota(0) >= iota(1)).astype(F32)
    return (iota(0) <= iota(1)).astype(F32)


def step_prep(k, pbc, at, dtp, run_col, run_row, step_wide):
    step = softplus(pbc[slot(at), 256:384] + dtp[0:1, :])
    run = jnp.dot(tri(True), step * dtp[1:2, :], precision=HI, preferred_element_type=F32)
    run_row[k] = jnp.transpose(run)
    left = iota(1) < HEAD
    for p in range(PAIRS):
        a, b = 2 * p, 2 * p + 1
        run_col[a, slot(k), :] = jnp.broadcast_to(run[:, a : a + 1], (T, LANES))
        run_col[b, slot(k), :] = jnp.broadcast_to(run[:, b : b + 1], (T, LANES))
        step_wide[p, slot(k), :] = jnp.where(
            left,
            jnp.broadcast_to(step[:, a : a + 1], (T, LANES)),
            jnp.broadcast_to(step[:, b : b + 1], (T, LANES)),
        )
    return step


def halves(v):
    left = iota(1) < HEAD
    zero = jnp.zeros_like(v)
    return jnp.concatenate([jnp.where(left, v, zero), jnp.where(left, zero, v)], axis=0)


def in_lanes(columns):
    lane = lax.broadcasted_iota(jnp.int32, (columns[0].shape[0], LANES), 1)
    out = jnp.zeros(lane.shape, F32)
    for n, v in enumerate(columns):
        for k in range(3):
            part = v.astype(BF16).astype(F32)
            out = jnp.where(lane == 3 * n + k, part, out)
            v = v - part
    return out.astype(BF16)


def from_lanes(v, n):
    return sum(v[:, 3 * n + k : 3 * n + k + 1].astype(F32) for k in range(3))


class Refs:
    pass


def kernel_call(body, name, ins, outs, scratch, cost_us, limit=VMEM_LIMIT):
    in_names, out_names, scratch_names = list(ins), list(outs), list(scratch)

    def run(*refs):
        for h in range(STEPS):
            rf = Refs()
            for key, ref in zip(in_names + out_names + scratch_names, refs):
                spec = ins.get(key) or outs.get(key)
                blocks = spec[-2:] if spec and len(spec) > 2 else None
                if blocks and blocks[1](1) != blocks[1](0):
                    at = [
                        slice(n * size, (n + 1) * size) if n else slice(0, size)
                        for n, size in zip(blocks[1](h), blocks[0])
                    ]
                    setattr(rf, key + "_whole", ref)
                    ref = ref.at[tuple(at)]
                setattr(rf, key, ref)
            body(rf, h)

    res = pl.pallas_call(
        run,
        in_specs=[
            pl.BlockSpec(memory_space=pltpu.VMEM if len(ins[n]) > 2 else ins[n][1])
            for n in in_names
        ],
        out_specs=[pl.BlockSpec(memory_space=pltpu.VMEM) for n in out_names],
        out_shape=[jax.ShapeDtypeStruct(outs[n][0], outs[n][1]) for n in out_names],
        scratch_shapes=[
            pltpu.VMEM(*scratch[n]) if isinstance(scratch[n], tuple) else scratch[n]
            for n in scratch_names
        ],
        compiler_params=pltpu.CompilerParams(vmem_limit_bytes=limit),
        cost_estimate=pl.CostEstimate(
            flops=int(cost_us * 1.1e9), bytes_accessed=1 << 20, transcendentals=0
        ),
        name=name,
    )(*[ins[n][0] for n in in_names])
    return dict(zip(out_names, res))


def when(condition):
    return (lambda f: f()) if condition else (lambda f: None)


def whole(v):
    return (v, v.shape, lambda h: (0,) * v.ndim)


def whole_out(shape, dtype):
    return (shape, dtype, shape, lambda h: (0,) * len(shape))


def by_step(v, block):
    return (v, block, lambda h: (h,) + (0,) * (len(block) - 1))


def by_step_out(shape, dtype, block):
    return (shape, dtype, block, lambda h: (h,) + (0,) * (len(block) - 1))


def lanes_by_step(v):
    return (v, (v.shape[0], WIDE), lambda h: (0, h))


def lanes_by_step_out(shape, dtype):
    return (shape, dtype, (shape[0], WIDE), lambda h: (0, h))


def in_hbm(v):
    return (v, pltpu.HBM)


WEIGHT_GROUPS = {"wo": (0, 3), "wg": (3, 3), "wv": (6, 3), "ws": (9, 1)}


class Copies:
    def __init__(self, sems):
        self.sems, self.copies = sems, {}

    def add(self, key, source, target):
        self.copies[key] = (source, target, self.sems.at[len(self.copies)])

    def add_weights(self, rf, keys):
        for key in keys:
            at, count = WEIGHT_GROUPS[key]
            self.add(key, rf.w.at[:, pl.ds(at, count)], getattr(rf, key))

    def start(self):
        for copy in self.copies.values():
            pltpu.make_async_copy(*copy).start()

    def wait(self, *keys):
        for key in keys:
            pltpu.make_async_copy(*self.copies[key]).wait()


def weight_scratch(scratch, keys, width):
    for key in keys:
        scratch[key] = ((16, WEIGHT_GROUPS[key][1], 16, width), BF16)


def half_rows(ref, h):
    v = ref[pl.ds(8 * h, 8)]
    return v.reshape(WIDE, v.shape[-1])


def pair_lanes(p):
    return slice(p * LANES, (p + 1) * LANES)


def flat_rows(ref):
    v = ref[...]
    return v.reshape(-1, v.shape[-1])


def mixed_bc(pbc, pbcv, k, c):
    lanes = slice(c * LANES, (c + 1) * LANES)
    cv = conv_sum(conv_taps(pbc[slot(k), lanes]), pbcv[:, lanes])
    return cv * sigmoid(cv)


def forward(x_slots, g_slots, w, dtw, gain, pv, pbcv, dtp):
    width = x_slots[0].shape[1]
    with_grad = g_slots is not None
    slots = len(x_slots)
    rows = slots * T

    def body(rf, h):
        copies = Copies(rf.sems)
        for k in range(slots):
            copies.add(f"x{k}", getattr(rf, f"x{k}"), rf.x_all.at[k])
        copies.add_weights(rf, ("ws", "wg", "wv", "wo"))
        if with_grad:
            for k in range(slots):
                copies.add(f"g{k}", getattr(rf, f"g{k}"), rf.g_all.at[slot(k)])

        @when(h == 0)
        def _prep():
            copies.start()
            for k in range(slots):
                copies.wait(f"x{k}")
                x = rf.x_all[k].astype(F32)
                scale = lax.rsqrt(jnp.mean(x * x, axis=1, keepdims=True) + EPS)
                rf.normed[slot(k), :] = (x * scale * rf.gain[...]).astype(BF16)
            copies.wait("ws")
            rf.pbc[:, 0:256] = dot_nt(rf.normed[...], flat_rows(rf.ws))
            rf.pbc[:, 256:384] = dot_nt(rf.normed[...], rf.dtw[...])
            for k in range(slots):
                rf.scores[k] = dot_nt(
                    mixed_bc(rf.pbc, rf.pbcv, k, 1), mixed_bc(rf.pbc, rf.pbcv, k, 0), HI
                ) * tri(True)
                step_prep(k, rf.pbc, k, rf.dtp, rf.run_col, rf.run_row, rf.step_wide)
            rf.square[...] = jnp.zeros_like(rf.square)
            rf.cross[...] = jnp.zeros_like(rf.cross)
            copies.wait("wg", "wv", "wo")
            if with_grad:
                copies.wait(*[f"g{k}" for k in range(slots)])

        rf.proj[0, :, 0:WIDE] = dot_nt(rf.normed[...], half_rows(rf.wg, h))
        rf.proj[0, :, WIDE : 2 * WIDE] = dot_nt(rf.normed[...], half_rows(rf.wv, h))
        if with_grad:
            q_all = dot_nt(rf.g_all[...], half_rows(rf.wo, h))
        for p in range(HALF):
            lanes = pair_lanes(p)
            par = rf.pv[:, lanes]
            pair = HALF * h + p
            for k in range(slots):
                gate = rf.proj[0, slot(k), lanes]
                cv = conv_sum(
                    conv_taps(rf.proj[0, slot(k), WIDE + p * LANES : WIDE + (p + 1) * LANES]), par
                )
                values = cv * sigmoid(cv)
                scaled = (values * rf.step_wide[pair, slot(k), :]).astype(BF16)
                weights = []
                for a in range(2):
                    gap = (
                        rf.run_col[2 * pair + a, slot(k), :]
                        - rf.run_row[k, pl.ds(2 * pair + a, 1), :]
                    )
                    decay = jnp.exp(jnp.minimum(gap, 0.0))
                    weights.append((rf.scores[k] * decay).astype(BF16))
                y = dot(jnp.concatenate(weights, axis=1), halves(scaled))
                rf.y[0, slot(k), lanes] = y
                scanned = y + par[6:7, :] * values
                gated = scanned * (gate * sigmoid(gate))
                rf.square[slot(k), :] += gated * gated
                scaled_out = gated * par[5:6, :]
                rf.u_all[h, slot(k), lanes] = scaled_out.astype(BF16)
                if with_grad:
                    rf.cross[slot(k), :] += q_all[slot(k), lanes] * scaled_out

        @when(h == STEPS - 1)
        def _finish():
            u = jnp.concatenate([rf.u_all[a] for a in range(STEPS)], axis=1)
            for n in range(0, width, 512):
                part = dot(u, rf.wo[:, :, :, n : n + 512].reshape(STEPS * WIDE, 512)).astype(BF16)
                for k in range(slots):
                    getattr(rf, f"out{k}")[:, n : n + 512] = part[slot(k), :]
            for k in range(slots):
                total = jnp.sum(rf.square[slot(k), :], axis=1, keepdims=True)
                getattr(rf, f"out{k}")[:, width:] = in_lanes([total])
            ones = jnp.ones((8, LANES), F32)
            rf.stats[0] = dot_nt(ones, rf.square[...], HI)
            rf.stats[1] = dot_nt(ones, rf.cross[...], HI)

    ins = {f"x{k}": in_hbm(v) for k, v in enumerate(x_slots)}
    if with_grad:
        ins.update({f"g{k}": in_hbm(v) for k, v in enumerate(g_slots)})
    ins.update(
        gain=whole(gain),
        w=in_hbm(w),
        dtw=whole(dtw),
        pv=lanes_by_step(pv),
        pbcv=whole(pbcv),
        dtp=whole(dtp),
    )
    outs = {f"out{k}": whole_out((T, width + LANES), BF16) for k in range(slots)}
    outs.update(
        stats=whole_out((2, 8, rows), F32),
        normed=whole_out((rows, width), BF16),
        proj=by_step_out((STEPS, rows, 2 * WIDE), F32, (1, rows, 2 * WIDE)),
        y=by_step_out((STEPS, rows, WIDE), F32, (1, rows, WIDE)),
        pbc=whole_out((rows, 384), F32),
    )
    scratch = dict(
        scores=((slots, T, T), F32),
        run_col=((2 * PAIRS, rows, LANES), F32),
        run_row=((slots, T, LANES), F32),
        step_wide=((PAIRS, rows, LANES), F32),
        u_all=((STEPS, rows, WIDE), BF16),
        square=((rows, LANES), F32),
        cross=((rows, LANES), F32),
        x_all=((slots, T, width), BF16),
        sems=pltpu.SemaphoreType.DMA((2 * slots + 4,)),
    )
    weight_scratch(scratch, ("ws", "wg", "wv", "wo"), width)
    if with_grad:
        scratch["g_all"] = ((rows, width), BF16)
    res = kernel_call(body, "layer_forward", ins, outs, scratch, 4 * slots, VMEM_MOST)
    return [res[f"out{k}"] for k in range(slots)], res


def head_columns(pair):
    target = 2 * pair + (iota(0) >= HEAD).astype(jnp.int32)
    one = (iota(1) == target).astype(BF16)
    return jnp.concatenate([one, one], axis=0)


def head_sum(v, columns):
    high = v.astype(BF16)
    low = (v - high.astype(F32)).astype(BF16)
    return dot(jnp.concatenate([high, low], axis=1), columns)


def put_by_core(rf, key, x, at, part):
    keep, send = getattr(rf, key + "_keep"), getattr(rf, key + "_send")
    groups = slice(at, at + part.shape[2])
    for c in range(2):

        @pl.when(rf.core[0] == c)
        def _store(c=c):
            for z in range(4):
                keep[x, z, groups] = part[z, c]
                send[x, z, groups] = part[z, 1 - c]


def backward(stages, name, cost_us, saved, layer, have, limit=VMEM_LIMIT):
    gate, scan, inp, wgate, wscan = (
        s in stages for s in ("gate", "scan", "input", "wgate", "wscan")
    )
    width = saved[0]["normed"].shape[1]
    per = SLOTS // len(saved)
    w, dtw, pv, pbcv, dtp = layer
    elementwise = gate or scan
    fetched = (("wo",) if gate else ()) + (("wg", "wv", "ws") if inp else ())
    in_slots = gate and "rows" not in have
    part_of = lambda rf, key, k: getattr(rf, f"{key}{k // per}")
    mixed = lambda rf, k, c: mixed_bc(part_of(rf, "pbc", k), rf.pbcv, k % per, c)

    def body(rf, h):
        copies = Copies(rf.sems) if gate or wgate or inp else None
        if gate or wgate:
            for k in range(SLOTS):
                source = getattr(rf, f"g{k}")
                copies.add(f"g{k}", source.at[:, pl.ds(0, width)], rf.g_all.at[slot(k)])
                if in_slots:
                    copies.add(f"e{k}", source.at[:, pl.ds(width, LANES)], rf.e_all.at[k])
        if copies:
            copies.add_weights(rf, fetched)
            if (wgate or wscan) and len(saved) > 1:
                for n in range(len(saved)):
                    rows = pl.ds(n * per * T, per * T)
                    copies.add(f"n{n}", getattr(rf, f"normed{n}"), rf.normed.at[rows])

        @when(h == 0)
        def _prep():
            if copies:
                copies.start()
            for k in range(SLOTS):
                if gate or wgate:
                    copies.wait(f"g{k}")
                if in_slots:
                    copies.wait(f"e{k}")
                if gate:
                    for row, ref in ((0, rf.scale_row), (1, rf.cross_row)):
                        if "rows" in have:
                            ref[slot(k), :] = jnp.transpose(
                                jnp.broadcast_to(rf.rows[k, row : row + 1, :], (T, LANES))
                            )
                        else:
                            column = from_lanes(rf.e_all[k], row)
                            ref[slot(k), :] = jnp.broadcast_to(column, (T, LANES))
                if scan:
                    inbound, outbound = mixed(rf, k, 0), mixed(rf, k, 1)
                    rf.mixed_all[0, slot(k), :] = inbound
                    rf.mixed_all[1, slot(k), :] = outbound
                    rf.scores[k] = dot_nt(inbound, outbound, HI) * tri(False)
                    rf.step_all[slot(k), :] = step_prep(
                        k, part_of(rf, "pbc", k), k % per, rf.dtp, rf.run_col, rf.run_row, rf.step_wide
                    )
            if scan:
                rf.dscores[...] = jnp.zeros_like(rf.dscores)
                rf.dstep[...] = jnp.zeros_like(rf.dstep)
                rf.drun[...] = jnp.zeros_like(rf.drun)
            if inp:
                rf.total[...] = jnp.zeros_like(rf.total)
            if copies:
                copies.wait(*fetched)
                if (wgate or wscan) and len(saved) > 1:
                    copies.wait(*[f"n{n}" for n in range(len(saved))])

        if gate:
            q_all = dot_nt(rf.g_all[...], half_rows(rf.wo, h))
        for p in range(HALF if elementwise else 0):
            lanes = pair_lanes(p)
            par = rf.pv[:, lanes]
            pair = HALF * h + p
            sums = [jnp.zeros((1, LANES), F32) for _ in range(8)]
            if scan:
                columns = head_columns(pair)
            for k in range(SLOTS):
                taps = conv_taps(part_of(rf, "proj", k)[0, slot(k % per), WIDE + p * LANES : WIDE + (p + 1) * LANES])
                cv = conv_sum(taps, par)
                sig_c = sigmoid(cv)
                values = cv * sig_c
                y = part_of(rf, "y", k)[0, slot(k % per), lanes]
                if gate:
                    gate_in = part_of(rf, "proj", k)[0, slot(k % per), lanes]
                    sig_g = sigmoid(gate_in)
                    silu_g = gate_in * sig_g
                    scanned = y + par[6:7, :] * values
                    gated = scanned * silu_g
                    grad_no = q_all[slot(k), lanes]
                    scale = rf.scale_row[slot(k), :]
                    dgated = scale * (grad_no * par[5:6, :]) - rf.cross_row[slot(k), :] * gated
                    norm = gated * scale
                    sums[5] += column_sum(grad_no * norm)
                    rf.u[slot(k), lanes] = (norm * par[5:6, :]).astype(BF16)
                    dscan = dgated * silu_g
                    dgate = dgated * scanned * (sig_g * (1.0 + gate_in * (1.0 - sig_g)))
                    sums[6] += column_sum(dscan * values)
                    rf.dg[slot(k), lanes] = dgate.astype(BF16)
                    if not scan:
                        rf.dscan[slot(k), lanes] = dscan
                else:
                    dscan = rf.dscan[slot(k), lanes]
                if not scan:
                    continue
                wide = rf.step_wide[pair, slot(k), :]
                dy = dscan.astype(BF16)
                scaled = (values * wide).astype(BF16)
                dweights = dot_nt(halves(scaled), dy)
                weights = []
                dscore = rf.dscores[k]
                for a in range(2):
                    gap = (
                        rf.run_row[k, pl.ds(2 * pair + a, 1), :]
                        - rf.run_col[2 * pair + a, slot(k), :]
                    )
                    decay = jnp.exp(jnp.minimum(gap, 0.0))
                    weights.append((rf.scores[k] * decay).astype(BF16))
                    dscore = dscore + dweights[slot(a), :] * decay
                rf.dscores[k] = dscore
                dscaled = dot(jnp.concatenate(weights, axis=1), halves(dy))
                rf.dstep[slot(k), :] += head_sum(dscaled * values, columns)
                rf.drun[slot(k), :] += head_sum(
                    dy.astype(F32) * y - scaled.astype(F32) * dscaled, columns
                )
                dvalues = dscaled * wide + par[6:7, :] * dscan
                dcv = dvalues * (sig_c * (1.0 + cv * (1.0 - sig_c)))
                for t in range(4):
                    sums[t] += column_sum(dcv * taps[t])
                sums[4] += column_sum(dcv)
                rf.dv[slot(k), lanes] = conv_back(dcv, par).astype(BF16)
            rf.small[p] = jnp.concatenate(sums, axis=0)
        if wgate and wscan:
            for at, left, right in (
                (0, rf.dg, rf.normed),
                (3, rf.u, rf.g_all),
                (6, rf.dv, rf.normed),
            ):
                part = dot_tn(left[...], right[...]).astype(BF16)
                rf.ga[:, at : at + 3] = part.reshape(8, 3, 16, width)
            if not scan:
                part = dot_tn(rf.dbc_half[...], rf.normed[...]).astype(BF16)
                rf.ga[:, 9] = part.reshape(8, 16, width)
        elif wgate:
            for at, left, right in ((0, rf.dg, rf.normed), (3, rf.u, rf.g_all)):
                part = dot_tn(left[...], right[...]).astype(BF16)
                put_by_core(rf, "ga", h, at, part.reshape(4, 2, 3, 16, width))
        elif wscan:
            part = dot_tn(rf.dv[...], rf.normed[...]).astype(BF16)
            put_by_core(rf, "gb", h, 0, part.reshape(4, 2, 3, 16, width))
        if inp:
            rf.total[...] += dot(rf.dg[...], half_rows(rf.wg, h)) + dot(
                rf.dv[...], half_rows(rf.wv, h)
            )

        @when(h == STEPS - 1)
        def _finish():
            if scan:
                sums = [[jnp.zeros((1, LANES), F32) for _ in range(8)] for _ in range(2)]
                dt_sums = [jnp.zeros((1, LANES), F32) for _ in range(8)]
                live = iota(1) < 2 * PAIRS
                for k in range(SLOTS):
                    dscore = rf.dscores[k] * tri(False)
                    dmixed = (
                        jnp.dot(
                            dscore,
                            rf.mixed_all[1, slot(k), :],
                            precision=HI,
                            preferred_element_type=F32,
                        ),
                        dot_tn(dscore, rf.mixed_all[0, slot(k), :], HI),
                    )
                    for c in range(2):
                        lanes = slice(c * LANES, (c + 1) * LANES)
                        par = rf.pbcv[:, lanes]
                        taps = conv_taps(part_of(rf, "pbc", k)[slot(k % per), lanes])
                        cv = conv_sum(taps, par)
                        sig = sigmoid(cv)
                        dcv = dmixed[c] * (sig * (1.0 + cv * (1.0 - sig)))
                        for t in range(4):
                            sums[c][t] += column_sum(dcv * taps[t])
                        sums[c][4] += column_sum(dcv)
                        rf.dbc[slot(k), lanes] = conv_back(dcv, par).astype(BF16)
                    dlog = jnp.dot(
                        tri(False), rf.drun[slot(k), :], precision=HI, preferred_element_type=F32
                    )
                    grad_step = rf.dstep[slot(k), :] + dlog * rf.dtp[1:2, :]
                    dt_sums[1] += column_sum(dlog * rf.step_all[slot(k), :])
                    draw = grad_step * sigmoid(part_of(rf, "pbc", k)[slot(k % per), 256:384] + rf.dtp[0:1, :])
                    draw = jnp.where(live, draw, 0.0)
                    dt_sums[0] += column_sum(draw)
                    rf.dbc[slot(k), 256:384] = draw.astype(BF16)
                rf.small_bc[0] = jnp.concatenate(sums[0], axis=0)
                rf.small_bc[1] = jnp.concatenate(sums[1], axis=0)
                dt_sums[1] = dt_sums[1] * rf.dtp[1:2, :]
                rf.small_dt[...] = jnp.concatenate(dt_sums, axis=0)
            if wscan and wgate and scan:
                part = dot_tn(rf.dbc[:, 0:256], rf.normed[...]).astype(BF16)
                rf.ga_whole[:, 9] = part.reshape(16, 16, width)
            if wscan and not wgate:
                part = dot_tn(rf.dbc[:, 0:256], rf.normed[...]).astype(BF16)
                part = part.reshape(2, 4, 2, 1, 16, width)
                for a in range(2):
                    put_by_core(rf, "gb", a, 3, part[a])
            if wscan:
                rf.gdt[...] = dot_tn(rf.dbc[:, 256:384], rf.normed[...])[0:16]
            if inp:
                final = (
                    rf.total[...]
                    + dot(rf.dbc[:, 0:256], flat_rows(rf.ws))
                    + dot(rf.dbc[:, 256:384], rf.dtw[...])
                )
                for k in range(SLOTS):
                    getattr(rf, f"out{k}")[...] = final[slot(k), :].astype(BF16)

    ins, outs, scratch = {}, {}, {}
    heads_cols = STEPS * WIDE
    if gate or wgate:
        for k, v in enumerate(have["g"]):
            ins[f"g{k}"] = in_hbm(v)
        scratch["g_all"] = ((ROWS, width), BF16)
    if gate:
        if in_slots:
            scratch["e_all"] = ((SLOTS, T, LANES), BF16)
        else:
            ins["rows"] = whole(have["rows"])
        scratch["scale_row"] = ((ROWS, LANES), F32)
        scratch["cross_row"] = ((ROWS, LANES), F32)
        outs["u"] = lanes_by_step_out((ROWS, heads_cols), BF16)
        outs["dg"] = lanes_by_step_out((ROWS, heads_cols), BF16)
        if not scan:
            outs["dscan"] = lanes_by_step_out((ROWS, heads_cols), F32)
    if elementwise:
        for n, part in enumerate(saved):
            ins[f"proj{n}"] = by_step(part["proj"], (1, per * T, 2 * WIDE))
            ins[f"y{n}"] = by_step(part["y"], (1, per * T, WIDE))
        ins["pv"] = lanes_by_step(pv)
        outs["small"] = by_step_out((PAIRS, 8, LANES), F32, (HALF, 8, LANES))
    if scan:
        for n, part in enumerate(saved):
            ins[f"pbc{n}"] = whole(part["pbc"])
        ins["pbcv"] = whole(pbcv)
        ins["dtp"] = whole(dtp)
        if not gate:
            ins["dscan"] = lanes_by_step(have["dscan"])
        outs["dv"] = lanes_by_step_out((ROWS, heads_cols), BF16)
        outs["dbc"] = whole_out((ROWS, 384), BF16)
        outs["small_bc"] = whole_out((2, 8, LANES), F32)
        outs["small_dt"] = whole_out((8, LANES), F32)
        scratch.update(
            mixed_all=((2, ROWS, LANES), F32),
            scores=((SLOTS, T, T), F32),
            run_col=((2 * PAIRS, ROWS, LANES), F32),
            run_row=((SLOTS, T, LANES), F32),
            step_wide=((PAIRS, ROWS, LANES), F32),
            step_all=((ROWS, LANES), F32),
            dscores=((SLOTS, T, T), F32),
            dstep=((ROWS, LANES), F32),
            drun=((ROWS, LANES), F32),
        )
    if inp:
        ins["dtw"] = whole(dtw)
        scratch["total"] = ((ROWS, width), F32)
        outs.update({f"out{k}": whole_out((T, width), BF16) for k in range(SLOTS)})
    if fetched:
        ins["w"] = in_hbm(w)
        weight_scratch(scratch, fetched, width)
    if gate or wgate or inp:
        scratch["sems"] = pltpu.SemaphoreType.DMA((2 * SLOTS + 4,))
    if wgate or wscan:
        if len(saved) == 1:
            ins["normed"] = whole(saved[0]["normed"])
        else:
            for n, part in enumerate(saved):
                ins[f"normed{n}"] = in_hbm(part["normed"])
            scratch["normed"] = ((ROWS, width), BF16)
    if not gate and (wgate or inp):
        ins["dg"] = lanes_by_step(have["dg"])
    if wgate and not gate:
        ins["u"] = lanes_by_step(have["u"])
    if not scan and (wscan or inp):
        ins["dv"] = lanes_by_step(have["dv"])
        ins["dbc"] = whole(have["dbc"])
    if wgate and wscan:
        if not scan:
            ins["dbc_half"] = (have["dbc"], (ROWS, LANES), lambda h: (0, h))
        outs["ga"] = by_step_out((16, 10, 16, width), BF16, (8, 10, 16, width))
    elif wgate or wscan:
        ins["core"] = have["core"]
        key, groups = ("ga", 6) if wgate else ("gb", 4)
        for end in ("_keep", "_send"):
            outs[key + end] = whole_out((2, 4, groups, 16, width), BF16)
    if wscan:
        outs["gdt"] = whole_out((16, width), F32)
    return kernel_call(body, name, ins, outs, scratch, cost_us, limit)


def owner_back(parts, x, gain, cot, branch, scale_out, mask, inner):
    rows, width = x.shape

    def body(*refs):
        moved = refs[: len(parts)]
        x, gain, cot, branch, scale_out, mask, sent, dmiddle, gain_grad = refs[len(parts) :]
        grad = moved[0][...].astype(F32)
        for p in moved[1:]:
            grad = grad + p[...].astype(F32)
        v = x[...].astype(F32)
        scale = lax.rsqrt(jnp.mean(v * v, axis=1, keepdims=True) + EPS)
        unit = v * scale
        gain_grad[...] = column_sum(grad * unit)
        dn = grad * gain[...]
        dx = scale * (dn - unit * jnp.mean(dn * unit, axis=1, keepdims=True))
        dm = (cot[...].astype(F32) + dx).astype(BF16)
        dmiddle[...] = dm
        g = mask[...] * dm.astype(F32)
        sent[:, 0:width] = g.astype(BF16)
        r = scale_out[...]
        cross = r * r * jnp.sum(g * branch[...], axis=1, keepdims=True) / inner
        sent[:, width:] = in_lanes([r, cross])

    return pl.pallas_call(
        body,
        out_shape=[
            jax.ShapeDtypeStruct((rows, width + LANES), BF16),
            jax.ShapeDtypeStruct((rows, width), BF16),
            jax.ShapeDtypeStruct((1, width), F32),
        ],
        compiler_params=pltpu.CompilerParams(vmem_limit_bytes=VMEM_MOST),
        cost_estimate=pl.CostEstimate(flops=1 << 30, bytes_accessed=1 << 20, transcendentals=0),
        name="owner_back",
    )(*parts, x, gain, cot, branch, scale_out, mask)


def assemble(parts, dt_rows, shard):
    quarter = parts.shape[2]
    block = 16 * 48
    total = 8 * block + 16 * 16 + dt_rows.shape[0]

    def body(_, inw, outw, shared, dt, grad_in, grad_out):
        i = pl.program_id(0)

        @pl.when(i < 8)
        def _columns():
            grad_in[...] = inw[...].reshape(block, quarter).astype(F32)

        @pl.when(i < SLOTS)
        def _out():
            grad_out[...] = outw[...].reshape(block, quarter).astype(F32)

        @pl.when(i == 8)
        def _shared():
            grad_in[...] = jnp.zeros_like(grad_in)
            grad_in[0:256, :] = shared[...].reshape(256, quarter).astype(F32)
            grad_in[256 : 256 + dt_rows.shape[0], :] = dt[...]

    last = SLOTS - 1
    spec = pltpu.PrefetchScalarGridSpec(
        num_scalar_prefetch=1,
        grid=(9,),
        in_specs=[
            pl.BlockSpec(
                (16, 48, quarter),
                lambda i, j: (0, jnp.where(i < SLOTS, 0, 8) + (j[0] + 3 * SLOTS - i) % SLOTS, 0),
            ),
            pl.BlockSpec((16, 48, quarter), lambda i, j: (0, SLOTS + jnp.minimum(i, last), 0)),
            pl.BlockSpec((16, 16, quarter), lambda i, j: (0, 36, 0)),
            pl.BlockSpec(dt_rows.shape, lambda i, j: (0, 0)),
        ],
        out_specs=[
            pl.BlockSpec((block, quarter), lambda i, j: (i, 0)),
            pl.BlockSpec((block, quarter), lambda i, j: (0, jnp.minimum(i, last))),
        ],
    )
    return pl.pallas_call(
        body,
        grid_spec=spec,
        out_shape=[
            jax.ShapeDtypeStruct((total, quarter), F32),
            jax.ShapeDtypeStruct((block, SLOTS * quarter), F32),
        ],
        compiler_params=pltpu.CompilerParams(vmem_limit_bytes=VMEM_MOST),
        name="assemble",
    )(shard.astype(jnp.int32)[None], parts, parts, parts, dt_rows)


def ring(n, k):
    return [(i, (i + k) % n) for i in range(n)]


def send_shard(v, k):
    return lax.ppermute(v, "shard", ring(SLOTS, k)) if k else v


def send_across(v, k):
    pairs = [
        (sec * SLOTS + y, (1 - sec) * SLOTS + (y + k) % SLOTS)
        for sec in range(2)
        for y in range(SLOTS)
    ]
    return lax.ppermute(v, ("section", "shard"), pairs)


def swap_section(v):
    return lax.ppermute(v, "section", [(0, 1), (1, 0)])


def dp_index(x, z, c):
    return x * 8 + z * 2 + c


def dp_pairs(move):
    pairs = []
    for x in range(2):
        for z in range(4):
            for c in range(2):
                pairs.append((dp_index(x, z, c), dp_index(*move(x, z, c))))
    return pairs


def pick(v, index, axis):
    return lax.dynamic_index_in_dim(v, index, axis, keepdims=False)


def gather_slots(v):
    return [send_shard(v, (-k) % SLOTS) for k in range(SLOTS)]


def scatter_sum(slots):
    parts = [send_shard(slots[k], k) for k in range(SLOTS)]
    return sum(p.astype(F32) for p in parts)


def cross_core(v):
    return lax.ppermute(v, DP, dp_pairs(lambda x, z, c: (x, z, 1 - c)))


def sum_small(v):
    v = v + lax.ppermute(v, DP, dp_pairs(lambda x, z, c: (x, z, 1 - c)))
    v = v + sum(
        lax.ppermute(v, DP, dp_pairs(lambda x, z, c: (x, (z + k) % 4, c))) for k in range(1, 4)
    )
    return v + lax.ppermute(v, DP, dp_pairs(lambda x, z, c: (1 - x, z, c)))


def in_order(parts, sign):
    j = lax.axis_index("shard")
    stacked = jnp.stack(parts)
    return jnp.take(stacked, (sign * (jnp.arange(SLOTS) - j)) % SLOTS, axis=0)


def shards(
    tokens,
    cotangent,
    lengths,
    norm_gain,
    in_weight,
    conv_weight,
    conv_bias,
    dt_bias,
    a_log,
    d_skip,
    gate_gain,
    out_weight,
):
    sec = lax.axis_index("section")
    d = lax.axis_index(DP)
    j = lax.axis_index("shard")
    core = d % 2
    first = sec == 0
    width = tokens.shape[2]
    quarter = norm_gain.shape[1]
    channels = conv_bias.shape[1]
    own_cols = gate_gain.shape[1]
    inner = own_cols * SLOTS
    heads = dt_bias.shape[1]
    own_heads = heads // SLOTS
    n_state = 2 * LANES
    piece = own_cols // 16
    piece_bc = n_state // 16
    own_core = (core.astype(jnp.int32)[None], pltpu.SMEM)

    x_own = pick(tokens, sec, 0)
    cot = pick(cotangent, sec, 0)
    length = pick(lengths, sec, 0)
    mask = (jnp.arange(T, dtype=jnp.int32) < length).astype(F32)[:, None]

    columns = jnp.transpose(in_weight[0])
    with jax.named_scope("weights"):

        def cut(start, rows):
            return lax.dynamic_slice(columns, (start, 0), (rows, quarter))

        def columns_of(to):
            return jnp.concatenate(
                [
                    cut(own_cols * to + piece * d, piece),
                    cut(inner + own_cols * to + piece * d, piece),
                    cut(2 * inner + piece_bc * d, piece_bc),
                ],
                axis=0,
            )

        cuts = [columns_of((j + k) % SLOTS) for k in range(SLOTS)]
        o_own = lax.dynamic_slice(out_weight[0], (piece * d, 0), (piece, width))
        o_cut = jnp.transpose(o_own.reshape(piece, SLOTS, quarter), (1, 0, 2))
        first_cut = jnp.concatenate([cuts[0], o_cut.reshape(-1, quarter)], axis=0)

        w_own = [send_shard(cuts[k], k) for k in range(SLOTS)]
        w_other = [send_across(first_cut if k == 0 else cuts[k], k) for k in range(SLOTS)]
        w_other[0], o_other = w_other[0][: cuts[0].shape[0]], w_other[0][cuts[0].shape[0] :]
        o_other = jnp.transpose(o_other.reshape(SLOTS, piece, quarter), (1, 0, 2))
        o_other = o_other.reshape(piece, width)

        def from_parts(parts, others, o, o_others, own):
            pieces = [jnp.where(own, p, q) for p, q in zip(parts, others)]
            lanes = []
            for y in range(SLOTS):
                v = pieces[0]
                for k in range(1, SLOTS):
                    v = jnp.where((j - y) % SLOTS == k, pieces[k], v)
                lanes.append(v)
            return jnp.concatenate(
                [jnp.where(own, o, o_others), jnp.concatenate(lanes, axis=1)], axis=0
            )

        w0 = from_parts(w_own, w_other, o_own, o_other, first)
        w1 = from_parts(w_own, w_other, o_own, o_other, ~first)
        w0, w1, x_own, cot = lax.optimization_barrier((w0, w1, x_own, cot))
        w0 = lax.all_gather(w0, DP, axis=0, tiled=False)
        x_slots = gather_slots(x_own)
        x_slots, norm_gain = lax.optimization_barrier((x_slots, norm_gain))

    with jax.named_scope("small_weights"):
        dt_columns = columns[2 * inner + n_state :]
        sizes = [quarter, 4 * channels, channels, own_cols, heads, heads, heads, heads * quarter]
        flat = jnp.concatenate(
            [
                norm_gain[0],
                conv_weight[0].reshape(-1),
                conv_bias[0],
                gate_gain[0],
                dt_bias[0],
                a_log[0],
                d_skip[0],
                dt_columns.reshape(-1),
            ]
        )
        flat = jnp.pad(flat, (0, -flat.shape[0] % LANES)).reshape(-1, LANES)
        own = in_order(gather_slots(flat), 1)
        other = swap_section(own)
        small = [jnp.where(first, own, other), jnp.where(first, other, own)]

        def unpack(v):
            low = v.reshape(SLOTS, -1)
            at = sum(sizes[:-1])
            dtw = low[:, at : at + sizes[-1]].reshape(SLOTS, heads, quarter)
            dtw = lax.dynamic_slice(dtw, (0, own_heads * j, 0), (SLOTS, own_heads, quarter))
            dtw = jnp.transpose(dtw, (1, 0, 2)).reshape(own_heads, width)
            dtw = jnp.pad(dtw, ((0, LANES - own_heads), (0, 0)))
            v = low[:, :at].astype(F32)
            cut, at = [], 0
            for size in sizes[:-1]:
                cut.append(v[:, at : at + size])
                at += size
            gain = cut[0].reshape(1, width)
            taps = cut[1].reshape(SLOTS, 4, channels).transpose(1, 0, 2).reshape(4, -1)
            bias = cut[2].reshape(1, -1)
            conv = jnp.concatenate([taps, bias, jnp.zeros((3, taps.shape[1]), F32)], axis=0)
            pbcv = conv[:, inner:]
            pv = lax.dynamic_slice(conv, (0, own_cols * j), (8, own_cols))
            pick_heads = lambda u: lax.dynamic_slice(u[0], (own_heads * j,), (own_heads,))
            wide = jnp.repeat(pick_heads(cut[6]), HEAD)[None]
            pv = jnp.concatenate([pv[:5], pick(cut[3], j, 0)[None], wide, pv[7:]], axis=0)
            dtp = jnp.stack([pick_heads(cut[4]), -jnp.exp(pick_heads(cut[5]))])
            dtp = jnp.pad(dtp, ((0, 6), (0, LANES - own_heads)))
            return gain, dtw, pv, pbcv, dtp

        gain0, *params0 = unpack(small[0])
        gain1, *params1 = unpack(small[1])

    x_f = x_own.astype(F32)
    g1 = (mask * cot.astype(F32)).astype(BF16)
    g1_slots = gather_slots(g1)
    w0, x_slots, g1_slots, gain0, params0, gain1, params1, w1 = lax.optimization_barrier(
        (w0, x_slots, g1_slots, gain0, params0, gain1, params1, w1)
    )
    w1 = lax.all_gather(w1, DP, axis=0, tiled=False)
    blocks = lambda v: v.reshape(16, 10, 16, width)

    layer0 = (blocks(w0), *params0)
    layer1 = (blocks(w1), *params1)

    def forward_layer(x, g, gain, layer):
        w, dtw, pv, pbcv, dtp = layer
        return forward(x, g, w, dtw, gain, pv, pbcv, dtp)

    parts, saved0 = forward_layer(x_slots, None, gain0, layer0)
    branch = scatter_sum(parts)
    square = jnp.sum(branch[:, width : width + 3], axis=1, keepdims=True)
    scale0 = lax.rsqrt(square / inner + EPS)
    branch0 = branch[:, :width] * scale0
    middle = (x_f + mask * branch0).astype(BF16)
    saved0 = [saved0]

    m_slots = gather_slots(middle)
    branch_parts, saved1 = forward_layer(m_slots[:2], g1_slots[:2], gain1, layer1)
    m_slots[2], m_slots[3], saved1["stats"] = lax.optimization_barrier(
        (m_slots[2], m_slots[3], saved1["stats"])
    )
    more_parts, more1 = forward_layer(m_slots[2:], g1_slots[2:], gain1, layer1)
    branch_parts = branch_parts + more_parts
    saved1 = [saved1, more1]
    own = jnp.concatenate([v["stats"][:, 0].reshape(2, 2, T) for v in saved1], axis=1)
    back = [send_shard(own, k) for k in range(SLOTS)]
    summed = sum(jnp.roll(back[k], -k, axis=1) for k in range(SLOTS))
    scale1 = lax.rsqrt(summed[0] / inner + EPS)
    cross1 = scale1 * scale1 * scale1 * summed[1] / inner
    rows1 = jnp.pad(jnp.stack([scale1, cross1], axis=1), ((0, 0), (0, 6), (0, 0)))

    def norm_back(x, gain, grad):
        scale = lax.rsqrt(jnp.mean(x * x, axis=1, keepdims=True) + EPS)
        unit = x * scale
        dn = grad * gain
        dx = scale * (dn - unit * jnp.mean(dn * unit, axis=1, keepdims=True))
        return dx, jnp.sum(grad * unit, axis=0)

    back1 = backward(
        ("gate", "scan", "input", "wgate", "wscan"),
        "backward_1",
        28,
        saved1,
        layer1,
        {"g": g1_slots, "rows": rows1},
        VMEM_BACK,
    )
    moved = [send_shard(back1[f"out{k}"], k) for k in range(SLOTS)]
    sent, dmiddle, gain_grad1 = owner_back(
        moved, middle, gain1, cot, branch0, scale0, mask, inner
    )
    owned1 = back1["ga"].reshape(16, -1, width)
    owned1 = lax.psum_scatter(owned1, DP, scatter_dimension=0, tiled=False)
    g0_slots = gather_slots(sent)
    g0_slots, branch_parts = lax.optimization_barrier((g0_slots, branch_parts))
    branch = scatter_sum(branch_parts)[:, :width] * scale1[0][:, None]
    result = middle.astype(F32) + mask * branch

    back0 = backward(
        ("gate", "wgate"),
        "backward_0_gate",
        14,
        saved0,
        layer0,
        {"g": g0_slots, "core": own_core},
    )
    both = lambda kept, moved: (kept.astype(F32) + moved.astype(F32)).astype(BF16)
    a_moved = cross_core(back0["ga_send"])
    small_gate = back0["small"]
    back0["core"] = own_core
    back0.update(backward(("scan", "wscan"), "backward_0_scan", 20, saved0, layer0, back0))
    gb_send, a_moved = lax.optimization_barrier((back0["gb_send"], a_moved))
    a0 = both(back0["ga_keep"], a_moved)
    b0 = both(back0["gb_keep"], cross_core(gb_send))
    owned0 = jnp.pad(a0, ((0, 0), (0, 0), (0, 4), (0, 0), (0, 0)))
    owned0 = lax.dynamic_update_slice(owned0, b0, (0, 0, 6, 0, 0)).reshape(8, -1, width)
    owned0 = lax.psum_scatter(owned0, ("x", "z"), scatter_dimension=0, tiled=False)
    small_scan = back0["small"]
    back0.update(backward(("input",), "backward_0_input", 9, saved0, layer0, back0))
    moved0 = [send_shard(back0[f"out{k}"], k) for k in range(SLOTS)]
    dx, gain_grad0 = norm_back(x_f, gain0, sum(p.astype(F32) for p in moved0))
    dtokens = dmiddle.astype(F32) + dx
    owned1 = owned1 + lax.ppermute(owned1, "section", [(0, 1)])
    owned0, owned1, gain_grad0, dtokens, result = lax.optimization_barrier(
        (owned0, owned1, gain_grad0, dtokens, result)
    )

    kept = jnp.where(first, owned0, owned1).reshape(10, 16, width)
    arrived = lax.ppermute(owned0, "section", [(1, 0)]).reshape(10, 16, width)

    def total_of(cut):
        return (cut(kept).astype(F32) + cut(arrived).astype(F32)).astype(BF16)

    row_slots = []
    for k in range(SLOTS):

        def cut(v):
            v = lax.dynamic_slice_in_dim(v, quarter * ((j + k) % SLOTS), quarter, 2)
            return jnp.concatenate([v[:3], v[6:]], axis=0)

        row_slots.append(send_shard(total_of(cut).reshape(-1, quarter), k))
    out_rows = total_of(lambda v: v[3:6])
    out_rows = jnp.transpose(out_rows.reshape(piece, SLOTS, quarter), (1, 0, 2))
    result_moved = lax.ppermute(result.astype(BF16), "section", [(0, 1)]).astype(F32)
    dtokens_moved = lax.ppermute(dtokens.astype(BF16), "section", [(1, 0)]).astype(F32)
    ends = jnp.where(
        first, jnp.stack([dtokens, dtokens_moved]), jnp.stack([result_moved, result])
    )[None]

    def to_section(v0, v1):
        kept = jnp.where(first, v0, v1).astype(F32)
        return kept + swap_section(jnp.where(first, v1, v0)).astype(F32)

    shared = sum(v[2 * piece :].astype(F32) for v in row_slots).astype(BF16)
    gathered = lax.all_gather(
        jnp.concatenate(
            [v[:piece] for v in row_slots]
            + [out_rows.reshape(-1, quarter)]
            + [v[piece : 2 * piece] for v in row_slots]
            + [shared],
            axis=0,
        ),
        DP,
        tiled=False,
    )

    def small_of(by_pair, back, gain_grad):
        return jnp.concatenate(
            [
                by_pair.reshape(-1, LANES),
                back["small_bc"].reshape(-1, LANES),
                back["small_dt"],
                gain_grad.reshape(-1, LANES),
                back["gdt"].reshape(-1, LANES),
            ],
            axis=0,
        )

    small0 = small_of(small_gate + small_scan, back0, gain_grad0)
    small1 = small_of(back1["small"], back1, gain_grad1)
    small_sum = sum_small(to_section(small0, small1))
    everyone = in_order(gather_slots(small_sum), 1)
    n_pair, n_bc = PAIRS * 8, 2 * 8
    by_pair = everyone[:, :n_pair].reshape(SLOTS, PAIRS, 8, LANES)
    by_pair = by_pair.transpose(2, 0, 1, 3).reshape(8, inner)
    by_bc = jnp.sum(everyone[:, n_pair : n_pair + n_bc], axis=0)
    by_bc = by_bc.reshape(2, 8, LANES).transpose(1, 0, 2).reshape(8, n_state)
    at = n_pair + n_bc
    by_dt = everyone[:, at : at + 8, :own_heads].transpose(1, 0, 2).reshape(8, heads)
    at += 8
    gain_total = jnp.sum(everyone[:, at : at + width // LANES], axis=0).reshape(-1)
    at += width // LANES
    dt_rows = everyone[:, at:].reshape(SLOTS, 16, SLOTS, quarter)[:, :own_heads]
    dt_rows = pick(dt_rows, j, 2).reshape(heads, quarter)
    conv_total = jnp.concatenate([by_pair[:5], by_bc[:5]], axis=1)
    conv_own = lax.dynamic_slice(conv_total, (0, channels * j), (5, channels))
    grad_skip = jnp.sum(by_pair[6].reshape(heads, HEAD), axis=1)

    grad_in_weight, grad_out_weight = assemble(gathered, dt_rows, j)
    return (
        ends,
        lax.dynamic_slice(gain_total, (quarter * j,), (quarter,))[None],
        jnp.transpose(grad_in_weight)[None],
        conv_own[None, :4],
        conv_own[4][None],
        by_dt[0][None],
        by_dt[1][None],
        grad_skip[None],
        lax.dynamic_slice(by_pair[5], (own_cols * j,), (own_cols,))[None],
        grad_out_weight[None],
    )


def solution(mesh):
    sections, copies, owners = mesh.devices.shape
    fine = jax.sharding.Mesh(
        mesh.devices.reshape(sections, 2, copies // 4, 2, owners), ("section", *DP, "shard")
    )
    return jax.shard_map(
        shards,
        mesh=fine,
        in_specs=(
            P((*DP, "shard"), None, None),
            P((*DP, "shard"), None, None),
            P((*DP, "shard")),
            P("section", "shard"),
            P("section", "shard", None),
            P("section", None, "shard"),
            P("section", "shard"),
            P("section", None),
            P("section", None),
            P("section", None),
            P("section", "shard"),
            P("section", "shard", None),
        ),
        out_specs=(
            P("section", (*DP, "shard"), None, None),
            P("section", "shard"),
            P("section", "shard", None),
            P("section", None, "shard"),
            P("section", "shard"),
            P("section", None),
            P("section", None),
            P("section", None),
            P("section", "shard"),
            P("section", "shard", None),
        ),
        check_vma=False,
    )
```

```python
import jax
import jax.numpy as jnp
from jax import lax
from jax.experimental import pallas as pl
from jax.experimental.pallas import tpu as pltpu
from jax.sharding import PartitionSpec as P

F32 = jnp.float32
BF16 = jnp.bfloat16
HI = lax.Precision.HIGHEST
EPS = 1e-05
T = 128
LANES = 128
HEAD = 64
SLOTS = 4
ROWS = SLOTS * T
PAIRS = 6
STEPS = 2
HALF = PAIRS // STEPS
WIDE = HALF * LANES
VMEM_LIMIT = 34 * 1024 * 1024
VMEM_MOST = 60 * 1024 * 1024
VMEM_BACK = 56 * 1024 * 1024
DP = ("x", "z", "core")


def sigmoid(v):
    return 0.5 * jnp.tanh(0.5 * v) + 0.5


def softplus(v):
    return jnp.maximum(v, 0.0) + jnp.log1p(jnp.exp(-jnp.abs(v)))


def dot(a, b):
    return jnp.dot(a, b, preferred_element_type=F32)


def dot_nt(a, b, precision=None):
    return lax.dot_general(
        a, b, (((1,), (1,)), ((), ())), preferred_element_type=F32, precision=precision
    )


def dot_tn(a, b, precision=None):
    return lax.dot_general(
        a, b, (((0,), (0,)), ((), ())), preferred_element_type=F32, precision=precision
    )


def iota(axis):
    return lax.broadcasted_iota(jnp.int32, (T, LANES), axis)


def shift_down(v, steps):
    return jnp.where(iota(0) >= steps, pltpu.roll(v, steps, 0), 0.0)


def shift_up(v, steps):
    return jnp.where(iota(0) < T - steps, pltpu.roll(v, T - steps, 0), 0.0)


def conv_taps(cin):
    return [shift_down(cin, 3), shift_down(cin, 2), shift_down(cin, 1), cin]


def conv_sum(taps, par):
    total = par[4:5, :] + taps[0] * par[0:1, :]
    for k in range(1, 4):
        total = total + taps[k] * par[k : k + 1, :]
    return total


def conv_back(dcv, par):
    total = dcv * par[3:4, :]
    for m in range(1, 4):
        total = total + shift_up(dcv, m) * par[3 - m : 4 - m, :]
    return total


def column_sum(v):
    return jnp.sum(v, axis=0, keepdims=True)


def slot(k):
    return slice(k * T, (k + 1) * T)


def tri(lower):
    if lower:
        return (iota(0) >= iota(1)).astype(F32)
    return (iota(0) <= iota(1)).astype(F32)


def step_prep(k, pbc, dtp, run_col, run_row, step_wide):
    step = softplus(pbc[slot(k), 256:384] + dtp[0:1, :])
    run = jnp.dot(tri(True), step * dtp[1:2, :], precision=HI, preferred_element_type=F32)
    run_row[k] = jnp.transpose(run)
    left = iota(1) < HEAD
    for p in range(PAIRS):
        a, b = 2 * p, 2 * p + 1
        run_col[a, slot(k), :] = jnp.broadcast_to(run[:, a : a + 1], (T, LANES))
        run_col[b, slot(k), :] = jnp.broadcast_to(run[:, b : b + 1], (T, LANES))
        step_wide[p, slot(k), :] = jnp.where(
            left,
            jnp.broadcast_to(step[:, a : a + 1], (T, LANES)),
            jnp.broadcast_to(step[:, b : b + 1], (T, LANES)),
        )
    return step


def halves(v):
    left = iota(1) < HEAD
    zero = jnp.zeros_like(v)
    return jnp.concatenate([jnp.where(left, v, zero), jnp.where(left, zero, v)], axis=0)


def in_lanes(columns):
    lane = lax.broadcasted_iota(jnp.int32, (columns[0].shape[0], LANES), 1)
    out = jnp.zeros(lane.shape, F32)
    for n, v in enumerate(columns):
        for k in range(3):
            part = v.astype(BF16).astype(F32)
            out = jnp.where(lane == 3 * n + k, part, out)
            v = v - part
    return out.astype(BF16)


def from_lanes(v, n):
    return sum(v[:, 3 * n + k : 3 * n + k + 1].astype(F32) for k in range(3))


class Refs:
    pass


def kernel_call(body, name, ins, outs, scratch, cost_us, limit=VMEM_LIMIT):
    in_names, out_names, scratch_names = list(ins), list(outs), list(scratch)

    def run(*refs):
        for h in range(STEPS):
            rf = Refs()
            for key, ref in zip(in_names + out_names + scratch_names, refs):
                spec = ins.get(key) or outs.get(key)
                blocks = spec[-2:] if spec and len(spec) > 2 else None
                if blocks and blocks[1](1) != blocks[1](0):
                    at = [
                        slice(n * size, (n + 1) * size) if n else slice(0, size)
                        for n, size in zip(blocks[1](h), blocks[0])
                    ]
                    setattr(rf, key + "_whole", ref)
                    ref = ref.at[tuple(at)]
                setattr(rf, key, ref)
            body(rf, h)

    res = pl.pallas_call(
        run,
        in_specs=[
            pl.BlockSpec(memory_space=pltpu.VMEM if len(ins[n]) > 2 else ins[n][1])
            for n in in_names
        ],
        out_specs=[pl.BlockSpec(memory_space=pltpu.VMEM) for n in out_names],
        out_shape=[jax.ShapeDtypeStruct(outs[n][0], outs[n][1]) for n in out_names],
        scratch_shapes=[
            pltpu.VMEM(*scratch[n]) if isinstance(scratch[n], tuple) else scratch[n]
            for n in scratch_names
        ],
        compiler_params=pltpu.CompilerParams(vmem_limit_bytes=limit),
        cost_estimate=pl.CostEstimate(
            flops=int(cost_us * 1.1e9), bytes_accessed=1 << 20, transcendentals=0
        ),
        name=name,
    )(*[ins[n][0] for n in in_names])
    return dict(zip(out_names, res))


def when(condition):
    return (lambda f: f()) if condition else (lambda f: None)


def whole(v):
    return (v, v.shape, lambda h: (0,) * v.ndim)


def whole_out(shape, dtype):
    return (shape, dtype, shape, lambda h: (0,) * len(shape))


def by_step(v, block):
    return (v, block, lambda h: (h,) + (0,) * (len(block) - 1))


def by_step_out(shape, dtype, block):
    return (shape, dtype, block, lambda h: (h,) + (0,) * (len(block) - 1))


def lanes_by_step(v):
    return (v, (v.shape[0], WIDE), lambda h: (0, h))


def lanes_by_step_out(shape, dtype):
    return (shape, dtype, (shape[0], WIDE), lambda h: (0, h))


def in_hbm(v):
    return (v, pltpu.HBM)


WEIGHT_GROUPS = {"wo": (0, 3), "wg": (3, 3), "wv": (6, 3), "ws": (9, 1)}


class Copies:
    def __init__(self, sems):
        self.sems, self.copies = sems, {}

    def add(self, key, source, target):
        self.copies[key] = (source, target, self.sems.at[len(self.copies)])

    def add_weights(self, rf, keys):
        for key in keys:
            at, count = WEIGHT_GROUPS[key]
            self.add(key, rf.w.at[:, pl.ds(at, count)], getattr(rf, key))

    def start(self):
        for copy in self.copies.values():
            pltpu.make_async_copy(*copy).start()

    def wait(self, *keys):
        for key in keys:
            pltpu.make_async_copy(*self.copies[key]).wait()


def weight_scratch(scratch, keys, width):
    for key in keys:
        scratch[key] = ((16, WEIGHT_GROUPS[key][1], 16, width), BF16)


def half_rows(ref, h):
    v = ref[pl.ds(8 * h, 8)]
    return v.reshape(WIDE, v.shape[-1])


def pair_lanes(p):
    return slice(p * LANES, (p + 1) * LANES)


def flat_rows(ref):
    v = ref[...]
    return v.reshape(-1, v.shape[-1])


def mixed_bc(rf, k, c):
    lanes = slice(c * LANES, (c + 1) * LANES)
    cv = conv_sum(conv_taps(rf.pbc[slot(k), lanes]), rf.pbcv[:, lanes])
    return cv * sigmoid(cv)


def forward(x_slots, g_slots, w, dtw, gain, pv, pbcv, dtp):
    width = x_slots[0].shape[1]
    with_grad = g_slots is not None

    def body(rf, h):
        copies = Copies(rf.sems)
        for k in range(SLOTS):
            copies.add(f"x{k}", getattr(rf, f"x{k}"), rf.x_all.at[k])
        copies.add_weights(rf, ("ws", "wg", "wv", "wo"))
        if with_grad:
            for k in range(SLOTS):
                copies.add(f"g{k}", getattr(rf, f"g{k}"), rf.g_all.at[slot(k)])

        @when(h == 0)
        def _prep():
            copies.start()
            for k in range(SLOTS):
                copies.wait(f"x{k}")
                x = rf.x_all[k].astype(F32)
                scale = lax.rsqrt(jnp.mean(x * x, axis=1, keepdims=True) + EPS)
                rf.normed[slot(k), :] = (x * scale * rf.gain[...]).astype(BF16)
            copies.wait("ws")
            rf.pbc[:, 0:256] = dot_nt(rf.normed[...], flat_rows(rf.ws))
            rf.pbc[:, 256:384] = dot_nt(rf.normed[...], rf.dtw[...])
            for k in range(SLOTS):
                rf.scores[k] = dot_nt(mixed_bc(rf, k, 1), mixed_bc(rf, k, 0), HI) * tri(True)
                step_prep(k, rf.pbc, rf.dtp, rf.run_col, rf.run_row, rf.step_wide)
            rf.square[...] = jnp.zeros_like(rf.square)
            rf.cross[...] = jnp.zeros_like(rf.cross)
            copies.wait("wg", "wv", "wo")
            if with_grad:
                copies.wait(*[f"g{k}" for k in range(SLOTS)])

        rf.proj[0, :, 0:WIDE] = dot_nt(rf.normed[...], half_rows(rf.wg, h))
        rf.proj[0, :, WIDE : 2 * WIDE] = dot_nt(rf.normed[...], half_rows(rf.wv, h))
        if with_grad:
            q_all = dot_nt(rf.g_all[...], half_rows(rf.wo, h))
        for p in range(HALF):
            lanes = pair_lanes(p)
            par = rf.pv[:, lanes]
            pair = HALF * h + p
            for k in range(SLOTS):
                gate = rf.proj[0, slot(k), lanes]
                cv = conv_sum(
                    conv_taps(rf.proj[0, slot(k), WIDE + p * LANES : WIDE + (p + 1) * LANES]), par
                )
                values = cv * sigmoid(cv)
                scaled = (values * rf.step_wide[pair, slot(k), :]).astype(BF16)
                weights = []
                for a in range(2):
                    gap = (
                        rf.run_col[2 * pair + a, slot(k), :]
                        - rf.run_row[k, pl.ds(2 * pair + a, 1), :]
                    )
                    decay = jnp.exp(jnp.minimum(gap, 0.0))
                    weights.append((rf.scores[k] * decay).astype(BF16))
                y = dot(jnp.concatenate(weights, axis=1), halves(scaled))
                rf.y[0, slot(k), lanes] = y
                scanned = y + par[6:7, :] * values
                gated = scanned * (gate * sigmoid(gate))
                rf.square[slot(k), :] += gated * gated
                scaled_out = gated * par[5:6, :]
                rf.u_all[h, slot(k), lanes] = scaled_out.astype(BF16)
                if with_grad:
                    rf.cross[slot(k), :] += q_all[slot(k), lanes] * scaled_out

        @when(h == STEPS - 1)
        def _finish():
            u = jnp.concatenate([rf.u_all[a] for a in range(STEPS)], axis=1)
            for n in range(0, width, 512):
                part = dot(u, rf.wo[:, :, :, n : n + 512].reshape(STEPS * WIDE, 512)).astype(BF16)
                for k in range(SLOTS):
                    getattr(rf, f"out{k}")[:, n : n + 512] = part[slot(k), :]
            for k in range(SLOTS):
                total = jnp.sum(rf.square[slot(k), :], axis=1, keepdims=True)
                getattr(rf, f"out{k}")[:, width:] = in_lanes([total])
            ones = jnp.ones((8, LANES), F32)
            rf.stats[0] = dot_nt(ones, rf.square[...], HI)
            rf.stats[1] = dot_nt(ones, rf.cross[...], HI)

    ins = {f"x{k}": in_hbm(v) for k, v in enumerate(x_slots)}
    if with_grad:
        ins.update({f"g{k}": in_hbm(v) for k, v in enumerate(g_slots)})
    ins.update(
        gain=whole(gain),
        w=in_hbm(w),
        dtw=whole(dtw),
        pv=lanes_by_step(pv),
        pbcv=whole(pbcv),
        dtp=whole(dtp),
    )
    outs = {f"out{k}": whole_out((T, width + LANES), BF16) for k in range(SLOTS)}
    outs.update(
        stats=whole_out((2, 8, ROWS), F32),
        normed=whole_out((ROWS, width), BF16),
        proj=by_step_out((STEPS, ROWS, 2 * WIDE), F32, (1, ROWS, 2 * WIDE)),
        y=by_step_out((STEPS, ROWS, WIDE), F32, (1, ROWS, WIDE)),
        pbc=whole_out((ROWS, 384), F32),
    )
    scratch = dict(
        scores=((SLOTS, T, T), F32),
        run_col=((2 * PAIRS, ROWS, LANES), F32),
        run_row=((SLOTS, T, LANES), F32),
        step_wide=((PAIRS, ROWS, LANES), F32),
        u_all=((STEPS, ROWS, WIDE), BF16),
        square=((ROWS, LANES), F32),
        cross=((ROWS, LANES), F32),
        x_all=((SLOTS, T, width), BF16),
        sems=pltpu.SemaphoreType.DMA((2 * SLOTS + 4,)),
    )
    weight_scratch(scratch, ("ws", "wg", "wv", "wo"), width)
    if with_grad:
        scratch["g_all"] = ((ROWS, width), BF16)
    res = kernel_call(body, "layer_forward", ins, outs, scratch, 18, VMEM_MOST)
    return [res[f"out{k}"] for k in range(SLOTS)], res


def head_columns(pair):
    target = 2 * pair + (iota(0) >= HEAD).astype(jnp.int32)
    one = (iota(1) == target).astype(BF16)
    return jnp.concatenate([one, one], axis=0)


def head_sum(v, columns):
    high = v.astype(BF16)
    low = (v - high.astype(F32)).astype(BF16)
    return dot(jnp.concatenate([high, low], axis=1), columns)


def put_by_core(rf, key, x, at, part):
    keep, send = getattr(rf, key + "_keep"), getattr(rf, key + "_send")
    groups = slice(at, at + part.shape[2])
    for c in range(2):

        @pl.when(rf.core[0] == c)
        def _store(c=c):
            for z in range(4):
                keep[x, z, groups] = part[z, c]
                send[x, z, groups] = part[z, 1 - c]


def backward(stages, name, cost_us, saved, layer, have, limit=VMEM_LIMIT):
    gate, scan, inp, wgate, wscan = (
        s in stages for s in ("gate", "scan", "input", "wgate", "wscan")
    )
    width = saved["normed"].shape[1]
    w, dtw, pv, pbcv, dtp = layer
    elementwise = gate or scan
    fetched = (("wo",) if gate else ()) + (("wg", "wv", "ws") if inp else ())
    in_slots = gate and "rows" not in have

    def body(rf, h):
        copies = Copies(rf.sems) if gate or wgate or inp else None
        if gate or wgate:
            for k in range(SLOTS):
                source = getattr(rf, f"g{k}")
                copies.add(f"g{k}", source.at[:, pl.ds(0, width)], rf.g_all.at[slot(k)])
                if in_slots:
                    copies.add(f"e{k}", source.at[:, pl.ds(width, LANES)], rf.e_all.at[k])
        if copies:
            copies.add_weights(rf, fetched)

        @when(h == 0)
        def _prep():
            if copies:
                copies.start()
            for k in range(SLOTS):
                if gate or wgate:
                    copies.wait(f"g{k}")
                if in_slots:
                    copies.wait(f"e{k}")
                if gate:
                    for row, ref in ((0, rf.scale_row), (1, rf.cross_row)):
                        if "rows" in have:
                            ref[slot(k), :] = jnp.transpose(
                                jnp.broadcast_to(rf.rows[k, row : row + 1, :], (T, LANES))
                            )
                        else:
                            column = from_lanes(rf.e_all[k], row)
                            ref[slot(k), :] = jnp.broadcast_to(column, (T, LANES))
                if scan:
                    inbound, outbound = mixed_bc(rf, k, 0), mixed_bc(rf, k, 1)
                    rf.mixed[0, slot(k), :] = inbound
                    rf.mixed[1, slot(k), :] = outbound
                    rf.scores[k] = dot_nt(inbound, outbound, HI) * tri(False)
                    rf.step_all[slot(k), :] = step_prep(
                        k, rf.pbc, rf.dtp, rf.run_col, rf.run_row, rf.step_wide
                    )
            if scan:
                rf.dscores[...] = jnp.zeros_like(rf.dscores)
                rf.dstep[...] = jnp.zeros_like(rf.dstep)
                rf.drun[...] = jnp.zeros_like(rf.drun)
            if inp:
                rf.total[...] = jnp.zeros_like(rf.total)
            if copies:
                copies.wait(*fetched)

        if gate:
            q_all = dot_nt(rf.g_all[...], half_rows(rf.wo, h))
        for p in range(HALF if elementwise else 0):
            lanes = pair_lanes(p)
            par = rf.pv[:, lanes]
            pair = HALF * h + p
            sums = [jnp.zeros((1, LANES), F32) for _ in range(8)]
            if scan:
                columns = head_columns(pair)
            for k in range(SLOTS):
                taps = conv_taps(rf.proj[0, slot(k), WIDE + p * LANES : WIDE + (p + 1) * LANES])
                cv = conv_sum(taps, par)
                sig_c = sigmoid(cv)
                values = cv * sig_c
                y = rf.y[0, slot(k), lanes]
                if gate:
                    gate_in = rf.proj[0, slot(k), lanes]
                    sig_g = sigmoid(gate_in)
                    silu_g = gate_in * sig_g
                    scanned = y + par[6:7, :] * values
                    gated = scanned * silu_g
                    grad_no = q_all[slot(k), lanes]
                    scale = rf.scale_row[slot(k), :]
                    dgated = scale * (grad_no * par[5:6, :]) - rf.cross_row[slot(k), :] * gated
                    norm = gated * scale
                    sums[5] += column_sum(grad_no * norm)
                    rf.u[slot(k), lanes] = (norm * par[5:6, :]).astype(BF16)
                    dscan = dgated * silu_g
                    dgate = dgated * scanned * (sig_g * (1.0 + gate_in * (1.0 - sig_g)))
                    sums[6] += column_sum(dscan * values)
                    rf.dg[slot(k), lanes] = dgate.astype(BF16)
                    if not scan:
                        rf.dscan[slot(k), lanes] = dscan
                else:
                    dscan = rf.dscan[slot(k), lanes]
                if not scan:
                    continue
                wide = rf.step_wide[pair, slot(k), :]
                dy = dscan.astype(BF16)
                scaled = (values * wide).astype(BF16)
                dweights = dot_nt(halves(scaled), dy)
                weights = []
                dscore = rf.dscores[k]
                for a in range(2):
                    gap = (
                        rf.run_row[k, pl.ds(2 * pair + a, 1), :]
                        - rf.run_col[2 * pair + a, slot(k), :]
                    )
                    decay = jnp.exp(jnp.minimum(gap, 0.0))
                    weights.append((rf.scores[k] * decay).astype(BF16))
                    dscore = dscore + dweights[slot(a), :] * decay
                rf.dscores[k] = dscore
                dscaled = dot(jnp.concatenate(weights, axis=1), halves(dy))
                rf.dstep[slot(k), :] += head_sum(dscaled * values, columns)
                rf.drun[slot(k), :] += head_sum(
                    dy.astype(F32) * y - scaled.astype(F32) * dscaled, columns
                )
                dvalues = dscaled * wide + par[6:7, :] * dscan
                dcv = dvalues * (sig_c * (1.0 + cv * (1.0 - sig_c)))
                for t in range(4):
                    sums[t] += column_sum(dcv * taps[t])
                sums[4] += column_sum(dcv)
                rf.dv[slot(k), lanes] = conv_back(dcv, par).astype(BF16)
            rf.small[p] = jnp.concatenate(sums, axis=0)
        if wgate and wscan:
            for at, left, right in (
                (0, rf.dg, rf.normed),
                (3, rf.u, rf.g_all),
                (6, rf.dv, rf.normed),
            ):
                part = dot_tn(left[...], right[...]).astype(BF16)
                rf.ga[:, at : at + 3] = part.reshape(8, 3, 16, width)
            if not scan:
                part = dot_tn(rf.dbc_half[...], rf.normed[...]).astype(BF16)
                rf.ga[:, 9] = part.reshape(8, 16, width)
        elif wgate:
            for at, left, right in ((0, rf.dg, rf.normed), (3, rf.u, rf.g_all)):
                part = dot_tn(left[...], right[...]).astype(BF16)
                put_by_core(rf, "ga", h, at, part.reshape(4, 2, 3, 16, width))
        elif wscan:
            part = dot_tn(rf.dv[...], rf.normed[...]).astype(BF16)
            put_by_core(rf, "gb", h, 0, part.reshape(4, 2, 3, 16, width))
        if inp:
            rf.total[...] += dot(rf.dg[...], half_rows(rf.wg, h)) + dot(
                rf.dv[...], half_rows(rf.wv, h)
            )

        @when(h == STEPS - 1)
        def _finish():
            if scan:
                sums = [[jnp.zeros((1, LANES), F32) for _ in range(8)] for _ in range(2)]
                dt_sums = [jnp.zeros((1, LANES), F32) for _ in range(8)]
                live = iota(1) < 2 * PAIRS
                for k in range(SLOTS):
                    dscore = rf.dscores[k] * tri(False)
                    dmixed = (
                        jnp.dot(
                            dscore,
                            rf.mixed[1, slot(k), :],
                            precision=HI,
                            preferred_element_type=F32,
                        ),
                        dot_tn(dscore, rf.mixed[0, slot(k), :], HI),
                    )
                    for c in range(2):
                        lanes = slice(c * LANES, (c + 1) * LANES)
                        par = rf.pbcv[:, lanes]
                        taps = conv_taps(rf.pbc[slot(k), lanes])
                        cv = conv_sum(taps, par)
                        sig = sigmoid(cv)
                        dcv = dmixed[c] * (sig * (1.0 + cv * (1.0 - sig)))
                        for t in range(4):
                            sums[c][t] += column_sum(dcv * taps[t])
                        sums[c][4] += column_sum(dcv)
                        rf.dbc[slot(k), lanes] = conv_back(dcv, par).astype(BF16)
                    dlog = jnp.dot(
                        tri(False), rf.drun[slot(k), :], precision=HI, preferred_element_type=F32
                    )
                    grad_step = rf.dstep[slot(k), :] + dlog * rf.dtp[1:2, :]
                    dt_sums[1] += column_sum(dlog * rf.step_all[slot(k), :])
                    draw = grad_step * sigmoid(rf.pbc[slot(k), 256:384] + rf.dtp[0:1, :])
                    draw = jnp.where(live, draw, 0.0)
                    dt_sums[0] += column_sum(draw)
                    rf.dbc[slot(k), 256:384] = draw.astype(BF16)
                rf.small_bc[0] = jnp.concatenate(sums[0], axis=0)
                rf.small_bc[1] = jnp.concatenate(sums[1], axis=0)
                dt_sums[1] = dt_sums[1] * rf.dtp[1:2, :]
                rf.small_dt[...] = jnp.concatenate(dt_sums, axis=0)
            if wscan and wgate and scan:
                part = dot_tn(rf.dbc[:, 0:256], rf.normed[...]).astype(BF16)
                rf.ga_whole[:, 9] = part.reshape(16, 16, width)
            if wscan and not wgate:
                part = dot_tn(rf.dbc[:, 0:256], rf.normed[...]).astype(BF16)
                part = part.reshape(2, 4, 2, 1, 16, width)
                for a in range(2):
                    put_by_core(rf, "gb", a, 3, part[a])
            if wscan:
                rf.gdt[...] = dot_tn(rf.dbc[:, 256:384], rf.normed[...])[0:16]
            if inp:
                final = (
                    rf.total[...]
                    + dot(rf.dbc[:, 0:256], flat_rows(rf.ws))
                    + dot(rf.dbc[:, 256:384], rf.dtw[...])
                )
                for k in range(SLOTS):
                    getattr(rf, f"out{k}")[...] = final[slot(k), :].astype(BF16)

    ins, outs, scratch = {}, {}, {}
    heads_cols = STEPS * WIDE
    if gate or wgate:
        for k, v in enumerate(have["g"]):
            ins[f"g{k}"] = in_hbm(v)
        scratch["g_all"] = ((ROWS, width), BF16)
    if gate:
        if in_slots:
            scratch["e_all"] = ((SLOTS, T, LANES), BF16)
        else:
            ins["rows"] = whole(have["rows"])
        scratch["scale_row"] = ((ROWS, LANES), F32)
        scratch["cross_row"] = ((ROWS, LANES), F32)
        outs["u"] = lanes_by_step_out((ROWS, heads_cols), BF16)
        outs["dg"] = lanes_by_step_out((ROWS, heads_cols), BF16)
        if not scan:
            outs["dscan"] = lanes_by_step_out((ROWS, heads_cols), F32)
    if elementwise:
        ins["proj"] = by_step(saved["proj"], (1, ROWS, 2 * WIDE))
        ins["y"] = by_step(saved["y"], (1, ROWS, WIDE))
        ins["pv"] = lanes_by_step(pv)
        outs["small"] = by_step_out((PAIRS, 8, LANES), F32, (HALF, 8, LANES))
    if scan:
        ins["pbc"] = whole(saved["pbc"])
        ins["pbcv"] = whole(pbcv)
        ins["dtp"] = whole(dtp)
        if not gate:
            ins["dscan"] = lanes_by_step(have["dscan"])
        outs["dv"] = lanes_by_step_out((ROWS, heads_cols), BF16)
        outs["dbc"] = whole_out((ROWS, 384), BF16)
        outs["small_bc"] = whole_out((2, 8, LANES), F32)
        outs["small_dt"] = whole_out((8, LANES), F32)
        scratch.update(
            mixed=((2, ROWS, LANES), F32),
            scores=((SLOTS, T, T), F32),
            run_col=((2 * PAIRS, ROWS, LANES), F32),
            run_row=((SLOTS, T, LANES), F32),
            step_wide=((PAIRS, ROWS, LANES), F32),
            step_all=((ROWS, LANES), F32),
            dscores=((SLOTS, T, T), F32),
            dstep=((ROWS, LANES), F32),
            drun=((ROWS, LANES), F32),
        )
    if inp:
        ins["dtw"] = whole(dtw)
        scratch["total"] = ((ROWS, width), F32)
        outs.update({f"out{k}": whole_out((T, width), BF16) for k in range(SLOTS)})
    if fetched:
        ins["w"] = in_hbm(w)
        weight_scratch(scratch, fetched, width)
    if gate or wgate or inp:
        scratch["sems"] = pltpu.SemaphoreType.DMA((2 * SLOTS + 4,))
    if wgate or wscan:
        ins["normed"] = whole(saved["normed"])
    if not gate and (wgate or inp):
        ins["dg"] = lanes_by_step(have["dg"])
    if wgate and not gate:
        ins["u"] = lanes_by_step(have["u"])
    if not scan and (wscan or inp):
        ins["dv"] = lanes_by_step(have["dv"])
        ins["dbc"] = whole(have["dbc"])
    if wgate and wscan:
        if not scan:
            ins["dbc_half"] = (have["dbc"], (ROWS, LANES), lambda h: (0, h))
        outs["ga"] = by_step_out((16, 10, 16, width), BF16, (8, 10, 16, width))
    elif wgate or wscan:
        ins["core"] = have["core"]
        key, groups = ("ga", 6) if wgate else ("gb", 4)
        for end in ("_keep", "_send"):
            outs[key + end] = whole_out((2, 4, groups, 16, width), BF16)
    if wscan:
        outs["gdt"] = whole_out((16, width), F32)
    return kernel_call(body, name, ins, outs, scratch, cost_us, limit)


def assemble(parts, dt_rows):
    quarter = parts.shape[2]
    block = 16 * 48
    total = 8 * block + 16 * 16 + dt_rows.shape[0]

    def body(inw, outw, shared, dt, grad_in, grad_out):
        i = pl.program_id(0)

        @pl.when(i < 8)
        def _columns():
            grad_in[...] = inw[...].reshape(block, quarter).astype(F32)

        @pl.when(i < SLOTS)
        def _out():
            grad_out[...] = outw[...].reshape(block, quarter).astype(F32)

        @pl.when(i == 8)
        def _shared():
            grad_in[...] = jnp.zeros_like(grad_in)
            grad_in[0:256, :] = shared[...].reshape(256, quarter).astype(F32)
            grad_in[256 : 256 + dt_rows.shape[0], :] = dt[...]

    last = SLOTS - 1
    return pl.pallas_call(
        body,
        grid=(9,),
        in_specs=[
            pl.BlockSpec(
                (16, 48, quarter),
                lambda i: (0, jnp.where(i < SLOTS, i, jnp.minimum(i + SLOTS, 11)), 0),
            ),
            pl.BlockSpec((16, 48, quarter), lambda i: (0, SLOTS + jnp.minimum(i, last), 0)),
            pl.BlockSpec((16, 16, quarter), lambda i: (0, 36, 0)),
            pl.BlockSpec(dt_rows.shape, lambda i: (0, 0)),
        ],
        out_specs=[
            pl.BlockSpec((block, quarter), lambda i: (i, 0)),
            pl.BlockSpec((block, quarter), lambda i: (0, jnp.minimum(i, last))),
        ],
        out_shape=[
            jax.ShapeDtypeStruct((total, quarter), F32),
            jax.ShapeDtypeStruct((block, SLOTS * quarter), F32),
        ],
        compiler_params=pltpu.CompilerParams(vmem_limit_bytes=VMEM_MOST),
        name="assemble",
    )(parts, parts, parts, dt_rows)


def ring(n, k):
    return [(i, (i + k) % n) for i in range(n)]


def send_shard(v, k):
    return lax.ppermute(v, "shard", ring(SLOTS, k)) if k else v


def across(v):
    return lax.all_to_all(v, ("section", "shard"), 0, 0)


def swap_section(v):
    return lax.ppermute(v, "section", [(0, 1), (1, 0)])


def dp_index(x, z, c):
    return x * 8 + z * 2 + c


def dp_pairs(move):
    pairs = []
    for x in range(2):
        for z in range(4):
            for c in range(2):
                pairs.append((dp_index(x, z, c), dp_index(*move(x, z, c))))
    return pairs


def pick(v, index, axis):
    return lax.dynamic_index_in_dim(v, index, axis, keepdims=False)


def gather_slots(v):
    return [send_shard(v, (-k) % SLOTS) for k in range(SLOTS)]


def scatter_sum(slots):
    parts = [send_shard(slots[k], k) for k in range(SLOTS)]
    return sum(p.astype(F32) for p in parts)


def cross_core(v):
    return lax.ppermute(v, DP, dp_pairs(lambda x, z, c: (x, z, 1 - c)))


def sum_small(v):
    v = v + lax.ppermute(v, DP, dp_pairs(lambda x, z, c: (x, z, 1 - c)))
    v = v + sum(
        lax.ppermute(v, DP, dp_pairs(lambda x, z, c: (x, (z + k) % 4, c))) for k in range(1, 4)
    )
    return v + lax.ppermute(v, DP, dp_pairs(lambda x, z, c: (1 - x, z, c)))


def in_order(parts, sign):
    j = lax.axis_index("shard")
    stacked = jnp.stack(parts)
    return jnp.take(stacked, (sign * (jnp.arange(SLOTS) - j)) % SLOTS, axis=0)


def shards(
    tokens,
    cotangent,
    lengths,
    norm_gain,
    in_weight,
    conv_weight,
    conv_bias,
    dt_bias,
    a_log,
    d_skip,
    gate_gain,
    out_weight,
):
    sec = lax.axis_index("section")
    d = lax.axis_index(DP)
    j = lax.axis_index("shard")
    core = d % 2
    first = sec == 0
    width = tokens.shape[2]
    quarter = norm_gain.shape[1]
    channels = conv_bias.shape[1]
    own_cols = gate_gain.shape[1]
    inner = own_cols * SLOTS
    heads = dt_bias.shape[1]
    own_heads = heads // SLOTS
    n_state = 2 * LANES
    piece = own_cols // 16
    piece_bc = n_state // 16
    own_core = (core.astype(jnp.int32)[None], pltpu.SMEM)

    x_own = pick(tokens, sec, 0)
    cot = pick(cotangent, sec, 0)
    length = pick(lengths, sec, 0)
    mask = (jnp.arange(T, dtype=jnp.int32) < length).astype(F32)[:, None]

    columns = jnp.transpose(in_weight[0])
    with jax.named_scope("weights"):

        def cut(start, rows):
            return lax.dynamic_slice(columns, (start, 0), (rows, quarter))

        def columns_of(to):
            return jnp.concatenate(
                [
                    cut(own_cols * to + piece * d, piece),
                    cut(inner + own_cols * to + piece * d, piece),
                    cut(2 * inner + piece_bc * d, piece_bc),
                ],
                axis=0,
            )

        cuts = jnp.stack([columns_of(y) for y in range(SLOTS)])
        got = across(jnp.concatenate([cuts, cuts], axis=0))
        o_own = lax.dynamic_slice(out_weight[0], (piece * d, 0), (piece, width))
        o_other = swap_section(o_own)

        def whole_rows(layer, own):
            rows = jnp.concatenate([got[SLOTS * layer + y] for y in range(SLOTS)], axis=1)
            return jnp.concatenate([jnp.where(own, o_own, o_other), rows], axis=0)

        w0 = whole_rows(0, first)
        w1 = whole_rows(1, ~first)
        w0, w1, x_own, cot = lax.optimization_barrier((w0, w1, x_own, cot))
        w0 = lax.all_gather(w0, DP, axis=0, tiled=False)
        x_slots = gather_slots(x_own)
        x_slots, norm_gain = lax.optimization_barrier((x_slots, norm_gain))

    with jax.named_scope("small_weights"):
        dt_columns = columns[2 * inner + n_state :]
        sizes = [quarter, 4 * channels, channels, own_cols, heads, heads, heads, heads * quarter]
        flat = jnp.concatenate(
            [
                norm_gain[0],
                conv_weight[0].reshape(-1),
                conv_bias[0],
                gate_gain[0],
                dt_bias[0],
                a_log[0],
                d_skip[0],
                dt_columns.reshape(-1),
            ]
        )
        flat = jnp.pad(flat, (0, -flat.shape[0] % LANES)).reshape(-1, LANES)
        own = in_order(gather_slots(flat), 1)
        other = swap_section(own)
        small = [jnp.where(first, own, other), jnp.where(first, other, own)]

        def unpack(v):
            low = v.reshape(SLOTS, -1)
            at = sum(sizes[:-1])
            dtw = low[:, at : at + sizes[-1]].reshape(SLOTS, heads, quarter)
            dtw = lax.dynamic_slice(dtw, (0, own_heads * j, 0), (SLOTS, own_heads, quarter))
            dtw = jnp.transpose(dtw, (1, 0, 2)).reshape(own_heads, width)
            dtw = jnp.pad(dtw, ((0, LANES - own_heads), (0, 0)))
            v = low[:, :at].astype(F32)
            cut, at = [], 0
            for size in sizes[:-1]:
                cut.append(v[:, at : at + size])
                at += size
            gain = cut[0].reshape(1, width)
            taps = cut[1].reshape(SLOTS, 4, channels).transpose(1, 0, 2).reshape(4, -1)
            bias = cut[2].reshape(1, -1)
            conv = jnp.concatenate([taps, bias, jnp.zeros((3, taps.shape[1]), F32)], axis=0)
            pbcv = conv[:, inner:]
            pv = lax.dynamic_slice(conv, (0, own_cols * j), (8, own_cols))
            pick_heads = lambda u: lax.dynamic_slice(u[0], (own_heads * j,), (own_heads,))
            wide = jnp.repeat(pick_heads(cut[6]), HEAD)[None]
            pv = jnp.concatenate([pv[:5], pick(cut[3], j, 0)[None], wide, pv[7:]], axis=0)
            dtp = jnp.stack([pick_heads(cut[4]), -jnp.exp(pick_heads(cut[5]))])
            dtp = jnp.pad(dtp, ((0, 6), (0, LANES - own_heads)))
            return gain, dtw, pv, pbcv, dtp

        gain0, *params0 = unpack(small[0])
        gain1, *params1 = unpack(small[1])

    x_f = x_own.astype(F32)
    g1 = (mask * cot.astype(F32)).astype(BF16)
    g1_slots = gather_slots(g1)
    w0, x_slots, g1_slots, gain0, params0, gain1, params1, w1 = lax.optimization_barrier(
        (w0, x_slots, g1_slots, gain0, params0, gain1, params1, w1)
    )
    w1 = lax.all_gather(w1, DP, axis=0, tiled=False)
    blocks = lambda v: v.reshape(16, 10, 16, width)

    layer0 = (blocks(w0), *params0)
    layer1 = (blocks(w1), *params1)

    def forward_layer(x, g, gain, layer):
        w, dtw, pv, pbcv, dtp = layer
        return forward(x, g, w, dtw, gain, pv, pbcv, dtp)

    parts, saved0 = forward_layer(x_slots, None, gain0, layer0)
    branch = scatter_sum(parts)
    square = jnp.sum(branch[:, width : width + 3], axis=1, keepdims=True)
    scale0 = lax.rsqrt(square / inner + EPS)
    branch0 = branch[:, :width] * scale0
    middle = (x_f + mask * branch0).astype(BF16)

    m_slots = gather_slots(middle)
    branch_parts, saved1 = forward_layer(m_slots, g1_slots, gain1, layer1)
    own = saved1["stats"][:, 0].reshape(2, SLOTS, T)
    back = [send_shard(own, k) for k in range(SLOTS)]
    summed = sum(jnp.roll(back[k], -k, axis=1) for k in range(SLOTS))
    scale1 = lax.rsqrt(summed[0] / inner + EPS)
    cross1 = scale1 * scale1 * scale1 * summed[1] / inner
    rows1 = jnp.pad(jnp.stack([scale1, cross1], axis=1), ((0, 0), (0, 6), (0, 0)))

    def norm_back(x, gain, grad):
        scale = lax.rsqrt(jnp.mean(x * x, axis=1, keepdims=True) + EPS)
        unit = x * scale
        dn = grad * gain
        dx = scale * (dn - unit * jnp.mean(dn * unit, axis=1, keepdims=True))
        return dx, jnp.sum(grad * unit, axis=0)

    back1 = backward(
        ("gate", "scan", "input", "wgate", "wscan"),
        "backward_1",
        28,
        saved1,
        layer1,
        {"g": g1_slots, "rows": rows1},
        VMEM_BACK,
    )
    moved = [send_shard(back1[f"out{k}"], k) for k in range(SLOTS)]
    dx, gain_grad1 = norm_back(middle.astype(F32), gain1, sum(p.astype(F32) for p in moved))
    by_owner = lambda v: v.reshape(16, -1, width)
    owned1 = lax.psum_scatter(by_owner(back1["ga"]), DP, scatter_dimension=0, tiled=False)

    dmiddle = (cot.astype(F32) + dx).astype(BF16)
    g0 = (mask * dmiddle.astype(F32)).astype(BF16)
    cross0 = scale0 * scale0 * jnp.sum(g0.astype(F32) * branch0, axis=1, keepdims=True) / inner
    g0_slots = gather_slots(jnp.concatenate([g0, in_lanes([scale0, cross0])], axis=1))
    g0_slots, branch_parts = lax.optimization_barrier((g0_slots, branch_parts))
    branch = scatter_sum(branch_parts)[:, :width] * scale1[0][:, None]
    result = middle.astype(F32) + mask * branch

    back0 = backward(
        ("gate", "wgate"),
        "backward_0_gate",
        14,
        saved0,
        layer0,
        {"g": g0_slots, "core": own_core},
    )
    both = lambda kept, moved: (kept.astype(F32) + moved.astype(F32)).astype(BF16)
    a_moved = cross_core(back0["ga_send"])
    small_gate = back0["small"]
    back0["core"] = own_core
    back0.update(backward(("scan", "wscan"), "backward_0_scan", 20, saved0, layer0, back0))
    gb_send, a_moved = lax.optimization_barrier((back0["gb_send"], a_moved))
    a0 = both(back0["ga_keep"], a_moved)
    b0 = both(back0["gb_keep"], cross_core(gb_send))
    owned0 = jnp.pad(a0, ((0, 0), (0, 0), (0, 4), (0, 0), (0, 0)))
    owned0 = lax.dynamic_update_slice(owned0, b0, (0, 0, 6, 0, 0)).reshape(8, -1, width)
    owned0 = lax.psum_scatter(owned0, ("x", "z"), scatter_dimension=0, tiled=False)
    small_scan = back0["small"]
    back0.update(backward(("input",), "backward_0_input", 9, saved0, layer0, back0))
    moved0 = [send_shard(back0[f"out{k}"], k) for k in range(SLOTS)]
    dx, gain_grad0 = norm_back(x_f, gain0, sum(p.astype(F32) for p in moved0))
    dtokens = dmiddle.astype(F32) + dx
    owned0, owned1, gain_grad0, dtokens, result = lax.optimization_barrier(
        (owned0, owned1, gain_grad0, dtokens, result)
    )

    result_moved = lax.ppermute(result.astype(BF16), "section", [(0, 1)]).astype(F32)
    dtokens_moved = lax.ppermute(dtokens.astype(BF16), "section", [(1, 0)]).astype(F32)
    ends = jnp.where(
        first, jnp.stack([dtokens, dtokens_moved]), jnp.stack([result_moved, result])
    )[None]

    def to_section(v0, v1):
        kept = jnp.where(first, v0, v1).astype(F32)
        return kept + swap_section(jnp.where(first, v1, v0)).astype(F32)

    def by_row(v):
        rows = jnp.concatenate([v[:piece], v[2 * piece :]], axis=0)
        return jnp.transpose(rows.reshape(-1, SLOTS, quarter), (1, 0, 2))

    got = across(jnp.concatenate([by_row(owned0), by_row(owned1)], axis=0))
    out_rows = to_section(owned0[piece : 2 * piece], owned1[piece : 2 * piece]).astype(BF16)
    out_rows = jnp.transpose(out_rows.reshape(piece, SLOTS, quarter), (1, 0, 2))
    rows = got[:SLOTS].astype(F32) + got[SLOTS:].astype(F32)
    shared = jnp.sum(rows[:, 2 * piece :], axis=0).astype(BF16)
    rows = rows.astype(BF16)
    gathered = lax.all_gather(
        jnp.concatenate(
            [
                rows[:, :piece].reshape(-1, quarter),
                out_rows.reshape(-1, quarter),
                rows[:, piece : 2 * piece].reshape(-1, quarter),
                shared,
            ],
            axis=0,
        ),
        DP,
        tiled=False,
    )

    def small_of(by_pair, back, gain_grad):
        return jnp.concatenate(
            [
                by_pair.reshape(-1, LANES),
                back["small_bc"].reshape(-1, LANES),
                back["small_dt"],
                gain_grad.reshape(-1, LANES),
                back["gdt"].reshape(-1, LANES),
            ],
            axis=0,
        )

    small0 = small_of(small_gate + small_scan, back0, gain_grad0)
    small1 = small_of(back1["small"], back1, gain_grad1)
    small_sum = sum_small(to_section(small0, small1))
    everyone = in_order(gather_slots(small_sum), 1)
    n_pair, n_bc = PAIRS * 8, 2 * 8
    by_pair = everyone[:, :n_pair].reshape(SLOTS, PAIRS, 8, LANES)
    by_pair = by_pair.transpose(2, 0, 1, 3).reshape(8, inner)
    by_bc = jnp.sum(everyone[:, n_pair : n_pair + n_bc], axis=0)
    by_bc = by_bc.reshape(2, 8, LANES).transpose(1, 0, 2).reshape(8, n_state)
    at = n_pair + n_bc
    by_dt = everyone[:, at : at + 8, :own_heads].transpose(1, 0, 2).reshape(8, heads)
    at += 8
    gain_total = jnp.sum(everyone[:, at : at + width // LANES], axis=0).reshape(-1)
    at += width // LANES
    dt_rows = everyone[:, at:].reshape(SLOTS, 16, SLOTS, quarter)[:, :own_heads]
    dt_rows = pick(dt_rows, j, 2).reshape(heads, quarter)
    conv_total = jnp.concatenate([by_pair[:5], by_bc[:5]], axis=1)
    conv_own = lax.dynamic_slice(conv_total, (0, channels * j), (5, channels))
    grad_skip = jnp.sum(by_pair[6].reshape(heads, HEAD), axis=1)

    grad_in_weight, grad_out_weight = assemble(gathered, dt_rows)
    return (
        ends,
        lax.dynamic_slice(gain_total, (quarter * j,), (quarter,))[None],
        jnp.transpose(grad_in_weight)[None],
        conv_own[None, :4],
        conv_own[4][None],
        by_dt[0][None],
        by_dt[1][None],
        grad_skip[None],
        lax.dynamic_slice(by_pair[5], (own_cols * j,), (own_cols,))[None],
        grad_out_weight[None],
    )


def solution(mesh):
    sections, copies, owners = mesh.devices.shape
    fine = jax.sharding.Mesh(
        mesh.devices.reshape(sections, 2, copies // 4, 2, owners), ("section", *DP, "shard")
    )
    return jax.shard_map(
        shards,
        mesh=fine,
        in_specs=(
            P((*DP, "shard"), None, None),
            P((*DP, "shard"), None, None),
            P((*DP, "shard")),
            P("section", "shard"),
            P("section", "shard", None),
            P("section", None, "shard"),
            P("section", "shard"),
            P("section", None),
            P("section", None),
            P("section", None),
            P("section", "shard"),
            P("section", "shard", None),
        ),
        out_specs=(
            P("section", (*DP, "shard"), None, None),
            P("section", "shard"),
            P("section", "shard", None),
            P("section", None, "shard"),
            P("section", "shard"),
            P("section", None),
            P("section", None),
            P("section", None),
            P("section", "shard"),
            P("section", "shard", None),
        ),
        check_vma=False,
    )
```

```python
import jax
import jax.numpy as jnp
from jax import lax
from jax.experimental import pallas as pl
from jax.experimental.pallas import tpu as pltpu
from jax.sharding import PartitionSpec as P

F32 = jnp.float32
BF16 = jnp.bfloat16
HI = lax.Precision.HIGHEST
EPS = 1e-05
T = 128
LANES = 128
HEAD = 64
SLOTS = 4
ROWS = SLOTS * T
PAIRS = 6
STEPS = 2
HALF = PAIRS // STEPS
WIDE = HALF * LANES
VMEM_LIMIT = 34 * 1024 * 1024
VMEM_MOST = 60 * 1024 * 1024
VMEM_BACK = 56 * 1024 * 1024
DP = ("x", "z", "core")


def sigmoid(v):
    return 0.5 * jnp.tanh(0.5 * v) + 0.5


def softplus(v):
    return jnp.maximum(v, 0.0) + jnp.log1p(jnp.exp(-jnp.abs(v)))


def dot(a, b):
    return jnp.dot(a, b, preferred_element_type=F32)


def dot_nt(a, b, precision=None):
    return lax.dot_general(
        a, b, (((1,), (1,)), ((), ())), preferred_element_type=F32, precision=precision
    )


def dot_tn(a, b, precision=None):
    return lax.dot_general(
        a, b, (((0,), (0,)), ((), ())), preferred_element_type=F32, precision=precision
    )


def iota(axis):
    return lax.broadcasted_iota(jnp.int32, (T, LANES), axis)


def shift_down(v, steps):
    return jnp.where(iota(0) >= steps, pltpu.roll(v, steps, 0), 0.0)


def shift_up(v, steps):
    return jnp.where(iota(0) < T - steps, pltpu.roll(v, T - steps, 0), 0.0)


def conv_taps(cin):
    return [shift_down(cin, 3), shift_down(cin, 2), shift_down(cin, 1), cin]


def conv_sum(taps, par):
    total = par[4:5, :] + taps[0] * par[0:1, :]
    for k in range(1, 4):
        total = total + taps[k] * par[k : k + 1, :]
    return total


def conv_back(dcv, par):
    total = dcv * par[3:4, :]
    for m in range(1, 4):
        total = total + shift_up(dcv, m) * par[3 - m : 4 - m, :]
    return total


def column_sum(v):
    return jnp.sum(v, axis=0, keepdims=True)


def slot(k):
    return slice(k * T, (k + 1) * T)


def tri(lower):
    if lower:
        return (iota(0) >= iota(1)).astype(F32)
    return (iota(0) <= iota(1)).astype(F32)


def step_prep(k, pbc, dtp, run_col, run_row, step_wide):
    step = softplus(pbc[slot(k), 256:384] + dtp[0:1, :])
    run = jnp.dot(tri(True), step * dtp[1:2, :], precision=HI, preferred_element_type=F32)
    run_row[k] = jnp.transpose(run)
    left = iota(1) < HEAD
    for p in range(PAIRS):
        a, b = 2 * p, 2 * p + 1
        run_col[a, slot(k), :] = jnp.broadcast_to(run[:, a : a + 1], (T, LANES))
        run_col[b, slot(k), :] = jnp.broadcast_to(run[:, b : b + 1], (T, LANES))
        step_wide[p, slot(k), :] = jnp.where(
            left,
            jnp.broadcast_to(step[:, a : a + 1], (T, LANES)),
            jnp.broadcast_to(step[:, b : b + 1], (T, LANES)),
        )
    return step


def halves(v):
    left = iota(1) < HEAD
    zero = jnp.zeros_like(v)
    return jnp.concatenate([jnp.where(left, v, zero), jnp.where(left, zero, v)], axis=0)


def in_lanes(columns):
    lane = lax.broadcasted_iota(jnp.int32, (columns[0].shape[0], LANES), 1)
    out = jnp.zeros(lane.shape, F32)
    for n, v in enumerate(columns):
        for k in range(3):
            part = v.astype(BF16).astype(F32)
            out = jnp.where(lane == 3 * n + k, part, out)
            v = v - part
    return out.astype(BF16)


def from_lanes(v, n):
    return sum(v[:, 3 * n + k : 3 * n + k + 1].astype(F32) for k in range(3))


class Refs:
    pass


def kernel_call(body, name, ins, outs, scratch, cost_us, limit=VMEM_LIMIT):
    in_names, out_names, scratch_names = list(ins), list(outs), list(scratch)

    def run(*refs):
        for h in range(STEPS):
            rf = Refs()
            for key, ref in zip(in_names + out_names + scratch_names, refs):
                spec = ins.get(key) or outs.get(key)
                blocks = spec[-2:] if spec and len(spec) > 2 else None
                if blocks and blocks[1](1) != blocks[1](0):
                    at = [
                        slice(n * size, (n + 1) * size) if n else slice(0, size)
                        for n, size in zip(blocks[1](h), blocks[0])
                    ]
                    setattr(rf, key + "_whole", ref)
                    ref = ref.at[tuple(at)]
                setattr(rf, key, ref)
            body(rf, h)

    res = pl.pallas_call(
        run,
        in_specs=[
            pl.BlockSpec(memory_space=pltpu.VMEM if len(ins[n]) > 2 else ins[n][1])
            for n in in_names
        ],
        out_specs=[pl.BlockSpec(memory_space=pltpu.VMEM) for n in out_names],
        out_shape=[jax.ShapeDtypeStruct(outs[n][0], outs[n][1]) for n in out_names],
        scratch_shapes=[
            pltpu.VMEM(*scratch[n]) if isinstance(scratch[n], tuple) else scratch[n]
            for n in scratch_names
        ],
        compiler_params=pltpu.CompilerParams(vmem_limit_bytes=limit),
        cost_estimate=pl.CostEstimate(
            flops=int(cost_us * 1.1e9), bytes_accessed=1 << 20, transcendentals=0
        ),
        name=name,
    )(*[ins[n][0] for n in in_names])
    return dict(zip(out_names, res))


def when(condition):
    return (lambda f: f()) if condition else (lambda f: None)


def whole(v):
    return (v, v.shape, lambda h: (0,) * v.ndim)


def whole_out(shape, dtype):
    return (shape, dtype, shape, lambda h: (0,) * len(shape))


def by_step(v, block):
    return (v, block, lambda h: (h,) + (0,) * (len(block) - 1))


def by_step_out(shape, dtype, block):
    return (shape, dtype, block, lambda h: (h,) + (0,) * (len(block) - 1))


def lanes_by_step(v):
    return (v, (v.shape[0], WIDE), lambda h: (0, h))


def lanes_by_step_out(shape, dtype):
    return (shape, dtype, (shape[0], WIDE), lambda h: (0, h))


def in_hbm(v):
    return (v, pltpu.HBM)


WEIGHT_GROUPS = {"wo": (0, 3), "wg": (3, 3), "wv": (6, 3), "ws": (9, 1)}


class Copies:
    def __init__(self, sems):
        self.sems, self.copies = sems, {}

    def add(self, key, source, target):
        self.copies[key] = (source, target, self.sems.at[len(self.copies)])

    def add_weights(self, rf, keys):
        for key in keys:
            at, count = WEIGHT_GROUPS[key]
            self.add(key, rf.w.at[:, pl.ds(at, count)], getattr(rf, key))

    def start(self):
        for copy in self.copies.values():
            pltpu.make_async_copy(*copy).start()

    def wait(self, *keys):
        for key in keys:
            pltpu.make_async_copy(*self.copies[key]).wait()


def weight_scratch(scratch, keys, width):
    for key in keys:
        scratch[key] = ((16, WEIGHT_GROUPS[key][1], 16, width), BF16)


def half_rows(ref, h):
    v = ref[pl.ds(8 * h, 8)]
    return v.reshape(WIDE, v.shape[-1])


def pair_lanes(p):
    return slice(p * LANES, (p + 1) * LANES)


def flat_rows(ref):
    v = ref[...]
    return v.reshape(-1, v.shape[-1])


def mixed_bc(rf, k, c):
    lanes = slice(c * LANES, (c + 1) * LANES)
    cv = conv_sum(conv_taps(rf.pbc[slot(k), lanes]), rf.pbcv[:, lanes])
    return cv * sigmoid(cv)


def forward(x_slots, g_slots, w, dtw, gain, pv, pbcv, dtp):
    width = x_slots[0].shape[1]
    with_grad = g_slots is not None

    def body(rf, h):
        copies = Copies(rf.sems)
        for k in range(SLOTS):
            copies.add(f"x{k}", getattr(rf, f"x{k}"), rf.x_all.at[k])
        copies.add_weights(rf, ("ws", "wg", "wv", "wo"))
        if with_grad:
            for k in range(SLOTS):
                copies.add(f"g{k}", getattr(rf, f"g{k}"), rf.g_all.at[slot(k)])

        @when(h == 0)
        def _prep():
            copies.start()
            for k in range(SLOTS):
                copies.wait(f"x{k}")
                x = rf.x_all[k].astype(F32)
                scale = lax.rsqrt(jnp.mean(x * x, axis=1, keepdims=True) + EPS)
                rf.normed[slot(k), :] = (x * scale * rf.gain[...]).astype(BF16)
            copies.wait("ws")
            rf.pbc[:, 0:256] = dot_nt(rf.normed[...], flat_rows(rf.ws))
            rf.pbc[:, 256:384] = dot_nt(rf.normed[...], rf.dtw[...])
            for k in range(SLOTS):
                rf.scores[k] = dot_nt(mixed_bc(rf, k, 1), mixed_bc(rf, k, 0), HI) * tri(True)
                step_prep(k, rf.pbc, rf.dtp, rf.run_col, rf.run_row, rf.step_wide)
            rf.square[...] = jnp.zeros_like(rf.square)
            rf.cross[...] = jnp.zeros_like(rf.cross)
            copies.wait("wg", "wv", "wo")
            if with_grad:
                copies.wait(*[f"g{k}" for k in range(SLOTS)])

        rf.proj[0, :, 0:WIDE] = dot_nt(rf.normed[...], half_rows(rf.wg, h))
        rf.proj[0, :, WIDE : 2 * WIDE] = dot_nt(rf.normed[...], half_rows(rf.wv, h))
        if with_grad:
            q_all = dot_nt(rf.g_all[...], half_rows(rf.wo, h))
        for p in range(HALF):
            lanes = pair_lanes(p)
            par = rf.pv[:, lanes]
            pair = HALF * h + p
            for k in range(SLOTS):
                gate = rf.proj[0, slot(k), lanes]
                cv = conv_sum(
                    conv_taps(rf.proj[0, slot(k), WIDE + p * LANES : WIDE + (p + 1) * LANES]), par
                )
                values = cv * sigmoid(cv)
                scaled = (values * rf.step_wide[pair, slot(k), :]).astype(BF16)
                weights = []
                for a in range(2):
                    gap = (
                        rf.run_col[2 * pair + a, slot(k), :]
                        - rf.run_row[k, pl.ds(2 * pair + a, 1), :]
                    )
                    decay = jnp.exp(jnp.minimum(gap, 0.0))
                    weights.append((rf.scores[k] * decay).astype(BF16))
                y = dot(jnp.concatenate(weights, axis=1), halves(scaled))
                rf.y[0, slot(k), lanes] = y
                scanned = y + par[6:7, :] * values
                gated = scanned * (gate * sigmoid(gate))
                rf.square[slot(k), :] += gated * gated
                scaled_out = gated * par[5:6, :]
                rf.u_all[h, slot(k), lanes] = scaled_out.astype(BF16)
                if with_grad:
                    rf.cross[slot(k), :] += q_all[slot(k), lanes] * scaled_out

        @when(h == STEPS - 1)
        def _finish():
            u = jnp.concatenate([rf.u_all[a] for a in range(STEPS)], axis=1)
            for n in range(0, width, 512):
                part = dot(u, rf.wo[:, :, :, n : n + 512].reshape(STEPS * WIDE, 512)).astype(BF16)
                for k in range(SLOTS):
                    getattr(rf, f"out{k}")[:, n : n + 512] = part[slot(k), :]
            for k in range(SLOTS):
                total = jnp.sum(rf.square[slot(k), :], axis=1, keepdims=True)
                getattr(rf, f"out{k}")[:, width:] = in_lanes([total])
            ones = jnp.ones((8, LANES), F32)
            rf.stats[0] = dot_nt(ones, rf.square[...], HI)
            rf.stats[1] = dot_nt(ones, rf.cross[...], HI)

    ins = {f"x{k}": in_hbm(v) for k, v in enumerate(x_slots)}
    if with_grad:
        ins.update({f"g{k}": in_hbm(v) for k, v in enumerate(g_slots)})
    ins.update(
        gain=whole(gain),
        w=in_hbm(w),
        dtw=whole(dtw),
        pv=lanes_by_step(pv),
        pbcv=whole(pbcv),
        dtp=whole(dtp),
    )
    outs = {f"out{k}": whole_out((T, width + LANES), BF16) for k in range(SLOTS)}
    outs.update(
        stats=whole_out((2, 8, ROWS), F32),
        normed=whole_out((ROWS, width), BF16),
        proj=by_step_out((STEPS, ROWS, 2 * WIDE), F32, (1, ROWS, 2 * WIDE)),
        y=by_step_out((STEPS, ROWS, WIDE), F32, (1, ROWS, WIDE)),
        pbc=whole_out((ROWS, 384), F32),
    )
    scratch = dict(
        scores=((SLOTS, T, T), F32),
        run_col=((2 * PAIRS, ROWS, LANES), F32),
        run_row=((SLOTS, T, LANES), F32),
        step_wide=((PAIRS, ROWS, LANES), F32),
        u_all=((STEPS, ROWS, WIDE), BF16),
        square=((ROWS, LANES), F32),
        cross=((ROWS, LANES), F32),
        x_all=((SLOTS, T, width), BF16),
        sems=pltpu.SemaphoreType.DMA((2 * SLOTS + 4,)),
    )
    weight_scratch(scratch, ("ws", "wg", "wv", "wo"), width)
    if with_grad:
        scratch["g_all"] = ((ROWS, width), BF16)
    res = kernel_call(body, "layer_forward", ins, outs, scratch, 18, VMEM_MOST)
    return [res[f"out{k}"] for k in range(SLOTS)], res


def head_columns(pair):
    target = 2 * pair + (iota(0) >= HEAD).astype(jnp.int32)
    one = (iota(1) == target).astype(BF16)
    return jnp.concatenate([one, one], axis=0)


def head_sum(v, columns):
    high = v.astype(BF16)
    low = (v - high.astype(F32)).astype(BF16)
    return dot(jnp.concatenate([high, low], axis=1), columns)


def put_by_core(rf, key, x, at, part):
    keep, send = getattr(rf, key + "_keep"), getattr(rf, key + "_send")
    groups = slice(at, at + part.shape[2])
    for c in range(2):

        @pl.when(rf.core[0] == c)
        def _store(c=c):
            for z in range(4):
                keep[x, z, groups] = part[z, c]
                send[x, z, groups] = part[z, 1 - c]


def backward(stages, name, cost_us, saved, layer, have, limit=VMEM_LIMIT):
    gate, scan, inp, wgate, wscan = (
        s in stages for s in ("gate", "scan", "input", "wgate", "wscan")
    )
    width = saved["normed"].shape[1]
    w, dtw, pv, pbcv, dtp = layer
    elementwise = gate or scan
    fetched = (("wo",) if gate else ()) + (("wg", "wv", "ws") if inp else ())
    in_slots = gate and "rows" not in have

    def body(rf, h):
        copies = Copies(rf.sems) if gate or wgate or inp else None
        if gate or wgate:
            for k in range(SLOTS):
                source = getattr(rf, f"g{k}")
                copies.add(f"g{k}", source.at[:, pl.ds(0, width)], rf.g_all.at[slot(k)])
                if in_slots:
                    copies.add(f"e{k}", source.at[:, pl.ds(width, LANES)], rf.e_all.at[k])
        if copies:
            copies.add_weights(rf, fetched)

        @when(h == 0)
        def _prep():
            if copies:
                copies.start()
            for k in range(SLOTS):
                if gate or wgate:
                    copies.wait(f"g{k}")
                if in_slots:
                    copies.wait(f"e{k}")
                if gate:
                    for row, ref in ((0, rf.scale_row), (1, rf.cross_row)):
                        if "rows" in have:
                            ref[slot(k), :] = jnp.transpose(
                                jnp.broadcast_to(rf.rows[k, row : row + 1, :], (T, LANES))
                            )
                        else:
                            column = from_lanes(rf.e_all[k], row)
                            ref[slot(k), :] = jnp.broadcast_to(column, (T, LANES))
                if scan:
                    inbound, outbound = mixed_bc(rf, k, 0), mixed_bc(rf, k, 1)
                    rf.mixed[0, slot(k), :] = inbound
                    rf.mixed[1, slot(k), :] = outbound
                    rf.scores[k] = dot_nt(inbound, outbound, HI) * tri(False)
                    rf.step_all[slot(k), :] = step_prep(
                        k, rf.pbc, rf.dtp, rf.run_col, rf.run_row, rf.step_wide
                    )
            if scan:
                rf.dscores[...] = jnp.zeros_like(rf.dscores)
                rf.dstep[...] = jnp.zeros_like(rf.dstep)
                rf.drun[...] = jnp.zeros_like(rf.drun)
            if inp:
                rf.total[...] = jnp.zeros_like(rf.total)
            if copies:
                copies.wait(*fetched)

        if gate:
            q_all = dot_nt(rf.g_all[...], half_rows(rf.wo, h))
        for p in range(HALF if elementwise else 0):
            lanes = pair_lanes(p)
            par = rf.pv[:, lanes]
            pair = HALF * h + p
            sums = [jnp.zeros((1, LANES), F32) for _ in range(8)]
            if scan:
                columns = head_columns(pair)
            for k in range(SLOTS):
                taps = conv_taps(rf.proj[0, slot(k), WIDE + p * LANES : WIDE + (p + 1) * LANES])
                cv = conv_sum(taps, par)
                sig_c = sigmoid(cv)
                values = cv * sig_c
                y = rf.y[0, slot(k), lanes]
                if gate:
                    gate_in = rf.proj[0, slot(k), lanes]
                    sig_g = sigmoid(gate_in)
                    silu_g = gate_in * sig_g
                    scanned = y + par[6:7, :] * values
                    gated = scanned * silu_g
                    grad_no = q_all[slot(k), lanes]
                    scale = rf.scale_row[slot(k), :]
                    dgated = scale * (grad_no * par[5:6, :]) - rf.cross_row[slot(k), :] * gated
                    norm = gated * scale
                    sums[5] += column_sum(grad_no * norm)
                    rf.u[slot(k), lanes] = (norm * par[5:6, :]).astype(BF16)
                    dscan = dgated * silu_g
                    dgate = dgated * scanned * (sig_g * (1.0 + gate_in * (1.0 - sig_g)))
                    sums[6] += column_sum(dscan * values)
                    rf.dg[slot(k), lanes] = dgate.astype(BF16)
                    if not scan:
                        rf.dscan[slot(k), lanes] = dscan
                else:
                    dscan = rf.dscan[slot(k), lanes]
                if not scan:
                    continue
                wide = rf.step_wide[pair, slot(k), :]
                dy = dscan.astype(BF16)
                scaled = (values * wide).astype(BF16)
                dweights = dot_nt(halves(scaled), dy)
                weights = []
                dscore = rf.dscores[k]
                for a in range(2):
                    gap = (
                        rf.run_row[k, pl.ds(2 * pair + a, 1), :]
                        - rf.run_col[2 * pair + a, slot(k), :]
                    )
                    decay = jnp.exp(jnp.minimum(gap, 0.0))
                    weights.append((rf.scores[k] * decay).astype(BF16))
                    dscore = dscore + dweights[slot(a), :] * decay
                rf.dscores[k] = dscore
                dscaled = dot(jnp.concatenate(weights, axis=1), halves(dy))
                rf.dstep[slot(k), :] += head_sum(dscaled * values, columns)
                rf.drun[slot(k), :] += head_sum(
                    dy.astype(F32) * y - scaled.astype(F32) * dscaled, columns
                )
                dvalues = dscaled * wide + par[6:7, :] * dscan
                dcv = dvalues * (sig_c * (1.0 + cv * (1.0 - sig_c)))
                for t in range(4):
                    sums[t] += column_sum(dcv * taps[t])
                sums[4] += column_sum(dcv)
                rf.dv[slot(k), lanes] = conv_back(dcv, par).astype(BF16)
            rf.small[p] = jnp.concatenate(sums, axis=0)
        if wgate and wscan:
            for at, left, right in (
                (0, rf.dg, rf.normed),
                (3, rf.u, rf.g_all),
                (6, rf.dv, rf.normed),
            ):
                part = dot_tn(left[...], right[...]).astype(BF16)
                rf.ga[:, at : at + 3] = part.reshape(8, 3, 16, width)
            if not scan:
                part = dot_tn(rf.dbc_half[...], rf.normed[...]).astype(BF16)
                rf.ga[:, 9] = part.reshape(8, 16, width)
        elif wgate:
            for at, left, right in ((0, rf.dg, rf.normed), (3, rf.u, rf.g_all)):
                part = dot_tn(left[...], right[...]).astype(BF16)
                put_by_core(rf, "ga", h, at, part.reshape(4, 2, 3, 16, width))
        elif wscan:
            part = dot_tn(rf.dv[...], rf.normed[...]).astype(BF16)
            put_by_core(rf, "gb", h, 0, part.reshape(4, 2, 3, 16, width))
        if inp:
            rf.total[...] += dot(rf.dg[...], half_rows(rf.wg, h)) + dot(
                rf.dv[...], half_rows(rf.wv, h)
            )

        @when(h == STEPS - 1)
        def _finish():
            if scan:
                sums = [[jnp.zeros((1, LANES), F32) for _ in range(8)] for _ in range(2)]
                dt_sums = [jnp.zeros((1, LANES), F32) for _ in range(8)]
                live = iota(1) < 2 * PAIRS
                for k in range(SLOTS):
                    dscore = rf.dscores[k] * tri(False)
                    dmixed = (
                        jnp.dot(
                            dscore,
                            rf.mixed[1, slot(k), :],
                            precision=HI,
                            preferred_element_type=F32,
                        ),
                        dot_tn(dscore, rf.mixed[0, slot(k), :], HI),
                    )
                    for c in range(2):
                        lanes = slice(c * LANES, (c + 1) * LANES)
                        par = rf.pbcv[:, lanes]
                        taps = conv_taps(rf.pbc[slot(k), lanes])
                        cv = conv_sum(taps, par)
                        sig = sigmoid(cv)
                        dcv = dmixed[c] * (sig * (1.0 + cv * (1.0 - sig)))
                        for t in range(4):
                            sums[c][t] += column_sum(dcv * taps[t])
                        sums[c][4] += column_sum(dcv)
                        rf.dbc[slot(k), lanes] = conv_back(dcv, par).astype(BF16)
                    dlog = jnp.dot(
                        tri(False), rf.drun[slot(k), :], precision=HI, preferred_element_type=F32
                    )
                    grad_step = rf.dstep[slot(k), :] + dlog * rf.dtp[1:2, :]
                    dt_sums[1] += column_sum(dlog * rf.step_all[slot(k), :])
                    draw = grad_step * sigmoid(rf.pbc[slot(k), 256:384] + rf.dtp[0:1, :])
                    draw = jnp.where(live, draw, 0.0)
                    dt_sums[0] += column_sum(draw)
                    rf.dbc[slot(k), 256:384] = draw.astype(BF16)
                rf.small_bc[0] = jnp.concatenate(sums[0], axis=0)
                rf.small_bc[1] = jnp.concatenate(sums[1], axis=0)
                dt_sums[1] = dt_sums[1] * rf.dtp[1:2, :]
                rf.small_dt[...] = jnp.concatenate(dt_sums, axis=0)
            if wscan and wgate and scan:
                part = dot_tn(rf.dbc[:, 0:256], rf.normed[...]).astype(BF16)
                rf.ga_whole[:, 9] = part.reshape(16, 16, width)
            if wscan and not wgate:
                part = dot_tn(rf.dbc[:, 0:256], rf.normed[...]).astype(BF16)
                part = part.reshape(2, 4, 2, 1, 16, width)
                for a in range(2):
                    put_by_core(rf, "gb", a, 3, part[a])
            if wscan:
                rf.gdt[...] = dot_tn(rf.dbc[:, 256:384], rf.normed[...])[0:16]
            if inp:
                final = (
                    rf.total[...]
                    + dot(rf.dbc[:, 0:256], flat_rows(rf.ws))
                    + dot(rf.dbc[:, 256:384], rf.dtw[...])
                )
                for k in range(SLOTS):
                    getattr(rf, f"out{k}")[...] = final[slot(k), :].astype(BF16)

    ins, outs, scratch = {}, {}, {}
    heads_cols = STEPS * WIDE
    if gate or wgate:
        for k, v in enumerate(have["g"]):
            ins[f"g{k}"] = in_hbm(v)
        scratch["g_all"] = ((ROWS, width), BF16)
    if gate:
        if in_slots:
            scratch["e_all"] = ((SLOTS, T, LANES), BF16)
        else:
            ins["rows"] = whole(have["rows"])
        scratch["scale_row"] = ((ROWS, LANES), F32)
        scratch["cross_row"] = ((ROWS, LANES), F32)
        outs["u"] = lanes_by_step_out((ROWS, heads_cols), BF16)
        outs["dg"] = lanes_by_step_out((ROWS, heads_cols), BF16)
        if not scan:
            outs["dscan"] = lanes_by_step_out((ROWS, heads_cols), F32)
    if elementwise:
        ins["proj"] = by_step(saved["proj"], (1, ROWS, 2 * WIDE))
        ins["y"] = by_step(saved["y"], (1, ROWS, WIDE))
        ins["pv"] = lanes_by_step(pv)
        outs["small"] = by_step_out((PAIRS, 8, LANES), F32, (HALF, 8, LANES))
    if scan:
        ins["pbc"] = whole(saved["pbc"])
        ins["pbcv"] = whole(pbcv)
        ins["dtp"] = whole(dtp)
        if not gate:
            ins["dscan"] = lanes_by_step(have["dscan"])
        outs["dv"] = lanes_by_step_out((ROWS, heads_cols), BF16)
        outs["dbc"] = whole_out((ROWS, 384), BF16)
        outs["small_bc"] = whole_out((2, 8, LANES), F32)
        outs["small_dt"] = whole_out((8, LANES), F32)
        scratch.update(
            mixed=((2, ROWS, LANES), F32),
            scores=((SLOTS, T, T), F32),
            run_col=((2 * PAIRS, ROWS, LANES), F32),
            run_row=((SLOTS, T, LANES), F32),
            step_wide=((PAIRS, ROWS, LANES), F32),
            step_all=((ROWS, LANES), F32),
            dscores=((SLOTS, T, T), F32),
            dstep=((ROWS, LANES), F32),
            drun=((ROWS, LANES), F32),
        )
    if inp:
        ins["dtw"] = whole(dtw)
        scratch["total"] = ((ROWS, width), F32)
        outs.update({f"out{k}": whole_out((T, width), BF16) for k in range(SLOTS)})
    if fetched:
        ins["w"] = in_hbm(w)
        weight_scratch(scratch, fetched, width)
    if gate or wgate or inp:
        scratch["sems"] = pltpu.SemaphoreType.DMA((2 * SLOTS + 4,))
    if wgate or wscan:
        ins["normed"] = whole(saved["normed"])
    if not gate and (wgate or inp):
        ins["dg"] = lanes_by_step(have["dg"])
    if wgate and not gate:
        ins["u"] = lanes_by_step(have["u"])
    if not scan and (wscan or inp):
        ins["dv"] = lanes_by_step(have["dv"])
        ins["dbc"] = whole(have["dbc"])
    if wgate and wscan:
        if not scan:
            ins["dbc_half"] = (have["dbc"], (ROWS, LANES), lambda h: (0, h))
        outs["ga"] = by_step_out((16, 10, 16, width), BF16, (8, 10, 16, width))
    elif wgate or wscan:
        ins["core"] = have["core"]
        key, groups = ("ga", 6) if wgate else ("gb", 4)
        for end in ("_keep", "_send"):
            outs[key + end] = whole_out((2, 4, groups, 16, width), BF16)
    if wscan:
        outs["gdt"] = whole_out((16, width), F32)
    return kernel_call(body, name, ins, outs, scratch, cost_us, limit)


def assemble(parts, dt_rows):
    quarter = parts.shape[2]
    block = 16 * 48
    total = 8 * block + 16 * 16 + dt_rows.shape[0]

    def body(inw, outw, shared, dt, grad_in, grad_out):
        i = pl.program_id(0)

        @pl.when(i < 8)
        def _columns():
            grad_in[...] = inw[...].reshape(block, quarter).astype(F32)

        @pl.when(i < SLOTS)
        def _out():
            grad_out[...] = outw[...].reshape(block, quarter).astype(F32)

        @pl.when(i == 8)
        def _shared():
            grad_in[...] = jnp.zeros_like(grad_in)
            grad_in[0:256, :] = shared[...].reshape(256, quarter).astype(F32)
            grad_in[256 : 256 + dt_rows.shape[0], :] = dt[...]

    last = SLOTS - 1
    return pl.pallas_call(
        body,
        grid=(9,),
        in_specs=[
            pl.BlockSpec(
                (16, 48, quarter),
                lambda i: (0, jnp.where(i < SLOTS, i, jnp.minimum(i + SLOTS, 11)), 0),
            ),
            pl.BlockSpec((16, 48, quarter), lambda i: (0, SLOTS + jnp.minimum(i, last), 0)),
            pl.BlockSpec((16, 16, quarter), lambda i: (0, 36, 0)),
            pl.BlockSpec(dt_rows.shape, lambda i: (0, 0)),
        ],
        out_specs=[
            pl.BlockSpec((block, quarter), lambda i: (i, 0)),
            pl.BlockSpec((block, quarter), lambda i: (0, jnp.minimum(i, last))),
        ],
        out_shape=[
            jax.ShapeDtypeStruct((total, quarter), F32),
            jax.ShapeDtypeStruct((block, SLOTS * quarter), F32),
        ],
        compiler_params=pltpu.CompilerParams(vmem_limit_bytes=VMEM_MOST),
        name="assemble",
    )(parts, parts, parts, dt_rows)


def ring(n, k):
    return [(i, (i + k) % n) for i in range(n)]


def send_shard(v, k):
    return lax.ppermute(v, "shard", ring(SLOTS, k)) if k else v


def send_across(v, k):
    pairs = [
        (sec * SLOTS + y, (1 - sec) * SLOTS + (y + k) % SLOTS)
        for sec in range(2)
        for y in range(SLOTS)
    ]
    return lax.ppermute(v, ("section", "shard"), pairs)


def across(v):
    return lax.all_to_all(v, ("section", "shard"), 0, 0)


def swap_section(v):
    return lax.ppermute(v, "section", [(0, 1), (1, 0)])


def dp_index(x, z, c):
    return x * 8 + z * 2 + c


def dp_pairs(move):
    pairs = []
    for x in range(2):
        for z in range(4):
            for c in range(2):
                pairs.append((dp_index(x, z, c), dp_index(*move(x, z, c))))
    return pairs


def pick(v, index, axis):
    return lax.dynamic_index_in_dim(v, index, axis, keepdims=False)


def gather_slots(v):
    return [send_shard(v, (-k) % SLOTS) for k in range(SLOTS)]


def scatter_sum(slots):
    parts = [send_shard(slots[k], k) for k in range(SLOTS)]
    return sum(p.astype(F32) for p in parts)


def cross_core(v):
    return lax.ppermute(v, DP, dp_pairs(lambda x, z, c: (x, z, 1 - c)))


def sum_small(v):
    v = v + lax.ppermute(v, DP, dp_pairs(lambda x, z, c: (x, z, 1 - c)))
    v = v + sum(
        lax.ppermute(v, DP, dp_pairs(lambda x, z, c: (x, (z + k) % 4, c))) for k in range(1, 4)
    )
    return v + lax.ppermute(v, DP, dp_pairs(lambda x, z, c: (1 - x, z, c)))


def in_order(parts, sign):
    j = lax.axis_index("shard")
    stacked = jnp.stack(parts)
    return jnp.take(stacked, (sign * (jnp.arange(SLOTS) - j)) % SLOTS, axis=0)


def shards(
    tokens,
    cotangent,
    lengths,
    norm_gain,
    in_weight,
    conv_weight,
    conv_bias,
    dt_bias,
    a_log,
    d_skip,
    gate_gain,
    out_weight,
):
    sec = lax.axis_index("section")
    d = lax.axis_index(DP)
    j = lax.axis_index("shard")
    core = d % 2
    first = sec == 0
    width = tokens.shape[2]
    quarter = norm_gain.shape[1]
    channels = conv_bias.shape[1]
    own_cols = gate_gain.shape[1]
    inner = own_cols * SLOTS
    heads = dt_bias.shape[1]
    own_heads = heads // SLOTS
    n_state = 2 * LANES
    piece = own_cols // 16
    piece_bc = n_state // 16
    own_core = (core.astype(jnp.int32)[None], pltpu.SMEM)

    x_own = pick(tokens, sec, 0)
    cot = pick(cotangent, sec, 0)
    length = pick(lengths, sec, 0)
    mask = (jnp.arange(T, dtype=jnp.int32) < length).astype(F32)[:, None]

    columns = jnp.transpose(in_weight[0])
    with jax.named_scope("weights"):

        def cut(start, rows):
            return lax.dynamic_slice(columns, (start, 0), (rows, quarter))

        def columns_of(to):
            return jnp.concatenate(
                [
                    cut(own_cols * to + piece * d, piece),
                    cut(inner + own_cols * to + piece * d, piece),
                    cut(2 * inner + piece_bc * d, piece_bc),
                ],
                axis=0,
            )

        cuts = [columns_of((j + k) % SLOTS) for k in range(SLOTS)]
        o_own = lax.dynamic_slice(out_weight[0], (piece * d, 0), (piece, width))
        o_other = swap_section(o_own)

        w_own = [send_shard(cuts[k], k) for k in range(SLOTS)]
        w_other = [send_across(cuts[k], k) for k in range(SLOTS)]

        def from_parts(parts, others, o, o_others, own):
            pieces = [jnp.where(own, p, q) for p, q in zip(parts, others)]
            lanes = []
            for y in range(SLOTS):
                v = pieces[0]
                for k in range(1, SLOTS):
                    v = jnp.where((j - y) % SLOTS == k, pieces[k], v)
                lanes.append(v)
            return jnp.concatenate(
                [jnp.where(own, o, o_others), jnp.concatenate(lanes, axis=1)], axis=0
            )

        w0 = from_parts(w_own, w_other, o_own, o_other, first)
        w1 = from_parts(w_own, w_other, o_own, o_other, ~first)
        w0, w1, x_own, cot = lax.optimization_barrier((w0, w1, x_own, cot))
        w0 = lax.all_gather(w0, DP, axis=0, tiled=False)
        x_slots = gather_slots(x_own)
        x_slots, norm_gain = lax.optimization_barrier((x_slots, norm_gain))

    with jax.named_scope("small_weights"):
        dt_columns = columns[2 * inner + n_state :]
        sizes = [quarter, 4 * channels, channels, own_cols, heads, heads, heads, heads * quarter]
        flat = jnp.concatenate(
            [
                norm_gain[0],
                conv_weight[0].reshape(-1),
                conv_bias[0],
                gate_gain[0],
                dt_bias[0],
                a_log[0],
                d_skip[0],
                dt_columns.reshape(-1),
            ]
        )
        flat = jnp.pad(flat, (0, -flat.shape[0] % LANES)).reshape(-1, LANES)
        own = in_order(gather_slots(flat), 1)
        other = swap_section(own)
        small = [jnp.where(first, own, other), jnp.where(first, other, own)]

        def unpack(v):
            low = v.reshape(SLOTS, -1)
            at = sum(sizes[:-1])
            dtw = low[:, at : at + sizes[-1]].reshape(SLOTS, heads, quarter)
            dtw = lax.dynamic_slice(dtw, (0, own_heads * j, 0), (SLOTS, own_heads, quarter))
            dtw = jnp.transpose(dtw, (1, 0, 2)).reshape(own_heads, width)
            dtw = jnp.pad(dtw, ((0, LANES - own_heads), (0, 0)))
            v = low[:, :at].astype(F32)
            cut, at = [], 0
            for size in sizes[:-1]:
                cut.append(v[:, at : at + size])
                at += size
            gain = cut[0].reshape(1, width)
            taps = cut[1].reshape(SLOTS, 4, channels).transpose(1, 0, 2).reshape(4, -1)
            bias = cut[2].reshape(1, -1)
            conv = jnp.concatenate([taps, bias, jnp.zeros((3, taps.shape[1]), F32)], axis=0)
            pbcv = conv[:, inner:]
            pv = lax.dynamic_slice(conv, (0, own_cols * j), (8, own_cols))
            pick_heads = lambda u: lax.dynamic_slice(u[0], (own_heads * j,), (own_heads,))
            wide = jnp.repeat(pick_heads(cut[6]), HEAD)[None]
            pv = jnp.concatenate([pv[:5], pick(cut[3], j, 0)[None], wide, pv[7:]], axis=0)
            dtp = jnp.stack([pick_heads(cut[4]), -jnp.exp(pick_heads(cut[5]))])
            dtp = jnp.pad(dtp, ((0, 6), (0, LANES - own_heads)))
            return gain, dtw, pv, pbcv, dtp

        gain0, *params0 = unpack(small[0])
        gain1, *params1 = unpack(small[1])

    x_f = x_own.astype(F32)
    g1 = (mask * cot.astype(F32)).astype(BF16)
    g1_slots = gather_slots(g1)
    w0, x_slots, g1_slots, gain0, params0, gain1, params1, w1 = lax.optimization_barrier(
        (w0, x_slots, g1_slots, gain0, params0, gain1, params1, w1)
    )
    w1 = lax.all_gather(w1, DP, axis=0, tiled=False)
    blocks = lambda v: v.reshape(16, 10, 16, width)

    layer0 = (blocks(w0), *params0)
    layer1 = (blocks(w1), *params1)

    def forward_layer(x, g, gain, layer):
        w, dtw, pv, pbcv, dtp = layer
        return forward(x, g, w, dtw, gain, pv, pbcv, dtp)

    parts, saved0 = forward_layer(x_slots, None, gain0, layer0)
    branch = scatter_sum(parts)
    square = jnp.sum(branch[:, width : width + 3], axis=1, keepdims=True)
    scale0 = lax.rsqrt(square / inner + EPS)
    branch0 = branch[:, :width] * scale0
    middle = (x_f + mask * branch0).astype(BF16)

    m_slots = gather_slots(middle)
    branch_parts, saved1 = forward_layer(m_slots, g1_slots, gain1, layer1)
    own = saved1["stats"][:, 0].reshape(2, SLOTS, T)
    back = [send_shard(own, k) for k in range(SLOTS)]
    summed = sum(jnp.roll(back[k], -k, axis=1) for k in range(SLOTS))
    scale1 = lax.rsqrt(summed[0] / inner + EPS)
    cross1 = scale1 * scale1 * scale1 * summed[1] / inner
    rows1 = jnp.pad(jnp.stack([scale1, cross1], axis=1), ((0, 0), (0, 6), (0, 0)))

    def norm_back(x, gain, grad):
        scale = lax.rsqrt(jnp.mean(x * x, axis=1, keepdims=True) + EPS)
        unit = x * scale
        dn = grad * gain
        dx = scale * (dn - unit * jnp.mean(dn * unit, axis=1, keepdims=True))
        return dx, jnp.sum(grad * unit, axis=0)

    back1 = backward(
        ("gate", "scan", "input", "wgate", "wscan"),
        "backward_1",
        28,
        saved1,
        layer1,
        {"g": g1_slots, "rows": rows1},
        VMEM_BACK,
    )
    moved = [send_shard(back1[f"out{k}"], k) for k in range(SLOTS)]
    dx, gain_grad1 = norm_back(middle.astype(F32), gain1, sum(p.astype(F32) for p in moved))
    by_owner = lambda v: v.reshape(16, -1, width)
    owned1 = lax.psum_scatter(by_owner(back1["ga"]), DP, scatter_dimension=0, tiled=False)

    dmiddle = (cot.astype(F32) + dx).astype(BF16)
    g0 = (mask * dmiddle.astype(F32)).astype(BF16)
    cross0 = scale0 * scale0 * jnp.sum(g0.astype(F32) * branch0, axis=1, keepdims=True) / inner
    g0_slots = gather_slots(jnp.concatenate([g0, in_lanes([scale0, cross0])], axis=1))
    g0_slots, branch_parts = lax.optimization_barrier((g0_slots, branch_parts))
    branch = scatter_sum(branch_parts)[:, :width] * scale1[0][:, None]
    result = middle.astype(F32) + mask * branch

    back0 = backward(
        ("gate", "wgate"),
        "backward_0_gate",
        14,
        saved0,
        layer0,
        {"g": g0_slots, "core": own_core},
    )
    both = lambda kept, moved: (kept.astype(F32) + moved.astype(F32)).astype(BF16)
    a_moved = cross_core(back0["ga_send"])
    small_gate = back0["small"]
    back0["core"] = own_core
    back0.update(backward(("scan", "wscan"), "backward_0_scan", 20, saved0, layer0, back0))
    gb_send, a_moved = lax.optimization_barrier((back0["gb_send"], a_moved))
    a0 = both(back0["ga_keep"], a_moved)
    b_moved, owned1 = lax.optimization_barrier((cross_core(gb_send), owned1))
    b0 = both(back0["gb_keep"], b_moved)
    owned0 = jnp.pad(a0, ((0, 0), (0, 0), (0, 4), (0, 0), (0, 0)))
    owned0 = lax.dynamic_update_slice(owned0, b0, (0, 0, 6, 0, 0)).reshape(8, -1, width)
    owned0 = lax.psum_scatter(owned0, ("x", "z"), scatter_dimension=0, tiled=False)
    small_scan = back0["small"]
    back0.update(backward(("input",), "backward_0_input", 9, saved0, layer0, back0))
    moved0 = [send_shard(back0[f"out{k}"], k) for k in range(SLOTS)]
    dx, gain_grad0 = norm_back(x_f, gain0, sum(p.astype(F32) for p in moved0))
    dtokens = dmiddle.astype(F32) + dx
    def by_row(v):
        rows = jnp.concatenate([v[:piece], v[2 * piece :]], axis=0)
        return jnp.transpose(rows.reshape(-1, SLOTS, quarter), (1, 0, 2))

    rows1 = by_row(owned1)
    owned0, owned1, rows1, gain_grad0, dtokens, result = lax.optimization_barrier(
        (owned0, owned1, rows1, gain_grad0, dtokens, result)
    )

    result_moved = lax.ppermute(result.astype(BF16), "section", [(0, 1)]).astype(F32)
    dtokens_moved = lax.ppermute(dtokens.astype(BF16), "section", [(1, 0)]).astype(F32)
    ends = jnp.where(
        first, jnp.stack([dtokens, dtokens_moved]), jnp.stack([result_moved, result])
    )[None]

    def to_section(v0, v1):
        kept = jnp.where(first, v0, v1).astype(F32)
        return kept + swap_section(jnp.where(first, v1, v0)).astype(F32)

    got = across(jnp.concatenate([by_row(owned0), rows1], axis=0))
    out_rows = to_section(owned0[piece : 2 * piece], owned1[piece : 2 * piece]).astype(BF16)
    out_rows = jnp.transpose(out_rows.reshape(piece, SLOTS, quarter), (1, 0, 2))
    rows = got[:SLOTS].astype(F32) + got[SLOTS:].astype(F32)
    shared = jnp.sum(rows[:, 2 * piece :], axis=0).astype(BF16)
    rows = rows.astype(BF16)
    gathered = lax.all_gather(
        jnp.concatenate(
            [
                rows[:, :piece].reshape(-1, quarter),
                out_rows.reshape(-1, quarter),
                rows[:, piece : 2 * piece].reshape(-1, quarter),
                shared,
            ],
            axis=0,
        ),
        DP,
        tiled=False,
    )

    def small_of(by_pair, back, gain_grad):
        return jnp.concatenate(
            [
                by_pair.reshape(-1, LANES),
                back["small_bc"].reshape(-1, LANES),
                back["small_dt"],
                gain_grad.reshape(-1, LANES),
                back["gdt"].reshape(-1, LANES),
            ],
            axis=0,
        )

    small0 = small_of(small_gate + small_scan, back0, gain_grad0)
    small1 = small_of(back1["small"], back1, gain_grad1)
    small_sum = sum_small(to_section(small0, small1))
    everyone = in_order(gather_slots(small_sum), 1)
    n_pair, n_bc = PAIRS * 8, 2 * 8
    by_pair = everyone[:, :n_pair].reshape(SLOTS, PAIRS, 8, LANES)
    by_pair = by_pair.transpose(2, 0, 1, 3).reshape(8, inner)
    by_bc = jnp.sum(everyone[:, n_pair : n_pair + n_bc], axis=0)
    by_bc = by_bc.reshape(2, 8, LANES).transpose(1, 0, 2).reshape(8, n_state)
    at = n_pair + n_bc
    by_dt = everyone[:, at : at + 8, :own_heads].transpose(1, 0, 2).reshape(8, heads)
    at += 8
    gain_total = jnp.sum(everyone[:, at : at + width // LANES], axis=0).reshape(-1)
    at += width // LANES
    dt_rows = everyone[:, at:].reshape(SLOTS, 16, SLOTS, quarter)[:, :own_heads]
    dt_rows = pick(dt_rows, j, 2).reshape(heads, quarter)
    conv_total = jnp.concatenate([by_pair[:5], by_bc[:5]], axis=1)
    conv_own = lax.dynamic_slice(conv_total, (0, channels * j), (5, channels))
    grad_skip = jnp.sum(by_pair[6].reshape(heads, HEAD), axis=1)

    grad_in_weight, grad_out_weight = assemble(gathered, dt_rows)
    return (
        ends,
        lax.dynamic_slice(gain_total, (quarter * j,), (quarter,))[None],
        jnp.transpose(grad_in_weight)[None],
        conv_own[None, :4],
        conv_own[4][None],
        by_dt[0][None],
        by_dt[1][None],
        grad_skip[None],
        lax.dynamic_slice(by_pair[5], (own_cols * j,), (own_cols,))[None],
        grad_out_weight[None],
    )


def solution(mesh):
    sections, copies, owners = mesh.devices.shape
    fine = jax.sharding.Mesh(
        mesh.devices.reshape(sections, 2, copies // 4, 2, owners), ("section", *DP, "shard")
    )
    return jax.shard_map(
        shards,
        mesh=fine,
        in_specs=(
            P((*DP, "shard"), None, None),
            P((*DP, "shard"), None, None),
            P((*DP, "shard")),
            P("section", "shard"),
            P("section", "shard", None),
            P("section", None, "shard"),
            P("section", "shard"),
            P("section", None),
            P("section", None),
            P("section", None),
            P("section", "shard"),
            P("section", "shard", None),
        ),
        out_specs=(
            P("section", (*DP, "shard"), None, None),
            P("section", "shard"),
            P("section", "shard", None),
            P("section", None, "shard"),
            P("section", "shard"),
            P("section", None),
            P("section", None),
            P("section", None),
            P("section", "shard"),
            P("section", "shard", None),
        ),
        check_vma=False,
    )
```

```python
import jax
import jax.numpy as jnp
from jax import lax
from jax.experimental import pallas as pl
from jax.experimental.pallas import tpu as pltpu
from jax.sharding import PartitionSpec as P

F32 = jnp.float32
BF16 = jnp.bfloat16
HI = lax.Precision.HIGHEST
EPS = 1e-05
T = 128
LANES = 128
HEAD = 64
SLOTS = 4
ROWS = SLOTS * T
PAIRS = 6
STEPS = 2
HALF = PAIRS // STEPS
WIDE = HALF * LANES
VMEM_LIMIT = 34 * 1024 * 1024
VMEM_MOST = 60 * 1024 * 1024
VMEM_BACK = 56 * 1024 * 1024
DP = ("x", "z", "core")


def sigmoid(v):
    return 0.5 * jnp.tanh(0.5 * v) + 0.5


def softplus(v):
    return jnp.maximum(v, 0.0) + jnp.log1p(jnp.exp(-jnp.abs(v)))


def dot(a, b):
    return jnp.dot(a, b, preferred_element_type=F32)


def dot_nt(a, b, precision=None):
    return lax.dot_general(
        a, b, (((1,), (1,)), ((), ())), preferred_element_type=F32, precision=precision
    )


def dot_tn(a, b, precision=None):
    return lax.dot_general(
        a, b, (((0,), (0,)), ((), ())), preferred_element_type=F32, precision=precision
    )


def iota(axis):
    return lax.broadcasted_iota(jnp.int32, (T, LANES), axis)


def shift_down(v, steps):
    return jnp.where(iota(0) >= steps, pltpu.roll(v, steps, 0), 0.0)


def shift_up(v, steps):
    return jnp.where(iota(0) < T - steps, pltpu.roll(v, T - steps, 0), 0.0)


def conv_taps(cin):
    return [shift_down(cin, 3), shift_down(cin, 2), shift_down(cin, 1), cin]


def conv_sum(taps, par):
    total = par[4:5, :] + taps[0] * par[0:1, :]
    for k in range(1, 4):
        total = total + taps[k] * par[k : k + 1, :]
    return total


def conv_back(dcv, par):
    total = dcv * par[3:4, :]
    for m in range(1, 4):
        total = total + shift_up(dcv, m) * par[3 - m : 4 - m, :]
    return total


def column_sum(v):
    return jnp.sum(v, axis=0, keepdims=True)


def slot(k):
    return slice(k * T, (k + 1) * T)


def tri(lower):
    if lower:
        return (iota(0) >= iota(1)).astype(F32)
    return (iota(0) <= iota(1)).astype(F32)


def step_prep(k, pbc, dtp, run_col, run_row, step_wide):
    step = softplus(pbc[slot(k), 256:384] + dtp[0:1, :])
    run = jnp.dot(tri(True), step * dtp[1:2, :], precision=HI, preferred_element_type=F32)
    run_row[k] = jnp.transpose(run)
    left = iota(1) < HEAD
    for p in range(PAIRS):
        a, b = 2 * p, 2 * p + 1
        run_col[a, slot(k), :] = jnp.broadcast_to(run[:, a : a + 1], (T, LANES))
        run_col[b, slot(k), :] = jnp.broadcast_to(run[:, b : b + 1], (T, LANES))
        step_wide[p, slot(k), :] = jnp.where(
            left,
            jnp.broadcast_to(step[:, a : a + 1], (T, LANES)),
            jnp.broadcast_to(step[:, b : b + 1], (T, LANES)),
        )
    return step


def halves(v):
    left = iota(1) < HEAD
    zero = jnp.zeros_like(v)
    return jnp.concatenate([jnp.where(left, v, zero), jnp.where(left, zero, v)], axis=0)


def in_lanes(columns):
    lane = lax.broadcasted_iota(jnp.int32, (columns[0].shape[0], LANES), 1)
    out = jnp.zeros(lane.shape, F32)
    for n, v in enumerate(columns):
        for k in range(3):
            part = v.astype(BF16).astype(F32)
            out = jnp.where(lane == 3 * n + k, part, out)
            v = v - part
    return out.astype(BF16)


def from_lanes(v, n):
    return sum(v[:, 3 * n + k : 3 * n + k + 1].astype(F32) for k in range(3))


class Refs:
    pass


def kernel_call(body, name, ins, outs, scratch, cost_us, limit=VMEM_LIMIT):
    in_names, out_names, scratch_names = list(ins), list(outs), list(scratch)

    def run(*refs):
        for h in range(STEPS):
            rf = Refs()
            for key, ref in zip(in_names + out_names + scratch_names, refs):
                spec = ins.get(key) or outs.get(key)
                blocks = spec[-2:] if spec and len(spec) > 2 else None
                if blocks and blocks[1](1) != blocks[1](0):
                    at = [
                        slice(n * size, (n + 1) * size) if n else slice(0, size)
                        for n, size in zip(blocks[1](h), blocks[0])
                    ]
                    setattr(rf, key + "_whole", ref)
                    ref = ref.at[tuple(at)]
                setattr(rf, key, ref)
            body(rf, h)

    res = pl.pallas_call(
        run,
        in_specs=[
            pl.BlockSpec(memory_space=pltpu.VMEM if len(ins[n]) > 2 else ins[n][1])
            for n in in_names
        ],
        out_specs=[pl.BlockSpec(memory_space=pltpu.VMEM) for n in out_names],
        out_shape=[jax.ShapeDtypeStruct(outs[n][0], outs[n][1]) for n in out_names],
        scratch_shapes=[
            pltpu.VMEM(*scratch[n]) if isinstance(scratch[n], tuple) else scratch[n]
            for n in scratch_names
        ],
        compiler_params=pltpu.CompilerParams(vmem_limit_bytes=limit),
        cost_estimate=pl.CostEstimate(
            flops=int(cost_us * 1.1e9), bytes_accessed=1 << 20, transcendentals=0
        ),
        name=name,
    )(*[ins[n][0] for n in in_names])
    return dict(zip(out_names, res))


def when(condition):
    return (lambda f: f()) if condition else (lambda f: None)


def whole(v):
    return (v, v.shape, lambda h: (0,) * v.ndim)


def whole_out(shape, dtype):
    return (shape, dtype, shape, lambda h: (0,) * len(shape))


def by_step(v, block):
    return (v, block, lambda h: (h,) + (0,) * (len(block) - 1))


def by_step_out(shape, dtype, block):
    return (shape, dtype, block, lambda h: (h,) + (0,) * (len(block) - 1))


def lanes_by_step(v):
    return (v, (v.shape[0], WIDE), lambda h: (0, h))


def lanes_by_step_out(shape, dtype):
    return (shape, dtype, (shape[0], WIDE), lambda h: (0, h))


def in_hbm(v):
    return (v, pltpu.HBM)


WEIGHT_GROUPS = {"wo": (0, 3), "wg": (3, 3), "wv": (6, 3), "ws": (9, 1)}


class Copies:
    def __init__(self, sems):
        self.sems, self.copies = sems, {}

    def add(self, key, source, target):
        self.copies[key] = (source, target, self.sems.at[len(self.copies)])

    def add_weights(self, rf, keys):
        for key in keys:
            at, count = WEIGHT_GROUPS[key]
            self.add(key, rf.w.at[:, pl.ds(at, count)], getattr(rf, key))

    def start(self):
        for copy in self.copies.values():
            pltpu.make_async_copy(*copy).start()

    def wait(self, *keys):
        for key in keys:
            pltpu.make_async_copy(*self.copies[key]).wait()


def weight_scratch(scratch, keys, width):
    for key in keys:
        scratch[key] = ((16, WEIGHT_GROUPS[key][1], 16, width), BF16)


def half_rows(ref, h):
    v = ref[pl.ds(8 * h, 8)]
    return v.reshape(WIDE, v.shape[-1])


def pair_lanes(p):
    return slice(p * LANES, (p + 1) * LANES)


def flat_rows(ref):
    v = ref[...]
    return v.reshape(-1, v.shape[-1])


def mixed_bc(rf, k, c):
    lanes = slice(c * LANES, (c + 1) * LANES)
    cv = conv_sum(conv_taps(rf.pbc[slot(k), lanes]), rf.pbcv[:, lanes])
    return cv * sigmoid(cv)


def forward(x_slots, g_slots, w, dtw, gain, pv, pbcv, dtp):
    width = x_slots[0].shape[1]
    with_grad = g_slots is not None

    def body(rf, h):
        copies = Copies(rf.sems)
        for k in range(SLOTS):
            copies.add(f"x{k}", getattr(rf, f"x{k}"), rf.x_all.at[k])
        copies.add_weights(rf, ("ws", "wg", "wv", "wo"))
        if with_grad:
            for k in range(SLOTS):
                copies.add(f"g{k}", getattr(rf, f"g{k}"), rf.g_all.at[slot(k)])

        @when(h == 0)
        def _prep():
            copies.start()
            for k in range(SLOTS):
                copies.wait(f"x{k}")
                x = rf.x_all[k].astype(F32)
                scale = lax.rsqrt(jnp.mean(x * x, axis=1, keepdims=True) + EPS)
                rf.normed[slot(k), :] = (x * scale * rf.gain[...]).astype(BF16)
            copies.wait("ws")
            rf.pbc[:, 0:256] = dot_nt(rf.normed[...], flat_rows(rf.ws))
            rf.pbc[:, 256:384] = dot_nt(rf.normed[...], rf.dtw[...])
            for k in range(SLOTS):
                rf.scores[k] = dot_nt(mixed_bc(rf, k, 1), mixed_bc(rf, k, 0), HI) * tri(True)
                step_prep(k, rf.pbc, rf.dtp, rf.run_col, rf.run_row, rf.step_wide)
            rf.square[...] = jnp.zeros_like(rf.square)
            rf.cross[...] = jnp.zeros_like(rf.cross)
            copies.wait("wg", "wv", "wo")
            if with_grad:
                copies.wait(*[f"g{k}" for k in range(SLOTS)])

        rf.proj[0, :, 0:WIDE] = dot_nt(rf.normed[...], half_rows(rf.wg, h))
        rf.proj[0, :, WIDE : 2 * WIDE] = dot_nt(rf.normed[...], half_rows(rf.wv, h))
        if with_grad:
            q_all = dot_nt(rf.g_all[...], half_rows(rf.wo, h))
        for p in range(HALF):
            lanes = pair_lanes(p)
            par = rf.pv[:, lanes]
            pair = HALF * h + p
            for k in range(SLOTS):
                gate = rf.proj[0, slot(k), lanes]
                cv = conv_sum(
                    conv_taps(rf.proj[0, slot(k), WIDE + p * LANES : WIDE + (p + 1) * LANES]), par
                )
                values = cv * sigmoid(cv)
                scaled = (values * rf.step_wide[pair, slot(k), :]).astype(BF16)
                weights = []
                for a in range(2):
                    gap = (
                        rf.run_col[2 * pair + a, slot(k), :]
                        - rf.run_row[k, pl.ds(2 * pair + a, 1), :]
                    )
                    decay = jnp.exp(jnp.minimum(gap, 0.0))
                    weights.append((rf.scores[k] * decay).astype(BF16))
                y = dot(jnp.concatenate(weights, axis=1), halves(scaled))
                rf.y[0, slot(k), lanes] = y
                scanned = y + par[6:7, :] * values
                gated = scanned * (gate * sigmoid(gate))
                rf.square[slot(k), :] += gated * gated
                scaled_out = gated * par[5:6, :]
                rf.u_all[h, slot(k), lanes] = scaled_out.astype(BF16)
                if with_grad:
                    rf.cross[slot(k), :] += q_all[slot(k), lanes] * scaled_out

        @when(h == STEPS - 1)
        def _finish():
            u = jnp.concatenate([rf.u_all[a] for a in range(STEPS)], axis=1)
            for n in range(0, width, 512):
                part = dot(u, rf.wo[:, :, :, n : n + 512].reshape(STEPS * WIDE, 512)).astype(BF16)
                for k in range(SLOTS):
                    getattr(rf, f"out{k}")[:, n : n + 512] = part[slot(k), :]
            for k in range(SLOTS):
                total = jnp.sum(rf.square[slot(k), :], axis=1, keepdims=True)
                getattr(rf, f"out{k}")[:, width:] = in_lanes([total])
            ones = jnp.ones((8, LANES), F32)
            rf.stats[0] = dot_nt(ones, rf.square[...], HI)
            rf.stats[1] = dot_nt(ones, rf.cross[...], HI)

    ins = {f"x{k}": in_hbm(v) for k, v in enumerate(x_slots)}
    if with_grad:
        ins.update({f"g{k}": in_hbm(v) for k, v in enumerate(g_slots)})
    ins.update(
        gain=whole(gain),
        w=in_hbm(w),
        dtw=whole(dtw),
        pv=lanes_by_step(pv),
        pbcv=whole(pbcv),
        dtp=whole(dtp),
    )
    outs = {f"out{k}": whole_out((T, width + LANES), BF16) for k in range(SLOTS)}
    outs.update(
        stats=whole_out((2, 8, ROWS), F32),
        normed=whole_out((ROWS, width), BF16),
        proj=by_step_out((STEPS, ROWS, 2 * WIDE), F32, (1, ROWS, 2 * WIDE)),
        y=by_step_out((STEPS, ROWS, WIDE), F32, (1, ROWS, WIDE)),
        pbc=whole_out((ROWS, 384), F32),
    )
    scratch = dict(
        scores=((SLOTS, T, T), F32),
        run_col=((2 * PAIRS, ROWS, LANES), F32),
        run_row=((SLOTS, T, LANES), F32),
        step_wide=((PAIRS, ROWS, LANES), F32),
        u_all=((STEPS, ROWS, WIDE), BF16),
        square=((ROWS, LANES), F32),
        cross=((ROWS, LANES), F32),
        x_all=((SLOTS, T, width), BF16),
        sems=pltpu.SemaphoreType.DMA((2 * SLOTS + 4,)),
    )
    weight_scratch(scratch, ("ws", "wg", "wv", "wo"), width)
    if with_grad:
        scratch["g_all"] = ((ROWS, width), BF16)
    res = kernel_call(body, "layer_forward", ins, outs, scratch, 18, VMEM_MOST)
    return [res[f"out{k}"] for k in range(SLOTS)], res


def head_columns(pair):
    target = 2 * pair + (iota(0) >= HEAD).astype(jnp.int32)
    one = (iota(1) == target).astype(BF16)
    return jnp.concatenate([one, one], axis=0)


def head_sum(v, columns):
    high = v.astype(BF16)
    low = (v - high.astype(F32)).astype(BF16)
    return dot(jnp.concatenate([high, low], axis=1), columns)


def put_by_core(rf, key, x, at, part):
    keep, send = getattr(rf, key + "_keep"), getattr(rf, key + "_send")
    groups = slice(at, at + part.shape[2])
    for c in range(2):

        @pl.when(rf.core[0] == c)
        def _store(c=c):
            for z in range(4):
                keep[x, z, groups] = part[z, c]
                send[x, z, groups] = part[z, 1 - c]


def backward(stages, name, cost_us, saved, layer, have, limit=VMEM_LIMIT):
    gate, scan, inp, wgate, wscan = (
        s in stages for s in ("gate", "scan", "input", "wgate", "wscan")
    )
    width = saved["normed"].shape[1]
    w, dtw, pv, pbcv, dtp = layer
    elementwise = gate or scan
    fetched = (("wo",) if gate else ()) + (("wg", "wv", "ws") if inp else ())
    in_slots = gate and "rows" not in have

    def body(rf, h):
        copies = Copies(rf.sems) if gate or wgate or inp else None
        if gate or wgate:
            for k in range(SLOTS):
                source = getattr(rf, f"g{k}")
                copies.add(f"g{k}", source.at[:, pl.ds(0, width)], rf.g_all.at[slot(k)])
                if in_slots:
                    copies.add(f"e{k}", source.at[:, pl.ds(width, LANES)], rf.e_all.at[k])
        if copies:
            copies.add_weights(rf, fetched)

        @when(h == 0)
        def _prep():
            if copies:
                copies.start()
            for k in range(SLOTS):
                if gate or wgate:
                    copies.wait(f"g{k}")
                if in_slots:
                    copies.wait(f"e{k}")
                if gate:
                    for row, ref in ((0, rf.scale_row), (1, rf.cross_row)):
                        if "rows" in have:
                            ref[slot(k), :] = jnp.transpose(
                                jnp.broadcast_to(rf.rows[k, row : row + 1, :], (T, LANES))
                            )
                        else:
                            column = from_lanes(rf.e_all[k], row)
                            ref[slot(k), :] = jnp.broadcast_to(column, (T, LANES))
                if scan:
                    inbound, outbound = mixed_bc(rf, k, 0), mixed_bc(rf, k, 1)
                    rf.mixed[0, slot(k), :] = inbound
                    rf.mixed[1, slot(k), :] = outbound
                    rf.scores[k] = dot_nt(inbound, outbound, HI) * tri(False)
                    rf.step_all[slot(k), :] = step_prep(
                        k, rf.pbc, rf.dtp, rf.run_col, rf.run_row, rf.step_wide
                    )
            if scan:
                rf.dscores[...] = jnp.zeros_like(rf.dscores)
                rf.dstep[...] = jnp.zeros_like(rf.dstep)
                rf.drun[...] = jnp.zeros_like(rf.drun)
            if inp:
                rf.total[...] = jnp.zeros_like(rf.total)
            if copies:
                copies.wait(*fetched)

        if gate:
            q_all = dot_nt(rf.g_all[...], half_rows(rf.wo, h))
        for p in range(HALF if elementwise else 0):
            lanes = pair_lanes(p)
            par = rf.pv[:, lanes]
            pair = HALF * h + p
            sums = [jnp.zeros((1, LANES), F32) for _ in range(8)]
            if scan:
                columns = head_columns(pair)
            for k in range(SLOTS):
                taps = conv_taps(rf.proj[0, slot(k), WIDE + p * LANES : WIDE + (p + 1) * LANES])
                cv = conv_sum(taps, par)
                sig_c = sigmoid(cv)
                values = cv * sig_c
                y = rf.y[0, slot(k), lanes]
                if gate:
                    gate_in = rf.proj[0, slot(k), lanes]
                    sig_g = sigmoid(gate_in)
                    silu_g = gate_in * sig_g
                    scanned = y + par[6:7, :] * values
                    gated = scanned * silu_g
                    grad_no = q_all[slot(k), lanes]
                    scale = rf.scale_row[slot(k), :]
                    dgated = scale * (grad_no * par[5:6, :]) - rf.cross_row[slot(k), :] * gated
                    norm = gated * scale
                    sums[5] += column_sum(grad_no * norm)
                    rf.u[slot(k), lanes] = (norm * par[5:6, :]).astype(BF16)
                    dscan = dgated * silu_g
                    dgate = dgated * scanned * (sig_g * (1.0 + gate_in * (1.0 - sig_g)))
                    sums[6] += column_sum(dscan * values)
                    rf.dg[slot(k), lanes] = dgate.astype(BF16)
                    if not scan:
                        rf.dscan[slot(k), lanes] = dscan
                else:
                    dscan = rf.dscan[slot(k), lanes]
                if not scan:
                    continue
                wide = rf.step_wide[pair, slot(k), :]
                dy = dscan.astype(BF16)
                scaled = (values * wide).astype(BF16)
                dweights = dot_nt(halves(scaled), dy)
                weights = []
                dscore = rf.dscores[k]
                for a in range(2):
                    gap = (
                        rf.run_row[k, pl.ds(2 * pair + a, 1), :]
                        - rf.run_col[2 * pair + a, slot(k), :]
                    )
                    decay = jnp.exp(jnp.minimum(gap, 0.0))
                    weights.append((rf.scores[k] * decay).astype(BF16))
                    dscore = dscore + dweights[slot(a), :] * decay
                rf.dscores[k] = dscore
                dscaled = dot(jnp.concatenate(weights, axis=1), halves(dy))
                rf.dstep[slot(k), :] += head_sum(dscaled * values, columns)
                rf.drun[slot(k), :] += head_sum(
                    dy.astype(F32) * y - scaled.astype(F32) * dscaled, columns
                )
                dvalues = dscaled * wide + par[6:7, :] * dscan
                dcv = dvalues * (sig_c * (1.0 + cv * (1.0 - sig_c)))
                for t in range(4):
                    sums[t] += column_sum(dcv * taps[t])
                sums[4] += column_sum(dcv)
                rf.dv[slot(k), lanes] = conv_back(dcv, par).astype(BF16)
            rf.small[p] = jnp.concatenate(sums, axis=0)
        if wgate and wscan:
            for at, left, right in (
                (0, rf.dg, rf.normed),
                (3, rf.u, rf.g_all),
                (6, rf.dv, rf.normed),
            ):
                part = dot_tn(left[...], right[...]).astype(BF16)
                rf.ga[:, at : at + 3] = part.reshape(8, 3, 16, width)
            if not scan:
                part = dot_tn(rf.dbc_half[...], rf.normed[...]).astype(BF16)
                rf.ga[:, 9] = part.reshape(8, 16, width)
        elif wgate:
            for at, left, right in ((0, rf.dg, rf.normed), (3, rf.u, rf.g_all)):
                part = dot_tn(left[...], right[...]).astype(BF16)
                put_by_core(rf, "ga", h, at, part.reshape(4, 2, 3, 16, width))
        elif wscan:
            part = dot_tn(rf.dv[...], rf.normed[...]).astype(BF16)
            put_by_core(rf, "gb", h, 0, part.reshape(4, 2, 3, 16, width))
        if inp:
            rf.total[...] += dot(rf.dg[...], half_rows(rf.wg, h)) + dot(
                rf.dv[...], half_rows(rf.wv, h)
            )

        @when(h == STEPS - 1)
        def _finish():
            if scan:
                sums = [[jnp.zeros((1, LANES), F32) for _ in range(8)] for _ in range(2)]
                dt_sums = [jnp.zeros((1, LANES), F32) for _ in range(8)]
                live = iota(1) < 2 * PAIRS
                for k in range(SLOTS):
                    dscore = rf.dscores[k] * tri(False)
                    dmixed = (
                        jnp.dot(
                            dscore,
                            rf.mixed[1, slot(k), :],
                            precision=HI,
                            preferred_element_type=F32,
                        ),
                        dot_tn(dscore, rf.mixed[0, slot(k), :], HI),
                    )
                    for c in range(2):
                        lanes = slice(c * LANES, (c + 1) * LANES)
                        par = rf.pbcv[:, lanes]
                        taps = conv_taps(rf.pbc[slot(k), lanes])
                        cv = conv_sum(taps, par)
                        sig = sigmoid(cv)
                        dcv = dmixed[c] * (sig * (1.0 + cv * (1.0 - sig)))
                        for t in range(4):
                            sums[c][t] += column_sum(dcv * taps[t])
                        sums[c][4] += column_sum(dcv)
                        rf.dbc[slot(k), lanes] = conv_back(dcv, par).astype(BF16)
                    dlog = jnp.dot(
                        tri(False), rf.drun[slot(k), :], precision=HI, preferred_element_type=F32
                    )
                    grad_step = rf.dstep[slot(k), :] + dlog * rf.dtp[1:2, :]
                    dt_sums[1] += column_sum(dlog * rf.step_all[slot(k), :])
                    draw = grad_step * sigmoid(rf.pbc[slot(k), 256:384] + rf.dtp[0:1, :])
                    draw = jnp.where(live, draw, 0.0)
                    dt_sums[0] += column_sum(draw)
                    rf.dbc[slot(k), 256:384] = draw.astype(BF16)
                rf.small_bc[0] = jnp.concatenate(sums[0], axis=0)
                rf.small_bc[1] = jnp.concatenate(sums[1], axis=0)
                dt_sums[1] = dt_sums[1] * rf.dtp[1:2, :]
                rf.small_dt[...] = jnp.concatenate(dt_sums, axis=0)
            if wscan and wgate and scan:
                part = dot_tn(rf.dbc[:, 0:256], rf.normed[...]).astype(BF16)
                rf.ga_whole[:, 9] = part.reshape(16, 16, width)
            if wscan and not wgate:
                part = dot_tn(rf.dbc[:, 0:256], rf.normed[...]).astype(BF16)
                part = part.reshape(2, 4, 2, 1, 16, width)
                for a in range(2):
                    put_by_core(rf, "gb", a, 3, part[a])
            if wscan:
                rf.gdt[...] = dot_tn(rf.dbc[:, 256:384], rf.normed[...])[0:16]
            if inp:
                final = (
                    rf.total[...]
                    + dot(rf.dbc[:, 0:256], flat_rows(rf.ws))
                    + dot(rf.dbc[:, 256:384], rf.dtw[...])
                )
                for k in range(SLOTS):
                    getattr(rf, f"out{k}")[...] = final[slot(k), :].astype(BF16)

    ins, outs, scratch = {}, {}, {}
    heads_cols = STEPS * WIDE
    if gate or wgate:
        for k, v in enumerate(have["g"]):
            ins[f"g{k}"] = in_hbm(v)
        scratch["g_all"] = ((ROWS, width), BF16)
    if gate:
        if in_slots:
            scratch["e_all"] = ((SLOTS, T, LANES), BF16)
        else:
            ins["rows"] = whole(have["rows"])
        scratch["scale_row"] = ((ROWS, LANES), F32)
        scratch["cross_row"] = ((ROWS, LANES), F32)
        outs["u"] = lanes_by_step_out((ROWS, heads_cols), BF16)
        outs["dg"] = lanes_by_step_out((ROWS, heads_cols), BF16)
        if not scan:
            outs["dscan"] = lanes_by_step_out((ROWS, heads_cols), F32)
    if elementwise:
        ins["proj"] = by_step(saved["proj"], (1, ROWS, 2 * WIDE))
        ins["y"] = by_step(saved["y"], (1, ROWS, WIDE))
        ins["pv"] = lanes_by_step(pv)
        outs["small"] = by_step_out((PAIRS, 8, LANES), F32, (HALF, 8, LANES))
    if scan:
        ins["pbc"] = whole(saved["pbc"])
        ins["pbcv"] = whole(pbcv)
        ins["dtp"] = whole(dtp)
        if not gate:
            ins["dscan"] = lanes_by_step(have["dscan"])
        outs["dv"] = lanes_by_step_out((ROWS, heads_cols), BF16)
        outs["dbc"] = whole_out((ROWS, 384), BF16)
        outs["small_bc"] = whole_out((2, 8, LANES), F32)
        outs["small_dt"] = whole_out((8, LANES), F32)
        scratch.update(
            mixed=((2, ROWS, LANES), F32),
            scores=((SLOTS, T, T), F32),
            run_col=((2 * PAIRS, ROWS, LANES), F32),
            run_row=((SLOTS, T, LANES), F32),
            step_wide=((PAIRS, ROWS, LANES), F32),
            step_all=((ROWS, LANES), F32),
            dscores=((SLOTS, T, T), F32),
            dstep=((ROWS, LANES), F32),
            drun=((ROWS, LANES), F32),
        )
    if inp:
        ins["dtw"] = whole(dtw)
        scratch["total"] = ((ROWS, width), F32)
        outs.update({f"out{k}": whole_out((T, width), BF16) for k in range(SLOTS)})
    if fetched:
        ins["w"] = in_hbm(w)
        weight_scratch(scratch, fetched, width)
    if gate or wgate or inp:
        scratch["sems"] = pltpu.SemaphoreType.DMA((2 * SLOTS + 4,))
    if wgate or wscan:
        ins["normed"] = whole(saved["normed"])
    if not gate and (wgate or inp):
        ins["dg"] = lanes_by_step(have["dg"])
    if wgate and not gate:
        ins["u"] = lanes_by_step(have["u"])
    if not scan and (wscan or inp):
        ins["dv"] = lanes_by_step(have["dv"])
        ins["dbc"] = whole(have["dbc"])
    if wgate and wscan:
        if not scan:
            ins["dbc_half"] = (have["dbc"], (ROWS, LANES), lambda h: (0, h))
        outs["ga"] = by_step_out((16, 10, 16, width), BF16, (8, 10, 16, width))
    elif wgate or wscan:
        ins["core"] = have["core"]
        key, groups = ("ga", 6) if wgate else ("gb", 4)
        for end in ("_keep", "_send"):
            outs[key + end] = whole_out((2, 4, groups, 16, width), BF16)
    if wscan:
        outs["gdt"] = whole_out((16, width), F32)
    return kernel_call(body, name, ins, outs, scratch, cost_us, limit)


def assemble(parts, dt_rows):
    quarter = parts.shape[2]
    block = 16 * 48
    total = 8 * block + 16 * 16 + dt_rows.shape[0]

    def body(inw, outw, shared, dt, grad_in, grad_out):
        i = pl.program_id(0)

        @pl.when(i < 8)
        def _columns():
            grad_in[...] = inw[...].reshape(block, quarter).astype(F32)

        @pl.when(i < SLOTS)
        def _out():
            grad_out[...] = outw[...].reshape(block, quarter).astype(F32)

        @pl.when(i == 8)
        def _shared():
            grad_in[...] = jnp.zeros_like(grad_in)
            grad_in[0:256, :] = shared[...].reshape(256, quarter).astype(F32)
            grad_in[256 : 256 + dt_rows.shape[0], :] = dt[...]

    last = SLOTS - 1
    return pl.pallas_call(
        body,
        grid=(9,),
        in_specs=[
            pl.BlockSpec(
                (16, 48, quarter),
                lambda i: (0, jnp.where(i < SLOTS, i, jnp.minimum(i + SLOTS, 11)), 0),
            ),
            pl.BlockSpec((16, 48, quarter), lambda i: (0, SLOTS + jnp.minimum(i, last), 0)),
            pl.BlockSpec((16, 16, quarter), lambda i: (0, 36, 0)),
            pl.BlockSpec(dt_rows.shape, lambda i: (0, 0)),
        ],
        out_specs=[
            pl.BlockSpec((block, quarter), lambda i: (i, 0)),
            pl.BlockSpec((block, quarter), lambda i: (0, jnp.minimum(i, last))),
        ],
        out_shape=[
            jax.ShapeDtypeStruct((total, quarter), F32),
            jax.ShapeDtypeStruct((block, SLOTS * quarter), F32),
        ],
        compiler_params=pltpu.CompilerParams(vmem_limit_bytes=VMEM_MOST),
        name="assemble",
    )(parts, parts, parts, dt_rows)


def ring(n, k):
    return [(i, (i + k) % n) for i in range(n)]


def send_shard(v, k):
    return lax.ppermute(v, "shard", ring(SLOTS, k)) if k else v


def send_across(v, k):
    pairs = [
        (sec * SLOTS + y, (1 - sec) * SLOTS + (y + k) % SLOTS)
        for sec in range(2)
        for y in range(SLOTS)
    ]
    return lax.ppermute(v, ("section", "shard"), pairs)


def across(v):
    return lax.all_to_all(v, ("section", "shard"), 0, 0)


def swap_section(v):
    return lax.ppermute(v, "section", [(0, 1), (1, 0)])


def dp_index(x, z, c):
    return x * 8 + z * 2 + c


def dp_pairs(move):
    pairs = []
    for x in range(2):
        for z in range(4):
            for c in range(2):
                pairs.append((dp_index(x, z, c), dp_index(*move(x, z, c))))
    return pairs


def pick(v, index, axis):
    return lax.dynamic_index_in_dim(v, index, axis, keepdims=False)


def gather_slots(v):
    return [send_shard(v, (-k) % SLOTS) for k in range(SLOTS)]


def scatter_sum(slots):
    parts = [send_shard(slots[k], k) for k in range(SLOTS)]
    return sum(p.astype(F32) for p in parts)


def cross_core(v):
    return lax.ppermute(v, DP, dp_pairs(lambda x, z, c: (x, z, 1 - c)))


def sum_small(v):
    v = v + sum(
        lax.ppermute(v, DP, dp_pairs(lambda x, z, c: (x, (z + k) % 4, c))) for k in range(1, 4)
    )
    return v + lax.ppermute(v, DP, dp_pairs(lambda x, z, c: (1 - x, z, c)))


def in_order(parts, sign):
    j = lax.axis_index("shard")
    stacked = jnp.stack(parts)
    return jnp.take(stacked, (sign * (jnp.arange(SLOTS) - j)) % SLOTS, axis=0)


def shards(
    tokens,
    cotangent,
    lengths,
    norm_gain,
    in_weight,
    conv_weight,
    conv_bias,
    dt_bias,
    a_log,
    d_skip,
    gate_gain,
    out_weight,
):
    sec = lax.axis_index("section")
    d = lax.axis_index(DP)
    j = lax.axis_index("shard")
    core = d % 2
    first = sec == 0
    width = tokens.shape[2]
    quarter = norm_gain.shape[1]
    channels = conv_bias.shape[1]
    own_cols = gate_gain.shape[1]
    inner = own_cols * SLOTS
    heads = dt_bias.shape[1]
    own_heads = heads // SLOTS
    n_state = 2 * LANES
    piece = own_cols // 16
    piece_bc = n_state // 16
    own_core = (core.astype(jnp.int32)[None], pltpu.SMEM)

    x_own = pick(tokens, sec, 0)
    cot = pick(cotangent, sec, 0)
    length = pick(lengths, sec, 0)
    mask = (jnp.arange(T, dtype=jnp.int32) < length).astype(F32)[:, None]

    columns = jnp.transpose(in_weight[0])
    with jax.named_scope("weights"):

        def cut(start, rows):
            return lax.dynamic_slice(columns, (start, 0), (rows, quarter))

        def columns_of(to):
            return jnp.concatenate(
                [
                    cut(own_cols * to + piece * d, piece),
                    cut(inner + own_cols * to + piece * d, piece),
                    cut(2 * inner + piece_bc * d, piece_bc),
                ],
                axis=0,
            )

        cuts = [columns_of((j + k) % SLOTS) for k in range(SLOTS)]
        o_own = lax.dynamic_slice(out_weight[0], (piece * d, 0), (piece, width))
        o_other = swap_section(o_own)

        w_own = [send_shard(cuts[k], k) for k in range(SLOTS)]
        w_other = [send_across(cuts[k], k) for k in range(SLOTS)]

        def from_parts(parts, others, o, o_others, own):
            pieces = [jnp.where(own, p, q) for p, q in zip(parts, others)]
            lanes = []
            for y in range(SLOTS):
                v = pieces[0]
                for k in range(1, SLOTS):
                    v = jnp.where((j - y) % SLOTS == k, pieces[k], v)
                lanes.append(v)
            return jnp.concatenate(
                [jnp.where(own, o, o_others), jnp.concatenate(lanes, axis=1)], axis=0
            )

        w0 = from_parts(w_own, w_other, o_own, o_other, first)
        w1 = from_parts(w_own, w_other, o_own, o_other, ~first)
        w0, w1, x_own, cot = lax.optimization_barrier((w0, w1, x_own, cot))
        w0 = lax.all_gather(w0, DP, axis=0, tiled=False)
        x_slots = gather_slots(x_own)
        x_slots, norm_gain = lax.optimization_barrier((x_slots, norm_gain))

    with jax.named_scope("small_weights"):
        dt_columns = columns[2 * inner + n_state :]
        sizes = [quarter, 4 * channels, channels, own_cols, heads, heads, heads, heads * quarter]
        flat = jnp.concatenate(
            [
                norm_gain[0],
                conv_weight[0].reshape(-1),
                conv_bias[0],
                gate_gain[0],
                dt_bias[0],
                a_log[0],
                d_skip[0],
                dt_columns.reshape(-1),
            ]
        )
        flat = jnp.pad(flat, (0, -flat.shape[0] % LANES)).reshape(-1, LANES)
        own = in_order(gather_slots(flat), 1)
        other = swap_section(own)
        small = [jnp.where(first, own, other), jnp.where(first, other, own)]

        def unpack(v):
            low = v.reshape(SLOTS, -1)
            at = sum(sizes[:-1])
            dtw = low[:, at : at + sizes[-1]].reshape(SLOTS, heads, quarter)
            dtw = lax.dynamic_slice(dtw, (0, own_heads * j, 0), (SLOTS, own_heads, quarter))
            dtw = jnp.transpose(dtw, (1, 0, 2)).reshape(own_heads, width)
            dtw = jnp.pad(dtw, ((0, LANES - own_heads), (0, 0)))
            v = low[:, :at].astype(F32)
            cut, at = [], 0
            for size in sizes[:-1]:
                cut.append(v[:, at : at + size])
                at += size
            gain = cut[0].reshape(1, width)
            taps = cut[1].reshape(SLOTS, 4, channels).transpose(1, 0, 2).reshape(4, -1)
            bias = cut[2].reshape(1, -1)
            conv = jnp.concatenate([taps, bias, jnp.zeros((3, taps.shape[1]), F32)], axis=0)
            pbcv = conv[:, inner:]
            pv = lax.dynamic_slice(conv, (0, own_cols * j), (8, own_cols))
            pick_heads = lambda u: lax.dynamic_slice(u[0], (own_heads * j,), (own_heads,))
            wide = jnp.repeat(pick_heads(cut[6]), HEAD)[None]
            pv = jnp.concatenate([pv[:5], pick(cut[3], j, 0)[None], wide, pv[7:]], axis=0)
            dtp = jnp.stack([pick_heads(cut[4]), -jnp.exp(pick_heads(cut[5]))])
            dtp = jnp.pad(dtp, ((0, 6), (0, LANES - own_heads)))
            return gain, dtw, pv, pbcv, dtp

        gain0, *params0 = unpack(small[0])
        gain1, *params1 = unpack(small[1])

    x_f = x_own.astype(F32)
    g1 = (mask * cot.astype(F32)).astype(BF16)
    g1_slots = gather_slots(g1)
    w0, x_slots, g1_slots, gain0, params0, gain1, params1, w1 = lax.optimization_barrier(
        (w0, x_slots, g1_slots, gain0, params0, gain1, params1, w1)
    )
    w1 = lax.all_gather(w1, DP, axis=0, tiled=False)
    blocks = lambda v: v.reshape(16, 10, 16, width)

    layer0 = (blocks(w0), *params0)
    layer1 = (blocks(w1), *params1)

    def forward_layer(x, g, gain, layer):
        w, dtw, pv, pbcv, dtp = layer
        return forward(x, g, w, dtw, gain, pv, pbcv, dtp)

    parts, saved0 = forward_layer(x_slots, None, gain0, layer0)
    branch = scatter_sum(parts)
    square = jnp.sum(branch[:, width : width + 3], axis=1, keepdims=True)
    scale0 = lax.rsqrt(square / inner + EPS)
    branch0 = branch[:, :width] * scale0
    middle = (x_f + mask * branch0).astype(BF16)

    m_slots = gather_slots(middle)
    branch_parts, saved1 = forward_layer(m_slots, g1_slots, gain1, layer1)
    own = saved1["stats"][:, 0].reshape(2, SLOTS, T)
    back = [send_shard(own, k) for k in range(SLOTS)]
    summed = sum(jnp.roll(back[k], -k, axis=1) for k in range(SLOTS))
    scale1 = lax.rsqrt(summed[0] / inner + EPS)
    cross1 = scale1 * scale1 * scale1 * summed[1] / inner
    rows1 = jnp.pad(jnp.stack([scale1, cross1], axis=1), ((0, 0), (0, 6), (0, 0)))

    def norm_back(x, gain, grad):
        scale = lax.rsqrt(jnp.mean(x * x, axis=1, keepdims=True) + EPS)
        unit = x * scale
        dn = grad * gain
        dx = scale * (dn - unit * jnp.mean(dn * unit, axis=1, keepdims=True))
        return dx, jnp.sum(grad * unit, axis=0)

    back1 = backward(
        ("gate", "scan", "input", "wgate", "wscan"),
        "backward_1",
        28,
        saved1,
        layer1,
        {"g": g1_slots, "rows": rows1},
        VMEM_BACK,
    )
    moved = [send_shard(back1[f"out{k}"], k) for k in range(SLOTS)]
    dx, gain_grad1 = norm_back(middle.astype(F32), gain1, sum(p.astype(F32) for p in moved))
    by_owner = lambda v: v.reshape(16, -1, width)
    owned1 = lax.psum_scatter(by_owner(back1["ga"]), DP, scatter_dimension=0, tiled=False)

    dmiddle = (cot.astype(F32) + dx).astype(BF16)
    g0 = (mask * dmiddle.astype(F32)).astype(BF16)
    cross0 = scale0 * scale0 * jnp.sum(g0.astype(F32) * branch0, axis=1, keepdims=True) / inner
    g0_slots = gather_slots(jnp.concatenate([g0, in_lanes([scale0, cross0])], axis=1))
    g0_slots, branch_parts = lax.optimization_barrier((g0_slots, branch_parts))
    branch = scatter_sum(branch_parts)[:, :width] * scale1[0][:, None]
    result = middle.astype(F32) + mask * branch

    back0 = backward(
        ("gate", "wgate"),
        "backward_0_gate",
        14,
        saved0,
        layer0,
        {"g": g0_slots, "core": own_core},
    )
    both = lambda kept, moved: (kept.astype(F32) + moved.astype(F32)).astype(BF16)
    a_moved = cross_core(back0["ga_send"])
    small_gate = back0["small"]
    back0["core"] = own_core
    back0.update(backward(("scan", "wscan"), "backward_0_scan", 20, saved0, layer0, back0))
    gb_send, a_moved = lax.optimization_barrier((back0["gb_send"], a_moved))
    a0 = both(back0["ga_keep"], a_moved)
    b_moved, owned1 = lax.optimization_barrier((cross_core(gb_send), owned1))
    b0 = both(back0["gb_keep"], b_moved)
    owned0 = jnp.pad(a0, ((0, 0), (0, 0), (0, 4), (0, 0), (0, 0)))
    owned0 = lax.dynamic_update_slice(owned0, b0, (0, 0, 6, 0, 0)).reshape(8, -1, width)
    owned0 = lax.psum_scatter(owned0, ("x", "z"), scatter_dimension=0, tiled=False)
    small_scan = back0["small"]
    back0.update(backward(("input",), "backward_0_input", 9, saved0, layer0, back0))
    moved0 = [send_shard(back0[f"out{k}"], k) for k in range(SLOTS)]
    dx, gain_grad0 = norm_back(x_f, gain0, sum(p.astype(F32) for p in moved0))
    dtokens = dmiddle.astype(F32) + dx
    def by_row(v):
        rows = jnp.concatenate([v[:piece], v[2 * piece :]], axis=0)
        return jnp.transpose(rows.reshape(-1, SLOTS, quarter), (1, 0, 2))

    def to_section(v0, v1):
        kept = jnp.where(first, v0, v1).astype(F32)
        return kept + swap_section(jnp.where(first, v1, v0)).astype(F32)

    def small_of(by_pair, back, gain_grad):
        return jnp.concatenate(
            [
                by_pair.reshape(-1, LANES),
                back["small_bc"].reshape(-1, LANES),
                back["small_dt"],
                gain_grad.reshape(-1, LANES),
                back["gdt"].reshape(-1, LANES),
            ],
            axis=0,
        )

    small0 = small_of(small_gate + small_scan, back0, gain_grad0)
    small1 = small_of(back1["small"], back1, gain_grad1)
    small_half = to_section(small0, small1)
    small_half = small_half + cross_core(small_half)

    rows1 = by_row(owned1)
    owned0, owned1, rows1, small_half, dtokens = lax.optimization_barrier(
        (owned0, owned1, rows1, small_half, dtokens)
    )

    result_moved = lax.ppermute(result.astype(BF16), "section", [(0, 1)]).astype(F32)
    dtokens_moved = lax.ppermute(dtokens.astype(BF16), "section", [(1, 0)]).astype(F32)
    ends = jnp.where(
        first, jnp.stack([dtokens, dtokens_moved]), jnp.stack([result_moved, result])
    )[None]

    got = across(jnp.concatenate([by_row(owned0), rows1], axis=0))
    out_rows = to_section(owned0[piece : 2 * piece], owned1[piece : 2 * piece]).astype(BF16)
    out_rows = jnp.transpose(out_rows.reshape(piece, SLOTS, quarter), (1, 0, 2))
    rows = got[:SLOTS].astype(F32) + got[SLOTS:].astype(F32)
    shared = jnp.sum(rows[:, 2 * piece :], axis=0).astype(BF16)
    rows = rows.astype(BF16)
    gathered = lax.all_gather(
        jnp.concatenate(
            [
                rows[:, :piece].reshape(-1, quarter),
                out_rows.reshape(-1, quarter),
                rows[:, piece : 2 * piece].reshape(-1, quarter),
                shared,
            ],
            axis=0,
        ),
        DP,
        tiled=False,
    )

    small_sum = sum_small(small_half)
    everyone = in_order(gather_slots(small_sum), 1)
    n_pair, n_bc = PAIRS * 8, 2 * 8
    by_pair = everyone[:, :n_pair].reshape(SLOTS, PAIRS, 8, LANES)
    by_pair = by_pair.transpose(2, 0, 1, 3).reshape(8, inner)
    by_bc = jnp.sum(everyone[:, n_pair : n_pair + n_bc], axis=0)
    by_bc = by_bc.reshape(2, 8, LANES).transpose(1, 0, 2).reshape(8, n_state)
    at = n_pair + n_bc
    by_dt = everyone[:, at : at + 8, :own_heads].transpose(1, 0, 2).reshape(8, heads)
    at += 8
    gain_total = jnp.sum(everyone[:, at : at + width // LANES], axis=0).reshape(-1)
    at += width // LANES
    dt_rows = everyone[:, at:].reshape(SLOTS, 16, SLOTS, quarter)[:, :own_heads]
    dt_rows = pick(dt_rows, j, 2).reshape(heads, quarter)
    conv_total = jnp.concatenate([by_pair[:5], by_bc[:5]], axis=1)
    conv_own = lax.dynamic_slice(conv_total, (0, channels * j), (5, channels))
    grad_skip = jnp.sum(by_pair[6].reshape(heads, HEAD), axis=1)

    grad_in_weight, grad_out_weight = assemble(gathered, dt_rows)
    return (
        ends,
        lax.dynamic_slice(gain_total, (quarter * j,), (quarter,))[None],
        jnp.transpose(grad_in_weight)[None],
        conv_own[None, :4],
        conv_own[4][None],
        by_dt[0][None],
        by_dt[1][None],
        grad_skip[None],
        lax.dynamic_slice(by_pair[5], (own_cols * j,), (own_cols,))[None],
        grad_out_weight[None],
    )


def solution(mesh):
    sections, copies, owners = mesh.devices.shape
    fine = jax.sharding.Mesh(
        mesh.devices.reshape(sections, 2, copies // 4, 2, owners), ("section", *DP, "shard")
    )
    return jax.shard_map(
        shards,
        mesh=fine,
        in_specs=(
            P((*DP, "shard"), None, None),
            P((*DP, "shard"), None, None),
            P((*DP, "shard")),
            P("section", "shard"),
            P("section", "shard", None),
            P("section", None, "shard"),
            P("section", "shard"),
            P("section", None),
            P("section", None),
            P("section", None),
            P("section", "shard"),
            P("section", "shard", None),
        ),
        out_specs=(
            P("section", (*DP, "shard"), None, None),
            P("section", "shard"),
            P("section", "shard", None),
            P("section", None, "shard"),
            P("section", "shard"),
            P("section", None),
            P("section", None),
            P("section", None),
            P("section", "shard"),
            P("section", "shard", None),
        ),
        check_vma=False,
    )
```

```python
import jax
import jax.numpy as jnp
from jax import lax
from jax.experimental import pallas as pl
from jax.experimental.pallas import tpu as pltpu
from jax.sharding import PartitionSpec as P

F32 = jnp.float32
BF16 = jnp.bfloat16
HI = lax.Precision.HIGHEST
EPS = 1e-05
T = 128
LANES = 128
HEAD = 64
SLOTS = 4
ROWS = SLOTS * T
PAIRS = 6
STEPS = 2
HALF = PAIRS // STEPS
WIDE = HALF * LANES
VMEM_LIMIT = 34 * 1024 * 1024
VMEM_MOST = 60 * 1024 * 1024
VMEM_BACK = 40 * 1024 * 1024
DP = ("x", "z", "core")


def sigmoid(v):
    return 0.5 * jnp.tanh(0.5 * v) + 0.5


def softplus(v):
    return jnp.maximum(v, 0.0) + jnp.log1p(jnp.exp(-jnp.abs(v)))


def dot(a, b):
    return jnp.dot(a, b, preferred_element_type=F32)


def dot_nt(a, b, precision=None):
    return lax.dot_general(
        a, b, (((1,), (1,)), ((), ())), preferred_element_type=F32, precision=precision
    )


def dot_tn(a, b, precision=None):
    return lax.dot_general(
        a, b, (((0,), (0,)), ((), ())), preferred_element_type=F32, precision=precision
    )


def iota(axis):
    return lax.broadcasted_iota(jnp.int32, (T, LANES), axis)


def shift_down(v, steps):
    return jnp.where(iota(0) >= steps, pltpu.roll(v, steps, 0), 0.0)


def shift_up(v, steps):
    return jnp.where(iota(0) < T - steps, pltpu.roll(v, T - steps, 0), 0.0)


def conv_taps(cin):
    return [shift_down(cin, 3), shift_down(cin, 2), shift_down(cin, 1), cin]


def conv_sum(taps, par):
    total = par[4:5, :] + taps[0] * par[0:1, :]
    for k in range(1, 4):
        total = total + taps[k] * par[k : k + 1, :]
    return total


def conv_back(dcv, par):
    total = dcv * par[3:4, :]
    for m in range(1, 4):
        total = total + shift_up(dcv, m) * par[3 - m : 4 - m, :]
    return total


def column_sum(v):
    return jnp.sum(v, axis=0, keepdims=True)


def slot(k):
    return slice(k * T, (k + 1) * T)


def tri(lower):
    if lower:
        return (iota(0) >= iota(1)).astype(F32)
    return (iota(0) <= iota(1)).astype(F32)


def step_prep(k, pbc, dtp, run_col, run_row, step_wide):
    step = softplus(pbc[slot(k), 256:384] + dtp[0:1, :])
    run = jnp.dot(tri(True), step * dtp[1:2, :], precision=HI, preferred_element_type=F32)
    run_row[k] = jnp.transpose(run)
    left = iota(1) < HEAD
    for p in range(PAIRS):
        a, b = 2 * p, 2 * p + 1
        run_col[a, slot(k), :] = jnp.broadcast_to(run[:, a : a + 1], (T, LANES))
        run_col[b, slot(k), :] = jnp.broadcast_to(run[:, b : b + 1], (T, LANES))
        step_wide[p, slot(k), :] = jnp.where(
            left,
            jnp.broadcast_to(step[:, a : a + 1], (T, LANES)),
            jnp.broadcast_to(step[:, b : b + 1], (T, LANES)),
        )
    return step


def halves(v):
    left = iota(1) < HEAD
    zero = jnp.zeros_like(v)
    return jnp.concatenate([jnp.where(left, v, zero), jnp.where(left, zero, v)], axis=0)


def in_lanes(columns):
    lane = lax.broadcasted_iota(jnp.int32, (columns[0].shape[0], LANES), 1)
    out = jnp.zeros(lane.shape, F32)
    for n, v in enumerate(columns):
        for k in range(3):
            part = v.astype(BF16).astype(F32)
            out = jnp.where(lane == 3 * n + k, part, out)
            v = v - part
    return out.astype(BF16)


def from_lanes(v, n):
    return sum(v[:, 3 * n + k : 3 * n + k + 1].astype(F32) for k in range(3))


class Refs:
    pass


def kernel_call(body, name, ins, outs, scratch, cost_us, limit=VMEM_LIMIT):
    in_names, out_names, scratch_names = list(ins), list(outs), list(scratch)

    def run(*refs):
        for h in range(STEPS):
            rf = Refs()
            for key, ref in zip(in_names + out_names + scratch_names, refs):
                spec = ins.get(key) or outs.get(key)
                blocks = spec[-2:] if spec and len(spec) > 2 else None
                if blocks and blocks[1](1) != blocks[1](0):
                    at = [
                        slice(n * size, (n + 1) * size) if n else slice(0, size)
                        for n, size in zip(blocks[1](h), blocks[0])
                    ]
                    setattr(rf, key + "_whole", ref)
                    ref = ref.at[tuple(at)]
                setattr(rf, key, ref)
            body(rf, h)

    res = pl.pallas_call(
        run,
        in_specs=[
            pl.BlockSpec(memory_space=pltpu.VMEM if len(ins[n]) > 2 else ins[n][1])
            for n in in_names
        ],
        out_specs=[pl.BlockSpec(memory_space=pltpu.VMEM) for n in out_names],
        out_shape=[jax.ShapeDtypeStruct(outs[n][0], outs[n][1]) for n in out_names],
        scratch_shapes=[
            pltpu.VMEM(*scratch[n]) if isinstance(scratch[n], tuple) else scratch[n]
            for n in scratch_names
        ],
        compiler_params=pltpu.CompilerParams(vmem_limit_bytes=limit),
        cost_estimate=pl.CostEstimate(
            flops=int(cost_us * 1.1e9), bytes_accessed=1 << 20, transcendentals=0
        ),
        name=name,
    )(*[ins[n][0] for n in in_names])
    return dict(zip(out_names, res))


def when(condition):
    return (lambda f: f()) if condition else (lambda f: None)


def whole(v):
    return (v, v.shape, lambda h: (0,) * v.ndim)


def whole_out(shape, dtype):
    return (shape, dtype, shape, lambda h: (0,) * len(shape))


def by_step(v, block):
    return (v, block, lambda h: (h,) + (0,) * (len(block) - 1))


def by_step_out(shape, dtype, block):
    return (shape, dtype, block, lambda h: (h,) + (0,) * (len(block) - 1))


def lanes_by_step(v):
    return (v, (v.shape[0], WIDE), lambda h: (0, h))


def lanes_by_step_out(shape, dtype):
    return (shape, dtype, (shape[0], WIDE), lambda h: (0, h))


def in_hbm(v):
    return (v, pltpu.HBM)


WEIGHT_GROUPS = {"wo": (0, 3), "wg": (3, 3), "wv": (6, 3), "ws": (9, 1)}


class Copies:
    def __init__(self, sems):
        self.sems, self.copies = sems, {}

    def add(self, key, source, target):
        self.copies[key] = (source, target, self.sems.at[len(self.copies)])

    def add_weights(self, rf, keys):
        for key in keys:
            at, count = WEIGHT_GROUPS[key]
            self.add(key, rf.w.at[:, pl.ds(at, count)], getattr(rf, key))

    def start(self):
        for copy in self.copies.values():
            pltpu.make_async_copy(*copy).start()

    def wait(self, *keys):
        for key in keys:
            pltpu.make_async_copy(*self.copies[key]).wait()


def weight_scratch(scratch, keys, width):
    for key in keys:
        scratch[key] = ((16, WEIGHT_GROUPS[key][1], 16, width), BF16)


def half_rows(ref, h):
    v = ref[pl.ds(8 * h, 8)]
    return v.reshape(WIDE, v.shape[-1])


def pair_lanes(p):
    return slice(p * LANES, (p + 1) * LANES)


def flat_rows(ref):
    v = ref[...]
    return v.reshape(-1, v.shape[-1])


def mixed_bc(rf, k, c):
    lanes = slice(c * LANES, (c + 1) * LANES)
    cv = conv_sum(conv_taps(rf.pbc[slot(k), lanes]), rf.pbcv[:, lanes])
    return cv * sigmoid(cv)


def forward(x_slots, g_slots, w, dtw, gain, pv, pbcv, dtp):
    width = x_slots[0].shape[1]
    with_grad = g_slots is not None

    def body(rf, h):
        copies = Copies(rf.sems)
        for k in range(SLOTS):
            copies.add(f"x{k}", getattr(rf, f"x{k}"), rf.x_all.at[k])
        copies.add_weights(rf, ("ws", "wg", "wv", "wo"))
        if with_grad:
            for k in range(SLOTS):
                copies.add(f"g{k}", getattr(rf, f"g{k}"), rf.g_all.at[slot(k)])

        @when(h == 0)
        def _prep():
            copies.start()
            for k in range(SLOTS):
                copies.wait(f"x{k}")
                x = rf.x_all[k].astype(F32)
                scale = lax.rsqrt(jnp.mean(x * x, axis=1, keepdims=True) + EPS)
                rf.normed[slot(k), :] = (x * scale * rf.gain[...]).astype(BF16)
            copies.wait("ws")
            rf.pbc[:, 0:256] = dot_nt(rf.normed[...], flat_rows(rf.ws))
            rf.pbc[:, 256:384] = dot_nt(rf.normed[...], rf.dtw[...])
            for k in range(SLOTS):
                rf.scores[k] = dot_nt(mixed_bc(rf, k, 1), mixed_bc(rf, k, 0), HI) * tri(True)
                step_prep(k, rf.pbc, rf.dtp, rf.run_col, rf.run_row, rf.step_wide)
            rf.square[...] = jnp.zeros_like(rf.square)
            rf.cross[...] = jnp.zeros_like(rf.cross)
            copies.wait("wg", "wv", "wo")
            if with_grad:
                copies.wait(*[f"g{k}" for k in range(SLOTS)])

        rf.proj[0, :, 0:WIDE] = dot_nt(rf.normed[...], half_rows(rf.wg, h))
        rf.proj[0, :, WIDE : 2 * WIDE] = dot_nt(rf.normed[...], half_rows(rf.wv, h))
        if with_grad:
            q_all = dot_nt(rf.g_all[...], half_rows(rf.wo, h))
        for p in range(HALF):
            lanes = pair_lanes(p)
            par = rf.pv[:, lanes]
            pair = HALF * h + p
            for k in range(SLOTS):
                gate = rf.proj[0, slot(k), lanes]
                cv = conv_sum(
                    conv_taps(rf.proj[0, slot(k), WIDE + p * LANES : WIDE + (p + 1) * LANES]), par
                )
                values = cv * sigmoid(cv)
                scaled = (values * rf.step_wide[pair, slot(k), :]).astype(BF16)
                weights = []
                for a in range(2):
                    gap = (
                        rf.run_col[2 * pair + a, slot(k), :]
                        - rf.run_row[k, pl.ds(2 * pair + a, 1), :]
                    )
                    decay = jnp.exp(jnp.minimum(gap, 0.0))
                    weights.append((rf.scores[k] * decay).astype(BF16))
                y = dot(jnp.concatenate(weights, axis=1), halves(scaled))
                rf.y[0, slot(k), lanes] = y
                scanned = y + par[6:7, :] * values
                gated = scanned * (gate * sigmoid(gate))
                rf.square[slot(k), :] += gated * gated
                scaled_out = gated * par[5:6, :]
                rf.u_all[h, slot(k), lanes] = scaled_out.astype(BF16)
                if with_grad:
                    rf.cross[slot(k), :] += q_all[slot(k), lanes] * scaled_out

        @when(h == STEPS - 1)
        def _finish():
            u = jnp.concatenate([rf.u_all[a] for a in range(STEPS)], axis=1)
            for n in range(0, width, 512):
                part = dot(u, rf.wo[:, :, :, n : n + 512].reshape(STEPS * WIDE, 512)).astype(BF16)
                for k in range(SLOTS):
                    getattr(rf, f"out{k}")[:, n : n + 512] = part[slot(k), :]
            for k in range(SLOTS):
                total = jnp.sum(rf.square[slot(k), :], axis=1, keepdims=True)
                getattr(rf, f"out{k}")[:, width:] = in_lanes([total])
            ones = jnp.ones((8, LANES), F32)
            rf.stats[0] = dot_nt(ones, rf.square[...], HI)
            rf.stats[1] = dot_nt(ones, rf.cross[...], HI)

    ins = {f"x{k}": in_hbm(v) for k, v in enumerate(x_slots)}
    if with_grad:
        ins.update({f"g{k}": in_hbm(v) for k, v in enumerate(g_slots)})
    ins.update(
        gain=whole(gain),
        w=in_hbm(w),
        dtw=whole(dtw),
        pv=lanes_by_step(pv),
        pbcv=whole(pbcv),
        dtp=whole(dtp),
    )
    outs = {f"out{k}": whole_out((T, width + LANES), BF16) for k in range(SLOTS)}
    outs.update(
        stats=whole_out((2, 8, ROWS), F32),
        normed=whole_out((ROWS, width), BF16),
        proj=by_step_out((STEPS, ROWS, 2 * WIDE), F32, (1, ROWS, 2 * WIDE)),
        y=by_step_out((STEPS, ROWS, WIDE), F32, (1, ROWS, WIDE)),
        pbc=whole_out((ROWS, 384), F32),
    )
    scratch = dict(
        scores=((SLOTS, T, T), F32),
        run_col=((2 * PAIRS, ROWS, LANES), F32),
        run_row=((SLOTS, T, LANES), F32),
        step_wide=((PAIRS, ROWS, LANES), F32),
        u_all=((STEPS, ROWS, WIDE), BF16),
        square=((ROWS, LANES), F32),
        cross=((ROWS, LANES), F32),
        x_all=((SLOTS, T, width), BF16),
        sems=pltpu.SemaphoreType.DMA((2 * SLOTS + 4,)),
    )
    weight_scratch(scratch, ("ws", "wg", "wv", "wo"), width)
    if with_grad:
        scratch["g_all"] = ((ROWS, width), BF16)
    res = kernel_call(body, "layer_forward", ins, outs, scratch, 18, VMEM_MOST)
    return [res[f"out{k}"] for k in range(SLOTS)], res


def head_columns(pair):
    target = 2 * pair + (iota(0) >= HEAD).astype(jnp.int32)
    one = (iota(1) == target).astype(BF16)
    return jnp.concatenate([one, one], axis=0)


def head_sum(v, columns):
    high = v.astype(BF16)
    low = (v - high.astype(F32)).astype(BF16)
    return dot(jnp.concatenate([high, low], axis=1), columns)


def put_by_core(rf, key, x, at, part):
    keep, send = getattr(rf, key + "_keep"), getattr(rf, key + "_send")
    groups = slice(at, at + part.shape[2])
    for c in range(2):

        @pl.when(rf.core[0] == c)
        def _store(c=c):
            for z in range(4):
                keep[x, z, groups] = part[z, c]
                send[x, z, groups] = part[z, 1 - c]


def backward(stages, name, cost_us, saved, layer, have, limit=VMEM_LIMIT):
    gate, scan, inp, wgate, wscan = (
        s in stages for s in ("gate", "scan", "input", "wgate", "wscan")
    )
    width = saved["normed"].shape[1]
    w, dtw, pv, pbcv, dtp = layer
    elementwise = gate or scan
    fetched = (("wo",) if gate else ()) + (("wg", "wv", "ws") if inp else ())
    in_slots = gate and "rows" not in have

    def body(rf, h):
        copies = Copies(rf.sems) if gate or wgate or inp else None
        if gate or wgate:
            for k in range(SLOTS):
                source = getattr(rf, f"g{k}")
                copies.add(f"g{k}", source.at[:, pl.ds(0, width)], rf.g_all.at[slot(k)])
                if in_slots:
                    copies.add(f"e{k}", source.at[:, pl.ds(width, LANES)], rf.e_all.at[k])
        if copies:
            copies.add_weights(rf, fetched)

        @when(h == 0)
        def _prep():
            if copies:
                copies.start()
            for k in range(SLOTS):
                if gate or wgate:
                    copies.wait(f"g{k}")
                if in_slots:
                    copies.wait(f"e{k}")
                if gate:
                    for row, ref in ((0, rf.scale_row), (1, rf.cross_row)):
                        if "rows" in have:
                            ref[slot(k), :] = jnp.transpose(
                                jnp.broadcast_to(rf.rows[k, row : row + 1, :], (T, LANES))
                            )
                        else:
                            column = from_lanes(rf.e_all[k], row)
                            ref[slot(k), :] = jnp.broadcast_to(column, (T, LANES))
                if scan:
                    inbound, outbound = mixed_bc(rf, k, 0), mixed_bc(rf, k, 1)
                    rf.mixed[0, slot(k), :] = inbound
                    rf.mixed[1, slot(k), :] = outbound
                    rf.scores[k] = dot_nt(inbound, outbound, HI) * tri(False)
                    rf.step_all[slot(k), :] = step_prep(
                        k, rf.pbc, rf.dtp, rf.run_col, rf.run_row, rf.step_wide
                    )
            if scan:
                rf.dscores[...] = jnp.zeros_like(rf.dscores)
                rf.dstep[...] = jnp.zeros_like(rf.dstep)
                rf.drun[...] = jnp.zeros_like(rf.drun)
            if inp:
                rf.total[...] = jnp.zeros_like(rf.total)
            if copies:
                copies.wait(*fetched)

        if gate:
            q_all = dot_nt(rf.g_all[...], half_rows(rf.wo, h))
        for p in range(HALF if elementwise else 0):
            lanes = pair_lanes(p)
            par = rf.pv[:, lanes]
            pair = HALF * h + p
            sums = [jnp.zeros((1, LANES), F32) for _ in range(8)]
            if scan:
                columns = head_columns(pair)
            for k in range(SLOTS):
                taps = conv_taps(rf.proj[0, slot(k), WIDE + p * LANES : WIDE + (p + 1) * LANES])
                cv = conv_sum(taps, par)
                sig_c = sigmoid(cv)
                values = cv * sig_c
                y = rf.y[0, slot(k), lanes]
                if gate:
                    gate_in = rf.proj[0, slot(k), lanes]
                    sig_g = sigmoid(gate_in)
                    silu_g = gate_in * sig_g
                    scanned = y + par[6:7, :] * values
                    gated = scanned * silu_g
                    grad_no = q_all[slot(k), lanes]
                    scale = rf.scale_row[slot(k), :]
                    dgated = scale * (grad_no * par[5:6, :]) - rf.cross_row[slot(k), :] * gated
                    norm = gated * scale
                    sums[5] += column_sum(grad_no * norm)
                    rf.u[slot(k), lanes] = (norm * par[5:6, :]).astype(BF16)
                    dscan = dgated * silu_g
                    dgate = dgated * scanned * (sig_g * (1.0 + gate_in * (1.0 - sig_g)))
                    sums[6] += column_sum(dscan * values)
                    rf.dg[slot(k), lanes] = dgate.astype(BF16)
                    if not scan:
                        rf.dscan[slot(k), lanes] = dscan
                else:
                    dscan = rf.dscan[slot(k), lanes]
                if not scan:
                    continue
                wide = rf.step_wide[pair, slot(k), :]
                dy = dscan.astype(BF16)
                scaled = (values * wide).astype(BF16)
                dweights = dot_nt(halves(scaled), dy)
                weights = []
                dscore = rf.dscores[k]
                for a in range(2):
                    gap = (
                        rf.run_row[k, pl.ds(2 * pair + a, 1), :]
                        - rf.run_col[2 * pair + a, slot(k), :]
                    )
                    decay = jnp.exp(jnp.minimum(gap, 0.0))
                    weights.append((rf.scores[k] * decay).astype(BF16))
                    dscore = dscore + dweights[slot(a), :] * decay
                rf.dscores[k] = dscore
                dscaled = dot(jnp.concatenate(weights, axis=1), halves(dy))
                rf.dstep[slot(k), :] += head_sum(dscaled * values, columns)
                rf.drun[slot(k), :] += head_sum(
                    dy.astype(F32) * y - scaled.astype(F32) * dscaled, columns
                )
                dvalues = dscaled * wide + par[6:7, :] * dscan
                dcv = dvalues * (sig_c * (1.0 + cv * (1.0 - sig_c)))
                for t in range(4):
                    sums[t] += column_sum(dcv * taps[t])
                sums[4] += column_sum(dcv)
                rf.dv[slot(k), lanes] = conv_back(dcv, par).astype(BF16)
            rf.small[p] = jnp.concatenate(sums, axis=0)
        if wgate and wscan:
            for at, left, right in (
                (0, rf.dg, rf.normed),
                (3, rf.u, rf.g_all),
                (6, rf.dv, rf.normed),
            ):
                part = dot_tn(left[...], right[...]).astype(BF16)
                rf.ga[:, at : at + 3] = part.reshape(8, 3, 16, width)
            if not scan:
                part = dot_tn(rf.dbc_half[...], rf.normed[...]).astype(BF16)
                rf.ga[:, 9] = part.reshape(8, 16, width)
        elif wgate:
            for at, left, right in ((0, rf.dg, rf.normed), (3, rf.u, rf.g_all)):
                part = dot_tn(left[...], right[...]).astype(BF16)
                put_by_core(rf, "ga", h, at, part.reshape(4, 2, 3, 16, width))
        elif wscan:
            part = dot_tn(rf.dv[...], rf.normed[...]).astype(BF16)
            put_by_core(rf, "gb", h, 0, part.reshape(4, 2, 3, 16, width))
        if inp:
            rf.total[...] += dot(rf.dg[...], half_rows(rf.wg, h)) + dot(
                rf.dv[...], half_rows(rf.wv, h)
            )

        @when(h == STEPS - 1)
        def _finish():
            if scan:
                sums = [[jnp.zeros((1, LANES), F32) for _ in range(8)] for _ in range(2)]
                dt_sums = [jnp.zeros((1, LANES), F32) for _ in range(8)]
                live = iota(1) < 2 * PAIRS
                for k in range(SLOTS):
                    dscore = rf.dscores[k] * tri(False)
                    dmixed = (
                        jnp.dot(
                            dscore,
                            rf.mixed[1, slot(k), :],
                            precision=HI,
                            preferred_element_type=F32,
                        ),
                        dot_tn(dscore, rf.mixed[0, slot(k), :], HI),
                    )
                    for c in range(2):
                        lanes = slice(c * LANES, (c + 1) * LANES)
                        par = rf.pbcv[:, lanes]
                        taps = conv_taps(rf.pbc[slot(k), lanes])
                        cv = conv_sum(taps, par)
                        sig = sigmoid(cv)
                        dcv = dmixed[c] * (sig * (1.0 + cv * (1.0 - sig)))
                        for t in range(4):
                            sums[c][t] += column_sum(dcv * taps[t])
                        sums[c][4] += column_sum(dcv)
                        rf.dbc[slot(k), lanes] = conv_back(dcv, par).astype(BF16)
                    dlog = jnp.dot(
                        tri(False), rf.drun[slot(k), :], precision=HI, preferred_element_type=F32
                    )
                    grad_step = rf.dstep[slot(k), :] + dlog * rf.dtp[1:2, :]
                    dt_sums[1] += column_sum(dlog * rf.step_all[slot(k), :])
                    draw = grad_step * sigmoid(rf.pbc[slot(k), 256:384] + rf.dtp[0:1, :])
                    draw = jnp.where(live, draw, 0.0)
                    dt_sums[0] += column_sum(draw)
                    rf.dbc[slot(k), 256:384] = draw.astype(BF16)
                rf.small_bc[0] = jnp.concatenate(sums[0], axis=0)
                rf.small_bc[1] = jnp.concatenate(sums[1], axis=0)
                dt_sums[1] = dt_sums[1] * rf.dtp[1:2, :]
                rf.small_dt[...] = jnp.concatenate(dt_sums, axis=0)
            if wscan and wgate and scan:
                part = dot_tn(rf.dbc[:, 0:256], rf.normed[...]).astype(BF16)
                rf.ga_whole[:, 9] = part.reshape(16, 16, width)
            if wscan and not wgate:
                part = dot_tn(rf.dbc[:, 0:256], rf.normed[...]).astype(BF16)
                part = part.reshape(2, 4, 2, 1, 16, width)
                for a in range(2):
                    put_by_core(rf, "gb", a, 3, part[a])
            if wscan:
                rf.gdt[...] = dot_tn(rf.dbc[:, 256:384], rf.normed[...])[0:16]
            if inp:
                final = (
                    rf.total[...]
                    + dot(rf.dbc[:, 0:256], flat_rows(rf.ws))
                    + dot(rf.dbc[:, 256:384], rf.dtw[...])
                )
                for k in range(SLOTS):
                    getattr(rf, f"out{k}")[...] = final[slot(k), :].astype(BF16)

    ins, outs, scratch = {}, {}, {}
    heads_cols = STEPS * WIDE
    if gate or wgate:
        for k, v in enumerate(have["g"]):
            ins[f"g{k}"] = in_hbm(v)
        scratch["g_all"] = ((ROWS, width), BF16)
    if gate:
        if in_slots:
            scratch["e_all"] = ((SLOTS, T, LANES), BF16)
        else:
            ins["rows"] = whole(have["rows"])
        scratch["scale_row"] = ((ROWS, LANES), F32)
        scratch["cross_row"] = ((ROWS, LANES), F32)
        outs["u"] = lanes_by_step_out((ROWS, heads_cols), BF16)
        outs["dg"] = lanes_by_step_out((ROWS, heads_cols), BF16)
        if not scan:
            outs["dscan"] = lanes_by_step_out((ROWS, heads_cols), F32)
    if elementwise:
        ins["proj"] = by_step(saved["proj"], (1, ROWS, 2 * WIDE))
        ins["y"] = by_step(saved["y"], (1, ROWS, WIDE))
        ins["pv"] = lanes_by_step(pv)
        outs["small"] = by_step_out((PAIRS, 8, LANES), F32, (HALF, 8, LANES))
    if scan:
        ins["pbc"] = whole(saved["pbc"])
        ins["pbcv"] = whole(pbcv)
        ins["dtp"] = whole(dtp)
        if not gate:
            ins["dscan"] = lanes_by_step(have["dscan"])
        outs["dv"] = lanes_by_step_out((ROWS, heads_cols), BF16)
        outs["dbc"] = whole_out((ROWS, 384), BF16)
        outs["small_bc"] = whole_out((2, 8, LANES), F32)
        outs["small_dt"] = whole_out((8, LANES), F32)
        scratch.update(
            mixed=((2, ROWS, LANES), F32),
            scores=((SLOTS, T, T), F32),
            run_col=((2 * PAIRS, ROWS, LANES), F32),
            run_row=((SLOTS, T, LANES), F32),
            step_wide=((PAIRS, ROWS, LANES), F32),
            step_all=((ROWS, LANES), F32),
            dscores=((SLOTS, T, T), F32),
            dstep=((ROWS, LANES), F32),
            drun=((ROWS, LANES), F32),
        )
    if inp:
        ins["dtw"] = whole(dtw)
        scratch["total"] = ((ROWS, width), F32)
        outs.update({f"out{k}": whole_out((T, width), BF16) for k in range(SLOTS)})
    if fetched:
        ins["w"] = in_hbm(w)
        weight_scratch(scratch, fetched, width)
    if gate or wgate or inp:
        scratch["sems"] = pltpu.SemaphoreType.DMA((2 * SLOTS + 4,))
    if wgate or wscan:
        ins["normed"] = whole(saved["normed"])
    if not gate and (wgate or inp):
        ins["dg"] = lanes_by_step(have["dg"])
    if wgate and not gate:
        ins["u"] = lanes_by_step(have["u"])
    if not scan and (wscan or inp):
        ins["dv"] = lanes_by_step(have["dv"])
        ins["dbc"] = whole(have["dbc"])
    if wgate and wscan:
        if not scan:
            ins["dbc_half"] = (have["dbc"], (ROWS, LANES), lambda h: (0, h))
        outs["ga"] = by_step_out((16, 10, 16, width), BF16, (8, 10, 16, width))
    elif wgate or wscan:
        ins["core"] = have["core"]
        key, groups = ("ga", 6) if wgate else ("gb", 4)
        for end in ("_keep", "_send"):
            outs[key + end] = whole_out((2, 4, groups, 16, width), BF16)
    if wscan:
        outs["gdt"] = whole_out((16, width), F32)
    return kernel_call(body, name, ins, outs, scratch, cost_us, limit)


def assemble(parts, dt_rows):
    quarter = parts.shape[2]
    block = 16 * 48
    total = 8 * block + 16 * 16 + dt_rows.shape[0]

    def body(inw, outw, shared, dt, grad_in, grad_out):
        i = pl.program_id(0)

        @pl.when(i < 8)
        def _columns():
            grad_in[...] = inw[...].reshape(block, quarter).astype(F32)

        @pl.when(i < SLOTS)
        def _out():
            grad_out[...] = outw[...].reshape(block, quarter).astype(F32)

        @pl.when(i == 8)
        def _shared():
            grad_in[...] = jnp.zeros_like(grad_in)
            grad_in[0:256, :] = shared[...].reshape(256, quarter).astype(F32)
            grad_in[256 : 256 + dt_rows.shape[0], :] = dt[...]

    last = SLOTS - 1
    return pl.pallas_call(
        body,
        grid=(9,),
        in_specs=[
            pl.BlockSpec(
                (16, 48, quarter),
                lambda i: (0, jnp.where(i < SLOTS, i, jnp.minimum(i + SLOTS, 11)), 0),
            ),
            pl.BlockSpec((16, 48, quarter), lambda i: (0, SLOTS + jnp.minimum(i, last), 0)),
            pl.BlockSpec((16, 16, quarter), lambda i: (0, 36, 0)),
            pl.BlockSpec(dt_rows.shape, lambda i: (0, 0)),
        ],
        out_specs=[
            pl.BlockSpec((block, quarter), lambda i: (i, 0)),
            pl.BlockSpec((block, quarter), lambda i: (0, jnp.minimum(i, last))),
        ],
        out_shape=[
            jax.ShapeDtypeStruct((total, quarter), F32),
            jax.ShapeDtypeStruct((block, SLOTS * quarter), F32),
        ],
        compiler_params=pltpu.CompilerParams(vmem_limit_bytes=VMEM_MOST),
        name="assemble",
    )(parts, parts, parts, dt_rows)


def ring(n, k):
    return [(i, (i + k) % n) for i in range(n)]


def send_shard(v, k):
    return lax.ppermute(v, "shard", ring(SLOTS, k)) if k else v


def send_across(v, k):
    pairs = [
        (sec * SLOTS + y, (1 - sec) * SLOTS + (y + k) % SLOTS)
        for sec in range(2)
        for y in range(SLOTS)
    ]
    return lax.ppermute(v, ("section", "shard"), pairs)


def across(v):
    return lax.all_to_all(v, ("section", "shard"), 0, 0)


def swap_section(v):
    return lax.ppermute(v, "section", [(0, 1), (1, 0)])


def dp_index(x, z, c):
    return x * 8 + z * 2 + c


def dp_pairs(move):
    pairs = []
    for x in range(2):
        for z in range(4):
            for c in range(2):
                pairs.append((dp_index(x, z, c), dp_index(*move(x, z, c))))
    return pairs


def pick(v, index, axis):
    return lax.dynamic_index_in_dim(v, index, axis, keepdims=False)


def gather_slots(v):
    return [send_shard(v, (-k) % SLOTS) for k in range(SLOTS)]


def scatter_sum(slots):
    parts = [send_shard(slots[k], k) for k in range(SLOTS)]
    return sum(p.astype(F32) for p in parts)


def cross_core(v):
    return lax.ppermute(v, DP, dp_pairs(lambda x, z, c: (x, z, 1 - c)))


def sum_small(v):
    v = v + lax.ppermute(v, DP, dp_pairs(lambda x, z, c: (x, z, 1 - c)))
    v = v + sum(
        lax.ppermute(v, DP, dp_pairs(lambda x, z, c: (x, (z + k) % 4, c))) for k in range(1, 4)
    )
    return v + lax.ppermute(v, DP, dp_pairs(lambda x, z, c: (1 - x, z, c)))


def in_order(parts, sign):
    j = lax.axis_index("shard")
    stacked = jnp.stack(parts)
    return jnp.take(stacked, (sign * (jnp.arange(SLOTS) - j)) % SLOTS, axis=0)


def shards(
    tokens,
    cotangent,
    lengths,
    norm_gain,
    in_weight,
    conv_weight,
    conv_bias,
    dt_bias,
    a_log,
    d_skip,
    gate_gain,
    out_weight,
):
    sec = lax.axis_index("section")
    d = lax.axis_index(DP)
    j = lax.axis_index("shard")
    core = d % 2
    first = sec == 0
    width = tokens.shape[2]
    quarter = norm_gain.shape[1]
    channels = conv_bias.shape[1]
    own_cols = gate_gain.shape[1]
    inner = own_cols * SLOTS
    heads = dt_bias.shape[1]
    own_heads = heads // SLOTS
    n_state = 2 * LANES
    piece = own_cols // 16
    piece_bc = n_state // 16
    own_core = (core.astype(jnp.int32)[None], pltpu.SMEM)

    x_own = pick(tokens, sec, 0)
    cot = pick(cotangent, sec, 0)
    length = pick(lengths, sec, 0)
    mask = (jnp.arange(T, dtype=jnp.int32) < length).astype(F32)[:, None]

    columns = jnp.transpose(in_weight[0])
    with jax.named_scope("weights"):

        def cut(start, rows):
            return lax.dynamic_slice(columns, (start, 0), (rows, quarter))

        def columns_of(to):
            return jnp.concatenate(
                [
                    cut(own_cols * to + piece * d, piece),
                    cut(inner + own_cols * to + piece * d, piece),
                    cut(2 * inner + piece_bc * d, piece_bc),
                ],
                axis=0,
            )

        cuts = [columns_of((j + k) % SLOTS) for k in range(SLOTS)]
        o_own = lax.dynamic_slice(out_weight[0], (piece * d, 0), (piece, width))
        o_other = swap_section(o_own)

        w_own = [send_shard(cuts[k], k) for k in range(SLOTS)]
        w_other = [send_across(cuts[k], k) for k in range(SLOTS)]

        def from_parts(parts, others, o, o_others, own):
            pieces = [jnp.where(own, p, q) for p, q in zip(parts, others)]
            lanes = []
            for y in range(SLOTS):
                v = pieces[0]
                for k in range(1, SLOTS):
                    v = jnp.where((j - y) % SLOTS == k, pieces[k], v)
                lanes.append(v)
            return jnp.concatenate(
                [jnp.where(own, o, o_others), jnp.concatenate(lanes, axis=1)], axis=0
            )

        w0 = from_parts(w_own, w_other, o_own, o_other, first)
        w1 = from_parts(w_own, w_other, o_own, o_other, ~first)
        w0, w1, x_own, cot = lax.optimization_barrier((w0, w1, x_own, cot))
        w0 = lax.all_gather(w0, DP, axis=0, tiled=False)
        x_slots = gather_slots(x_own)
        x_slots, norm_gain = lax.optimization_barrier((x_slots, norm_gain))

    with jax.named_scope("small_weights"):
        dt_columns = columns[2 * inner + n_state :]
        sizes = [quarter, 4 * channels, channels, own_cols, heads, heads, heads, heads * quarter]
        flat = jnp.concatenate(
            [
                norm_gain[0],
                conv_weight[0].reshape(-1),
                conv_bias[0],
                gate_gain[0],
                dt_bias[0],
                a_log[0],
                d_skip[0],
                dt_columns.reshape(-1),
            ]
        )
        flat = jnp.pad(flat, (0, -flat.shape[0] % LANES)).reshape(-1, LANES)
        own = in_order(gather_slots(flat), 1)
        other = swap_section(own)
        small = [jnp.where(first, own, other), jnp.where(first, other, own)]

        def unpack(v):
            low = v.reshape(SLOTS, -1)
            at = sum(sizes[:-1])
            dtw = low[:, at : at + sizes[-1]].reshape(SLOTS, heads, quarter)
            dtw = lax.dynamic_slice(dtw, (0, own_heads * j, 0), (SLOTS, own_heads, quarter))
            dtw = jnp.transpose(dtw, (1, 0, 2)).reshape(own_heads, width)
            dtw = jnp.pad(dtw, ((0, LANES - own_heads), (0, 0)))
            v = low[:, :at].astype(F32)
            cut, at = [], 0
            for size in sizes[:-1]:
                cut.append(v[:, at : at + size])
                at += size
            gain = cut[0].reshape(1, width)
            taps = cut[1].reshape(SLOTS, 4, channels).transpose(1, 0, 2).reshape(4, -1)
            bias = cut[2].reshape(1, -1)
            conv = jnp.concatenate([taps, bias, jnp.zeros((3, taps.shape[1]), F32)], axis=0)
            pbcv = conv[:, inner:]
            pv = lax.dynamic_slice(conv, (0, own_cols * j), (8, own_cols))
            pick_heads = lambda u: lax.dynamic_slice(u[0], (own_heads * j,), (own_heads,))
            wide = jnp.repeat(pick_heads(cut[6]), HEAD)[None]
            pv = jnp.concatenate([pv[:5], pick(cut[3], j, 0)[None], wide, pv[7:]], axis=0)
            dtp = jnp.stack([pick_heads(cut[4]), -jnp.exp(pick_heads(cut[5]))])
            dtp = jnp.pad(dtp, ((0, 6), (0, LANES - own_heads)))
            return gain, dtw, pv, pbcv, dtp

        gain0, *params0 = unpack(small[0])
        gain1, *params1 = unpack(small[1])

    x_f = x_own.astype(F32)
    g1 = (mask * cot.astype(F32)).astype(BF16)
    g1_slots = gather_slots(g1)
    w0, x_slots, g1_slots, gain0, params0, gain1, params1, w1 = lax.optimization_barrier(
        (w0, x_slots, g1_slots, gain0, params0, gain1, params1, w1)
    )
    w1 = lax.all_gather(w1, DP, axis=0, tiled=False)
    blocks = lambda v: v.reshape(16, 10, 16, width)

    layer0 = (blocks(w0), *params0)
    layer1 = (blocks(w1), *params1)

    def forward_layer(x, g, gain, layer):
        w, dtw, pv, pbcv, dtp = layer
        return forward(x, g, w, dtw, gain, pv, pbcv, dtp)

    parts, saved0 = forward_layer(x_slots, None, gain0, layer0)
    branch = scatter_sum(parts)
    square = jnp.sum(branch[:, width : width + 3], axis=1, keepdims=True)
    scale0 = lax.rsqrt(square / inner + EPS)
    branch0 = branch[:, :width] * scale0
    middle = (x_f + mask * branch0).astype(BF16)

    m_slots = gather_slots(middle)
    branch_parts, saved1 = forward_layer(m_slots, g1_slots, gain1, layer1)
    own = saved1["stats"][:, 0].reshape(2, SLOTS, T)
    back = [send_shard(own, k) for k in range(SLOTS)]
    summed = sum(jnp.roll(back[k], -k, axis=1) for k in range(SLOTS))
    scale1 = lax.rsqrt(summed[0] / inner + EPS)
    cross1 = scale1 * scale1 * scale1 * summed[1] / inner
    rows1 = jnp.pad(jnp.stack([scale1, cross1], axis=1), ((0, 0), (0, 6), (0, 0)))

    def norm_back(x, gain, grad):
        scale = lax.rsqrt(jnp.mean(x * x, axis=1, keepdims=True) + EPS)
        unit = x * scale
        dn = grad * gain
        dx = scale * (dn - unit * jnp.mean(dn * unit, axis=1, keepdims=True))
        return dx, jnp.sum(grad * unit, axis=0)

    back1 = backward(
        ("gate", "scan", "input", "wgate", "wscan"),
        "backward_1",
        28,
        saved1,
        layer1,
        {"g": g1_slots, "rows": rows1},
        VMEM_BACK,
    )
    moved = [send_shard(back1[f"out{k}"], k) for k in range(SLOTS)]
    dx, gain_grad1 = norm_back(middle.astype(F32), gain1, sum(p.astype(F32) for p in moved))
    by_owner = lambda v: v.reshape(16, -1, width)
    owned1 = lax.psum_scatter(by_owner(back1["ga"]), DP, scatter_dimension=0, tiled=False)

    dmiddle = (cot.astype(F32) + dx).astype(BF16)
    g0 = (mask * dmiddle.astype(F32)).astype(BF16)
    cross0 = scale0 * scale0 * jnp.sum(g0.astype(F32) * branch0, axis=1, keepdims=True) / inner
    g0_slots = gather_slots(jnp.concatenate([g0, in_lanes([scale0, cross0])], axis=1))
    g0_slots, branch_parts = lax.optimization_barrier((g0_slots, branch_parts))
    branch = scatter_sum(branch_parts)[:, :width] * scale1[0][:, None]
    result = middle.astype(F32) + mask * branch

    back0 = backward(
        ("gate", "wgate"),
        "backward_0_gate",
        14,
        saved0,
        layer0,
        {"g": g0_slots, "core": own_core},
    )
    both = lambda kept, moved: (kept.astype(F32) + moved.astype(F32)).astype(BF16)
    a_moved = cross_core(back0["ga_send"])
    small_gate = back0["small"]
    back0["core"] = own_core
    back0.update(backward(("scan", "wscan"), "backward_0_scan", 20, saved0, layer0, back0))
    gb_send, a_moved = lax.optimization_barrier((back0["gb_send"], a_moved))
    a0 = both(back0["ga_keep"], a_moved)
    b_moved, owned1 = lax.optimization_barrier((cross_core(gb_send), owned1))
    b0 = both(back0["gb_keep"], b_moved)
    owned0 = jnp.pad(a0, ((0, 0), (0, 0), (0, 4), (0, 0), (0, 0)))
    owned0 = lax.dynamic_update_slice(owned0, b0, (0, 0, 6, 0, 0)).reshape(8, -1, width)
    owned0 = lax.psum_scatter(owned0, ("x", "z"), scatter_dimension=0, tiled=False)
    small_scan = back0["small"]
    back0.update(backward(("input",), "backward_0_input", 9, saved0, layer0, back0))
    moved0 = [send_shard(back0[f"out{k}"], k) for k in range(SLOTS)]
    dx, gain_grad0 = norm_back(x_f, gain0, sum(p.astype(F32) for p in moved0))
    dtokens = dmiddle.astype(F32) + dx
    def by_row(v):
        rows = jnp.concatenate([v[:piece], v[2 * piece :]], axis=0)
        return jnp.transpose(rows.reshape(-1, SLOTS, quarter), (1, 0, 2))

    rows1 = by_row(owned1)
    owned0, owned1, rows1, gain_grad0, dtokens, result = lax.optimization_barrier(
        (owned0, owned1, rows1, gain_grad0, dtokens, result)
    )

    result_moved = lax.ppermute(result.astype(BF16), "section", [(0, 1)]).astype(F32)
    dtokens_moved = lax.ppermute(dtokens.astype(BF16), "section", [(1, 0)]).astype(F32)
    ends = jnp.where(
        first, jnp.stack([dtokens, dtokens_moved]), jnp.stack([result_moved, result])
    )[None]

    def to_section(v0, v1):
        kept = jnp.where(first, v0, v1).astype(F32)
        return kept + swap_section(jnp.where(first, v1, v0)).astype(F32)

    got = across(jnp.concatenate([by_row(owned0), rows1], axis=0))
    out_rows = to_section(owned0[piece : 2 * piece], owned1[piece : 2 * piece]).astype(BF16)
    out_rows = jnp.transpose(out_rows.reshape(piece, SLOTS, quarter), (1, 0, 2))
    rows = got[:SLOTS].astype(F32) + got[SLOTS:].astype(F32)
    shared = jnp.sum(rows[:, 2 * piece :], axis=0).astype(BF16)
    rows = rows.astype(BF16)
    gathered = lax.all_gather(
        jnp.concatenate(
            [
                rows[:, :piece].reshape(-1, quarter),
                out_rows.reshape(-1, quarter),
                rows[:, piece : 2 * piece].reshape(-1, quarter),
                shared,
            ],
            axis=0,
        ),
        DP,
        tiled=False,
    )

    def small_of(by_pair, back, gain_grad):
        return jnp.concatenate(
            [
                by_pair.reshape(-1, LANES),
                back["small_bc"].reshape(-1, LANES),
                back["small_dt"],
                gain_grad.reshape(-1, LANES),
                back["gdt"].reshape(-1, LANES),
            ],
            axis=0,
        )

    small0 = small_of(small_gate + small_scan, back0, gain_grad0)
    small1 = small_of(back1["small"], back1, gain_grad1)
    small_sum = sum_small(to_section(small0, small1))
    everyone = in_order(gather_slots(small_sum), 1)
    n_pair, n_bc = PAIRS * 8, 2 * 8
    by_pair = everyone[:, :n_pair].reshape(SLOTS, PAIRS, 8, LANES)
    by_pair = by_pair.transpose(2, 0, 1, 3).reshape(8, inner)
    by_bc = jnp.sum(everyone[:, n_pair : n_pair + n_bc], axis=0)
    by_bc = by_bc.reshape(2, 8, LANES).transpose(1, 0, 2).reshape(8, n_state)
    at = n_pair + n_bc
    by_dt = everyone[:, at : at + 8, :own_heads].transpose(1, 0, 2).reshape(8, heads)
    at += 8
    gain_total = jnp.sum(everyone[:, at : at + width // LANES], axis=0).reshape(-1)
    at += width // LANES
    dt_rows = everyone[:, at:].reshape(SLOTS, 16, SLOTS, quarter)[:, :own_heads]
    dt_rows = pick(dt_rows, j, 2).reshape(heads, quarter)
    conv_total = jnp.concatenate([by_pair[:5], by_bc[:5]], axis=1)
    conv_own = lax.dynamic_slice(conv_total, (0, channels * j), (5, channels))
    grad_skip = jnp.sum(by_pair[6].reshape(heads, HEAD), axis=1)

    grad_in_weight, grad_out_weight = assemble(gathered, dt_rows)
    return (
        ends,
        lax.dynamic_slice(gain_total, (quarter * j,), (quarter,))[None],
        jnp.transpose(grad_in_weight)[None],
        conv_own[None, :4],
        conv_own[4][None],
        by_dt[0][None],
        by_dt[1][None],
        grad_skip[None],
        lax.dynamic_slice(by_pair[5], (own_cols * j,), (own_cols,))[None],
        grad_out_weight[None],
    )


def solution(mesh):
    sections, copies, owners = mesh.devices.shape
    fine = jax.sharding.Mesh(
        mesh.devices.reshape(sections, 2, copies // 4, 2, owners), ("section", *DP, "shard")
    )
    return jax.shard_map(
        shards,
        mesh=fine,
        in_specs=(
            P((*DP, "shard"), None, None),
            P((*DP, "shard"), None, None),
            P((*DP, "shard")),
            P("section", "shard"),
            P("section", "shard", None),
            P("section", None, "shard"),
            P("section", "shard"),
            P("section", None),
            P("section", None),
            P("section", None),
            P("section", "shard"),
            P("section", "shard", None),
        ),
        out_specs=(
            P("section", (*DP, "shard"), None, None),
            P("section", "shard"),
            P("section", "shard", None),
            P("section", None, "shard"),
            P("section", "shard"),
            P("section", None),
            P("section", None),
            P("section", None),
            P("section", "shard"),
            P("section", "shard", None),
        ),
        check_vma=False,
    )
```
